512 devices in a mesh: lon: 32 (over y, z_hi, core), lat: 16 (over x, z_lo).
Axes of the slice: x: 4, y: 8, z: 8 (z_hi: 2, z_lo: 4; z = z_hi * 4 + z_lo), core: 2. Of those that a mesh axis runs over, the one named last changes fastest.
Arguments:
- temp: float32 [8, 384, 4096], P(None, 'lat', 'lon'), may hold values from -6 to 6
- kmt: int32 [384, 4096], P('lat', 'lon'), may hold values from 0 to 8
- kappa: float32 [384, 4096], P('lat', 'lon'), may hold values from 0.05 to 0.5
- helm: float32 [384, 4096], P('lat', 'lon'), may hold values from 0.02 to 0.2
- forcing: float32 [384, 4096], P('lat', 'lon'), may hold values from -6 to 6
- cutoff: int32 [384], P('lat'), may hold values from 256 to 2049, as said below
- conv_in: bfloat16 [9, 64, 8], replicated, may hold values from -0.75 to 0.75
- conv_mid: bfloat16 [9, 64, 64], replicated, may hold values from -0.25 to 0.25
- conv_late: bfloat16 [9, 64, 64], replicated, may hold values from -0.25 to 0.25
- conv_out: bfloat16 [9, 8, 64], replicated, may hold values from -0.25 to 0.25
Outputs:
- temp_new: float32 [8, 384, 4096], P(None, 'lat', 'lon')
- surface: float32 [384, 4096], P('lat', 'lon')
- residual: float32 [384, 4096], P('lat', 'lon')
The draws below stay inside these ranges and needn't reach their ends.
Inputs may be any that keep to these rules, and one draw needn't show every extreme that they name: `cutoff`: rows outside the 48 rows nearest each pole keep every wavenumber; the first row keeps 4096 // 16.
All inputs are finite; a program needn't handle non-finite values.
Results may differ from the reference program's by a relative error of at most 0.0003.
Values may be sent and summed in bfloat16 or wider, within the bound.
No kernel may reach another device: no remote copies, remote signals or barrier semaphores. Data moves between devices by JAX's collectives and lax.ppermute only.
A program may use at most 64 MiB of HBM per device.

```python
import math
import jax
import jax.numpy as jnp
from jax import lax

LEV = 8
CH = 64
CLAT = 24
ITERS = 4
NLAT = 384
NLON = 4096


def draw_cutoff(key, part):
    key = jax.random.fold_in(key, 11)
    rows = jnp.arange(NLAT, dtype=jnp.int32)
    band = NLAT // 8
    polar = (rows < band) | (rows >= NLAT - band)
    lowest = NLON // 16
    full = NLON // 2 + 1
    drawn = jax.random.randint(key, (NLAT,), lowest, full, dtype=jnp.int32)
    kept = jnp.where(polar, drawn, full)
    return jnp.where(rows == 0, lowest, kept).astype(jnp.int32)


def touch_ends(values, own_key, least, high):
    longest = values.shape.index(max(values.shape))
    spots = []
    for shift in (0, 1):
        where = [jax.random.randint(jax.random.fold_in(own_key, axis), (), 0, length) for axis, length in enumerate(values.shape)]
        where[longest] = (where[longest] + shift) % values.shape[longest]
        spots.append(tuple(where))
    return values.at[spots[0]].set(least).at[spots[1]].set(high)


def block_levels(stream_key, dims, pieces, low, high):
    def one(axis_at, parts):
        draws = jax.random.uniform(jax.random.fold_in(jax.random.fold_in(stream_key, 6), axis_at), (parts,), jnp.float32, low / len(pieces), high / len(pieces))
        return jnp.repeat(jnp.exp(draws), dims[axis_at] // parts).reshape((-1,) + (1,) * (len(dims) - axis_at - 1))

    gain = one(*pieces[0])
    for cut in pieces[1:]:
        gain = gain * one(*cut)
    return gain


def scatter_about(key, dims, scale, reach, cuts=(), held_as=jnp.bfloat16):
    array = scale * jax.random.normal(key, dims, jnp.float32)
    if cuts:
        array = array * block_levels(key, dims, cuts, -0.22, 0.18)
    return jnp.clip(array, -reach, reach).astype(held_as)


def setup_inputs(seed: int = 0) -> dict:
    key_of = jax.random.split(jax.random.key(seed), 11)
    return {
        "temp": scatter_about(key_of[0], (LEV, NLAT, NLON), 1.0, 6.0, ((1, 16), (2, 32)), jnp.float32),
        "kmt": touch_ends(jax.random.randint(key_of[1], (NLAT, NLON), 0, LEV + 1), jax.random.fold_in(key_of[1], 1), 0, LEV).astype(jnp.int32),
        "kappa": jnp.clip(jnp.exp(math.log(0.5) - 2.3025851 * jax.random.uniform(key_of[2], (NLAT, NLON), jnp.float32) ** block_levels(key_of[2], (NLAT, NLON), ((0, 16), (1, 32)), -0.2, 0.2)), 0.05, 0.5),
        "helm": jnp.clip(jnp.exp(math.log(0.2) - 2.3025851 * jax.random.uniform(key_of[3], (NLAT, NLON), jnp.float32) ** block_levels(key_of[3], (NLAT, NLON), ((0, 16), (1, 32)), -0.2, 0.2)), 0.02, 0.2),
        "forcing": scatter_about(key_of[4], (NLAT, NLON), 1.0, 6.0, ((0, 16), (1, 32)), jnp.float32),
        "cutoff": draw_cutoff(jax.random.fold_in(key_of[10], 71), 0),
        "conv_in": scatter_about(key_of[6], (9, CH, LEV), (9 * LEV) ** -0.5, 0.75),
        "conv_mid": scatter_about(key_of[7], (9, CH, CH), (9 * CH) ** -0.5, 0.25),
        "conv_late": scatter_about(key_of[8], (9, CH, CH), (9 * CH) ** -0.5, 0.25),
        "conv_out": scatter_about(key_of[9], (9, LEV, CH), (9 * CH) ** -0.5, 0.25),
    }


step_size = 0.25


def pad_whole(field, width):
    wide = jnp.concatenate([field[..., -width:], field, field[..., :width]], axis=-1)
    return jnp.pad(wide, ((0, 0), (width, width), (0, 0)))


def neighbours(padded):
    return [padded[:, 2:, 1:-1], padded[:, :-2, 1:-1], padded[:, 1:-1, 2:], padded[:, 1:-1, :-2]]


def centre(padded):
    return padded[:, 1:-1, 1:-1]


def diffuse(padded, levels):
    tracer = padded[:levels]
    wetness = padded[levels:2 * levels]
    diffusive = padded[2 * levels:]
    total = jnp.zeros(centre(tracer).shape, jnp.float32)
    for near_t, near_w, near_k in zip(neighbours(tracer), neighbours(wetness), neighbours(diffusive)):
        total = total + near_w * 0.5 * (centre(diffusive) + near_k) * (near_t - centre(tracer))
    return centre(wetness) * total


def convolve(padded, weight):
    rows = padded.shape[1] - 2
    cols = padded.shape[2] - 2
    total = jnp.zeros((weight.shape[1], rows, cols), jnp.float32)
    for tap in range(9):
        shift_a = tap // 3
        shift_b = tap % 3
        piece = padded[:, shift_a:shift_a + rows, shift_b:shift_b + cols].astype(jnp.float32)
        total = total + jnp.einsum('oc,chw->ohw', weight[tap].astype(jnp.float32), piece)
    return total


def operate(field, sea_pad, helm):
    padded = pad_whole(field, 1)
    result = helm[None] * field
    for near_v, near_s in zip(neighbours(padded), neighbours(sea_pad)):
        result = result + centre(sea_pad) * near_s * (field - near_v)
    return result


def reference(temp, kmt, kappa, helm, forcing, cutoff, conv_in, conv_mid, conv_late, conv_out):
    levels = jnp.arange(LEV, dtype=jnp.int32)[:, None, None]
    wet = (levels < kmt[None]).astype(jnp.float32)
    sea = wet[0]
    stack = jnp.concatenate([wet * temp, wet, kappa[None]], axis=0)
    padded = pad_whole(stack, 1)
    diff = diffuse(padded, LEV)
    inputs = jnp.concatenate([(wet * temp).astype(jnp.bfloat16), sea[None].astype(jnp.bfloat16)], axis=0)
    big = pad_whole(inputs, 4)

    def block(index):
        part = lax.dynamic_slice_in_dim(big, (index * CLAT).astype(jnp.int32), CLAT + 8, 1)
        seam = part[LEV:].astype(jnp.float32)
        hidden = part[:LEV]
        for depth, weight in enumerate([conv_in, conv_mid, conv_late]):
            mask = seam[:, 1 + depth:seam.shape[1] - 1 - depth, 1 + depth:seam.shape[2] - 1 - depth]
            hidden = (mask * jax.nn.silu(convolve(hidden, weight))).astype(jnp.bfloat16)
        return convolve(hidden, conv_out)

    blocks = lax.map(block, jnp.arange(NLAT // CLAT, dtype=jnp.int32))
    eddy = wet * jnp.transpose(blocks, (1, 0, 2, 3)).reshape(LEV, NLAT, NLON)
    advanced = wet * (temp + step_size * (diff + eddy))
    spectrum = jnp.fft.fft(advanced, axis=-1)
    wave = jnp.arange(NLON, dtype=jnp.int32)
    folded = jnp.minimum(wave, NLON - wave)
    keep = folded[None, None, :] < cutoff[None, :, None]
    temp_new = jnp.fft.ifft(jnp.where(keep, spectrum, 0.0), axis=-1).real.astype(jnp.float32)
    rhs = sea * (jnp.sum(wet * temp_new, axis=0) / LEV + forcing)
    sea_pad = pad_whole(sea[None], 1)
    surface = jnp.zeros((1, NLAT, NLON), jnp.float32)
    residual = rhs[None]
    direction = residual
    norm_now = jnp.sum(residual * residual)
    for step in range(ITERS):
        image = operate(direction, sea_pad, helm)
        alpha = norm_now / jnp.sum(direction * image)
        surface = surface + alpha * direction
        residual = residual - alpha * image
        norm_next = jnp.sum(residual * residual)
        direction = residual + (norm_next / norm_now) * direction
        norm_now = norm_next
    return temp_new, surface[0], residual[0]
```

```python
import functools
import math

import jax
import jax.numpy as jnp
import numpy as np
from jax import lax
from jax.experimental import pallas as pl
from jax.experimental.pallas import tpu as pltpu
from jax.sharding import PartitionSpec as P

ITERS = 4
STEP = 0.25
LEV = 8
FIELDS = 16
KMT, KAPPA, HELM, FORCING, CUT = 8, 9, 10, 11, 12
HALO = 4
DEEP = 8
ROWS = 24
COLS = 128
TALL = ROWS + 2 * DEEP
WIDE = COLS + 2 * HALO
MID = ROWS + 2 * HALO
SLOTS = 20
VMEM_LIMIT = 48 * 1024 * 1024
highest = lax.Precision.HIGHEST


def call(kernel, outs, scratch=(), ins=None):
    spec = pl.BlockSpec(memory_space=pltpu.VMEM)
    return pl.pallas_call(
        kernel,
        out_shape=outs,
        out_specs=jax.tree.map(lambda _: spec, outs),
        scratch_shapes=scratch,
        compiler_params=pltpu.CompilerParams(vmem_limit_bytes=VMEM_LIMIT),
    )


def lane_index(shape):
    return lax.broadcasted_iota(jnp.int32, shape, len(shape) - 1)


def pack_kernel(own_ref, north_ref, south_ref, west_ref, east_ref):
    lane = lane_index((FIELDS, COLS))
    for part in range(TALL // SLOTS):
        first = jnp.zeros((FIELDS, COLS), jnp.float32)
        last = jnp.zeros((FIELDS, COLS), jnp.float32)
        for slot in range(SLOTS):
            row = part * SLOTS + slot
            if row < DEEP:
                here = north_ref[row]
            elif row < DEEP + ROWS:
                here = own_ref[row - DEEP]
            else:
                here = south_ref[row - DEEP - ROWS]
            inside = (lane >= HALO * slot) & (lane < HALO * (slot + 1))
            first = jnp.where(inside, pltpu.roll(here, HALO * slot, 1) if slot else here, first)
            last = jnp.where(inside, pltpu.roll(here, HALO * (slot + 1), 1), last)
        west_ref[part] = first
        east_ref[part] = last


def closure_kernel(
    own_ref,
    north_ref,
    south_ref,
    from_west_ref,
    from_east_ref,
    w_in_ref,
    w_mid_ref,
    w_late_ref,
    w_out_ref,
    out_ref,
    planes_ref,
    line_ref,
    ext,
    start,
    mask_odd,
    mask_even,
    act_a,
    act_b,
):
    lane = lane_index((FIELDS, COLS))
    depth = lax.broadcasted_iota(jnp.int32, (LEV, 2 * COLS), 0).astype(jnp.float32)
    for row in range(TALL):
        if row < DEEP:
            here = north_ref[row]
        elif row < DEEP + ROWS:
            here = own_ref[row - DEEP]
        else:
            here = south_ref[row - DEEP - ROWS]
        part, slot = row // SLOTS, row % SLOTS
        west = from_west_ref[part]
        if slot:
            west = pltpu.roll(west, COLS - HALO * slot, 1)
        east = from_east_ref[part]
        shift = (HALO - HALO * slot) % COLS
        if shift:
            east = pltpu.roll(east, shift, 1)
        moved = pltpu.roll(here, HALO, 1)
        ext[row, :, 0:COLS] = jnp.where(lane < HALO, west, moved)
        ext[row, :, COLS:] = jnp.where(
            lane < HALO, moved, jnp.where(lane < 2 * HALO, east, 0.0)
        )
    for row in range(TALL):
        wet = (depth < ext[row, KMT : KMT + 1, :]).astype(jnp.float32)
        start[row * FIELDS : row * FIELDS + LEV] = (wet * ext[row, 0:LEV, :]).astype(jnp.bfloat16)
        start[row * FIELDS + LEV : (row + 1) * FIELDS] = jnp.where(depth == 0, wet, 0.0).astype(
            jnp.bfloat16
        )

    def finish(total, mask):
        v = (
            pltpu.roll(total[:, 0:128], 1, 0)
            + total[:, 128:256]
            + pltpu.roll(total[:, 256:384], WIDE - 1, 0)
        )
        return (mask * (v / (1.0 + jnp.exp(-v)))).astype(jnp.bfloat16)

    for pair in range(19):
        window = start[2 * FIELDS * pair : 2 * FIELDS * (pair + 2), 0:WIDE]
        total = lax.dot_general(
            window, w_in_ref[...], (((0,), (0,)), ((), ())), preferred_element_type=jnp.float32
        )
        mask_odd[pair] = total[:, 384:512]
        mask_even[pair] = total[:, 512:640]
        act_a[pair] = finish(total, total[:, 384:512])
    for pair in range(18):
        both = jnp.concatenate([act_a[pair], act_a[pair + 1]], axis=1)
        total = jnp.dot(both, w_mid_ref[...], preferred_element_type=jnp.float32)
        act_b[pair] = finish(total, mask_even[pair])
    for pair in range(17):
        both = jnp.concatenate([act_b[pair], act_b[pair + 1]], axis=1)
        total = jnp.dot(both, w_late_ref[...], preferred_element_type=jnp.float32)
        act_a[pair] = finish(total, mask_odd[pair + 1])

    def cut(block, by):
        return pltpu.roll(block, 2 * COLS - by, 1)[:, 0:COLS]

    def wetness(row):
        return (depth < ext[row, KMT : KMT + 1, :]).astype(jnp.float32)

    for pair in range(16):
        both = jnp.concatenate([act_a[pair], act_a[pair + 1]], axis=1)
        total = lax.dot_general(
            w_out_ref[...], both, (((1,), (1,)), ((), ())), preferred_element_type=jnp.float32
        )
        total = jnp.concatenate(
            [total, jnp.zeros((48, 2 * COLS - WIDE), jnp.float32)], axis=1
        )
        closure = cut(total[0:16], HALO - 1) + cut(total[16:32], HALO) + cut(total[32:48], HALO + 1)
        for parity in range(2):
            row = DEEP - HALO + 2 * pair + parity
            wet_wide = wetness(row)
            tracer_wide = wet_wide * ext[row, 0:LEV, :]
            kappa_wide = ext[row, KAPPA : KAPPA + 1, :]
            wet = cut(wet_wide, HALO)
            tracer = cut(tracer_wide, HALO)
            kappa = cut(jnp.broadcast_to(kappa_wide, (LEV, 2 * COLS)), HALO)
            diff = jnp.zeros((LEV, COLS), jnp.float32)
            for near in (row + 1, row - 1):
                near_w = wetness(near)
                near_t = near_w * ext[near, 0:LEV, :]
                near_k = jnp.broadcast_to(ext[near, KAPPA : KAPPA + 1, :], (LEV, 2 * COLS))
                diff = diff + cut(near_w, HALO) * 0.5 * (kappa + cut(near_k, HALO)) * (
                    cut(near_t, HALO) - tracer
                )
            for by in (HALO + 1, HALO - 1):
                diff = diff + cut(wet_wide, by) * 0.5 * (
                    kappa + cut(jnp.broadcast_to(kappa_wide, (LEV, 2 * COLS)), by)
                ) * (cut(tracer_wide, by) - tracer)
            diff = wet * diff
            eddy = wet * closure[LEV * parity : LEV * (parity + 1)]
            temp = cut(ext[row, 0:LEV, :], HALO)
            out_ref[2 * pair + parity] = wet * (temp + STEP * (diff + eddy))
    first = DEEP - HALO
    for index, field in enumerate((KMT, HELM, FORCING)):
        planes_ref[index] = jnp.concatenate(
            [ext[row, field : field + 1, :] for row in range(first, first + MID)], axis=0
        )
    own_line = lax.axis_index("lon") + first
    line_ref[...] = ext[own_line, LEV:FIELDS, HALO : HALO + 1] + jnp.zeros((LEV, COLS), jnp.float32)


def filter_tables(blocks, width):
    length = blocks * width
    half = LEV // 2
    k = np.arange(blocks)
    outer = np.exp(-2j * np.pi * ((k[:, None] * k[None, :]) % blocks) / blocks)
    spread = np.zeros((blocks, 2, half, blocks, 2, half))
    for line in range(half):
        spread[:, 0, line, :, 0, line] = outer.real
        spread[:, 0, line, :, 1, line] = -outer.imag
        spread[:, 1, line, :, 0, line] = outer.imag
        spread[:, 1, line, :, 1, line] = outer.real
    spread = spread.reshape(blocks * LEV, blocks * LEV)
    m = np.arange(width)
    twist = np.exp(-2j * np.pi * (k[:, None] * m[None, :]) / length)
    sign = np.where(np.arange(LEV) < half, -1.0, 1.0)[None, :, None]
    twist_re = np.broadcast_to(twist.real[:, None, :], (blocks, LEV, width))
    twist_im = twist.imag[:, None, :] * sign
    inner = np.exp(-2j * np.pi * ((m[:, None] * m[None, :]) % width) / width)
    inner = np.concatenate([inner.real, inner.imag], axis=1)
    return [
        np.asarray(t, np.float32)
        for t in (spread, spread.T / length, twist_re, twist_im, inner)
    ]


def filter_kernel(
    x_ref, line_ref, spread_ref, back_ref, twist_re_ref, twist_im_ref, inner_ref, out_ref
):
    blocks, lev, width = x_ref.shape
    shape = (blocks, lev, width)
    length = blocks * width

    def partner(block):
        return pltpu.roll(block, lev // 2, 1)

    sign = jnp.where(lax.broadcasted_iota(jnp.int32, shape, 1) < lev // 2, -1.0, 1.0)
    x = x_ref[...].reshape(blocks * lev, width)
    y = jnp.dot(spread_ref[...], x, precision=highest, preferred_element_type=jnp.float32)
    y = y.reshape(shape)
    y = y * twist_re_ref[...] + partner(y) * twist_im_ref[...]
    s = jnp.dot(
        y.reshape(blocks * lev, width),
        inner_ref[...],
        precision=highest,
        preferred_element_type=jnp.float32,
    )
    s = s[:, 0:width].reshape(shape) + partner(s[:, width:].reshape(shape)) * sign
    wave = lax.broadcasted_iota(jnp.int32, shape, 0) + blocks * lane_index(shape)
    folded = jnp.minimum(wave, length - wave).astype(jnp.float32)
    s = jnp.where(folded < line_ref[CUT - LEV : CUT - LEV + 1, :][None], s, 0.0)
    y = jnp.dot(
        s.reshape(blocks * lev, width),
        inner_ref[...],
        precision=highest,
        preferred_element_type=jnp.float32,
    )
    y = y[:, 0:width].reshape(shape) - partner(y[:, width:].reshape(shape)) * sign
    y = y * twist_re_ref[...] - partner(y) * twist_im_ref[...]
    x = jnp.dot(
        back_ref[...],
        y.reshape(blocks * lev, width),
        precision=highest,
        preferred_element_type=jnp.float32,
    ).reshape(shape)
    out_ref[:, 0:lev, :] = x
    lane = lane_index((lev, width))
    for block in range(blocks):
        west = pltpu.roll(x[(block - 1) % blocks], HALO, 1)
        east = pltpu.roll(x[(block + 1) % blocks], HALO, 1)
        out_ref[block, lev : 2 * lev, :] = jnp.where(lane < HALO, west, east)


def two_sum(a, b):
    s = a + b
    t = s - a
    return s, (a - (s - t)) + (b - t)


def quick_sum(a, b):
    s = a + b
    return s, b - (s - a)


def split(a):
    c = a * 4097.0
    high = c - (c - a)
    return high, a - high


def two_product(a, b):
    p = a * b
    ah, al = split(a)
    bh, bl = split(b)
    return p, ((ah * bh - p) + ah * bl + al * bh) + al * bl


def pair_add(a, b):
    s, e = two_sum(a[0], b[0])
    return quick_sum(s, e + (a[1] + b[1]))


def pair_neg(a):
    return -a[0], -a[1]


def pair_mul(a, b):
    p, e = two_product(a[0], b[0])
    return quick_sum(p, e + (a[0] * b[1] + a[1] * b[0]))


def pair_div(a, b):
    q = a[0] / b[0]
    rest = pair_add(a, pair_neg(pair_mul((q, jnp.zeros_like(q)), b)))
    r = rest[0] / b[0]
    rest = pair_add(rest, pair_neg(pair_mul((r, jnp.zeros_like(r)), b)))
    return quick_sum(*quick_sum(q, r + rest[0] / b[0]))


def powers_kernel(x_ref, planes_ref, temp_ref, powers_ref, parts_ref, mean):
    depth = lax.broadcasted_iota(jnp.int32, (LEV, 2 * COLS), 0).astype(jnp.float32)
    lane = lane_index((LEV, COLS))
    for level in range(LEV):
        temp_ref[level] = x_ref[HALO : HALO + ROWS, level, :]
    for row in range(MID):
        moved = pltpu.roll(x_ref[row, 0:LEV, :], HALO, 1)
        edge = x_ref[row, LEV:, :]
        left = jnp.where(lane < HALO, edge, moved)
        right = jnp.where(lane < HALO, moved, jnp.where(lane < 2 * HALO, edge, 0.0))
        wide = jnp.concatenate([left, right], axis=1)
        wet = depth < planes_ref[0, row : row + 1, :]
        mean[row : row + 1, :] = jnp.sum(jnp.where(wet, wide, 0.0), axis=0, keepdims=True)
    sea = (planes_ref[0] > 0.0).astype(jnp.float32)

    def around(v):
        return (
            pltpu.roll(v, 1, 0)
            + pltpu.roll(v, MID - 1, 0)
            + pltpu.roll(v, 1, 1)
            + pltpu.roll(v, 2 * COLS - 1, 1)
        )

    diagonal = planes_ref[1] + sea * around(sea)
    powers = [sea * (mean[...] * (1.0 / LEV) + planes_ref[2])]
    for _ in range(ITERS):
        v = powers[-1]
        powers.append((diagonal * v - sea * around(v)) * 0.125)
    for index, v in enumerate(powers):
        powers_ref[index] = v
    row = lax.broadcasted_iota(jnp.int32, (MID, 2 * COLS), 0)
    column = lane_index((MID, 2 * COLS))
    own = (
        (row >= HALO) & (row < HALO + ROWS) & (column >= HALO) & (column < HALO + COLS)
    )
    owned = [jnp.where(own, v, 0.0) for v in powers]
    high_rows, low_rows = [], []
    for order in range(2 * ITERS):
        p, e = two_product(owned[order // 2], owned[order - order // 2])
        tiles = [
            (p[8 * i : 8 * i + 8, 128 * j : 128 * j + 128], e[8 * i : 8 * i + 8, 128 * j : 128 * j + 128])
            for i in range(MID // 8)
            for j in range(2)
        ]
        while len(tiles) > 1:
            tiles = [pair_add(a, b) for a, b in zip(tiles[::2], tiles[1::2])]
        total = tiles[0]
        for by in (4, 2, 1):
            total = pair_add(total, tuple(pltpu.roll(t, by, 0) for t in total))
        high_rows.append(total[0])
        low_rows.append(total[1])
    where = lax.broadcasted_iota(jnp.int32, (8, COLS), 0)
    high, low = high_rows[0], low_rows[0]
    for order in range(1, 2 * ITERS):
        high = jnp.where(where == order, high_rows[order], high)
        low = jnp.where(where == order, low_rows[order], low)
    total = (high, low)
    for by in (64, 32, 16, 8, 4, 2, 1):
        total = pair_add(total, tuple(pltpu.roll(t, by, 1) for t in total))
    spot = lax.broadcasted_iota(jnp.int32, (8, COLS), 0)
    message = jnp.where(lane == spot, total[0], 0.0) + jnp.where(lane == spot + 64, total[1], 0.0)
    message = jnp.sum(message, axis=0, keepdims=True)
    parts_ref[...] = jnp.broadcast_to(message, parts_ref.shape)


def combine_kernel(parts_ref, powers_ref, surface_ref, residual_ref, wide):
    count = parts_ref.shape[0] // 8
    tiles = [(parts_ref[8 * i : 8 * i + 8, :], None) for i in range(count)]
    merged = []
    for a, b in zip(tiles[::2], tiles[1::2]):
        merged.append(two_sum(a[0], b[0]))
    tiles = merged
    while len(tiles) > 1:
        tiles = [pair_add(a, b) for a, b in zip(tiles[::2], tiles[1::2])]
    total = tiles[0]
    for by in (4, 2, 1):
        total = pair_add(total, tuple(pltpu.roll(t, by, 0) for t in total))
    other = tuple(pltpu.roll(t, 64, 1) for t in total)
    total = pair_add(total, other)
    moments = [
        tuple(jnp.broadcast_to(t[:, order : order + 1], (8, COLS)) for t in total)
        for order in range(2 * ITERS)
    ]
    rho = list(moments)
    delta = list(moments)
    one = jnp.ones((8, COLS), jnp.float32)
    zero = jnp.zeros((8, COLS), jnp.float32)
    res = [one] + [zero] * ITERS
    way = [one] + [zero] * ITERS
    sol = [zero] * ITERS
    for step in range(ITERS):
        alpha = pair_div(rho[step], delta[step + 1])
        sol = [s + alpha[0] * w for s, w in zip(sol, way)]
        res = [res[0]] + [r - alpha[0] * w for r, w in zip(res[1:], way)]
        if step == ITERS - 1:
            break
        before = rho[step]
        last = 2 * ITERS - 1 - step
        rho = [
            None if order <= step or order >= last
            else pair_add(rho[order], pair_neg(pair_mul(alpha, delta[order + 1])))
            for order in range(2 * ITERS)
        ]
        beta = pair_neg(pair_mul(alpha, pair_div(rho[step + 1], before)))
        delta = [
            None if order <= step or order >= last
            else pair_add(rho[order], pair_mul(beta, delta[order]))
            for order in range(2 * ITERS)
        ]
        way = [r + beta[0] * w for r, w in zip(res, way)]
    for weights, target, factor in ((sol, surface_ref, 0.125), (res, residual_ref, 1.0)):
        for i in range(MID // 8):
            for j in range(2):
                spot = (slice(8 * i, 8 * i + 8), slice(128 * j, 128 * j + 128))
                value = weights[0] * powers_ref[(0,) + spot]
                for index in range(1, len(weights)):
                    value = value + weights[index] * powers_ref[(index,) + spot]
                wide[spot] = value * factor
        target[...] = wide[HALO : HALO + ROWS, HALO : HALO + COLS]


def paired(weight):
    _, outs, ins = weight.shape
    taps = jnp.transpose(weight.reshape(3, 3, outs, ins), (0, 3, 1, 2))
    upper = jnp.pad(taps, ((0, 1), (0, 0), (0, 0), (0, 0)))
    lower = jnp.pad(taps, ((1, 0), (0, 0), (0, 0), (0, 0)))
    return jnp.stack([upper, lower], axis=3)


def first_weight(weight):
    _, outs, _ = weight.shape
    taps = paired(weight).reshape(4, LEV, 6 * outs)
    taps = jnp.pad(taps, ((0, 0), (0, FIELDS - LEV), (0, 0)))
    masks = np.zeros((4, FIELDS, 4, outs), np.float32)
    for at, row in enumerate((1, 2, 2, 3)):
        masks[row, LEV, at] = 1.0
    masks = jnp.asarray(masks.reshape(4, FIELDS, 4 * outs), jnp.bfloat16)
    return jnp.concatenate([taps, masks], axis=2).reshape(4 * FIELDS, 10 * outs)


def forward(axis, periodic):
    count = lax.axis_size(axis)
    pairs = [(i, i + 1) for i in range(count - 1)]
    return pairs + [(count - 1, 0)] if periodic else pairs


def backward(axis, periodic):
    return [(target, source) for source, target in forward(axis, periodic)]


def body(temp, kmt, kappa, helm, forcing, cutoff, conv_in, conv_mid, conv_late, conv_out):
    f32 = jnp.float32
    shape = jax.ShapeDtypeStruct
    blocks = lax.axis_size("lon")
    cuts = jnp.broadcast_to(cutoff.astype(f32)[:, None], (ROWS, COLS))
    rest = jnp.zeros((FIELDS - CUT - 1, ROWS, COLS), f32)
    flat = jnp.stack([kmt.astype(f32), kappa, helm, forcing, cuts])
    own = jnp.transpose(jnp.concatenate([temp, flat, rest]), (1, 0, 2))
    north = lax.ppermute(own[ROWS - DEEP :], "lat", forward("lat", False))
    south = lax.ppermute(own[:DEEP], "lat", backward("lat", False))
    slab = shape((TALL // SLOTS, FIELDS, COLS), f32)
    first, last = call(pack_kernel, (slab, slab))(own, north, south)
    from_west = lax.ppermute(last, "lon", forward("lon", True))
    from_east = lax.ppermute(first, "lon", backward("lon", True))
    w_in = first_weight(conv_in)
    w_mid = paired(conv_mid).reshape(256, 384)
    w_late = paired(conv_late).reshape(256, 384)
    w_out = jnp.transpose(paired(conv_out).reshape(256, 48))
    lines, planes, line = call(
        closure_kernel,
        (
            shape((MID, LEV, COLS), f32),
            shape((3, MID, 2 * COLS), f32),
            shape((LEV, COLS), f32),
        ),
        (
            pltpu.VMEM((TALL, FIELDS, 2 * COLS), f32),
            pltpu.VMEM((TALL * FIELDS, 2 * COLS), jnp.bfloat16),
            pltpu.VMEM((19, WIDE, 128), f32),
            pltpu.VMEM((19, WIDE, 128), f32),
            pltpu.VMEM((19, WIDE, 128), jnp.bfloat16),
            pltpu.VMEM((19, WIDE, 128), jnp.bfloat16),
        ),
    )(own, north, south, from_west, from_east, w_in, w_mid, w_late, w_out)
    whole = lax.all_to_all(lines, "lon", split_axis=0, concat_axis=0, tiled=True)
    filtered = call(filter_kernel, shape((blocks, 2 * LEV, COLS), f32))(
        whole, line, *(jnp.asarray(t) for t in filter_tables(blocks, COLS))
    )
    back = lax.all_to_all(filtered, "lon", split_axis=0, concat_axis=0, tiled=True)
    everyone = blocks * lax.axis_size("lat")
    temp_new, powers, parts = call(
        powers_kernel,
        (
            shape((LEV, ROWS, COLS), f32),
            shape((ITERS + 1, MID, 2 * COLS), f32),
            shape((everyone, COLS), f32),
        ),
        (pltpu.VMEM((MID, 2 * COLS), f32),),
    )(back, planes)
    gathered = lax.all_to_all(parts, ("lon", "lat"), split_axis=0, concat_axis=0, tiled=True)
    surface, residual = call(
        combine_kernel,
        (shape((ROWS, COLS), f32), shape((ROWS, COLS), f32)),
        (pltpu.VMEM((MID, 2 * COLS), f32),),
    )(gathered, powers)
    return temp_new, surface, residual


def solution(mesh):
    return jax.shard_map(
        body,
        mesh=mesh,
        in_specs=(
            P(None, "lat", "lon"),
            P("lat", "lon"),
            P("lat", "lon"),
            P("lat", "lon"),
            P("lat", "lon"),
            P("lat"),
            P(),
            P(),
            P(),
            P(),
        ),
        out_specs=(P(None, "lat", "lon"), P("lat", "lon"), P("lat", "lon")),
        check_vma=False,
    )
```

```python
import math

import jax
import jax.numpy as jnp
import numpy as np
from jax import lax
from jax.experimental import pallas as pl
from jax.experimental.pallas import tpu as pltpu
from jax.sharding import PartitionSpec as P

ITERS = 4
STEP = 0.25
LEV = 8
FIELDS = 16
KMT, KAPPA, HELM, FORCING, CUT = 8, 9, 10, 11, 12
HALO = 4
DEEP = 8
ROWS = 24
COLS = 128
TALL = ROWS + 2 * DEEP
WIDE = COLS + 2 * HALO
MID = ROWS + 2 * HALO
SLOTS = 20
VMEM_LIMIT = 48 * 1024 * 1024
highest = lax.Precision.HIGHEST


def call(kernel, outs, scratch=()):
    spec = pl.BlockSpec(memory_space=pltpu.VMEM)
    return pl.pallas_call(
        kernel,
        out_shape=outs,
        out_specs=jax.tree.map(lambda _: spec, outs),
        scratch_shapes=scratch,
        compiler_params=pltpu.CompilerParams(vmem_limit_bytes=VMEM_LIMIT),
    )


def lane_index(shape):
    return lax.broadcasted_iota(jnp.int32, shape, len(shape) - 1)


def gather_kernel(
    temp_hbm, kmt_hbm, kappa_hbm, helm_hbm, forcing_hbm, cutoff_hbm,
    own_ref, top_ref, bottom_ref,
    temp, kmt, planes, cutoff, sems,
):
    moves = [
        pltpu.make_async_copy(source, target, sems.at[index])
        for index, (source, target) in enumerate(
            (
                (temp_hbm, temp),
                (kmt_hbm, kmt),
                (kappa_hbm, planes.at[0]),
                (helm_hbm, planes.at[1]),
                (forcing_hbm, planes.at[2]),
                (cutoff_hbm, cutoff),
            )
        )
    ]
    for move in moves:
        move.start()
    own_ref[:, CUT + 1 :, :] = jnp.zeros((ROWS, FIELDS - CUT - 1, COLS), jnp.float32)
    for move in moves:
        move.wait()
    for level in range(LEV):
        own_ref[:, level, :] = temp[level]
    own_ref[:, KMT, :] = kmt[...].astype(jnp.float32)
    for index, field in enumerate((KAPPA, HELM, FORCING)):
        own_ref[:, field, :] = planes[index]
    kept = jnp.broadcast_to(cutoff[...].astype(jnp.float32), (ROWS, ROWS))
    row = lax.broadcasted_iota(jnp.int32, (ROWS, ROWS), 0)
    kept = jnp.sum(jnp.where(row == lane_index((ROWS, ROWS)), kept, 0.0), axis=1, keepdims=True)
    own_ref[:, CUT, :] = jnp.broadcast_to(kept, (ROWS, COLS))
    top_ref[...] = own_ref[0:DEEP]
    bottom_ref[...] = own_ref[ROWS - DEEP :]


def weights_kernel(first_ref, mid_ref, late_ref, last_ref, w_in_ref, w_mid_ref, w_late_ref, w_out_ref):
    w_in_ref[...] = jnp.zeros(w_in_ref.shape, w_in_ref.dtype)
    width = mid_ref.shape[1]
    none = jnp.zeros((LEV, width), jnp.float32)
    for row in range(4):
        parts = []
        for tap in range(3):
            for parity in range(2):
                a = row - parity
                parts.append(first_ref[3 * a + tap].astype(jnp.float32) if 0 <= a < 3 else none)
        top = jnp.concatenate(parts, axis=1)
        marks = [jnp.ones((1, width), jnp.float32) if row == at else none[:1] for at in (1, 2, 2, 3)]
        marks = jnp.concatenate(marks, axis=1)
        block = jnp.concatenate(
            [
                jnp.concatenate([top, jnp.zeros((LEV, 4 * width), jnp.float32)], axis=1),
                jnp.concatenate(
                    [
                        jnp.concatenate([jnp.zeros((1, 6 * width), jnp.float32), marks], axis=1),
                        jnp.zeros((LEV - 1, 10 * width), jnp.float32),
                    ],
                    axis=0,
                ),
            ],
            axis=0,
        )
        w_in_ref[FIELDS * row : FIELDS * (row + 1)] = block.astype(jnp.bfloat16)

    def rows_of(ref, tap, parity):
        outs = ref.shape[1]
        blank = jnp.zeros((outs, width), jnp.float32)
        parts = []
        for row in range(4):
            a = row - parity
            parts.append(ref[3 * a + tap].astype(jnp.float32) if 0 <= a < 3 else blank)
        return jnp.concatenate(parts, axis=1)

    for ref, out_ref in ((mid_ref, w_mid_ref), (late_ref, w_late_ref)):
        for tap in range(3):
            both = jnp.concatenate([rows_of(ref, tap, 0), rows_of(ref, tap, 1)], axis=0)
            out_ref[:, 2 * width * tap : 2 * width * (tap + 1)] = both.T.astype(jnp.bfloat16)
    w_out_ref[...] = jnp.concatenate(
        [rows_of(last_ref, tap, parity) for tap in range(3) for parity in range(2)], axis=0
    ).astype(jnp.bfloat16)


def pack_kernel(own_ref, north_ref, south_ref, far_ref, near_ref):
    even = lax.rem(lax.axis_index("lon"), 2) == 0
    lane = lane_index((FIELDS, COLS))
    for part in range(TALL // SLOTS):
        first = jnp.zeros((FIELDS, COLS), jnp.float32)
        last = jnp.zeros((FIELDS, COLS), jnp.float32)
        for slot in range(SLOTS):
            row = part * SLOTS + slot
            if row < DEEP:
                here = north_ref[row]
            elif row < DEEP + ROWS:
                here = own_ref[row - DEEP]
            else:
                here = south_ref[row - DEEP - ROWS]
            inside = (lane >= HALO * slot) & (lane < HALO * (slot + 1))
            first = jnp.where(inside, pltpu.roll(here, HALO * slot, 1) if slot else here, first)
            last = jnp.where(inside, pltpu.roll(here, HALO * (slot + 1), 1), last)
        far_ref[part] = jnp.where(even, first, last)
        near_ref[part] = jnp.where(even, last, first)


def closure_kernel(
    own_ref,
    north_ref,
    south_ref,
    far_ref,
    near_ref,
    w_in_ref,
    w_mid_ref,
    w_late_ref,
    w_out_ref,
    out_ref,
    planes_ref,
    line_ref,
    ext,
    start,
    mask_odd,
    mask_even,
    act_a,
    act_b,
):
    lane = lane_index((FIELDS, COLS))
    depth = lax.broadcasted_iota(jnp.int32, (LEV, 2 * COLS), 0).astype(jnp.float32)
    even = lax.rem(lax.axis_index("lon"), 2) == 0
    parts = range(TALL // SLOTS)
    from_west = [jnp.where(even, far_ref[part], near_ref[part]) for part in parts]
    from_east = [jnp.where(even, near_ref[part], far_ref[part]) for part in parts]
    for row in range(TALL):
        if row < DEEP:
            here = north_ref[row]
        elif row < DEEP + ROWS:
            here = own_ref[row - DEEP]
        else:
            here = south_ref[row - DEEP - ROWS]
        part, slot = row // SLOTS, row % SLOTS
        west = from_west[part]
        if slot:
            west = pltpu.roll(west, COLS - HALO * slot, 1)
        east = from_east[part]
        shift = (HALO - HALO * slot) % COLS
        if shift:
            east = pltpu.roll(east, shift, 1)
        moved = pltpu.roll(here, HALO, 1)
        ext[row, :, 0:COLS] = jnp.where(lane < HALO, west, moved)
        ext[row, :, COLS:] = jnp.where(
            lane < HALO, moved, jnp.where(lane < 2 * HALO, east, 0.0)
        )
    for row in range(TALL):
        wet = (depth < ext[row, KMT : KMT + 1, :]).astype(jnp.float32)
        start[row * FIELDS : row * FIELDS + LEV] = (wet * ext[row, 0:LEV, :]).astype(jnp.bfloat16)
        start[row * FIELDS + LEV : (row + 1) * FIELDS] = jnp.where(depth == 0, wet, 0.0).astype(
            jnp.bfloat16
        )

    def finish(total, mask):
        v = (
            pltpu.roll(total[:, 0:128], 1, 0)
            + total[:, 128:256]
            + pltpu.roll(total[:, 256:384], WIDE - 1, 0)
        )
        return (mask * (v / (1.0 + jnp.exp(-v)))).astype(jnp.bfloat16)

    for pair in range(19):
        window = start[2 * FIELDS * pair : 2 * FIELDS * (pair + 2), 0:WIDE]
        total = lax.dot_general(
            window, w_in_ref[...], (((0,), (0,)), ((), ())), preferred_element_type=jnp.float32
        )
        mask_odd[pair] = total[:, 384:512]
        mask_even[pair] = total[:, 512:640]
        act_a[pair] = finish(total, total[:, 384:512])
    for pair in range(18):
        both = jnp.concatenate([act_a[pair], act_a[pair + 1]], axis=1)
        total = jnp.dot(both, w_mid_ref[...], preferred_element_type=jnp.float32)
        act_b[pair] = finish(total, mask_even[pair])
    for pair in range(17):
        both = jnp.concatenate([act_b[pair], act_b[pair + 1]], axis=1)
        total = jnp.dot(both, w_late_ref[...], preferred_element_type=jnp.float32)
        act_a[pair] = finish(total, mask_odd[pair + 1])

    def cut(block, by):
        return pltpu.roll(block, 2 * COLS - by, 1)[:, 0:COLS]

    def wetness(row):
        return (depth < ext[row, KMT : KMT + 1, :]).astype(jnp.float32)

    for pair in range(16):
        both = jnp.concatenate([act_a[pair], act_a[pair + 1]], axis=1)
        total = lax.dot_general(
            w_out_ref[...], both, (((1,), (1,)), ((), ())), preferred_element_type=jnp.float32
        )
        total = jnp.concatenate(
            [total, jnp.zeros((48, 2 * COLS - WIDE), jnp.float32)], axis=1
        )
        closure = cut(total[0:16], HALO - 1) + cut(total[16:32], HALO) + cut(total[32:48], HALO + 1)
        for parity in range(2):
            row = DEEP - HALO + 2 * pair + parity
            wet_wide = wetness(row)
            tracer_wide = wet_wide * ext[row, 0:LEV, :]
            kappa_wide = ext[row, KAPPA : KAPPA + 1, :]
            wet = cut(wet_wide, HALO)
            tracer = cut(tracer_wide, HALO)
            kappa = cut(jnp.broadcast_to(kappa_wide, (LEV, 2 * COLS)), HALO)
            diff = jnp.zeros((LEV, COLS), jnp.float32)
            for near in (row + 1, row - 1):
                near_w = wetness(near)
                near_t = near_w * ext[near, 0:LEV, :]
                near_k = jnp.broadcast_to(ext[near, KAPPA : KAPPA + 1, :], (LEV, 2 * COLS))
                diff = diff + cut(near_w, HALO) * 0.5 * (kappa + cut(near_k, HALO)) * (
                    cut(near_t, HALO) - tracer
                )
            for by in (HALO + 1, HALO - 1):
                diff = diff + cut(wet_wide, by) * 0.5 * (
                    kappa + cut(jnp.broadcast_to(kappa_wide, (LEV, 2 * COLS)), by)
                ) * (cut(tracer_wide, by) - tracer)
            diff = wet * diff
            eddy = wet * closure[LEV * parity : LEV * (parity + 1)]
            temp = cut(ext[row, 0:LEV, :], HALO)
            out_ref[2 * pair + parity] = wet * (temp + STEP * (diff + eddy))
    first = DEEP - HALO
    for index, field in enumerate((KMT, HELM, FORCING)):
        planes_ref[index] = jnp.concatenate(
            [ext[row, field : field + 1, :] for row in range(first, first + MID)], axis=0
        )
    own_line = lax.axis_index("lon") + first
    line_ref[...] = ext[own_line, LEV:FIELDS, HALO : HALO + 1] + jnp.zeros((LEV, COLS), jnp.float32)


def filter_tables(blocks, width):
    length = blocks * width
    half = LEV // 2
    k = np.arange(blocks)
    outer = np.exp(-2j * np.pi * ((k[:, None] * k[None, :]) % blocks) / blocks)
    spread = np.zeros((blocks, 2, half, blocks, 2, half))
    for line in range(half):
        spread[:, 0, line, :, 0, line] = outer.real
        spread[:, 0, line, :, 1, line] = -outer.imag
        spread[:, 1, line, :, 0, line] = outer.imag
        spread[:, 1, line, :, 1, line] = outer.real
    spread = spread.reshape(blocks * LEV, blocks * LEV)
    m = np.arange(width)
    twist = np.exp(-2j * np.pi * (k[:, None] * m[None, :]) / length)
    sign = np.where(np.arange(LEV) < half, -1.0, 1.0)[None, :, None]
    twist_re = np.broadcast_to(twist.real[:, None, :], (blocks, LEV, width))
    twist_im = twist.imag[:, None, :] * sign
    inner = np.exp(-2j * np.pi * ((m[:, None] * m[None, :]) % width) / width)
    inner = np.concatenate([inner.real, inner.imag], axis=1)
    return [
        np.asarray(t, np.float32)
        for t in (spread, spread.T / length, twist_re, twist_im, inner)
    ]


def filter_kernel(
    x_ref, line_ref, spread_ref, back_ref, twist_re_ref, twist_im_ref, inner_ref, out_ref
):
    blocks, lev, width = x_ref.shape
    shape = (blocks, lev, width)
    length = blocks * width

    def partner(block):
        return pltpu.roll(block, lev // 2, 1)

    sign = jnp.where(lax.broadcasted_iota(jnp.int32, shape, 1) < lev // 2, -1.0, 1.0)
    x = x_ref[...].reshape(blocks * lev, width)
    y = jnp.dot(spread_ref[...], x, precision=highest, preferred_element_type=jnp.float32)
    y = y.reshape(shape)
    y = y * twist_re_ref[...] + partner(y) * twist_im_ref[...]
    s = jnp.dot(
        y.reshape(blocks * lev, width),
        inner_ref[...],
        precision=highest,
        preferred_element_type=jnp.float32,
    )
    s = s[:, 0:width].reshape(shape) + partner(s[:, width:].reshape(shape)) * sign
    wave = lax.broadcasted_iota(jnp.int32, shape, 0) + blocks * lane_index(shape)
    folded = jnp.minimum(wave, length - wave).astype(jnp.float32)
    s = jnp.where(folded < line_ref[CUT - LEV : CUT - LEV + 1, :][None], s, 0.0)
    y = jnp.dot(
        s.reshape(blocks * lev, width),
        inner_ref[...],
        precision=highest,
        preferred_element_type=jnp.float32,
    )
    y = y[:, 0:width].reshape(shape) - partner(y[:, width:].reshape(shape)) * sign
    y = y * twist_re_ref[...] - partner(y) * twist_im_ref[...]
    x = jnp.dot(
        back_ref[...],
        y.reshape(blocks * lev, width),
        precision=highest,
        preferred_element_type=jnp.float32,
    ).reshape(shape)
    out_ref[:, 0:lev, :] = x
    lane = lane_index((lev, width))
    for block in range(blocks):
        west = pltpu.roll(x[(block - 1) % blocks], HALO, 1)
        east = pltpu.roll(x[(block + 1) % blocks], HALO, 1)
        out_ref[block, lev : 2 * lev, :] = jnp.where(lane < HALO, west, east)


def two_sum(a, b):
    s = a + b
    t = s - a
    return s, (a - (s - t)) + (b - t)


def quick_sum(a, b):
    s = a + b
    return s, b - (s - a)


def split(a):
    c = a * 4097.0
    high = c - (c - a)
    return high, a - high


def two_product(a, b):
    p = a * b
    ah, al = split(a)
    bh, bl = split(b)
    return p, ((ah * bh - p) + ah * bl + al * bh) + al * bl


def pair_add(a, b):
    s, e = two_sum(a[0], b[0])
    return quick_sum(s, e + (a[1] + b[1]))


def pair_neg(a):
    return -a[0], -a[1]


def pair_mul(a, b):
    p, e = two_product(a[0], b[0])
    return quick_sum(p, e + (a[0] * b[1] + a[1] * b[0]))


def pair_div(a, b):
    q = a[0] / b[0]
    rest = pair_add(a, pair_neg(pair_mul((q, jnp.zeros_like(q)), b)))
    r = rest[0] / b[0]
    rest = pair_add(rest, pair_neg(pair_mul((r, jnp.zeros_like(r)), b)))
    return quick_sum(*quick_sum(q, r + rest[0] / b[0]))


def powers_kernel(x_ref, planes_ref, temp_ref, powers_ref, parts_ref, mean):
    depth = lax.broadcasted_iota(jnp.int32, (LEV, 2 * COLS), 0).astype(jnp.float32)
    lane = lane_index((LEV, COLS))
    for level in range(LEV):
        temp_ref[level] = x_ref[HALO : HALO + ROWS, level, :]
    for row in range(MID):
        moved = pltpu.roll(x_ref[row, 0:LEV, :], HALO, 1)
        edge = x_ref[row, LEV:, :]
        left = jnp.where(lane < HALO, edge, moved)
        right = jnp.where(lane < HALO, moved, jnp.where(lane < 2 * HALO, edge, 0.0))
        wide = jnp.concatenate([left, right], axis=1)
        wet = depth < planes_ref[0, row : row + 1, :]
        mean[row : row + 1, :] = jnp.sum(jnp.where(wet, wide, 0.0), axis=0, keepdims=True)
    sea = (planes_ref[0] > 0.0).astype(jnp.float32)

    def around(v):
        return (
            pltpu.roll(v, 1, 0)
            + pltpu.roll(v, MID - 1, 0)
            + pltpu.roll(v, 1, 1)
            + pltpu.roll(v, 2 * COLS - 1, 1)
        )

    diagonal = planes_ref[1] + sea * around(sea)
    powers = [sea * (mean[...] * (1.0 / LEV) + planes_ref[2])]
    for _ in range(ITERS):
        v = powers[-1]
        powers.append((diagonal * v - sea * around(v)) * 0.125)
    for index, v in enumerate(powers):
        powers_ref[index] = v
    row = lax.broadcasted_iota(jnp.int32, (MID, 2 * COLS), 0)
    column = lane_index((MID, 2 * COLS))
    own = (
        (row >= HALO) & (row < HALO + ROWS) & (column >= HALO) & (column < HALO + COLS)
    )
    owned = [jnp.where(own, v, 0.0) for v in powers]
    high_rows, low_rows = [], []
    for order in range(2 * ITERS):
        p, e = two_product(owned[order // 2], owned[order - order // 2])
        tiles = [
            (p[8 * i : 8 * i + 8, 128 * j : 128 * j + 128], e[8 * i : 8 * i + 8, 128 * j : 128 * j + 128])
            for i in range(MID // 8)
            for j in range(2)
        ]
        while len(tiles) > 1:
            tiles = [pair_add(a, b) for a, b in zip(tiles[::2], tiles[1::2])]
        total = tiles[0]
        for by in (4, 2, 1):
            total = pair_add(total, tuple(pltpu.roll(t, by, 0) for t in total))
        high_rows.append(total[0])
        low_rows.append(total[1])
    where = lax.broadcasted_iota(jnp.int32, (8, COLS), 0)
    high, low = high_rows[0], low_rows[0]
    for order in range(1, 2 * ITERS):
        high = jnp.where(where == order, high_rows[order], high)
        low = jnp.where(where == order, low_rows[order], low)
    total = (high, low)
    for by in (64, 32, 16, 8, 4, 2, 1):
        total = pair_add(total, tuple(pltpu.roll(t, by, 1) for t in total))
    spot = lax.broadcasted_iota(jnp.int32, (8, COLS), 0)
    message = jnp.where(lane == spot, total[0], 0.0) + jnp.where(lane == spot + 64, total[1], 0.0)
    message = jnp.sum(message, axis=0, keepdims=True)
    parts_ref[...] = jnp.broadcast_to(message, parts_ref.shape)


def sum_messages(parts_ref):
    count = parts_ref.shape[0] // 8
    if count == 1:
        total = (parts_ref[...], jnp.zeros((8, COLS), jnp.float32))
        for by in (4, 2, 1):
            total = pair_add(total, tuple(pltpu.roll(t, by, 0) for t in total))
        return pair_add(total, tuple(pltpu.roll(t, 64, 1) for t in total))
    tiles = [(parts_ref[8 * i : 8 * i + 8, :], None) for i in range(count)]
    merged = []
    for a, b in zip(tiles[::2], tiles[1::2]):
        merged.append(two_sum(a[0], b[0]))
    tiles = merged
    while len(tiles) > 1:
        tiles = [pair_add(a, b) for a, b in zip(tiles[::2], tiles[1::2])]
    total = tiles[0]
    for by in (4, 2, 1):
        total = pair_add(total, tuple(pltpu.roll(t, by, 0) for t in total))
    return pair_add(total, tuple(pltpu.roll(t, 64, 1) for t in total))


def merge_kernel(parts_ref, out_ref):
    total = sum_messages(parts_ref)
    lane = lane_index((8, COLS))
    out_ref[...] = jnp.where(lane < 64, total[0], total[1])


def combine_kernel(parts_ref, powers_ref, surface_ref, residual_ref, wide):
    total = sum_messages(parts_ref)
    moments = [
        tuple(jnp.broadcast_to(t[:, order : order + 1], (8, COLS)) for t in total)
        for order in range(2 * ITERS)
    ]
    rho = list(moments)
    delta = list(moments)
    one = jnp.ones((8, COLS), jnp.float32)
    zero = jnp.zeros((8, COLS), jnp.float32)
    res = [one] + [zero] * ITERS
    way = [one] + [zero] * ITERS
    sol = [zero] * ITERS
    for step in range(ITERS):
        alpha = pair_div(rho[step], delta[step + 1])
        sol = [s + alpha[0] * w for s, w in zip(sol, way)]
        res = [res[0]] + [r - alpha[0] * w for r, w in zip(res[1:], way)]
        if step == ITERS - 1:
            break
        before = rho[step]
        last = 2 * ITERS - 1 - step
        rho = [
            None if order <= step or order >= last
            else pair_add(rho[order], pair_neg(pair_mul(alpha, delta[order + 1])))
            for order in range(2 * ITERS)
        ]
        beta = pair_neg(pair_mul(alpha, pair_div(rho[step + 1], before)))
        delta = [
            None if order <= step or order >= last
            else pair_add(rho[order], pair_mul(beta, delta[order]))
            for order in range(2 * ITERS)
        ]
        way = [r + beta[0] * w for r, w in zip(res, way)]
    for weights, target, factor in ((sol, surface_ref, 0.125), (res, residual_ref, 1.0)):
        for i in range(MID // 8):
            for j in range(2):
                spot = (slice(8 * i, 8 * i + 8), slice(128 * j, 128 * j + 128))
                value = weights[0] * powers_ref[(0,) + spot]
                for index in range(1, len(weights)):
                    value = value + weights[index] * powers_ref[(index,) + spot]
                wide[spot] = value * factor
        target[...] = wide[HALO : HALO + ROWS, HALO : HALO + COLS]


def forward(axis, periodic):
    count = lax.axis_size(axis)
    pairs = [(i, i + 1) for i in range(count - 1)]
    return pairs + [(count - 1, 0)] if periodic else pairs


def backward(axis, periodic):
    return [(target, source) for source, target in forward(axis, periodic)]


def swap_near():
    return [(i, i ^ 1) for i in range(lax.axis_size("lon"))]


def swap_far():
    count = lax.axis_size("lon")
    return [(i, (i + 1) % count if i % 2 else (i - 1) % count) for i in range(count)]


def body(temp, kmt, kappa, helm, forcing, cutoff, conv_in, conv_mid, conv_late, conv_out):
    f32 = jnp.float32
    shape = jax.ShapeDtypeStruct
    blocks = lax.axis_size("lon")
    own, top, bottom = pl.pallas_call(
        gather_kernel,
        out_shape=(
            shape((ROWS, FIELDS, COLS), f32),
            shape((DEEP, FIELDS, COLS), f32),
            shape((DEEP, FIELDS, COLS), f32),
        ),
        in_specs=[pl.BlockSpec(memory_space=pltpu.HBM)] * 6,
        out_specs=(pl.BlockSpec(memory_space=pltpu.VMEM),) * 3,
        scratch_shapes=(
            pltpu.VMEM((LEV, ROWS, COLS), f32),
            pltpu.VMEM((ROWS, COLS), jnp.int32),
            pltpu.VMEM((3, ROWS, COLS), f32),
            pltpu.VMEM((1, ROWS), jnp.int32),
            pltpu.SemaphoreType.DMA((6,)),
        ),
    )(temp, kmt, kappa, helm, forcing, cutoff.reshape(1, ROWS))
    north = lax.ppermute(bottom, "lat", forward("lat", False))
    south = lax.ppermute(top, "lat", backward("lat", False))
    bf16 = jnp.bfloat16
    weights = call(
        weights_kernel,
        (
            shape((4 * FIELDS, 640), bf16),
            shape((256, 384), bf16),
            shape((256, 384), bf16),
            shape((48, 256), bf16),
        ),
    )(jnp.transpose(conv_in, (0, 2, 1)), conv_mid, conv_late, conv_out)
    slab = shape((TALL // SLOTS, FIELDS, COLS), f32)
    to_far, to_near = call(pack_kernel, (slab, slab))(own, north, south)
    far = lax.ppermute(to_far, "lon", swap_far())
    near = lax.ppermute(to_near, "lon", swap_near())
    lines, planes, line = call(
        closure_kernel,
        (
            shape((MID, LEV, COLS), f32),
            shape((3, MID, 2 * COLS), f32),
            shape((LEV, COLS), f32),
        ),
        (
            pltpu.VMEM((TALL, FIELDS, 2 * COLS), f32),
            pltpu.VMEM((TALL * FIELDS, 2 * COLS), jnp.bfloat16),
            pltpu.VMEM((19, WIDE, 128), f32),
            pltpu.VMEM((19, WIDE, 128), f32),
            pltpu.VMEM((19, WIDE, 128), jnp.bfloat16),
            pltpu.VMEM((19, WIDE, 128), jnp.bfloat16),
        ),
    )(own, north, south, far, near, *weights)
    whole = lax.all_to_all(lines, "lon", split_axis=0, concat_axis=0, tiled=True)
    filtered = call(filter_kernel, shape((blocks, 2 * LEV, COLS), f32))(
        whole, line, *(jnp.asarray(t) for t in filter_tables(blocks, COLS))
    )
    back = lax.all_to_all(filtered, "lon", split_axis=0, concat_axis=0, tiled=True)
    everyone = blocks * lax.axis_size("lat")
    wide = everyone // 8
    both = ("lon", "lat")
    inner = [[wide * i + k for k in range(wide)] for i in range(8)]
    outer = [[wide * i + k for i in range(8)] for k in range(wide)]
    temp_new, powers, parts = call(
        powers_kernel,
        (
            shape((LEV, ROWS, COLS), f32),
            shape((ITERS + 1, MID, 2 * COLS), f32),
            shape((wide, COLS), f32),
        ),
        (pltpu.VMEM((MID, 2 * COLS), f32),),
    )(back, planes)
    parts = lax.all_to_all(
        parts, both, split_axis=0, concat_axis=0, tiled=True, axis_index_groups=inner
    )
    parts = call(merge_kernel, shape((8, COLS), f32))(parts)
    parts = lax.all_to_all(
        parts, both, split_axis=0, concat_axis=0, tiled=True, axis_index_groups=outer
    )
    surface, residual = call(
        combine_kernel,
        (shape((ROWS, COLS), f32), shape((ROWS, COLS), f32)),
        (pltpu.VMEM((MID, 2 * COLS), f32),),
    )(parts, powers)
    return temp_new, surface, residual


def solution(mesh):
    return jax.shard_map(
        body,
        mesh=mesh,
        in_specs=(
            P(None, "lat", "lon"),
            P("lat", "lon"),
            P("lat", "lon"),
            P("lat", "lon"),
            P("lat", "lon"),
            P("lat"),
            P(),
            P(),
            P(),
            P(),
        ),
        out_specs=(P(None, "lat", "lon"), P("lat", "lon"), P("lat", "lon")),
        check_vma=False,
    )
```

```python
import math

import jax
import jax.numpy as jnp
import numpy as np
from jax import lax
from jax.experimental import pallas as pl
from jax.experimental.pallas import tpu as pltpu
from jax.sharding import PartitionSpec as P

ITERS = 4
STEP = 0.25
LEV = 8
FIELDS = 16
KMT, KAPPA, HELM, FORCING, CUT = 8, 9, 10, 11, 12
HALO = 4
DEEP = 8
ROWS = 24
COLS = 128
TALL = ROWS + 2 * DEEP
MID = ROWS + 2 * HALO
BLOCK = LEV + 1
SLOTS = 20
VMEM_LIMIT = 48 * 1024 * 1024


def call(kernel, outs, scratch=(), flops=None):
    spec = pl.BlockSpec(memory_space=pltpu.VMEM)
    return pl.pallas_call(
        kernel,
        out_shape=outs,
        out_specs=jax.tree.map(lambda _: spec, outs),
        scratch_shapes=scratch,
        compiler_params=pltpu.CompilerParams(vmem_limit_bytes=VMEM_LIMIT),
        cost_estimate=flops
        and pl.CostEstimate(flops=flops, bytes_accessed=10**6, transcendentals=flops // 500),
    )


def lane_index(shape):
    return lax.broadcasted_iota(jnp.int32, shape, len(shape) - 1)


def slab_kernel(
    temp_hbm, kmt_hbm, kappa_hbm, helm_hbm, forcing_hbm, cutoff_hbm,
    top_ref, bottom_ref, kmt, cutoff, sems,
):
    pairs = [(kmt_hbm, kmt), (cutoff_hbm, cutoff)]
    for target, start in ((top_ref, 0), (bottom_ref, ROWS - DEEP)):
        rows = pl.ds(start, DEEP)
        pairs.append((temp_hbm.at[:, rows], target.at[pl.ds(0, LEV)]))
        for source, field in ((kappa_hbm, KAPPA), (helm_hbm, HELM), (forcing_hbm, FORCING)):
            pairs.append((source.at[rows], target.at[field]))
    moves = [
        pltpu.make_async_copy(source, target, sems.at[index])
        for index, (source, target) in enumerate(pairs)
    ]
    for move in moves:
        move.start()
    for move in moves:
        move.wait()
    kept = cutoff_rows(cutoff)
    for target, start in ((top_ref, 0), (bottom_ref, ROWS - DEEP)):
        target[KMT] = kmt[start : start + DEEP].astype(jnp.float32)
        target[CUT] = kept[start : start + DEEP]


def cutoff_rows(cutoff_ref):
    kept = jnp.broadcast_to(cutoff_ref[...].astype(jnp.float32), (ROWS, ROWS))
    row = lax.broadcasted_iota(jnp.int32, (ROWS, ROWS), 0)
    kept = jnp.sum(jnp.where(row == lane_index((ROWS, ROWS)), kept, 0.0), axis=1, keepdims=True)
    return jnp.broadcast_to(kept, (ROWS, COLS))


def rows_kernel(temp_ref, kmt_ref, kappa_ref, helm_ref, forcing_ref, cutoff_ref, own_ref):
    own_ref[:, CUT + 1 :, :] = jnp.zeros((ROWS, FIELDS - CUT - 1, COLS), jnp.float32)
    for level in range(LEV):
        own_ref[:, level, :] = temp_ref[level]
    own_ref[:, KMT, :] = kmt_ref[...].astype(jnp.float32)
    own_ref[:, KAPPA, :] = kappa_ref[...]
    own_ref[:, HELM, :] = helm_ref[...]
    own_ref[:, FORCING, :] = forcing_ref[...]
    own_ref[:, CUT, :] = cutoff_rows(cutoff_ref)


def weights_kernel(
    first_ref, mid_ref, late_ref, last_ref, *refs
):
    tables, outs = refs[:3], refs[3:]
    w_in_ref, w_mid_ref, w_late_ref, w_out_ref = outs[:4]
    for index, table_ref in enumerate(tables):
        outs[4 + 2 * index][...], outs[5 + 2 * index][...] = halves(table_ref[...])
    w_in_ref[...] = jnp.zeros(w_in_ref.shape, w_in_ref.dtype)
    width = mid_ref.shape[1]
    none = jnp.zeros((LEV, width), jnp.float32)
    for row in range(4):
        parts = []
        for tap in range(3):
            for parity in range(2):
                a = row - parity
                parts.append(first_ref[3 * a + tap].astype(jnp.float32) if 0 <= a < 3 else none)
        top = jnp.concatenate(parts, axis=1)
        marks = [jnp.ones((1, width), jnp.float32) if row == at else none[:1] for at in (1, 2, 2, 3)]
        marks = jnp.concatenate(marks, axis=1)
        block = jnp.concatenate(
            [
                jnp.concatenate([top, jnp.zeros((LEV, 4 * width), jnp.float32)], axis=1),
                jnp.concatenate(
                    [
                        jnp.concatenate([jnp.zeros((1, 6 * width), jnp.float32), marks], axis=1),
                        jnp.zeros((LEV - 1, 10 * width), jnp.float32),
                    ],
                    axis=0,
                ),
            ],
            axis=0,
        )
        w_in_ref[FIELDS * row : FIELDS * (row + 1)] = block.astype(jnp.bfloat16)

    def rows_of(ref, tap, parity):
        outs = ref.shape[1]
        blank = jnp.zeros((outs, width), jnp.float32)
        parts = []
        for row in range(4):
            a = row - parity
            parts.append(ref[3 * a + tap].astype(jnp.float32) if 0 <= a < 3 else blank)
        return jnp.concatenate(parts, axis=1)

    for ref, out_ref in ((mid_ref, w_mid_ref), (late_ref, w_late_ref)):
        for tap in range(3):
            both = jnp.concatenate([rows_of(ref, tap, 0), rows_of(ref, tap, 1)], axis=0)
            out_ref[:, 2 * width * tap : 2 * width * (tap + 1)] = both.T.astype(jnp.bfloat16)
    w_out_ref[...] = jnp.concatenate(
        [rows_of(last_ref, tap, parity) for tap in range(3) for parity in range(2)], axis=0
    ).astype(jnp.bfloat16)


def pack_kernel(own_ref, north_ref, south_ref, rows_ref, far_ref, near_ref):
    even = lax.rem(lax.axis_index("lon"), 2) == 0
    rows_ref[DEEP : DEEP + ROWS] = own_ref[...]
    for slab_ref, start in ((north_ref, 0), (south_ref, DEEP + ROWS)):
        rows = slice(start, start + DEEP)
        rows_ref[rows, CUT + 1 :, :] = jnp.zeros((DEEP, FIELDS - CUT - 1, COLS), jnp.float32)
        for field in range(CUT + 1):
            rows_ref[rows, field, :] = slab_ref[field]
    lane = lane_index((FIELDS, COLS))
    for part in range(TALL // SLOTS):
        first = jnp.zeros((FIELDS, COLS), jnp.float32)
        last = jnp.zeros((FIELDS, COLS), jnp.float32)
        for slot in range(SLOTS):
            here = rows_ref[part * SLOTS + slot]
            inside = (lane >= HALO * slot) & (lane < HALO * (slot + 1))
            first = jnp.where(inside, pltpu.roll(here, HALO * slot, 1) if slot else here, first)
            last = jnp.where(inside, pltpu.roll(here, HALO * (slot + 1), 1), last)
        far_ref[part] = jnp.where(even, first, last)
        near_ref[part] = jnp.where(even, last, first)


def closure_layers(window, pairs, stride, weights, acts, masks):
    w_in_ref, w_mid_ref, w_late_ref, w_out_ref = weights
    act_a, act_b = acts
    mask_odd, mask_even = masks

    def chunks(count):
        return range(-(-count * stride // COLS))

    def at(chunk, shift=0):
        return slice(COLS * chunk + shift, COLS * (chunk + 1) + shift)

    def both(act, chunk):
        return jnp.concatenate([act[at(chunk)], act[at(chunk, stride)]], axis=1)

    def finish(total, mask):
        v = (
            pltpu.roll(total[:, 0:128], 1, 0)
            + total[:, 128:256]
            + pltpu.roll(total[:, 256:384], COLS - 1, 0)
        )
        return (mask * (v / (1.0 + jnp.exp(-v)))).astype(jnp.bfloat16)

    for chunk in chunks(pairs):
        total = lax.dot_general(
            window(chunk),
            w_in_ref[...],
            (((0,), (0,)), ((), ())),
            preferred_element_type=jnp.float32,
        )
        mask_odd[at(chunk)] = total[:, 384:512]
        mask_even[at(chunk)] = total[:, 512:640]
        act_a[at(chunk)] = finish(total, total[:, 384:512])
    for chunk in chunks(pairs - 1):
        total = jnp.dot(both(act_a, chunk), w_mid_ref[...], preferred_element_type=jnp.float32)
        act_b[at(chunk)] = finish(total, mask_even[at(chunk)])
    for chunk in chunks(pairs - 2):
        total = jnp.dot(both(act_b, chunk), w_late_ref[...], preferred_element_type=jnp.float32)
        act_a[at(chunk)] = finish(total, mask_odd[at(chunk, stride)])
    results = []
    for chunk in chunks(pairs - 3):
        total = lax.dot_general(
            w_out_ref[...],
            both(act_a, chunk),
            (((1,), (1,)), ((), ())),
            preferred_element_type=jnp.float32,
        )
        results.append(
            pltpu.roll(total[0:16], 1, 1) + total[16:32] + pltpu.roll(total[32:48], COLS - 1, 1)
        )
    return results


def level_index():
    return lax.broadcasted_iota(jnp.int32, (LEV, COLS), 0).astype(jnp.float32)


def wetness(block):
    return (level_index() < block[KMT : KMT + 1]).astype(jnp.float32)


def first_input(block):
    wet = wetness(block)
    sea = jnp.where(level_index() == 0.0, wet, 0.0)
    return jnp.concatenate([wet * block[0:LEV], sea], axis=0).astype(jnp.bfloat16)


def advance(here, north, south, closure):
    wet = wetness(here)
    temp = here[0:LEV]
    tracer = wet * temp
    kappa = jnp.broadcast_to(here[KAPPA : KAPPA + 1], (LEV, COLS))
    diff = jnp.zeros((LEV, COLS), jnp.float32)
    for near in (south, north):
        near_w = wetness(near)
        diff = diff + near_w * 0.5 * (kappa + near[KAPPA : KAPPA + 1]) * (
            near_w * near[0:LEV] - tracer
        )
    for by in (COLS - 1, 1):
        diff = diff + pltpu.roll(wet, by, 1) * 0.5 * (kappa + pltpu.roll(kappa, by, 1)) * (
            pltpu.roll(tracer, by, 1) - tracer
        )
    diff = wet * diff
    eddy = wet * closure
    return wet * (temp + STEP * (diff + eddy))


FIRST = DEEP - HALO


def interior_kernel(
    rows_ref, w_in_ref, w_mid_ref, w_late_ref, w_out_ref, out_ref, line_ref,
    start, mask_odd, mask_even, act_a, act_b,
):
    for row in range(TALL):
        start[row * FIELDS : (row + 1) * FIELDS] = first_input(rows_ref[row])
    results = closure_layers(
        lambda chunk: start[2 * FIELDS * chunk : 2 * FIELDS * (chunk + 2)],
        TALL // 2 - 1,
        COLS,
        (w_in_ref, w_mid_ref, w_late_ref, w_out_ref),
        (act_a, act_b),
        (mask_odd, mask_even),
    )
    for pair, closure in enumerate(results):
        for parity in range(2):
            row = FIRST + 2 * pair + parity
            out_ref[2 * pair + parity] = advance(
                rows_ref[row],
                rows_ref[row - 1],
                rows_ref[row + 1],
                closure[LEV * parity : LEV * (parity + 1)],
            )
    own_line = lax.axis_index("lon") + FIRST
    line_ref[...] = rows_ref[own_line, LEV:FIELDS, :]


STRIP = 32
PER = COLS // STRIP


def edge_kernel(
    rows_ref, far_ref, near_ref, inside_ref, w_in_ref, w_mid_ref, w_late_ref, w_out_ref,
    out_ref, planes_ref, strips, mask_odd, mask_even, act_a, act_b,
):
    lane = lane_index((FIELDS, COLS))
    even = lax.rem(lax.axis_index("lon"), 2) == 0
    parts = range(TALL // SLOTS)
    from_west = [jnp.where(even, far_ref[part], near_ref[part]) for part in parts]
    from_east = [jnp.where(even, near_ref[part], far_ref[part]) for part in parts]
    for row in range(TALL):
        part, slot = row // SLOTS, row % SLOTS
        here = rows_ref[row]
        strip = jnp.where(lane < 24, pltpu.roll(from_east[part], (20 - HALO * slot) % COLS, 1) if slot != 5 else from_east[part], 0.0)
        strip = jnp.where(lane < 20, pltpu.roll(here, 20, 1), strip)
        strip = jnp.where(lane < 12, pltpu.roll(here, 4, 1), strip)
        west = pltpu.roll(from_west[part], COLS - HALO * slot, 1) if slot else from_west[part]
        strips[row] = jnp.where(lane < 4, west, strip)

    def side_by_side(parity, start):
        total = None
        for slot in range(PER):
            row = 2 * (start + slot) + parity
            if row >= TALL:
                continue
            piece = strips[row]
            piece = pltpu.roll(piece, STRIP * slot, 1) if slot else piece
            total = piece if total is None else total + piece
        return total

    def window(chunk):
        at = PER * chunk
        return jnp.concatenate(
            [
                first_input(block)
                for block in (
                    side_by_side(0, at),
                    side_by_side(1, at),
                    side_by_side(0, at + 1),
                    side_by_side(1, at + 1),
                )
            ],
            axis=0,
        )

    act_a[5 * COLS :] = jnp.zeros((COLS, COLS), jnp.bfloat16)
    act_b[5 * COLS :] = jnp.zeros((COLS, COLS), jnp.bfloat16)
    mask_odd[5 * COLS :] = jnp.zeros((COLS, COLS), jnp.float32)
    results = closure_layers(
        window,
        TALL // 2 - 1,
        STRIP,
        (w_in_ref, w_mid_ref, w_late_ref, w_out_ref),
        (act_a, act_b),
        (mask_odd, mask_even),
    )
    at_lane = lane_index((LEV, COLS))
    for chunk in range(4):
        at = PER * chunk + FIRST // 2
        closure = results[chunk]
        north = side_by_side(1, at - 1)
        upper = side_by_side(0, at)
        lower = side_by_side(1, at)
        south = side_by_side(0, at + 1)
        for parity, value in (
            (0, advance(upper, north, lower, closure[0:LEV])),
            (1, advance(lower, upper, south, closure[LEV : 2 * LEV])),
        ):
            for slot in range(PER):
                row = 2 * (PER * chunk + slot) + parity
                left = pltpu.roll(value, COLS - STRIP * slot - 4, 1)
                shift = (108 - STRIP * slot) % COLS
                right = pltpu.roll(value, shift, 1)
                out_ref[row] = jnp.where(
                    at_lane < HALO,
                    left,
                    jnp.where(at_lane >= COLS - HALO, right, inside_ref[row]),
                )
    plane_lane = lane_index((MID, COLS))
    for index, field in enumerate((KMT, HELM, FORCING)):
        moved = pltpu.roll(rows_ref[FIRST : FIRST + MID, field, :], HALO, 1)
        edge = strips[FIRST : FIRST + MID, field, :]
        planes_ref[index, :, 0:COLS] = jnp.where(plane_lane < HALO, edge, moved)
        planes_ref[index, :, COLS:] = jnp.where(
            plane_lane < HALO,
            moved,
            jnp.where(plane_lane < 2 * HALO, pltpu.roll(edge, COLS - 16, 1), 0.0),
        )


def filter_tables(blocks, width):
    length = blocks * width
    half = LEV // 2
    k = np.arange(blocks)
    outer = np.exp(-2j * np.pi * ((k[:, None] * k[None, :]) % blocks) / blocks)
    spread = np.zeros((blocks, 2, half, blocks, 2, half))
    for line in range(half):
        spread[:, 0, line, :, 0, line] = outer.real
        spread[:, 0, line, :, 1, line] = -outer.imag
        spread[:, 1, line, :, 0, line] = outer.imag
        spread[:, 1, line, :, 1, line] = outer.real
    spread = spread.reshape(blocks * LEV, blocks * LEV)
    m = np.arange(width)
    twist = np.exp(-2j * np.pi * (k[:, None] * m[None, :]) / length)
    sign = np.where(np.arange(LEV) < half, -1.0, 1.0)[None, :, None]
    twist_re = np.broadcast_to(twist.real[:, None, :], (blocks, LEV, width))
    twist_im = twist.imag[:, None, :] * sign
    inner = np.exp(-2j * np.pi * ((m[:, None] * m[None, :]) % width) / width)
    inner = np.concatenate([inner.real, inner.imag], axis=1)
    return [
        np.asarray(t, np.float32)
        for t in (spread, spread.T / length, inner, twist_re, twist_im)
    ]


def halves(x):
    high = x.astype(jnp.bfloat16)
    return high, (x - high.astype(jnp.float32)).astype(jnp.bfloat16)


def split_dot(a, b):
    def dot(x, y):
        return jnp.dot(x, y, preferred_element_type=jnp.float32)

    return dot(a[0], b[0]) + (dot(a[0], b[1]) + dot(a[1], b[0]))


def filter_kernel(
    x_ref, line_ref, spread_ref, spread_low, back_ref, back_low, inner_ref, inner_low,
    twist_re_ref, twist_im_ref, out_ref,
):
    blocks, lev, width = x_ref.shape
    shape = (blocks, lev, width)
    flat = (blocks * lev, width)
    length = blocks * width
    inner = (inner_ref[...], inner_low[...])

    def partner(block):
        return pltpu.roll(block, lev // 2, 1)

    sign = jnp.where(lax.broadcasted_iota(jnp.int32, shape, 1) < lev // 2, -1.0, 1.0)
    y = split_dot((spread_ref[...], spread_low[...]), halves(x_ref[...].reshape(flat)))
    y = y.reshape(shape)
    y = y * twist_re_ref[...] + partner(y) * twist_im_ref[...]
    s = split_dot(halves(y.reshape(flat)), inner)
    s = s[:, 0:width].reshape(shape) + partner(s[:, width:].reshape(shape)) * sign
    wave = lax.broadcasted_iota(jnp.int32, shape, 0) + blocks * lane_index(shape)
    folded = jnp.minimum(wave, length - wave).astype(jnp.float32)
    s = jnp.where(folded < line_ref[CUT - LEV : CUT - LEV + 1, :][None], s, 0.0)
    y = split_dot(halves(s.reshape(flat)), inner)
    y = y[:, 0:width].reshape(shape) - partner(y[:, width:].reshape(shape)) * sign
    y = y * twist_re_ref[...] - partner(y) * twist_im_ref[...]
    x = split_dot((back_ref[...], back_low[...]), halves(y.reshape(flat))).reshape(shape)
    lane = lane_index((lev, width))
    moved = [pltpu.roll(x[block], HALO, 1) for block in range(blocks)]
    for block in range(blocks):
        edge = jnp.where(lane < HALO, moved[block - 1], moved[(block + 1) % blocks])
        edge = jnp.where(lane < 2 * HALO, edge, 0.0)
        edge = pltpu.roll(edge, 0, 1, stride=2 * HALO, stride_axis=0)
        row = BLOCK * block
        out_ref[row : row + lev, :] = x[block]
        out_ref[row + lev : row + BLOCK, :] = jnp.sum(edge, axis=0, keepdims=True)


def two_sum(a, b):
    s = a + b
    t = s - a
    return s, (a - (s - t)) + (b - t)


def quick_sum(a, b):
    s = a + b
    return s, b - (s - a)


def split(a):
    c = a * 4097.0
    high = c - (c - a)
    return high, a - high


def two_product(a, b):
    p = a * b
    ah, al = split(a)
    bh, bl = split(b)
    return p, ((ah * bh - p) + ah * bl + al * bh) + al * bl


def pair_add(a, b):
    s, e = two_sum(a[0], b[0])
    return quick_sum(s, e + (a[1] + b[1]))


def pair_neg(a):
    return -a[0], -a[1]


def pair_mul(a, b):
    p, e = two_product(a[0], b[0])
    return quick_sum(p, e + (a[0] * b[1] + a[1] * b[0]))


def pair_div(a, b):
    q = a[0] / b[0]
    rest = pair_add(a, pair_neg(pair_mul((q, jnp.zeros_like(q)), b)))
    r = rest[0] / b[0]
    rest = pair_add(rest, pair_neg(pair_mul((r, jnp.zeros_like(r)), b)))
    return quick_sum(*quick_sum(q, r + rest[0] / b[0]))


def powers_kernel(x_ref, planes_ref, temp_ref, powers_ref, parts_ref):
    lane = lane_index((LEV, COLS))
    wide_lane = lane_index((MID, COLS))
    kmt_left = planes_ref[0, :, 0:COLS]
    kmt_right = planes_ref[0, :, COLS:]
    kmt = pltpu.roll(jnp.where(wide_lane < HALO, kmt_right, kmt_left), COLS - HALO, 1)
    mean = jnp.zeros((MID, COLS), jnp.float32)
    for level in range(LEV):
        temp_ref[level] = x_ref[pl.ds(HALO * BLOCK + level, ROWS, stride=BLOCK), :]
        here = x_ref[pl.ds(level, MID, stride=BLOCK), :]
        mean = mean + jnp.where(kmt > level, here, 0.0)
    edge = x_ref[pl.ds(LEV, MID, stride=BLOCK), :]
    edge_kmt = jnp.where(wide_lane < HALO, kmt_left, kmt_right)
    edge_kmt = jnp.where(wide_lane < 2 * HALO, edge_kmt, 0.0)
    for by in (8, 16, 32, 64):
        edge_kmt = edge_kmt + pltpu.roll(edge_kmt, by, 1)
    edge = jnp.where(edge_kmt > (wide_lane // (2 * HALO)).astype(jnp.float32), edge, 0.0)
    for by in (64, 32, 16, 8):
        edge = edge + pltpu.roll(edge, by, 1)
    moved = pltpu.roll(mean, HALO, 1)
    mean = jnp.concatenate(
        [
            jnp.where(wide_lane < HALO, edge, moved),
            jnp.where(wide_lane < HALO, moved, jnp.where(wide_lane < 2 * HALO, edge, 0.0)),
        ],
        axis=1,
    )
    sea = (planes_ref[0] > 0.0).astype(jnp.float32)

    def around(v):
        return (
            pltpu.roll(v, 1, 0)
            + pltpu.roll(v, MID - 1, 0)
            + pltpu.roll(v, 1, 1)
            + pltpu.roll(v, 2 * COLS - 1, 1)
        )

    diagonal = planes_ref[1] + sea * around(sea)
    powers = [sea * (mean * (1.0 / LEV) + planes_ref[2])]
    for _ in range(ITERS):
        v = powers[-1]
        powers.append((diagonal * v - sea * around(v)) * 0.125)
    for index, v in enumerate(powers):
        powers_ref[index] = v
    row = lax.broadcasted_iota(jnp.int32, (MID, 2 * COLS), 0)
    column = lane_index((MID, 2 * COLS))
    own = (
        (row >= HALO) & (row < HALO + ROWS) & (column >= HALO) & (column < HALO + COLS)
    )
    owned = [jnp.where(own, v, 0.0) for v in powers]
    high_rows, low_rows = [], []
    for order in range(2 * ITERS):
        p, e = two_product(owned[order // 2], owned[order - order // 2])
        tiles = [
            (p[8 * i : 8 * i + 8, 128 * j : 128 * j + 128], e[8 * i : 8 * i + 8, 128 * j : 128 * j + 128])
            for i in range(MID // 8)
            for j in range(2)
        ]
        while len(tiles) > 1:
            tiles = [pair_add(a, b) for a, b in zip(tiles[::2], tiles[1::2])]
        total = tiles[0]
        for by in (4, 2, 1):
            total = pair_add(total, tuple(pltpu.roll(t, by, 0) for t in total))
        high_rows.append(total[0])
        low_rows.append(total[1])
    where = lax.broadcasted_iota(jnp.int32, (8, COLS), 0)
    high, low = high_rows[0], low_rows[0]
    for order in range(1, 2 * ITERS):
        high = jnp.where(where == order, high_rows[order], high)
        low = jnp.where(where == order, low_rows[order], low)
    total = (high, low)
    for by in (64, 32, 16, 8, 4, 2, 1):
        total = pair_add(total, tuple(pltpu.roll(t, by, 1) for t in total))
    spot = lax.broadcasted_iota(jnp.int32, (8, COLS), 0)
    message = jnp.where(lane == spot, total[0], 0.0) + jnp.where(lane == spot + 64, total[1], 0.0)
    message = jnp.sum(message, axis=0, keepdims=True)
    parts_ref[...] = jnp.broadcast_to(message, parts_ref.shape)


def sum_messages(parts_ref):
    count = parts_ref.shape[0] // 8
    if count == 1:
        total = (parts_ref[...], jnp.zeros((8, COLS), jnp.float32))
        for by in (4, 2, 1):
            total = pair_add(total, tuple(pltpu.roll(t, by, 0) for t in total))
        return pair_add(total, tuple(pltpu.roll(t, 64, 1) for t in total))
    tiles = [(parts_ref[8 * i : 8 * i + 8, :], None) for i in range(count)]
    merged = []
    for a, b in zip(tiles[::2], tiles[1::2]):
        merged.append(two_sum(a[0], b[0]))
    tiles = merged
    while len(tiles) > 1:
        tiles = [pair_add(a, b) for a, b in zip(tiles[::2], tiles[1::2])]
    total = tiles[0]
    for by in (4, 2, 1):
        total = pair_add(total, tuple(pltpu.roll(t, by, 0) for t in total))
    return pair_add(total, tuple(pltpu.roll(t, 64, 1) for t in total))


def merge_kernel(parts_ref, out_ref):
    total = sum_messages(parts_ref)
    lane = lane_index((8, COLS))
    out_ref[...] = jnp.where(lane < 64, total[0], total[1])


def combine_kernel(parts_ref, powers_ref, surface_ref, residual_ref, wide):
    total = sum_messages(parts_ref)
    moments = [
        tuple(jnp.broadcast_to(t[:, order : order + 1], (8, COLS)) for t in total)
        for order in range(2 * ITERS)
    ]
    rho = list(moments)
    delta = list(moments)
    one = jnp.ones((8, COLS), jnp.float32)
    zero = jnp.zeros((8, COLS), jnp.float32)
    res = [one] + [zero] * ITERS
    way = [one] + [zero] * ITERS
    sol = [zero] * ITERS
    for step in range(ITERS):
        alpha = pair_div(rho[step], delta[step + 1])
        sol = [s + alpha[0] * w for s, w in zip(sol, way)]
        res = [res[0]] + [r - alpha[0] * w for r, w in zip(res[1:], way)]
        if step == ITERS - 1:
            break
        before = rho[step]
        last = 2 * ITERS - 1 - step
        rho = [
            None if order <= step or order >= last
            else pair_add(rho[order], pair_neg(pair_mul(alpha, delta[order + 1])))
            for order in range(2 * ITERS)
        ]
        beta = pair_neg(pair_mul(alpha, pair_div(rho[step + 1], before)))
        delta = [
            None if order <= step or order >= last
            else pair_add(rho[order], pair_mul(beta, delta[order]))
            for order in range(2 * ITERS)
        ]
        way = [r + beta[0] * w for r, w in zip(res, way)]
    for weights, target, factor in ((sol, surface_ref, 0.125), (res, residual_ref, 1.0)):
        for i in range(MID // 8):
            for j in range(2):
                spot = (slice(8 * i, 8 * i + 8), slice(128 * j, 128 * j + 128))
                value = weights[0] * powers_ref[(0,) + spot]
                for index in range(1, len(weights)):
                    value = value + weights[index] * powers_ref[(index,) + spot]
                wide[spot] = value * factor
        target[...] = wide[HALO : HALO + ROWS, HALO : HALO + COLS]


def forward(axis, periodic):
    count = lax.axis_size(axis)
    pairs = [(i, i + 1) for i in range(count - 1)]
    return pairs + [(count - 1, 0)] if periodic else pairs


def backward(axis, periodic):
    return [(target, source) for source, target in forward(axis, periodic)]


def swap_near():
    return [(i, i ^ 1) for i in range(lax.axis_size("lon"))]


def swap_far():
    count = lax.axis_size("lon")
    return [(i, (i + 1) % count if i % 2 else (i - 1) % count) for i in range(count)]


def body(temp, kmt, kappa, helm, forcing, cutoff, conv_in, conv_mid, conv_late, conv_out):
    f32 = jnp.float32
    shape = jax.ShapeDtypeStruct
    blocks = lax.axis_size("lon")
    bf16 = jnp.bfloat16
    vmem = pl.BlockSpec(memory_space=pltpu.VMEM)
    cutoff = cutoff.reshape(1, ROWS)
    fields = (temp, kmt, kappa, helm, forcing, cutoff)
    slab = shape((CUT + 1, DEEP, COLS), f32)
    top, bottom = pl.pallas_call(
        slab_kernel,
        out_shape=(slab, slab),
        in_specs=[pl.BlockSpec(memory_space=pltpu.HBM)] * 6,
        out_specs=(vmem, vmem),
        scratch_shapes=(
            pltpu.VMEM((ROWS, COLS), jnp.int32),
            pltpu.VMEM((1, ROWS), jnp.int32),
            pltpu.SemaphoreType.DMA((10,)),
        ),
        compiler_params=pltpu.CompilerParams(vmem_limit_bytes=VMEM_LIMIT),
    )(*(pltpu.with_memory_space_constraint(field, pltpu.HBM) for field in fields))
    north = lax.ppermute(bottom, "lat", forward("lat", False))
    south = lax.ppermute(top, "lat", backward("lat", False))
    own = call(rows_kernel, shape((ROWS, FIELDS, COLS), f32), (), 10**6)(*fields)
    tables = [jnp.asarray(table) for table in filter_tables(blocks, COLS)]
    weights = call(
        weights_kernel,
        (
            shape((4 * FIELDS, 640), bf16),
            shape((256, 384), bf16),
            shape((256, 384), bf16),
            shape((48, 256), bf16),
        )
        + tuple(shape(table.shape, bf16) for table in tables[:3] for _ in range(2)),
        (),
        10**6,
    )(jnp.transpose(conv_in, (0, 2, 1)), conv_mid, conv_late, conv_out, *tables[:3])
    weights, splits = weights[:4], weights[4:]
    ends = shape((TALL // SLOTS, FIELDS, COLS), f32)
    rows, to_far, to_near = call(
        pack_kernel, (shape((TALL, FIELDS, COLS), f32), ends, ends)
    )(own, north, south)
    far = lax.ppermute(to_far, "lon", swap_far())
    near = lax.ppermute(to_near, "lon", swap_near())

    def closure_scratch(chunks):
        cells = chunks * COLS
        return (
            pltpu.VMEM((cells, 128), f32),
            pltpu.VMEM((cells, 128), f32),
            pltpu.VMEM((cells, 128), bf16),
            pltpu.VMEM((cells, 128), bf16),
        )

    block = shape((MID, LEV, COLS), f32)
    inside, line = call(
        interior_kernel,
        (block, shape((LEV, COLS), f32)),
        (pltpu.VMEM((TALL * FIELDS, COLS), bf16),) + closure_scratch(19),
        10**9,
    )(rows, *weights)
    lines, planes = call(
        edge_kernel,
        (block, shape((3, MID, 2 * COLS), f32)),
        (pltpu.VMEM((TALL, FIELDS, COLS), f32),) + closure_scratch(6),
    )(rows, far, near, inside, *weights)
    whole = lax.all_to_all(lines, "lon", split_axis=0, concat_axis=0, tiled=True)
    filtered = call(filter_kernel, shape((BLOCK * blocks, COLS), f32))(
        whole, line, *splits, *tables[3:]
    )
    back = lax.all_to_all(
        filtered.reshape(BLOCK * blocks, 1, COLS), "lon", split_axis=0, concat_axis=0, tiled=True
    ).reshape(BLOCK * blocks, COLS)
    everyone = blocks * lax.axis_size("lat")
    wide = everyone // 8
    both = ("lon", "lat")
    inner = [[wide * i + k for k in range(wide)] for i in range(8)]
    outer = [[wide * i + k for i in range(8)] for k in range(wide)]
    temp_new, powers, parts = call(
        powers_kernel,
        (
            shape((LEV, ROWS, COLS), f32),
            shape((ITERS + 1, MID, 2 * COLS), f32),
            shape((wide, COLS), f32),
        ),
    )(back, planes)
    parts = lax.all_to_all(
        parts, both, split_axis=0, concat_axis=0, tiled=True, axis_index_groups=inner
    )
    parts = call(merge_kernel, shape((8, COLS), f32))(parts)
    parts = lax.all_to_all(
        parts, both, split_axis=0, concat_axis=0, tiled=True, axis_index_groups=outer
    )
    surface, residual = call(
        combine_kernel,
        (shape((ROWS, COLS), f32), shape((ROWS, COLS), f32)),
        (pltpu.VMEM((MID, 2 * COLS), f32),),
    )(parts, powers)
    return temp_new, surface, residual


def solution(mesh):
    return jax.shard_map(
        body,
        mesh=mesh,
        in_specs=(
            P(None, "lat", "lon"),
            P("lat", "lon"),
            P("lat", "lon"),
            P("lat", "lon"),
            P("lat", "lon"),
            P("lat"),
            P(),
            P(),
            P(),
            P(),
        ),
        out_specs=(P(None, "lat", "lon"), P("lat", "lon"), P("lat", "lon")),
        check_vma=False,
    )
```

```python
import math

import jax
import jax.numpy as jnp
import numpy as np
from jax import lax
from jax.experimental import pallas as pl
from jax.experimental.pallas import tpu as pltpu
from jax.sharding import PartitionSpec as P

ITERS = 4
STEP = 0.25
LEV = 8
FIELDS = 16
KMT, KAPPA, HELM, FORCING, CUT = 8, 9, 10, 11, 12
HALO = 4
DEEP = 8
ROWS = 24
COLS = 128
TALL = ROWS + 2 * DEEP
MID = ROWS + 2 * HALO
BLOCK = LEV + 1
SLOTS = 20
VMEM_LIMIT = 48 * 1024 * 1024


def call(kernel, outs, scratch=(), flops=None):
    spec = pl.BlockSpec(memory_space=pltpu.VMEM)
    return pl.pallas_call(
        kernel,
        out_shape=outs,
        out_specs=jax.tree.map(lambda _: spec, outs),
        scratch_shapes=scratch,
        compiler_params=pltpu.CompilerParams(vmem_limit_bytes=VMEM_LIMIT),
        cost_estimate=flops
        and pl.CostEstimate(flops=flops, bytes_accessed=10**6, transcendentals=flops // 500),
    )


def lane_index(shape):
    return lax.broadcasted_iota(jnp.int32, shape, len(shape) - 1)


def slab_kernel(
    temp_hbm, kmt_hbm, kappa_hbm, helm_hbm, forcing_hbm, cutoff_hbm,
    top_ref, bottom_ref, kmt, cutoff, sems,
):
    pairs = [(kmt_hbm, kmt), (cutoff_hbm, cutoff)]
    for target, start in ((top_ref, 0), (bottom_ref, ROWS - DEEP)):
        rows = pl.ds(start, DEEP)
        pairs.append((temp_hbm.at[:, rows], target.at[pl.ds(0, LEV)]))
        for source, field in ((kappa_hbm, KAPPA), (helm_hbm, HELM), (forcing_hbm, FORCING)):
            pairs.append((source.at[rows], target.at[field]))
    moves = [
        pltpu.make_async_copy(source, target, sems.at[index])
        for index, (source, target) in enumerate(pairs)
    ]
    for move in moves:
        move.start()
    for move in moves:
        move.wait()
    kept = cutoff_rows(cutoff)
    for target, start in ((top_ref, 0), (bottom_ref, ROWS - DEEP)):
        target[KMT] = kmt[start : start + DEEP].astype(jnp.float32)
        target[CUT] = kept[start : start + DEEP]


def cutoff_rows(cutoff_ref):
    kept = jnp.broadcast_to(cutoff_ref[...].astype(jnp.float32), (ROWS, ROWS))
    row = lax.broadcasted_iota(jnp.int32, (ROWS, ROWS), 0)
    kept = jnp.sum(jnp.where(row == lane_index((ROWS, ROWS)), kept, 0.0), axis=1, keepdims=True)
    return jnp.broadcast_to(kept, (ROWS, COLS))


def prepare_kernel(*refs):
    sources, refs = refs[:13], refs[13:]
    outs, refs = refs[:11], refs[11:]
    held, sems = refs[:13], refs[13]
    moves = [
        pltpu.make_async_copy(source, target, sems.at[index])
        for index, (source, target) in enumerate(zip(sources, held))
    ]
    for move in moves:
        move.start()
    for move in moves:
        move.wait()
    fill_rows(*held[:6], outs[0])
    fill_weights(*held[6:10], *outs[1:5])
    for index, table in enumerate(held[10:]):
        outs[5 + 2 * index][...], outs[6 + 2 * index][...] = halves(table[...])


def fill_rows(temp_ref, kmt_ref, kappa_ref, helm_ref, forcing_ref, cutoff_ref, own_ref):
    own_ref[:, CUT + 1 :, :] = jnp.zeros((ROWS, FIELDS - CUT - 1, COLS), jnp.float32)
    for level in range(LEV):
        own_ref[:, level, :] = temp_ref[level]
    own_ref[:, KMT, :] = kmt_ref[...].astype(jnp.float32)
    own_ref[:, KAPPA, :] = kappa_ref[...]
    own_ref[:, HELM, :] = helm_ref[...]
    own_ref[:, FORCING, :] = forcing_ref[...]
    own_ref[:, CUT, :] = cutoff_rows(cutoff_ref)


def fill_weights(
    first_ref, mid_ref, late_ref, last_ref, w_in_ref, w_mid_ref, w_late_ref, w_out_ref
):
    w_in_ref[...] = jnp.zeros(w_in_ref.shape, w_in_ref.dtype)
    width = mid_ref.shape[1]
    none = jnp.zeros((LEV, width), jnp.float32)
    for row in range(4):
        parts = []
        for tap in range(3):
            for parity in range(2):
                a = row - parity
                parts.append(first_ref[3 * a + tap].astype(jnp.float32) if 0 <= a < 3 else none)
        top = jnp.concatenate(parts, axis=1)
        marks = [jnp.ones((1, width), jnp.float32) if row == at else none[:1] for at in (1, 2, 2, 3)]
        marks = jnp.concatenate(marks, axis=1)
        block = jnp.concatenate(
            [
                jnp.concatenate([top, jnp.zeros((LEV, 4 * width), jnp.float32)], axis=1),
                jnp.concatenate(
                    [
                        jnp.concatenate([jnp.zeros((1, 6 * width), jnp.float32), marks], axis=1),
                        jnp.zeros((LEV - 1, 10 * width), jnp.float32),
                    ],
                    axis=0,
                ),
            ],
            axis=0,
        )
        w_in_ref[FIELDS * row : FIELDS * (row + 1)] = block.astype(jnp.bfloat16)

    def rows_of(ref, tap, parity):
        outs = ref.shape[1]
        blank = jnp.zeros((outs, width), jnp.float32)
        parts = []
        for row in range(4):
            a = row - parity
            parts.append(ref[3 * a + tap].astype(jnp.float32) if 0 <= a < 3 else blank)
        return jnp.concatenate(parts, axis=1)

    for ref, out_ref in ((mid_ref, w_mid_ref), (late_ref, w_late_ref)):
        for tap in range(3):
            both = jnp.concatenate([rows_of(ref, tap, 0), rows_of(ref, tap, 1)], axis=0)
            out_ref[:, 2 * width * tap : 2 * width * (tap + 1)] = both.T.astype(jnp.bfloat16)
    w_out_ref[...] = jnp.concatenate(
        [rows_of(last_ref, tap, parity) for tap in range(3) for parity in range(2)], axis=0
    ).astype(jnp.bfloat16)


def pack_kernel(own_ref, north_ref, south_ref, rows_ref, far_ref, near_ref):
    even = lax.rem(lax.axis_index("lon"), 2) == 0
    rows_ref[DEEP : DEEP + ROWS] = own_ref[...]
    for slab_ref, start in ((north_ref, 0), (south_ref, DEEP + ROWS)):
        rows = slice(start, start + DEEP)
        rows_ref[rows, CUT + 1 :, :] = jnp.zeros((DEEP, FIELDS - CUT - 1, COLS), jnp.float32)
        for field in range(CUT + 1):
            rows_ref[rows, field, :] = slab_ref[field]
    lane = lane_index((FIELDS, COLS))
    for part in range(TALL // SLOTS):
        first = jnp.zeros((FIELDS, COLS), jnp.float32)
        last = jnp.zeros((FIELDS, COLS), jnp.float32)
        for slot in range(SLOTS):
            here = rows_ref[part * SLOTS + slot]
            inside = (lane >= HALO * slot) & (lane < HALO * (slot + 1))
            first = jnp.where(inside, pltpu.roll(here, HALO * slot, 1) if slot else here, first)
            last = jnp.where(inside, pltpu.roll(here, HALO * (slot + 1), 1), last)
        far_ref[part] = jnp.where(even, first, last)
        near_ref[part] = jnp.where(even, last, first)


def closure_layers(window, pairs, stride, weights, acts, masks):
    w_in_ref, w_mid_ref, w_late_ref, w_out_ref = weights
    act_a, act_b = acts
    mask_odd, mask_even = masks

    def chunks(count):
        return range(-(-count * stride // COLS))

    def at(chunk, shift=0):
        return slice(COLS * chunk + shift, COLS * (chunk + 1) + shift)

    def both(act, chunk):
        return jnp.concatenate([act[at(chunk)], act[at(chunk, stride)]], axis=1)

    def finish(total, mask):
        v = (
            pltpu.roll(total[:, 0:128], 1, 0)
            + total[:, 128:256]
            + pltpu.roll(total[:, 256:384], COLS - 1, 0)
        )
        return (mask * (v / (1.0 + jnp.exp(-v)))).astype(jnp.bfloat16)

    for chunk in chunks(pairs):
        total = lax.dot_general(
            window(chunk),
            w_in_ref[...],
            (((0,), (0,)), ((), ())),
            preferred_element_type=jnp.float32,
        )
        mask_odd[at(chunk)] = total[:, 384:512]
        mask_even[at(chunk)] = total[:, 512:640]
        act_a[at(chunk)] = finish(total, total[:, 384:512])
    for chunk in chunks(pairs - 1):
        total = jnp.dot(both(act_a, chunk), w_mid_ref[...], preferred_element_type=jnp.float32)
        act_b[at(chunk)] = finish(total, mask_even[at(chunk)])
    for chunk in chunks(pairs - 2):
        total = jnp.dot(both(act_b, chunk), w_late_ref[...], preferred_element_type=jnp.float32)
        act_a[at(chunk)] = finish(total, mask_odd[at(chunk, stride)])
    results = []
    for chunk in chunks(pairs - 3):
        total = lax.dot_general(
            w_out_ref[...],
            both(act_a, chunk),
            (((1,), (1,)), ((), ())),
            preferred_element_type=jnp.float32,
        )
        results.append(
            pltpu.roll(total[0:16], 1, 1) + total[16:32] + pltpu.roll(total[32:48], COLS - 1, 1)
        )
    return results


def level_index():
    return lax.broadcasted_iota(jnp.int32, (LEV, COLS), 0).astype(jnp.float32)


def wetness(block):
    return (level_index() < block[KMT : KMT + 1]).astype(jnp.float32)


def first_input(block):
    wet = wetness(block)
    sea = jnp.where(level_index() == 0.0, wet, 0.0)
    return jnp.concatenate([wet * block[0:LEV], sea], axis=0).astype(jnp.bfloat16)


def advance(here, north, south, closure):
    wet = wetness(here)
    temp = here[0:LEV]
    tracer = wet * temp
    kappa = jnp.broadcast_to(here[KAPPA : KAPPA + 1], (LEV, COLS))
    diff = jnp.zeros((LEV, COLS), jnp.float32)
    for near in (south, north):
        near_w = wetness(near)
        diff = diff + near_w * 0.5 * (kappa + near[KAPPA : KAPPA + 1]) * (
            near_w * near[0:LEV] - tracer
        )
    for by in (COLS - 1, 1):
        diff = diff + pltpu.roll(wet, by, 1) * 0.5 * (kappa + pltpu.roll(kappa, by, 1)) * (
            pltpu.roll(tracer, by, 1) - tracer
        )
    diff = wet * diff
    eddy = wet * closure
    return wet * (temp + STEP * (diff + eddy))


FIRST = DEEP - HALO


def interior_kernel(
    rows_ref, w_in_ref, w_mid_ref, w_late_ref, w_out_ref, out_ref, line_ref,
    start, mask_odd, mask_even, act_a, act_b,
):
    for row in range(TALL):
        start[row * FIELDS : (row + 1) * FIELDS] = first_input(rows_ref[row])
    results = closure_layers(
        lambda chunk: start[2 * FIELDS * chunk : 2 * FIELDS * (chunk + 2)],
        TALL // 2 - 1,
        COLS,
        (w_in_ref, w_mid_ref, w_late_ref, w_out_ref),
        (act_a, act_b),
        (mask_odd, mask_even),
    )
    for pair, closure in enumerate(results):
        for parity in range(2):
            row = FIRST + 2 * pair + parity
            out_ref[2 * pair + parity] = advance(
                rows_ref[row],
                rows_ref[row - 1],
                rows_ref[row + 1],
                closure[LEV * parity : LEV * (parity + 1)],
            )
    own_line = lax.axis_index("lon") + FIRST
    line_ref[...] = rows_ref[own_line, LEV:FIELDS, :]


STRIP = 32
PER = COLS // STRIP


def edge_kernel(
    rows_ref, far_ref, near_ref, inside_ref, w_in_ref, w_mid_ref, w_late_ref, w_out_ref,
    out_ref, planes_ref, strips, mask_odd, mask_even, act_a, act_b,
):
    lane = lane_index((FIELDS, COLS))
    even = lax.rem(lax.axis_index("lon"), 2) == 0
    parts = range(TALL // SLOTS)
    from_west = [jnp.where(even, far_ref[part], near_ref[part]) for part in parts]
    from_east = [jnp.where(even, near_ref[part], far_ref[part]) for part in parts]
    for row in range(TALL):
        part, slot = row // SLOTS, row % SLOTS
        here = rows_ref[row]
        strip = jnp.where(lane < 24, pltpu.roll(from_east[part], (20 - HALO * slot) % COLS, 1) if slot != 5 else from_east[part], 0.0)
        strip = jnp.where(lane < 20, pltpu.roll(here, 20, 1), strip)
        strip = jnp.where(lane < 12, pltpu.roll(here, 4, 1), strip)
        west = pltpu.roll(from_west[part], COLS - HALO * slot, 1) if slot else from_west[part]
        strips[row] = jnp.where(lane < 4, west, strip)

    def side_by_side(parity, start):
        total = None
        for slot in range(PER):
            row = 2 * (start + slot) + parity
            if row >= TALL:
                continue
            piece = strips[row]
            piece = pltpu.roll(piece, STRIP * slot, 1) if slot else piece
            total = piece if total is None else total + piece
        return total

    def window(chunk):
        at = PER * chunk
        return jnp.concatenate(
            [
                first_input(block)
                for block in (
                    side_by_side(0, at),
                    side_by_side(1, at),
                    side_by_side(0, at + 1),
                    side_by_side(1, at + 1),
                )
            ],
            axis=0,
        )

    act_a[5 * COLS :] = jnp.zeros((COLS, COLS), jnp.bfloat16)
    act_b[5 * COLS :] = jnp.zeros((COLS, COLS), jnp.bfloat16)
    mask_odd[5 * COLS :] = jnp.zeros((COLS, COLS), jnp.float32)
    results = closure_layers(
        window,
        TALL // 2 - 1,
        STRIP,
        (w_in_ref, w_mid_ref, w_late_ref, w_out_ref),
        (act_a, act_b),
        (mask_odd, mask_even),
    )
    at_lane = lane_index((LEV, COLS))
    for chunk in range(4):
        at = PER * chunk + FIRST // 2
        closure = results[chunk]
        north = side_by_side(1, at - 1)
        upper = side_by_side(0, at)
        lower = side_by_side(1, at)
        south = side_by_side(0, at + 1)
        for parity, value in (
            (0, advance(upper, north, lower, closure[0:LEV])),
            (1, advance(lower, upper, south, closure[LEV : 2 * LEV])),
        ):
            for slot in range(PER):
                row = 2 * (PER * chunk + slot) + parity
                left = pltpu.roll(value, COLS - STRIP * slot - 4, 1)
                shift = (108 - STRIP * slot) % COLS
                right = pltpu.roll(value, shift, 1)
                out_ref[row] = jnp.where(
                    at_lane < HALO,
                    left,
                    jnp.where(at_lane >= COLS - HALO, right, inside_ref[row]),
                )
    plane_lane = lane_index((MID, COLS))
    for index, field in enumerate((KMT, HELM, FORCING)):
        moved = pltpu.roll(rows_ref[FIRST : FIRST + MID, field, :], HALO, 1)
        edge = strips[FIRST : FIRST + MID, field, :]
        planes_ref[index, :, 0:COLS] = jnp.where(plane_lane < HALO, edge, moved)
        planes_ref[index, :, COLS:] = jnp.where(
            plane_lane < HALO,
            moved,
            jnp.where(plane_lane < 2 * HALO, pltpu.roll(edge, COLS - 16, 1), 0.0),
        )


def filter_tables(blocks, width):
    length = blocks * width
    half = LEV // 2
    k = np.arange(blocks)
    outer = np.exp(-2j * np.pi * ((k[:, None] * k[None, :]) % blocks) / blocks)
    spread = np.zeros((blocks, 2, half, blocks, 2, half))
    for line in range(half):
        spread[:, 0, line, :, 0, line] = outer.real
        spread[:, 0, line, :, 1, line] = -outer.imag
        spread[:, 1, line, :, 0, line] = outer.imag
        spread[:, 1, line, :, 1, line] = outer.real
    spread = spread.reshape(blocks * LEV, blocks * LEV)
    m = np.arange(width)
    twist = np.exp(-2j * np.pi * (k[:, None] * m[None, :]) / length)
    sign = np.where(np.arange(LEV) < half, -1.0, 1.0)[None, :, None]
    twist_re = np.broadcast_to(twist.real[:, None, :], (blocks, LEV, width))
    twist_im = twist.imag[:, None, :] * sign
    inner = np.exp(-2j * np.pi * ((m[:, None] * m[None, :]) % width) / width)
    inner = np.concatenate([inner.real, inner.imag], axis=1)
    return [
        np.asarray(t, np.float32)
        for t in (spread, spread.T / length, inner, twist_re, twist_im)
    ]


def halves(x):
    high = x.astype(jnp.bfloat16)
    return high, (x - high.astype(jnp.float32)).astype(jnp.bfloat16)


def split_dot(a, b):
    def dot(x, y):
        return jnp.dot(x, y, preferred_element_type=jnp.float32)

    return dot(a[0], b[0]) + (dot(a[0], b[1]) + dot(a[1], b[0]))


def filter_kernel(
    x_ref, line_ref, spread_ref, spread_low, back_ref, back_low, inner_ref, inner_low,
    twist_re_ref, twist_im_ref, out_ref,
):
    blocks, lev, width = x_ref.shape
    shape = (blocks, lev, width)
    flat = (blocks * lev, width)
    length = blocks * width
    inner = (inner_ref[...], inner_low[...])

    def partner(block):
        return pltpu.roll(block, lev // 2, 1)

    sign = jnp.where(lax.broadcasted_iota(jnp.int32, shape, 1) < lev // 2, -1.0, 1.0)
    y = split_dot((spread_ref[...], spread_low[...]), halves(x_ref[...].reshape(flat)))
    y = y.reshape(shape)
    y = y * twist_re_ref[...] + partner(y) * twist_im_ref[...]
    s = split_dot(halves(y.reshape(flat)), inner)
    s = s[:, 0:width].reshape(shape) + partner(s[:, width:].reshape(shape)) * sign
    wave = lax.broadcasted_iota(jnp.int32, shape, 0) + blocks * lane_index(shape)
    folded = jnp.minimum(wave, length - wave).astype(jnp.float32)
    s = jnp.where(folded < line_ref[CUT - LEV : CUT - LEV + 1, :][None], s, 0.0)
    y = split_dot(halves(s.reshape(flat)), inner)
    y = y[:, 0:width].reshape(shape) - partner(y[:, width:].reshape(shape)) * sign
    y = y * twist_re_ref[...] - partner(y) * twist_im_ref[...]
    x = split_dot((back_ref[...], back_low[...]), halves(y.reshape(flat))).reshape(shape)
    lane = lane_index((lev, width))
    moved = [pltpu.roll(x[block], HALO, 1) for block in range(blocks)]
    for block in range(blocks):
        edge = jnp.where(lane < HALO, moved[block - 1], moved[(block + 1) % blocks])
        edge = jnp.where(lane < 2 * HALO, edge, 0.0)
        edge = pltpu.roll(edge, 0, 1, stride=2 * HALO, stride_axis=0)
        row = BLOCK * block
        out_ref[row : row + lev, :] = x[block]
        out_ref[row + lev : row + BLOCK, :] = jnp.sum(edge, axis=0, keepdims=True)


def two_sum(a, b):
    s = a + b
    t = s - a
    return s, (a - (s - t)) + (b - t)


def quick_sum(a, b):
    s = a + b
    return s, b - (s - a)


def split(a):
    c = a * 4097.0
    high = c - (c - a)
    return high, a - high


def two_product(a, b):
    p = a * b
    ah, al = split(a)
    bh, bl = split(b)
    return p, ((ah * bh - p) + ah * bl + al * bh) + al * bl


def pair_add(a, b):
    s, e = two_sum(a[0], b[0])
    return quick_sum(s, e + (a[1] + b[1]))


def pair_neg(a):
    return -a[0], -a[1]


def pair_mul(a, b):
    p, e = two_product(a[0], b[0])
    return quick_sum(p, e + (a[0] * b[1] + a[1] * b[0]))


def pair_div(a, b):
    q = a[0] / b[0]
    rest = pair_add(a, pair_neg(pair_mul((q, jnp.zeros_like(q)), b)))
    r = rest[0] / b[0]
    rest = pair_add(rest, pair_neg(pair_mul((r, jnp.zeros_like(r)), b)))
    return quick_sum(*quick_sum(q, r + rest[0] / b[0]))


def powers_kernel(x_ref, planes_ref, temp_ref, powers_ref, parts_ref):
    lane = lane_index((LEV, COLS))
    wide_lane = lane_index((MID, COLS))
    kmt_left = planes_ref[0, :, 0:COLS]
    kmt_right = planes_ref[0, :, COLS:]
    kmt = pltpu.roll(jnp.where(wide_lane < HALO, kmt_right, kmt_left), COLS - HALO, 1)
    mean = jnp.zeros((MID, COLS), jnp.float32)
    for level in range(LEV):
        temp_ref[level] = x_ref[pl.ds(HALO * BLOCK + level, ROWS, stride=BLOCK), :]
        here = x_ref[pl.ds(level, MID, stride=BLOCK), :]
        mean = mean + jnp.where(kmt > level, here, 0.0)
    edge = x_ref[pl.ds(LEV, MID, stride=BLOCK), :]
    edge_kmt = jnp.where(wide_lane < HALO, kmt_left, kmt_right)
    edge_kmt = jnp.where(wide_lane < 2 * HALO, edge_kmt, 0.0)
    for by in (8, 16, 32, 64):
        edge_kmt = edge_kmt + pltpu.roll(edge_kmt, by, 1)
    edge = jnp.where(edge_kmt > (wide_lane // (2 * HALO)).astype(jnp.float32), edge, 0.0)
    for by in (64, 32, 16, 8):
        edge = edge + pltpu.roll(edge, by, 1)
    moved = pltpu.roll(mean, HALO, 1)
    mean = jnp.concatenate(
        [
            jnp.where(wide_lane < HALO, edge, moved),
            jnp.where(wide_lane < HALO, moved, jnp.where(wide_lane < 2 * HALO, edge, 0.0)),
        ],
        axis=1,
    )
    sea = (planes_ref[0] > 0.0).astype(jnp.float32)

    def around(v):
        return (
            pltpu.roll(v, 1, 0)
            + pltpu.roll(v, MID - 1, 0)
            + pltpu.roll(v, 1, 1)
            + pltpu.roll(v, 2 * COLS - 1, 1)
        )

    diagonal = planes_ref[1] + sea * around(sea)
    powers = [sea * (mean * (1.0 / LEV) + planes_ref[2])]
    for _ in range(ITERS):
        v = powers[-1]
        powers.append((diagonal * v - sea * around(v)) * 0.125)
    for index, v in enumerate(powers):
        powers_ref[index] = v
    row = lax.broadcasted_iota(jnp.int32, (MID, 2 * COLS), 0)
    column = lane_index((MID, 2 * COLS))
    own = (
        (row >= HALO) & (row < HALO + ROWS) & (column >= HALO) & (column < HALO + COLS)
    )
    owned = [jnp.where(own, v, 0.0) for v in powers]
    high_rows, low_rows = [], []
    for order in range(2 * ITERS):
        p, e = two_product(owned[order // 2], owned[order - order // 2])
        tiles = [
            (p[8 * i : 8 * i + 8, 128 * j : 128 * j + 128], e[8 * i : 8 * i + 8, 128 * j : 128 * j + 128])
            for i in range(MID // 8)
            for j in range(2)
        ]
        while len(tiles) > 1:
            tiles = [pair_add(a, b) for a, b in zip(tiles[::2], tiles[1::2])]
        total = tiles[0]
        for by in (4, 2, 1):
            total = pair_add(total, tuple(pltpu.roll(t, by, 0) for t in total))
        high_rows.append(total[0])
        low_rows.append(total[1])
    where = lax.broadcasted_iota(jnp.int32, (8, COLS), 0)
    high, low = high_rows[0], low_rows[0]
    for order in range(1, 2 * ITERS):
        high = jnp.where(where == order, high_rows[order], high)
        low = jnp.where(where == order, low_rows[order], low)
    total = (high, low)
    for by in (64, 32, 16, 8, 4, 2, 1):
        total = pair_add(total, tuple(pltpu.roll(t, by, 1) for t in total))
    spot = lax.broadcasted_iota(jnp.int32, (8, COLS), 0)
    message = jnp.where(lane == spot, total[0], 0.0) + jnp.where(lane == spot + 64, total[1], 0.0)
    message = jnp.sum(message, axis=0, keepdims=True)
    parts_ref[...] = jnp.broadcast_to(message, parts_ref.shape)


def sum_messages(parts_ref):
    count = parts_ref.shape[0] // 8
    if count == 1:
        total = (parts_ref[...], jnp.zeros((8, COLS), jnp.float32))
        for by in (4, 2, 1):
            total = pair_add(total, tuple(pltpu.roll(t, by, 0) for t in total))
        return pair_add(total, tuple(pltpu.roll(t, 64, 1) for t in total))
    tiles = [(parts_ref[8 * i : 8 * i + 8, :], None) for i in range(count)]
    merged = []
    for a, b in zip(tiles[::2], tiles[1::2]):
        merged.append(two_sum(a[0], b[0]))
    tiles = merged
    while len(tiles) > 1:
        tiles = [pair_add(a, b) for a, b in zip(tiles[::2], tiles[1::2])]
    total = tiles[0]
    for by in (4, 2, 1):
        total = pair_add(total, tuple(pltpu.roll(t, by, 0) for t in total))
    return pair_add(total, tuple(pltpu.roll(t, 64, 1) for t in total))


def merge_kernel(parts_ref, out_ref):
    total = sum_messages(parts_ref)
    lane = lane_index((8, COLS))
    out_ref[...] = jnp.where(lane < 64, total[0], total[1])


def combine_kernel(parts_ref, powers_ref, surface_ref, residual_ref, wide):
    total = sum_messages(parts_ref)
    moments = [
        tuple(jnp.broadcast_to(t[:, order : order + 1], (8, COLS)) for t in total)
        for order in range(2 * ITERS)
    ]
    rho = list(moments)
    delta = list(moments)
    one = jnp.ones((8, COLS), jnp.float32)
    zero = jnp.zeros((8, COLS), jnp.float32)
    res = [one] + [zero] * ITERS
    way = [one] + [zero] * ITERS
    sol = [zero] * ITERS
    for step in range(ITERS):
        alpha = pair_div(rho[step], delta[step + 1])
        sol = [s + alpha[0] * w for s, w in zip(sol, way)]
        res = [res[0]] + [r - alpha[0] * w for r, w in zip(res[1:], way)]
        if step == ITERS - 1:
            break
        before = rho[step]
        last = 2 * ITERS - 1 - step
        rho = [
            None if order <= step or order >= last
            else pair_add(rho[order], pair_neg(pair_mul(alpha, delta[order + 1])))
            for order in range(2 * ITERS)
        ]
        beta = pair_neg(pair_mul(alpha, pair_div(rho[step + 1], before)))
        delta = [
            None if order <= step or order >= last
            else pair_add(rho[order], pair_mul(beta, delta[order]))
            for order in range(2 * ITERS)
        ]
        way = [r + beta[0] * w for r, w in zip(res, way)]
    for weights, target, factor in ((sol, surface_ref, 0.125), (res, residual_ref, 1.0)):
        for i in range(MID // 8):
            for j in range(2):
                spot = (slice(8 * i, 8 * i + 8), slice(128 * j, 128 * j + 128))
                value = weights[0] * powers_ref[(0,) + spot]
                for index in range(1, len(weights)):
                    value = value + weights[index] * powers_ref[(index,) + spot]
                wide[spot] = value * factor
        target[...] = wide[HALO : HALO + ROWS, HALO : HALO + COLS]


def forward(axis, periodic):
    count = lax.axis_size(axis)
    pairs = [(i, i + 1) for i in range(count - 1)]
    return pairs + [(count - 1, 0)] if periodic else pairs


def backward(axis, periodic):
    return [(target, source) for source, target in forward(axis, periodic)]


def swap_near():
    return [(i, i ^ 1) for i in range(lax.axis_size("lon"))]


def swap_far():
    count = lax.axis_size("lon")
    return [(i, (i + 1) % count if i % 2 else (i - 1) % count) for i in range(count)]


def body(temp, kmt, kappa, helm, forcing, cutoff, conv_in, conv_mid, conv_late, conv_out):
    f32 = jnp.float32
    shape = jax.ShapeDtypeStruct
    blocks = lax.axis_size("lon")
    bf16 = jnp.bfloat16
    vmem = pl.BlockSpec(memory_space=pltpu.VMEM)
    cutoff = cutoff.reshape(1, ROWS)
    fields = (temp, kmt, kappa, helm, forcing, cutoff)
    slab = shape((CUT + 1, DEEP, COLS), f32)
    top, bottom = pl.pallas_call(
        slab_kernel,
        out_shape=(slab, slab),
        in_specs=[pl.BlockSpec(memory_space=pltpu.HBM)] * 6,
        out_specs=(vmem, vmem),
        scratch_shapes=(
            pltpu.VMEM((ROWS, COLS), jnp.int32),
            pltpu.VMEM((1, ROWS), jnp.int32),
            pltpu.SemaphoreType.DMA((10,)),
        ),
        compiler_params=pltpu.CompilerParams(vmem_limit_bytes=VMEM_LIMIT),
    )(*(pltpu.with_memory_space_constraint(field, pltpu.HBM) for field in fields))
    north = lax.ppermute(bottom, "lat", forward("lat", False))
    south = lax.ppermute(top, "lat", backward("lat", False))
    tables = [jnp.asarray(table) for table in filter_tables(blocks, COLS)]
    sources = fields + (jnp.transpose(conv_in, (0, 2, 1)), conv_mid, conv_late, conv_out)
    sources = sources + tuple(tables[:3])
    outs = (
        shape((ROWS, FIELDS, COLS), f32),
        shape((4 * FIELDS, 640), bf16),
        shape((256, 384), bf16),
        shape((256, 384), bf16),
        shape((48, 256), bf16),
    ) + tuple(shape(table.shape, bf16) for table in tables[:3] for _ in range(2))
    own, *prepared = pl.pallas_call(
        prepare_kernel,
        out_shape=outs,
        in_specs=[pl.BlockSpec(memory_space=pltpu.HBM)] * len(sources),
        out_specs=(vmem,) * len(outs),
        scratch_shapes=tuple(pltpu.VMEM(source.shape, source.dtype) for source in sources)
        + (pltpu.SemaphoreType.DMA((len(sources),)),),
        compiler_params=pltpu.CompilerParams(vmem_limit_bytes=VMEM_LIMIT),
        cost_estimate=pl.CostEstimate(flops=10**6, bytes_accessed=2 * 10**6, transcendentals=0),
    )(*(pltpu.with_memory_space_constraint(source, pltpu.HBM) for source in sources))
    weights, splits = prepared[:4], prepared[4:]
    ends = shape((TALL // SLOTS, FIELDS, COLS), f32)
    rows, to_far, to_near = call(
        pack_kernel, (shape((TALL, FIELDS, COLS), f32), ends, ends)
    )(own, north, south)
    far = lax.ppermute(to_far, "lon", swap_far())
    near = lax.ppermute(to_near, "lon", swap_near())

    def closure_scratch(chunks):
        cells = chunks * COLS
        return (
            pltpu.VMEM((cells, 128), f32),
            pltpu.VMEM((cells, 128), f32),
            pltpu.VMEM((cells, 128), bf16),
            pltpu.VMEM((cells, 128), bf16),
        )

    block = shape((MID, LEV, COLS), f32)
    inside, line = call(
        interior_kernel,
        (block, shape((LEV, COLS), f32)),
        (pltpu.VMEM((TALL * FIELDS, COLS), bf16),) + closure_scratch(19),
        10**9,
    )(rows, *weights)
    lines, planes = call(
        edge_kernel,
        (block, shape((3, MID, 2 * COLS), f32)),
        (pltpu.VMEM((TALL, FIELDS, COLS), f32),) + closure_scratch(6),
    )(rows, far, near, inside, *weights)
    whole = lax.all_to_all(lines, "lon", split_axis=0, concat_axis=0, tiled=True)
    filtered = call(filter_kernel, shape((BLOCK * blocks, COLS), f32))(
        whole, line, *splits, *tables[3:]
    )
    back = lax.all_to_all(
        filtered.reshape(BLOCK * blocks, 1, COLS), "lon", split_axis=0, concat_axis=0, tiled=True
    ).reshape(BLOCK * blocks, COLS)
    everyone = blocks * lax.axis_size("lat")
    wide = everyone // 8
    both = ("lon", "lat")
    inner = [[wide * i + k for k in range(wide)] for i in range(8)]
    outer = [[wide * i + k for i in range(8)] for k in range(wide)]
    temp_new, powers, parts = call(
        powers_kernel,
        (
            shape((LEV, ROWS, COLS), f32),
            shape((ITERS + 1, MID, 2 * COLS), f32),
            shape((wide, COLS), f32),
        ),
    )(back, planes)
    parts = lax.all_to_all(
        parts, both, split_axis=0, concat_axis=0, tiled=True, axis_index_groups=inner
    )
    parts = call(merge_kernel, shape((8, COLS), f32))(parts)
    parts = lax.all_to_all(
        parts, both, split_axis=0, concat_axis=0, tiled=True, axis_index_groups=outer
    )
    surface, residual = call(
        combine_kernel,
        (shape((ROWS, COLS), f32), shape((ROWS, COLS), f32)),
        (pltpu.VMEM((MID, 2 * COLS), f32),),
    )(parts, powers)
    return temp_new, surface, residual


def solution(mesh):
    return jax.shard_map(
        body,
        mesh=mesh,
        in_specs=(
            P(None, "lat", "lon"),
            P("lat", "lon"),
            P("lat", "lon"),
            P("lat", "lon"),
            P("lat", "lon"),
            P("lat"),
            P(),
            P(),
            P(),
            P(),
        ),
        out_specs=(P(None, "lat", "lon"), P("lat", "lon"), P("lat", "lon")),
        check_vma=False,
    )
```

```python
import math

import jax
import jax.numpy as jnp
import numpy as np
from jax import lax
from jax.experimental import pallas as pl
from jax.experimental.pallas import tpu as pltpu
from jax.sharding import PartitionSpec as P

ITERS = 4
STEP = 0.25
LEV = 8
FIELDS = 16
KMT, KAPPA, HELM, FORCING, CUT = 8, 9, 10, 11, 12
BAND = 48
HALO = 4
DEEP = 8
ROWS = 24
COLS = 128
TALL = ROWS + 2 * DEEP
MID = ROWS + 2 * HALO
BLOCK = LEV + 1
SLOTS = 20
VMEM_LIMIT = 48 * 1024 * 1024


def call(kernel, outs, scratch=(), flops=None):
    spec = pl.BlockSpec(memory_space=pltpu.VMEM)
    return pl.pallas_call(
        kernel,
        out_shape=outs,
        out_specs=jax.tree.map(lambda _: spec, outs),
        scratch_shapes=scratch,
        compiler_params=pltpu.CompilerParams(vmem_limit_bytes=VMEM_LIMIT),
        cost_estimate=flops
        and pl.CostEstimate(flops=flops, bytes_accessed=10**6, transcendentals=flops // 500),
    )


def lane_index(shape):
    return lax.broadcasted_iota(jnp.int32, shape, len(shape) - 1)


def fetching(kernel, outs, sources, held, before=()):
    spec = pl.BlockSpec(memory_space=pltpu.VMEM)
    return pl.pallas_call(
        kernel,
        out_shape=outs,
        in_specs=[pl.BlockSpec(memory_space=pl.ANY)] * len(before)
        + [pl.BlockSpec(memory_space=pltpu.HBM)] * len(sources),
        out_specs=jax.tree.map(lambda _: spec, outs),
        scratch_shapes=tuple(pltpu.VMEM(source.shape, source.dtype) for source in held)
        + (pltpu.SemaphoreType.DMA((len(sources),)),),
        compiler_params=pltpu.CompilerParams(vmem_limit_bytes=VMEM_LIMIT),
        cost_estimate=pl.CostEstimate(flops=10**6, bytes_accessed=2 * 10**6, transcendentals=0),
    )(*before, *(pltpu.with_memory_space_constraint(source, pltpu.HBM) for source in sources))


def slab_kernel(
    temp_hbm, kmt_hbm, kappa_hbm, helm_hbm, forcing_hbm, cutoff_hbm,
    top_ref, bottom_ref, kmt, cutoff, sems,
):
    pairs = [(kmt_hbm, kmt), (cutoff_hbm, cutoff)]
    for target, start in ((top_ref, 0), (bottom_ref, ROWS - DEEP)):
        rows = pl.ds(start, DEEP)
        pairs.append((temp_hbm.at[:, rows], target.at[pl.ds(0, LEV)]))
        for source, field in ((kappa_hbm, KAPPA), (helm_hbm, HELM), (forcing_hbm, FORCING)):
            pairs.append((source.at[rows], target.at[field]))
    moves = [
        pltpu.make_async_copy(source, target, sems.at[index])
        for index, (source, target) in enumerate(pairs)
    ]
    for move in moves:
        move.start()
    for move in moves:
        move.wait()
    kept = cutoff_rows(cutoff)
    for target, start in ((top_ref, 0), (bottom_ref, ROWS - DEEP)):
        target[KMT] = kmt[start : start + DEEP].astype(jnp.float32)
        target[CUT] = kept[start : start + DEEP]


def cutoff_rows(cutoff_ref):
    kept = jnp.broadcast_to(cutoff_ref[...].astype(jnp.float32), (ROWS, ROWS))
    row = lax.broadcasted_iota(jnp.int32, (ROWS, ROWS), 0)
    kept = jnp.sum(jnp.where(row == lane_index((ROWS, ROWS)), kept, 0.0), axis=1, keepdims=True)
    return jnp.broadcast_to(kept, (ROWS, COLS))


def fetch(sources, targets, sems):
    moves = [
        pltpu.make_async_copy(source, target, sems.at[index])
        for index, (source, target) in enumerate(zip(sources, targets))
    ]
    for move in moves:
        move.start()
    for move in moves:
        move.wait()


def rows_kernel(*refs):
    fetch(refs[:6], refs[7:13], refs[13])
    fill_rows(*refs[7:13], refs[6])


def weights_kernel(_, *refs):
    sources, refs = refs[:9], refs[9:]
    outs, refs = refs[:12], refs[12:]
    held, sems = refs[:7], refs[7]
    fetch(sources, tuple(held) + tuple(outs[10:]), sems)
    fill_weights(*held[:4], *outs[:4])
    for index, table in enumerate(held[4:]):
        outs[4 + 2 * index][...], outs[5 + 2 * index][...] = halves(table[...])


def fill_rows(temp_ref, kmt_ref, kappa_ref, helm_ref, forcing_ref, cutoff_ref, own_ref):
    own_ref[:, CUT + 1 :, :] = jnp.zeros((ROWS, FIELDS - CUT - 1, COLS), jnp.float32)
    for level in range(LEV):
        own_ref[:, level, :] = temp_ref[level]
    own_ref[:, KMT, :] = kmt_ref[...].astype(jnp.float32)
    own_ref[:, KAPPA, :] = kappa_ref[...]
    own_ref[:, HELM, :] = helm_ref[...]
    own_ref[:, FORCING, :] = forcing_ref[...]
    own_ref[:, CUT, :] = cutoff_rows(cutoff_ref)


def fill_weights(
    first_ref, mid_ref, late_ref, last_ref, w_in_ref, w_mid_ref, w_late_ref, w_out_ref
):
    w_in_ref[...] = jnp.zeros(w_in_ref.shape, w_in_ref.dtype)
    width = mid_ref.shape[1]
    none = jnp.zeros((LEV, width), jnp.float32)
    for row in range(4):
        parts = []
        for tap in range(3):
            for parity in range(2):
                a = row - parity
                parts.append(first_ref[3 * a + tap].astype(jnp.float32) if 0 <= a < 3 else none)
        top = jnp.concatenate(parts, axis=1)
        marks = [jnp.ones((1, width), jnp.float32) if row == at else none[:1] for at in (1, 2, 2, 3)]
        marks = jnp.concatenate(marks, axis=1)
        block = jnp.concatenate(
            [
                jnp.concatenate([top, jnp.zeros((LEV, 4 * width), jnp.float32)], axis=1),
                jnp.concatenate(
                    [
                        jnp.concatenate([jnp.zeros((1, 6 * width), jnp.float32), marks], axis=1),
                        jnp.zeros((LEV - 1, 10 * width), jnp.float32),
                    ],
                    axis=0,
                ),
            ],
            axis=0,
        )
        w_in_ref[FIELDS * row : FIELDS * (row + 1)] = block.astype(jnp.bfloat16)

    def rows_of(ref, tap, parity):
        outs = ref.shape[1]
        blank = jnp.zeros((outs, width), jnp.float32)
        parts = []
        for row in range(4):
            a = row - parity
            parts.append(ref[3 * a + tap].astype(jnp.float32) if 0 <= a < 3 else blank)
        return jnp.concatenate(parts, axis=1)

    for ref, out_ref in ((mid_ref, w_mid_ref), (late_ref, w_late_ref)):
        for tap in range(3):
            both = jnp.concatenate([rows_of(ref, tap, 0), rows_of(ref, tap, 1)], axis=0)
            out_ref[:, 2 * width * tap : 2 * width * (tap + 1)] = both.T.astype(jnp.bfloat16)
    w_out_ref[...] = jnp.concatenate(
        [rows_of(last_ref, tap, parity) for tap in range(3) for parity in range(2)], axis=0
    ).astype(jnp.bfloat16)


def pack_kernel(own_ref, north_ref, south_ref, rows_ref, far_ref, near_ref):
    even = lax.rem(lax.axis_index("lon"), 2) == 0
    rows_ref[DEEP : DEEP + ROWS] = own_ref[...]
    for slab_ref, start in ((north_ref, 0), (south_ref, DEEP + ROWS)):
        rows = slice(start, start + DEEP)
        rows_ref[rows, CUT + 1 :, :] = jnp.zeros((DEEP, FIELDS - CUT - 1, COLS), jnp.float32)
        for field in range(CUT + 1):
            rows_ref[rows, field, :] = slab_ref[field]
    lane = lane_index((FIELDS, COLS))
    for part in range(TALL // SLOTS):
        first = jnp.zeros((FIELDS, COLS), jnp.float32)
        last = jnp.zeros((FIELDS, COLS), jnp.float32)
        for slot in range(SLOTS):
            here = rows_ref[part * SLOTS + slot]
            inside = (lane >= HALO * slot) & (lane < HALO * (slot + 1))
            first = jnp.where(inside, pltpu.roll(here, HALO * slot, 1) if slot else here, first)
            last = jnp.where(inside, pltpu.roll(here, HALO * (slot + 1), 1), last)
        far_ref[part] = jnp.where(even, first, last)
        near_ref[part] = jnp.where(even, last, first)


def closure_layers(window, pairs, stride, weights, acts, masks):
    w_in_ref, w_mid_ref, w_late_ref, w_out_ref = weights
    act_a, act_b = acts
    mask_odd, mask_even = masks

    def chunks(count):
        return range(-(-count * stride // COLS))

    def at(chunk, shift=0):
        return slice(COLS * chunk + shift, COLS * (chunk + 1) + shift)

    def both(act, chunk):
        return jnp.concatenate([act[at(chunk)], act[at(chunk, stride)]], axis=1)

    def finish(total, mask):
        v = (
            pltpu.roll(total[:, 0:128], 1, 0)
            + total[:, 128:256]
            + pltpu.roll(total[:, 256:384], COLS - 1, 0)
        )
        return (mask * (v / (1.0 + jnp.exp(-v)))).astype(jnp.bfloat16)

    for chunk in chunks(pairs):
        total = lax.dot_general(
            window(chunk),
            w_in_ref[...],
            (((0,), (0,)), ((), ())),
            preferred_element_type=jnp.float32,
        )
        mask_odd[at(chunk)] = total[:, 384:512]
        mask_even[at(chunk)] = total[:, 512:640]
        act_a[at(chunk)] = finish(total, total[:, 384:512])
    for chunk in chunks(pairs - 1):
        total = jnp.dot(both(act_a, chunk), w_mid_ref[...], preferred_element_type=jnp.float32)
        act_b[at(chunk)] = finish(total, mask_even[at(chunk)])
    for chunk in chunks(pairs - 2):
        total = jnp.dot(both(act_b, chunk), w_late_ref[...], preferred_element_type=jnp.float32)
        act_a[at(chunk)] = finish(total, mask_odd[at(chunk, stride)])
    results = []
    for chunk in chunks(pairs - 3):
        total = lax.dot_general(
            w_out_ref[...],
            both(act_a, chunk),
            (((1,), (1,)), ((), ())),
            preferred_element_type=jnp.float32,
        )
        results.append(
            pltpu.roll(total[0:16], 1, 1) + total[16:32] + pltpu.roll(total[32:48], COLS - 1, 1)
        )
    return results


def level_index():
    return lax.broadcasted_iota(jnp.int32, (LEV, COLS), 0).astype(jnp.float32)


def wetness(block):
    return (level_index() < block[KMT : KMT + 1]).astype(jnp.float32)


def first_input(block):
    wet = wetness(block)
    sea = jnp.where(level_index() == 0.0, wet, 0.0)
    return jnp.concatenate([wet * block[0:LEV], sea], axis=0).astype(jnp.bfloat16)


def advance(here, north, south, closure):
    wet = wetness(here)
    temp = here[0:LEV]
    tracer = wet * temp
    kappa = jnp.broadcast_to(here[KAPPA : KAPPA + 1], (LEV, COLS))
    diff = jnp.zeros((LEV, COLS), jnp.float32)
    for near in (south, north):
        near_w = wetness(near)
        diff = diff + near_w * 0.5 * (kappa + near[KAPPA : KAPPA + 1]) * (
            near_w * near[0:LEV] - tracer
        )
    for by in (COLS - 1, 1):
        diff = diff + pltpu.roll(wet, by, 1) * 0.5 * (kappa + pltpu.roll(kappa, by, 1)) * (
            pltpu.roll(tracer, by, 1) - tracer
        )
    diff = wet * diff
    eddy = wet * closure
    return wet * (temp + STEP * (diff + eddy))


FIRST = DEEP - HALO


def interior_kernel(
    rows_ref, w_in_ref, w_mid_ref, w_late_ref, w_out_ref, out_ref, line_ref,
    start, mask_odd, mask_even, act_a, act_b,
):
    for row in range(TALL):
        start[row * FIELDS : (row + 1) * FIELDS] = first_input(rows_ref[row])
    results = closure_layers(
        lambda chunk: start[2 * FIELDS * chunk : 2 * FIELDS * (chunk + 2)],
        TALL // 2 - 1,
        COLS,
        (w_in_ref, w_mid_ref, w_late_ref, w_out_ref),
        (act_a, act_b),
        (mask_odd, mask_even),
    )
    for pair, closure in enumerate(results):
        for parity in range(2):
            row = FIRST + 2 * pair + parity
            out_ref[2 * pair + parity] = advance(
                rows_ref[row],
                rows_ref[row - 1],
                rows_ref[row + 1],
                closure[LEV * parity : LEV * (parity + 1)],
            )
    own_line = lax.axis_index("lon") + FIRST
    line_ref[...] = rows_ref[own_line, LEV:FIELDS, :]


STRIP = 32
PER = COLS // STRIP


def edge_kernel(
    rows_ref, far_ref, near_ref, inside_ref, w_in_ref, w_mid_ref, w_late_ref, w_out_ref,
    out_ref, planes_ref, strips, mask_odd, mask_even, act_a, act_b,
):
    lane = lane_index((FIELDS, COLS))
    even = lax.rem(lax.axis_index("lon"), 2) == 0
    parts = range(TALL // SLOTS)
    from_west = [jnp.where(even, far_ref[part], near_ref[part]) for part in parts]
    from_east = [jnp.where(even, near_ref[part], far_ref[part]) for part in parts]
    for row in range(TALL):
        part, slot = row // SLOTS, row % SLOTS
        here = rows_ref[row]
        strip = jnp.where(lane < 24, pltpu.roll(from_east[part], (20 - HALO * slot) % COLS, 1) if slot != 5 else from_east[part], 0.0)
        strip = jnp.where(lane < 20, pltpu.roll(here, 20, 1), strip)
        strip = jnp.where(lane < 12, pltpu.roll(here, 4, 1), strip)
        west = pltpu.roll(from_west[part], COLS - HALO * slot, 1) if slot else from_west[part]
        strips[row] = jnp.where(lane < 4, west, strip)

    def side_by_side(parity, start):
        total = None
        for slot in range(PER):
            row = 2 * (start + slot) + parity
            if row >= TALL:
                continue
            piece = strips[row]
            piece = pltpu.roll(piece, STRIP * slot, 1) if slot else piece
            total = piece if total is None else total + piece
        return total

    def window(chunk):
        at = PER * chunk
        return jnp.concatenate(
            [
                first_input(block)
                for block in (
                    side_by_side(0, at),
                    side_by_side(1, at),
                    side_by_side(0, at + 1),
                    side_by_side(1, at + 1),
                )
            ],
            axis=0,
        )

    act_a[5 * COLS :] = jnp.zeros((COLS, COLS), jnp.bfloat16)
    act_b[5 * COLS :] = jnp.zeros((COLS, COLS), jnp.bfloat16)
    mask_odd[5 * COLS :] = jnp.zeros((COLS, COLS), jnp.float32)
    results = closure_layers(
        window,
        TALL // 2 - 1,
        STRIP,
        (w_in_ref, w_mid_ref, w_late_ref, w_out_ref),
        (act_a, act_b),
        (mask_odd, mask_even),
    )
    at_lane = lane_index((LEV, COLS))
    for chunk in range(4):
        at = PER * chunk + FIRST // 2
        closure = results[chunk]
        north = side_by_side(1, at - 1)
        upper = side_by_side(0, at)
        lower = side_by_side(1, at)
        south = side_by_side(0, at + 1)
        for parity, value in (
            (0, advance(upper, north, lower, closure[0:LEV])),
            (1, advance(lower, upper, south, closure[LEV : 2 * LEV])),
        ):
            for slot in range(PER):
                row = 2 * (PER * chunk + slot) + parity
                left = pltpu.roll(value, COLS - STRIP * slot - 4, 1)
                shift = (108 - STRIP * slot) % COLS
                right = pltpu.roll(value, shift, 1)
                out_ref[row] = jnp.where(
                    at_lane < HALO,
                    left,
                    jnp.where(at_lane >= COLS - HALO, right, inside_ref[row]),
                )
    plane_lane = lane_index((MID, COLS))
    for index, field in enumerate((KMT, HELM, FORCING)):
        moved = pltpu.roll(rows_ref[FIRST : FIRST + MID, field, :], HALO, 1)
        edge = strips[FIRST : FIRST + MID, field, :]
        planes_ref[index, :, 0:COLS] = jnp.where(plane_lane < HALO, edge, moved)
        planes_ref[index, :, COLS:] = jnp.where(
            plane_lane < HALO,
            moved,
            jnp.where(plane_lane < 2 * HALO, pltpu.roll(edge, COLS - 16, 1), 0.0),
        )


def filter_tables(blocks, width):
    length = blocks * width
    half = LEV // 2
    k = np.arange(blocks)
    outer = np.exp(-2j * np.pi * ((k[:, None] * k[None, :]) % blocks) / blocks)
    spread = np.zeros((blocks, 2, half, blocks, 2, half))
    for line in range(half):
        spread[:, 0, line, :, 0, line] = outer.real
        spread[:, 0, line, :, 1, line] = -outer.imag
        spread[:, 1, line, :, 0, line] = outer.imag
        spread[:, 1, line, :, 1, line] = outer.real
    spread = spread.reshape(blocks * LEV, blocks * LEV)
    m = np.arange(width)
    twist = np.exp(-2j * np.pi * (k[:, None] * m[None, :]) / length)
    sign = np.where(np.arange(LEV) < half, -1.0, 1.0)[None, :, None]
    twist_re = np.broadcast_to(twist.real[:, None, :], (blocks, LEV, width))
    twist_im = twist.imag[:, None, :] * sign
    inner = np.exp(-2j * np.pi * ((m[:, None] * m[None, :]) % width) / width)
    inner = np.concatenate([inner.real, inner.imag], axis=1)
    return [
        np.asarray(t, np.float32)
        for t in (spread, spread.T / length, inner, twist_re, twist_im)
    ]


def halves(x):
    high = x.astype(jnp.bfloat16)
    return high, (x - high.astype(jnp.float32)).astype(jnp.bfloat16)


def split_dot(a, b):
    def dot(x, y):
        return jnp.dot(x, y, preferred_element_type=jnp.float32)

    return dot(a[0], b[0]) + (dot(a[0], b[1]) + dot(a[1], b[0]))


def filter_kernel(
    x_ref, line_ref, spread_ref, spread_low, back_ref, back_low, inner_ref, inner_low,
    twist_re_ref, twist_im_ref, out_ref,
):
    blocks, lev, width = x_ref.shape
    shape = (blocks, lev, width)
    flat = (blocks * lev, width)
    length = blocks * width
    inner = (inner_ref[...], inner_low[...])

    def partner(block):
        return pltpu.roll(block, lev // 2, 1)

    sign = jnp.where(lax.broadcasted_iota(jnp.int32, shape, 1) < lev // 2, -1.0, 1.0)
    y = split_dot((spread_ref[...], spread_low[...]), halves(x_ref[...].reshape(flat)))
    y = y.reshape(shape)
    y = y * twist_re_ref[...] + partner(y) * twist_im_ref[...]
    s = split_dot(halves(y.reshape(flat)), inner)
    s = s[:, 0:width].reshape(shape) + partner(s[:, width:].reshape(shape)) * sign
    wave = lax.broadcasted_iota(jnp.int32, shape, 0) + blocks * lane_index(shape)
    folded = jnp.minimum(wave, length - wave).astype(jnp.float32)
    s = jnp.where(folded < line_ref[CUT - LEV : CUT - LEV + 1, :][None], s, 0.0)
    y = split_dot(halves(s.reshape(flat)), inner)
    y = y[:, 0:width].reshape(shape) - partner(y[:, width:].reshape(shape)) * sign
    y = y * twist_re_ref[...] - partner(y) * twist_im_ref[...]
    x = split_dot((back_ref[...], back_low[...]), halves(y.reshape(flat))).reshape(shape)
    lane = lane_index((lev, width))
    moved = [pltpu.roll(x[block], HALO, 1) for block in range(blocks)]
    for block in range(blocks):
        edge = jnp.where(lane < HALO, moved[block - 1], moved[(block + 1) % blocks])
        edge = jnp.where(lane < 2 * HALO, edge, 0.0)
        edge = pltpu.roll(edge, 0, 1, stride=2 * HALO, stride_axis=0)
        row = BLOCK * block
        out_ref[row : row + lev, :] = x[block]
        out_ref[row + lev : row + BLOCK, :] = jnp.sum(edge, axis=0, keepdims=True)


def ends_kernel(x_ref, far_ref, near_ref):
    even = lax.rem(lax.axis_index("lon"), 2) == 0
    lane = lane_index((LEV, COLS))
    packed = []
    for row in range(MID):
        edge = jnp.where(lane < 2 * HALO, pltpu.roll(x_ref[row], HALO, 1), 0.0)
        edge = pltpu.roll(edge, 0, 1, stride=2 * HALO, stride_axis=0)
        packed.append(jnp.sum(edge, axis=0, keepdims=True))
    packed = jnp.concatenate(packed, axis=0)
    to_east = lax.rem(lane_index((MID, COLS)), 2 * HALO) < HALO
    last = jnp.where(to_east, packed, 0.0)
    first = jnp.where(to_east, 0.0, packed)
    far_ref[...] = jnp.where(even, first, last)
    near_ref[...] = jnp.where(even, last, first)


def plain_kernel(x_ref, far_ref, near_ref, out_ref):
    edge = far_ref[...] + near_ref[...]
    for row in range(MID):
        out_ref[BLOCK * row : BLOCK * row + LEV, :] = x_ref[row]
        out_ref[BLOCK * row + LEV : BLOCK * (row + 1), :] = edge[row : row + 1]


def two_sum(a, b):
    s = a + b
    t = s - a
    return s, (a - (s - t)) + (b - t)


def quick_sum(a, b):
    s = a + b
    return s, b - (s - a)


def split(a):
    c = a * 4097.0
    high = c - (c - a)
    return high, a - high


def two_product(a, b):
    p = a * b
    ah, al = split(a)
    bh, bl = split(b)
    return p, ((ah * bh - p) + ah * bl + al * bh) + al * bl


def pair_add(a, b):
    s, e = two_sum(a[0], b[0])
    return quick_sum(s, e + (a[1] + b[1]))


def pair_neg(a):
    return -a[0], -a[1]


def pair_mul(a, b):
    p, e = two_product(a[0], b[0])
    return quick_sum(p, e + (a[0] * b[1] + a[1] * b[0]))


def pair_div(a, b):
    q = a[0] / b[0]
    rest = pair_add(a, pair_neg(pair_mul((q, jnp.zeros_like(q)), b)))
    r = rest[0] / b[0]
    rest = pair_add(rest, pair_neg(pair_mul((r, jnp.zeros_like(r)), b)))
    return quick_sum(*quick_sum(q, r + rest[0] / b[0]))


def powers_kernel(x_ref, planes_ref, powers_ref, parts_ref):
    lane = lane_index((LEV, COLS))
    wide_lane = lane_index((MID, COLS))
    kmt_left = planes_ref[0, :, 0:COLS]
    kmt_right = planes_ref[0, :, COLS:]
    kmt = pltpu.roll(jnp.where(wide_lane < HALO, kmt_right, kmt_left), COLS - HALO, 1)
    mean = jnp.zeros((MID, COLS), jnp.float32)
    for level in range(LEV):
        here = x_ref[pl.ds(level, MID, stride=BLOCK), :]
        mean = mean + jnp.where(kmt > level, here, 0.0)
    edge = x_ref[pl.ds(LEV, MID, stride=BLOCK), :]
    edge_kmt = jnp.where(wide_lane < HALO, kmt_left, kmt_right)
    edge_kmt = jnp.where(wide_lane < 2 * HALO, edge_kmt, 0.0)
    for by in (8, 16, 32, 64):
        edge_kmt = edge_kmt + pltpu.roll(edge_kmt, by, 1)
    edge = jnp.where(edge_kmt > (wide_lane // (2 * HALO)).astype(jnp.float32), edge, 0.0)
    for by in (64, 32, 16, 8):
        edge = edge + pltpu.roll(edge, by, 1)
    moved = pltpu.roll(mean, HALO, 1)
    mean = jnp.concatenate(
        [
            jnp.where(wide_lane < HALO, edge, moved),
            jnp.where(wide_lane < HALO, moved, jnp.where(wide_lane < 2 * HALO, edge, 0.0)),
        ],
        axis=1,
    )
    sea = (planes_ref[0] > 0.0).astype(jnp.float32)

    def around(v):
        return (
            pltpu.roll(v, 1, 0)
            + pltpu.roll(v, MID - 1, 0)
            + pltpu.roll(v, 1, 1)
            + pltpu.roll(v, 2 * COLS - 1, 1)
        )

    diagonal = planes_ref[1] + sea * around(sea)
    powers = [sea * (mean * (1.0 / LEV) + planes_ref[2])]
    for _ in range(ITERS):
        v = powers[-1]
        powers.append((diagonal * v - sea * around(v)) * 0.125)
    for index, v in enumerate(powers):
        powers_ref[index] = v
    row = lax.broadcasted_iota(jnp.int32, (MID, 2 * COLS), 0)
    column = lane_index((MID, 2 * COLS))
    own = (
        (row >= HALO) & (row < HALO + ROWS) & (column >= HALO) & (column < HALO + COLS)
    )
    owned = [jnp.where(own, v, 0.0) for v in powers]
    high_rows, low_rows = [], []
    for order in range(2 * ITERS):
        p, e = two_product(owned[order // 2], owned[order - order // 2])
        tiles = [
            (p[8 * i : 8 * i + 8, 128 * j : 128 * j + 128], e[8 * i : 8 * i + 8, 128 * j : 128 * j + 128])
            for i in range(MID // 8)
            for j in range(2)
        ]
        while len(tiles) > 1:
            tiles = [pair_add(a, b) for a, b in zip(tiles[::2], tiles[1::2])]
        total = tiles[0]
        for by in (4, 2, 1):
            total = pair_add(total, tuple(pltpu.roll(t, by, 0) for t in total))
        high_rows.append(total[0])
        low_rows.append(total[1])
    where = lax.broadcasted_iota(jnp.int32, (8, COLS), 0)
    high, low = high_rows[0], low_rows[0]
    for order in range(1, 2 * ITERS):
        high = jnp.where(where == order, high_rows[order], high)
        low = jnp.where(where == order, low_rows[order], low)
    total = (high, low)
    for by in (64, 32, 16, 8, 4, 2, 1):
        total = pair_add(total, tuple(pltpu.roll(t, by, 1) for t in total))
    spot = lax.broadcasted_iota(jnp.int32, (8, COLS), 0)
    message = jnp.where(lane == spot, total[0], 0.0) + jnp.where(lane == spot + 64, total[1], 0.0)
    message = jnp.sum(message, axis=0, keepdims=True)
    parts_ref[...] = jnp.broadcast_to(message, parts_ref.shape)


def sum_messages(parts_ref):
    count = parts_ref.shape[0] // 8
    if count == 1:
        total = (parts_ref[...], jnp.zeros((8, COLS), jnp.float32))
        for by in (4, 2, 1):
            total = pair_add(total, tuple(pltpu.roll(t, by, 0) for t in total))
        return pair_add(total, tuple(pltpu.roll(t, 64, 1) for t in total))
    tiles = [(parts_ref[8 * i : 8 * i + 8, :], None) for i in range(count)]
    merged = []
    for a, b in zip(tiles[::2], tiles[1::2]):
        merged.append(two_sum(a[0], b[0]))
    tiles = merged
    while len(tiles) > 1:
        tiles = [pair_add(a, b) for a, b in zip(tiles[::2], tiles[1::2])]
    total = tiles[0]
    for by in (4, 2, 1):
        total = pair_add(total, tuple(pltpu.roll(t, by, 0) for t in total))
    return pair_add(total, tuple(pltpu.roll(t, 64, 1) for t in total))


def merge_kernel(parts_ref, out_ref):
    total = sum_messages(parts_ref)
    lane = lane_index((8, COLS))
    out_ref[...] = jnp.where(lane < 64, total[0], total[1])


def combine_kernel(
    parts_ref, powers_ref, x_ref, temp_hbm, surface_ref, residual_ref, wide, temp, sem
):
    for level in range(LEV):
        temp[level] = x_ref[pl.ds(HALO * BLOCK + level, ROWS, stride=BLOCK), :]
    move = pltpu.make_async_copy(temp, temp_hbm, sem)
    move.start()
    total = sum_messages(parts_ref)
    moments = [
        tuple(jnp.broadcast_to(t[:, order : order + 1], (8, COLS)) for t in total)
        for order in range(2 * ITERS)
    ]
    rho = list(moments)
    delta = list(moments)
    one = jnp.ones((8, COLS), jnp.float32)
    zero = jnp.zeros((8, COLS), jnp.float32)
    res = [one] + [zero] * ITERS
    way = [one] + [zero] * ITERS
    sol = [zero] * ITERS
    for step in range(ITERS):
        alpha = pair_div(rho[step], delta[step + 1])
        sol = [s + alpha[0] * w for s, w in zip(sol, way)]
        res = [res[0]] + [r - alpha[0] * w for r, w in zip(res[1:], way)]
        if step == ITERS - 1:
            break
        before = rho[step]
        last = 2 * ITERS - 1 - step
        rho = [
            None if order <= step or order >= last
            else pair_add(rho[order], pair_neg(pair_mul(alpha, delta[order + 1])))
            for order in range(2 * ITERS)
        ]
        beta = pair_neg(pair_mul(alpha, pair_div(rho[step + 1], before)))
        delta = [
            None if order <= step or order >= last
            else pair_add(rho[order], pair_mul(beta, delta[order]))
            for order in range(2 * ITERS)
        ]
        way = [r + beta[0] * w for r, w in zip(res, way)]
    for weights, target, factor in ((sol, surface_ref, 0.125), (res, residual_ref, 1.0)):
        for i in range(MID // 8):
            for j in range(2):
                spot = (slice(8 * i, 8 * i + 8), slice(128 * j, 128 * j + 128))
                value = weights[0] * powers_ref[(0,) + spot]
                for index in range(1, len(weights)):
                    value = value + weights[index] * powers_ref[(index,) + spot]
                wide[spot] = value * factor
        target[...] = wide[HALO : HALO + ROWS, HALO : HALO + COLS]
    move.wait()


def forward(axis, periodic):
    count = lax.axis_size(axis)
    pairs = [(i, i + 1) for i in range(count - 1)]
    return pairs + [(count - 1, 0)] if periodic else pairs


def backward(axis, periodic):
    return [(target, source) for source, target in forward(axis, periodic)]


def swap_near():
    return [(i, i ^ 1) for i in range(lax.axis_size("lon"))]


def swap_far():
    count = lax.axis_size("lon")
    return [(i, (i + 1) % count if i % 2 else (i - 1) % count) for i in range(count)]


def body(temp, kmt, kappa, helm, forcing, cutoff, conv_in, conv_mid, conv_late, conv_out):
    f32 = jnp.float32
    shape = jax.ShapeDtypeStruct
    blocks = lax.axis_size("lon")
    bf16 = jnp.bfloat16
    vmem = pl.BlockSpec(memory_space=pltpu.VMEM)
    cutoff = cutoff.reshape(1, ROWS)
    fields = (temp, kmt, kappa, helm, forcing, cutoff)
    slab = shape((CUT + 1, DEEP, COLS), f32)
    top, bottom = pl.pallas_call(
        slab_kernel,
        out_shape=(slab, slab),
        in_specs=[pl.BlockSpec(memory_space=pltpu.HBM)] * 6,
        out_specs=(vmem, vmem),
        scratch_shapes=(
            pltpu.VMEM((ROWS, COLS), jnp.int32),
            pltpu.VMEM((1, ROWS), jnp.int32),
            pltpu.SemaphoreType.DMA((10,)),
        ),
        compiler_params=pltpu.CompilerParams(vmem_limit_bytes=VMEM_LIMIT),
    )(*(pltpu.with_memory_space_constraint(field, pltpu.HBM) for field in fields))
    north = lax.ppermute(bottom, "lat", forward("lat", False))
    south = lax.ppermute(top, "lat", backward("lat", False))
    own = fetching(rows_kernel, shape((ROWS, FIELDS, COLS), f32), fields, fields)
    ends = shape((TALL // SLOTS, FIELDS, COLS), f32)
    rows, to_far, to_near = call(
        pack_kernel, (shape((TALL, FIELDS, COLS), f32), ends, ends)
    )(own, north, south)
    far = lax.ppermute(to_far, "lon", swap_far())
    near = lax.ppermute(to_near, "lon", swap_near())

    tables = [jnp.asarray(table) for table in filter_tables(blocks, COLS)]
    sources = (jnp.transpose(conv_in, (0, 2, 1)), conv_mid, conv_late, conv_out, *tables)
    outs = (
        shape((4 * FIELDS, 640), bf16),
        shape((256, 384), bf16),
        shape((256, 384), bf16),
        shape((48, 256), bf16),
    )
    outs = outs + tuple(shape(table.shape, bf16) for table in tables[:3] for _ in range(2))
    outs = outs + tuple(shape(table.shape, f32) for table in tables[3:])
    prepared = fetching(weights_kernel, outs, sources, sources[:7], (to_near,))
    weights, tables = prepared[:4], prepared[4:]

    def closure_scratch(chunks):
        cells = chunks * COLS
        return (
            pltpu.VMEM((cells, 128), f32),
            pltpu.VMEM((cells, 128), f32),
            pltpu.VMEM((cells, 128), bf16),
            pltpu.VMEM((cells, 128), bf16),
        )

    block = shape((MID, LEV, COLS), f32)
    inside, line = call(
        interior_kernel,
        (block, shape((LEV, COLS), f32)),
        (pltpu.VMEM((TALL * FIELDS, COLS), bf16),) + closure_scratch(19),
        10**9,
    )(rows, *weights)
    lines, planes = call(
        edge_kernel,
        (block, shape((3, MID, 2 * COLS), f32)),
        (pltpu.VMEM((TALL, FIELDS, COLS), f32),) + closure_scratch(6),
    )(rows, far, near, inside, *weights)

    def filtered_block(lines, line, tables):
        whole = lax.all_to_all(lines, "lon", split_axis=0, concat_axis=0, tiled=True)
        result = call(filter_kernel, shape((BLOCK * blocks, COLS), f32))(whole, line, *tables)
        result = result.reshape(BLOCK * blocks, 1, COLS)
        result = lax.all_to_all(result, "lon", split_axis=0, concat_axis=0, tiled=True)
        return result.reshape(BLOCK * blocks, COLS)

    def plain_block(lines, line, tables):
        ends = shape((MID, COLS), f32)
        to_far, to_near = call(ends_kernel, (ends, ends))(lines)
        far = lax.ppermute(to_far, "lon", swap_far())
        near = lax.ppermute(to_near, "lon", swap_near())
        return call(plain_kernel, shape((BLOCK * MID, COLS), f32))(lines, far, near)

    top_row = lax.axis_index("lat") * ROWS - HALO
    polar = (top_row < BAND) | (top_row + MID > ROWS * lax.axis_size("lat") - BAND)
    back = lax.cond(polar, filtered_block, plain_block, lines, line, tables)
    everyone = blocks * lax.axis_size("lat")
    wide = everyone // 8
    both = ("lon", "lat")
    inner = [[wide * i + k for k in range(wide)] for i in range(8)]
    outer = [[wide * i + k for i in range(8)] for k in range(wide)]
    powers, parts = call(
        powers_kernel,
        (
            shape((ITERS + 1, MID, 2 * COLS), f32),
            shape((wide, COLS), f32),
        ),
    )(back, planes)
    parts = lax.all_to_all(
        parts, both, split_axis=0, concat_axis=0, tiled=True, axis_index_groups=inner
    )
    parts = call(merge_kernel, shape((8, COLS), f32))(parts)
    parts = lax.all_to_all(
        parts, both, split_axis=0, concat_axis=0, tiled=True, axis_index_groups=outer
    )
    temp_new, surface, residual = pl.pallas_call(
        combine_kernel,
        out_shape=(
            shape((LEV, ROWS, COLS), f32),
            shape((ROWS, COLS), f32),
            shape((ROWS, COLS), f32),
        ),
        in_specs=[vmem] * 3,
        out_specs=(pl.BlockSpec(memory_space=pltpu.HBM), vmem, vmem),
        scratch_shapes=(
            pltpu.VMEM((MID, 2 * COLS), f32),
            pltpu.VMEM((LEV, ROWS, COLS), f32),
            pltpu.SemaphoreType.DMA,
        ),
        compiler_params=pltpu.CompilerParams(vmem_limit_bytes=VMEM_LIMIT),
    )(parts, powers, back)
    return temp_new, surface, residual


def solution(mesh):
    return jax.shard_map(
        body,
        mesh=mesh,
        in_specs=(
            P(None, "lat", "lon"),
            P("lat", "lon"),
            P("lat", "lon"),
            P("lat", "lon"),
            P("lat", "lon"),
            P("lat"),
            P(),
            P(),
            P(),
            P(),
        ),
        out_specs=(P(None, "lat", "lon"), P("lat", "lon"), P("lat", "lon")),
        check_vma=False,
    )
```

```python
import math

import jax
import jax.numpy as jnp
import numpy as np
from jax import lax
from jax.experimental import pallas as pl
from jax.experimental.pallas import tpu as pltpu
from jax.sharding import PartitionSpec as P

ITERS = 4
STEP = 0.25
LEV = 8
FIELDS = 16
KMT, KAPPA, HELM, FORCING, CUT = 8, 9, 10, 11, 12
BAND = 48
HALO = 4
DEEP = 8
ROWS = 24
COLS = 128
TALL = ROWS + 2 * DEEP
MID = ROWS + 2 * HALO
BLOCK = LEV + 1
SLOTS = 20
VMEM_LIMIT = 48 * 1024 * 1024


def call(kernel, outs, scratch=()):
    spec = pl.BlockSpec(memory_space=pltpu.VMEM)
    return pl.pallas_call(
        kernel,
        out_shape=outs,
        out_specs=jax.tree.map(lambda _: spec, outs),
        scratch_shapes=scratch,
        compiler_params=pltpu.CompilerParams(vmem_limit_bytes=VMEM_LIMIT),
    )


def lane_index(shape):
    return lax.broadcasted_iota(jnp.int32, shape, len(shape) - 1)


def fetching(kernel, outs, sources, held, rest=(), scratch=(), flops=10**6):
    spec = pl.BlockSpec(memory_space=pltpu.VMEM)
    return pl.pallas_call(
        kernel,
        out_shape=outs,
        in_specs=[pl.BlockSpec(memory_space=pltpu.HBM)] * len(sources) + [spec] * len(rest),
        out_specs=jax.tree.map(lambda _: spec, outs),
        scratch_shapes=tuple(pltpu.VMEM(source.shape, source.dtype) for source in held)
        + (pltpu.SemaphoreType.DMA((len(sources),)),)
        + tuple(scratch),
        compiler_params=pltpu.CompilerParams(vmem_limit_bytes=VMEM_LIMIT),
        cost_estimate=pl.CostEstimate(
            flops=flops, bytes_accessed=2 * 10**6, transcendentals=flops // 500
        ),
    )(*(pltpu.with_memory_space_constraint(source, pltpu.HBM) for source in sources), *rest)


def slab_kernel(
    temp_hbm, kmt_hbm, kappa_hbm, helm_hbm, forcing_hbm, cutoff_hbm,
    top_ref, bottom_ref, kmt, cutoff, sems,
):
    pairs = [(kmt_hbm, kmt), (cutoff_hbm, cutoff)]
    for target, start in ((top_ref, 0), (bottom_ref, ROWS - DEEP)):
        rows = pl.ds(start, DEEP)
        pairs.append((temp_hbm.at[:, rows], target.at[pl.ds(0, LEV)]))
        for source, field in ((kappa_hbm, KAPPA), (helm_hbm, HELM), (forcing_hbm, FORCING)):
            pairs.append((source.at[rows], target.at[field]))
    moves = [
        pltpu.make_async_copy(source, target, sems.at[index])
        for index, (source, target) in enumerate(pairs)
    ]
    for move in moves:
        move.start()
    for move in moves:
        move.wait()
    kept = cutoff_rows(cutoff)
    for target, start in ((top_ref, 0), (bottom_ref, ROWS - DEEP)):
        target[KMT] = kmt[start : start + DEEP].astype(jnp.float32)
        target[CUT] = kept[start : start + DEEP]


def cutoff_rows(cutoff_ref):
    kept = jnp.broadcast_to(cutoff_ref[...].astype(jnp.float32), (ROWS, ROWS))
    row = lax.broadcasted_iota(jnp.int32, (ROWS, ROWS), 0)
    kept = jnp.sum(jnp.where(row == lane_index((ROWS, ROWS)), kept, 0.0), axis=1, keepdims=True)
    return jnp.broadcast_to(kept, (ROWS, COLS))


def fetch(sources, targets, sems):
    moves = [
        pltpu.make_async_copy(source, target, sems.at[index])
        for index, (source, target) in enumerate(zip(sources, targets))
    ]
    for move in moves:
        move.start()
    return moves


def rows_kernel(*refs):
    for move in fetch(refs[:6], refs[7:13], refs[13]):
        move.wait()
    fill_rows(*refs[7:13], refs[6])


def fill_rows(temp_ref, kmt_ref, kappa_ref, helm_ref, forcing_ref, cutoff_ref, own_ref):
    own_ref[:, CUT + 1 :, :] = jnp.zeros((ROWS, FIELDS - CUT - 1, COLS), jnp.float32)
    for level in range(LEV):
        own_ref[:, level, :] = temp_ref[level]
    own_ref[:, KMT, :] = kmt_ref[...].astype(jnp.float32)
    own_ref[:, KAPPA, :] = kappa_ref[...]
    own_ref[:, HELM, :] = helm_ref[...]
    own_ref[:, FORCING, :] = forcing_ref[...]
    own_ref[:, CUT, :] = cutoff_rows(cutoff_ref)


def fill_weights(
    first_ref, mid_ref, late_ref, last_ref, w_in_ref, w_mid_ref, w_late_ref, w_out_ref
):
    w_in_ref[...] = jnp.zeros(w_in_ref.shape, w_in_ref.dtype)
    width = mid_ref.shape[1]
    none = jnp.zeros((LEV, width), jnp.float32)
    for row in range(4):
        parts = []
        for tap in range(3):
            for parity in range(2):
                a = row - parity
                parts.append(first_ref[3 * a + tap].astype(jnp.float32) if 0 <= a < 3 else none)
        top = jnp.concatenate(parts, axis=1)
        marks = [jnp.ones((1, width), jnp.float32) if row == at else none[:1] for at in (1, 2, 2, 3)]
        marks = jnp.concatenate(marks, axis=1)
        block = jnp.concatenate(
            [
                jnp.concatenate([top, jnp.zeros((LEV, 4 * width), jnp.float32)], axis=1),
                jnp.concatenate(
                    [
                        jnp.concatenate([jnp.zeros((1, 6 * width), jnp.float32), marks], axis=1),
                        jnp.zeros((LEV - 1, 10 * width), jnp.float32),
                    ],
                    axis=0,
                ),
            ],
            axis=0,
        )
        w_in_ref[FIELDS * row : FIELDS * (row + 1)] = block.astype(jnp.bfloat16)

    def rows_of(ref, tap, parity):
        outs = ref.shape[1]
        blank = jnp.zeros((outs, width), jnp.float32)
        parts = []
        for row in range(4):
            a = row - parity
            parts.append(ref[3 * a + tap].astype(jnp.float32) if 0 <= a < 3 else blank)
        return jnp.concatenate(parts, axis=1)

    for ref, out_ref in ((mid_ref, w_mid_ref), (late_ref, w_late_ref)):
        for tap in range(3):
            both = jnp.concatenate([rows_of(ref, tap, 0), rows_of(ref, tap, 1)], axis=0)
            out_ref[:, 2 * width * tap : 2 * width * (tap + 1)] = both.T.astype(jnp.bfloat16)
    w_out_ref[...] = jnp.concatenate(
        [rows_of(last_ref, tap, parity) for tap in range(3) for parity in range(2)], axis=0
    ).astype(jnp.bfloat16)


def pack_kernel(own_ref, north_ref, south_ref, rows_ref, far_ref, near_ref):
    even = lax.rem(lax.axis_index("lon"), 2) == 0
    rows_ref[DEEP : DEEP + ROWS] = own_ref[...]
    for slab_ref, start in ((north_ref, 0), (south_ref, DEEP + ROWS)):
        rows = slice(start, start + DEEP)
        rows_ref[rows, CUT + 1 :, :] = jnp.zeros((DEEP, FIELDS - CUT - 1, COLS), jnp.float32)
        for field in range(CUT + 1):
            rows_ref[rows, field, :] = slab_ref[field]
    lane = lane_index((FIELDS, COLS))
    for part in range(TALL // SLOTS):
        first = jnp.zeros((FIELDS, COLS), jnp.float32)
        last = jnp.zeros((FIELDS, COLS), jnp.float32)
        for slot in range(SLOTS):
            here = rows_ref[part * SLOTS + slot]
            inside = (lane >= HALO * slot) & (lane < HALO * (slot + 1))
            first = jnp.where(inside, pltpu.roll(here, HALO * slot, 1) if slot else here, first)
            last = jnp.where(inside, pltpu.roll(here, HALO * (slot + 1), 1), last)
        far_ref[part] = jnp.where(even, first, last)
        near_ref[part] = jnp.where(even, last, first)


def closure_layers(window, pairs, stride, weights, acts, masks):
    w_in_ref, w_mid_ref, w_late_ref, w_out_ref = weights
    act_a, act_b = acts
    mask_odd, mask_even = masks

    def chunks(count):
        return range(-(-count * stride // COLS))

    def at(chunk, shift=0):
        return slice(COLS * chunk + shift, COLS * (chunk + 1) + shift)

    def both(act, chunk):
        return jnp.concatenate([act[at(chunk)], act[at(chunk, stride)]], axis=1)

    def finish(total, mask):
        v = (
            pltpu.roll(total[:, 0:128], 1, 0)
            + total[:, 128:256]
            + pltpu.roll(total[:, 256:384], COLS - 1, 0)
        )
        return (mask * (v / (1.0 + jnp.exp(-v)))).astype(jnp.bfloat16)

    for chunk in chunks(pairs):
        total = lax.dot_general(
            window(chunk),
            w_in_ref[...],
            (((0,), (0,)), ((), ())),
            preferred_element_type=jnp.float32,
        )
        mask_odd[at(chunk)] = total[:, 384:512]
        mask_even[at(chunk)] = total[:, 512:640]
        act_a[at(chunk)] = finish(total, total[:, 384:512])
    for chunk in chunks(pairs - 1):
        total = jnp.dot(both(act_a, chunk), w_mid_ref[...], preferred_element_type=jnp.float32)
        act_b[at(chunk)] = finish(total, mask_even[at(chunk)])
    for chunk in chunks(pairs - 2):
        total = jnp.dot(both(act_b, chunk), w_late_ref[...], preferred_element_type=jnp.float32)
        act_a[at(chunk)] = finish(total, mask_odd[at(chunk, stride)])
    results = []
    for chunk in chunks(pairs - 3):
        total = lax.dot_general(
            w_out_ref[...],
            both(act_a, chunk),
            (((1,), (1,)), ((), ())),
            preferred_element_type=jnp.float32,
        )
        results.append(
            pltpu.roll(total[0:16], 1, 1) + total[16:32] + pltpu.roll(total[32:48], COLS - 1, 1)
        )
    return results


def level_index():
    return lax.broadcasted_iota(jnp.int32, (LEV, COLS), 0).astype(jnp.float32)


def wetness(block):
    return (level_index() < block[KMT : KMT + 1]).astype(jnp.float32)


def first_input(block):
    wet = wetness(block)
    sea = jnp.where(level_index() == 0.0, wet, 0.0)
    return jnp.concatenate([wet * block[0:LEV], sea], axis=0).astype(jnp.bfloat16)


def advance(here, north, south, closure):
    wet = wetness(here)
    temp = here[0:LEV]
    tracer = wet * temp
    kappa = jnp.broadcast_to(here[KAPPA : KAPPA + 1], (LEV, COLS))
    diff = jnp.zeros((LEV, COLS), jnp.float32)
    for near in (south, north):
        near_w = wetness(near)
        diff = diff + near_w * 0.5 * (kappa + near[KAPPA : KAPPA + 1]) * (
            near_w * near[0:LEV] - tracer
        )
    for by in (COLS - 1, 1):
        diff = diff + pltpu.roll(wet, by, 1) * 0.5 * (kappa + pltpu.roll(kappa, by, 1)) * (
            pltpu.roll(tracer, by, 1) - tracer
        )
    diff = wet * diff
    eddy = wet * closure
    return wet * (temp + STEP * (diff + eddy))


FIRST = DEEP - HALO


def interior_kernel(*refs):
    sources, rows_ref, refs = refs[:9], refs[9], refs[10:]
    out_ref, line_ref, weights, tables, refs = refs[0], refs[1], refs[2:6], refs[6:14], refs[14:]
    held, sems = refs[:7], refs[7]
    start, mask_odd, mask_even, act_a, act_b = refs[8:]
    moves = fetch(sources, tuple(held) + tuple(tables[6:]), sems)
    for row in range(TALL):
        start[row * FIELDS : (row + 1) * FIELDS] = first_input(rows_ref[row])
    for move in moves:
        move.wait()
    fill_weights(*held[:4], *weights)
    for index, table in enumerate(held[4:]):
        tables[2 * index][...], tables[2 * index + 1][...] = halves(table[...])
    results = closure_layers(
        lambda chunk: start[2 * FIELDS * chunk : 2 * FIELDS * (chunk + 2)],
        TALL // 2 - 1,
        COLS,
        weights,
        (act_a, act_b),
        (mask_odd, mask_even),
    )
    for pair, closure in enumerate(results):
        for parity in range(2):
            row = FIRST + 2 * pair + parity
            out_ref[2 * pair + parity] = advance(
                rows_ref[row],
                rows_ref[row - 1],
                rows_ref[row + 1],
                closure[LEV * parity : LEV * (parity + 1)],
            )
    own_line = lax.axis_index("lon") + FIRST
    line_ref[...] = rows_ref[own_line, LEV:FIELDS, :]


STRIP = 32
PER = COLS // STRIP


def edge_kernel(
    rows_ref, far_ref, near_ref, inside_ref, w_in_ref, w_mid_ref, w_late_ref, w_out_ref,
    out_ref, planes_ref, strips, mask_odd, mask_even, act_a, act_b,
):
    lane = lane_index((FIELDS, COLS))
    even = lax.rem(lax.axis_index("lon"), 2) == 0
    parts = range(TALL // SLOTS)
    from_west = [jnp.where(even, far_ref[part], near_ref[part]) for part in parts]
    from_east = [jnp.where(even, near_ref[part], far_ref[part]) for part in parts]
    for row in range(TALL):
        part, slot = row // SLOTS, row % SLOTS
        here = rows_ref[row]
        strip = jnp.where(lane < 24, pltpu.roll(from_east[part], (20 - HALO * slot) % COLS, 1) if slot != 5 else from_east[part], 0.0)
        strip = jnp.where(lane < 20, pltpu.roll(here, 20, 1), strip)
        strip = jnp.where(lane < 12, pltpu.roll(here, 4, 1), strip)
        west = pltpu.roll(from_west[part], COLS - HALO * slot, 1) if slot else from_west[part]
        strips[row] = jnp.where(lane < 4, west, strip)

    def side_by_side(parity, start):
        total = None
        for slot in range(PER):
            row = 2 * (start + slot) + parity
            if row >= TALL:
                continue
            piece = strips[row]
            piece = pltpu.roll(piece, STRIP * slot, 1) if slot else piece
            total = piece if total is None else total + piece
        return total

    def window(chunk):
        at = PER * chunk
        return jnp.concatenate(
            [
                first_input(block)
                for block in (
                    side_by_side(0, at),
                    side_by_side(1, at),
                    side_by_side(0, at + 1),
                    side_by_side(1, at + 1),
                )
            ],
            axis=0,
        )

    act_a[5 * COLS :] = jnp.zeros((COLS, COLS), jnp.bfloat16)
    act_b[5 * COLS :] = jnp.zeros((COLS, COLS), jnp.bfloat16)
    mask_odd[5 * COLS :] = jnp.zeros((COLS, COLS), jnp.float32)
    results = closure_layers(
        window,
        TALL // 2 - 1,
        STRIP,
        (w_in_ref, w_mid_ref, w_late_ref, w_out_ref),
        (act_a, act_b),
        (mask_odd, mask_even),
    )
    at_lane = lane_index((LEV, COLS))
    for chunk in range(4):
        at = PER * chunk + FIRST // 2
        closure = results[chunk]
        north = side_by_side(1, at - 1)
        upper = side_by_side(0, at)
        lower = side_by_side(1, at)
        south = side_by_side(0, at + 1)
        for parity, value in (
            (0, advance(upper, north, lower, closure[0:LEV])),
            (1, advance(lower, upper, south, closure[LEV : 2 * LEV])),
        ):
            for slot in range(PER):
                row = 2 * (PER * chunk + slot) + parity
                left = pltpu.roll(value, COLS - STRIP * slot - 4, 1)
                shift = (108 - STRIP * slot) % COLS
                right = pltpu.roll(value, shift, 1)
                out_ref[row] = jnp.where(
                    at_lane < HALO,
                    left,
                    jnp.where(at_lane >= COLS - HALO, right, inside_ref[row]),
                )
    plane_lane = lane_index((MID, COLS))
    for index, field in enumerate((KMT, HELM, FORCING)):
        moved = pltpu.roll(rows_ref[FIRST : FIRST + MID, field, :], HALO, 1)
        edge = strips[FIRST : FIRST + MID, field, :]
        planes_ref[index, :, 0:COLS] = jnp.where(plane_lane < HALO, edge, moved)
        planes_ref[index, :, COLS:] = jnp.where(
            plane_lane < HALO,
            moved,
            jnp.where(plane_lane < 2 * HALO, pltpu.roll(edge, COLS - 16, 1), 0.0),
        )


def filter_tables(blocks, width):
    length = blocks * width
    half = LEV // 2
    k = np.arange(blocks)
    outer = np.exp(-2j * np.pi * ((k[:, None] * k[None, :]) % blocks) / blocks)
    spread = np.zeros((blocks, 2, half, blocks, 2, half))
    for line in range(half):
        spread[:, 0, line, :, 0, line] = outer.real
        spread[:, 0, line, :, 1, line] = -outer.imag
        spread[:, 1, line, :, 0, line] = outer.imag
        spread[:, 1, line, :, 1, line] = outer.real
    spread = spread.reshape(blocks * LEV, blocks * LEV)
    m = np.arange(width)
    twist = np.exp(-2j * np.pi * (k[:, None] * m[None, :]) / length)
    sign = np.where(np.arange(LEV) < half, -1.0, 1.0)[None, :, None]
    twist_re = np.broadcast_to(twist.real[:, None, :], (blocks, LEV, width))
    twist_im = twist.imag[:, None, :] * sign
    inner = np.exp(-2j * np.pi * ((m[:, None] * m[None, :]) % width) / width)
    inner = np.concatenate([inner.real, inner.imag], axis=1)
    return [
        np.asarray(t, np.float32)
        for t in (spread, spread.T / length, inner, twist_re, twist_im)
    ]


def halves(x):
    high = x.astype(jnp.bfloat16)
    return high, (x - high.astype(jnp.float32)).astype(jnp.bfloat16)


def split_dot(a, b):
    def dot(x, y):
        return jnp.dot(x, y, preferred_element_type=jnp.float32)

    return dot(a[0], b[0]) + (dot(a[0], b[1]) + dot(a[1], b[0]))


def filter_kernel(
    x_ref, line_ref, spread_ref, spread_low, back_ref, back_low, inner_ref, inner_low,
    twist_re_ref, twist_im_ref, out_ref,
):
    blocks, lev, width = x_ref.shape
    shape = (blocks, lev, width)
    flat = (blocks * lev, width)
    length = blocks * width
    inner = (inner_ref[...], inner_low[...])

    def partner(block):
        return pltpu.roll(block, lev // 2, 1)

    sign = jnp.where(lax.broadcasted_iota(jnp.int32, shape, 1) < lev // 2, -1.0, 1.0)
    y = split_dot((spread_ref[...], spread_low[...]), halves(x_ref[...].reshape(flat)))
    y = y.reshape(shape)
    y = y * twist_re_ref[...] + partner(y) * twist_im_ref[...]
    s = split_dot(halves(y.reshape(flat)), inner)
    s = s[:, 0:width].reshape(shape) + partner(s[:, width:].reshape(shape)) * sign
    wave = lax.broadcasted_iota(jnp.int32, shape, 0) + blocks * lane_index(shape)
    folded = jnp.minimum(wave, length - wave).astype(jnp.float32)
    s = jnp.where(folded < line_ref[CUT - LEV : CUT - LEV + 1, :][None], s, 0.0)
    y = split_dot(halves(s.reshape(flat)), inner)
    y = y[:, 0:width].reshape(shape) - partner(y[:, width:].reshape(shape)) * sign
    y = y * twist_re_ref[...] - partner(y) * twist_im_ref[...]
    x = split_dot((back_ref[...], back_low[...]), halves(y.reshape(flat))).reshape(shape)
    lane = lane_index((lev, width))
    moved = [pltpu.roll(x[block], HALO, 1) for block in range(blocks)]
    for block in range(blocks):
        edge = jnp.where(lane < HALO, moved[block - 1], moved[(block + 1) % blocks])
        edge = jnp.where(lane < 2 * HALO, edge, 0.0)
        edge = pltpu.roll(edge, 0, 1, stride=2 * HALO, stride_axis=0)
        row = BLOCK * block
        out_ref[row : row + lev, :] = x[block]
        out_ref[row + lev : row + BLOCK, :] = jnp.sum(edge, axis=0, keepdims=True)


def ends_kernel(x_ref, far_ref, near_ref):
    even = lax.rem(lax.axis_index("lon"), 2) == 0
    lane = lane_index((LEV, COLS))
    packed = []
    for row in range(MID):
        edge = jnp.where(lane < 2 * HALO, pltpu.roll(x_ref[row], HALO, 1), 0.0)
        edge = pltpu.roll(edge, 0, 1, stride=2 * HALO, stride_axis=0)
        packed.append(jnp.sum(edge, axis=0, keepdims=True))
    packed = jnp.concatenate(packed, axis=0)
    to_east = lax.rem(lane_index((MID, COLS)), 2 * HALO) < HALO
    last = jnp.where(to_east, packed, 0.0)
    first = jnp.where(to_east, 0.0, packed)
    far_ref[...] = jnp.where(even, first, last)
    near_ref[...] = jnp.where(even, last, first)


def plain_kernel(x_ref, far_ref, near_ref, out_ref):
    edge = far_ref[...] + near_ref[...]
    for row in range(MID):
        out_ref[BLOCK * row : BLOCK * row + LEV, :] = x_ref[row]
        out_ref[BLOCK * row + LEV : BLOCK * (row + 1), :] = edge[row : row + 1]


def two_sum(a, b):
    s = a + b
    t = s - a
    return s, (a - (s - t)) + (b - t)


def quick_sum(a, b):
    s = a + b
    return s, b - (s - a)


def split(a):
    c = a * 4097.0
    high = c - (c - a)
    return high, a - high


def two_product(a, b):
    p = a * b
    ah, al = split(a)
    bh, bl = split(b)
    return p, ((ah * bh - p) + ah * bl + al * bh) + al * bl


def pair_add(a, b):
    s, e = two_sum(a[0], b[0])
    return quick_sum(s, e + (a[1] + b[1]))


def pair_neg(a):
    return -a[0], -a[1]


def pair_mul(a, b):
    p, e = two_product(a[0], b[0])
    return quick_sum(p, e + (a[0] * b[1] + a[1] * b[0]))


def pair_div(a, b):
    q = a[0] / b[0]
    rest = pair_add(a, pair_neg(pair_mul((q, jnp.zeros_like(q)), b)))
    r = rest[0] / b[0]
    rest = pair_add(rest, pair_neg(pair_mul((r, jnp.zeros_like(r)), b)))
    return quick_sum(*quick_sum(q, r + rest[0] / b[0]))


def powers_kernel(x_ref, planes_ref, powers_ref, parts_ref):
    lane = lane_index((LEV, COLS))
    wide_lane = lane_index((MID, COLS))
    kmt_left = planes_ref[0, :, 0:COLS]
    kmt_right = planes_ref[0, :, COLS:]
    kmt = pltpu.roll(jnp.where(wide_lane < HALO, kmt_right, kmt_left), COLS - HALO, 1)
    mean = jnp.zeros((MID, COLS), jnp.float32)
    for level in range(LEV):
        here = x_ref[pl.ds(level, MID, stride=BLOCK), :]
        mean = mean + jnp.where(kmt > level, here, 0.0)
    edge = x_ref[pl.ds(LEV, MID, stride=BLOCK), :]
    edge_kmt = jnp.where(wide_lane < HALO, kmt_left, kmt_right)
    edge_kmt = jnp.where(wide_lane < 2 * HALO, edge_kmt, 0.0)
    for by in (8, 16, 32, 64):
        edge_kmt = edge_kmt + pltpu.roll(edge_kmt, by, 1)
    edge = jnp.where(edge_kmt > (wide_lane // (2 * HALO)).astype(jnp.float32), edge, 0.0)
    for by in (64, 32, 16, 8):
        edge = edge + pltpu.roll(edge, by, 1)
    moved = pltpu.roll(mean, HALO, 1)
    mean = jnp.concatenate(
        [
            jnp.where(wide_lane < HALO, edge, moved),
            jnp.where(wide_lane < HALO, moved, jnp.where(wide_lane < 2 * HALO, edge, 0.0)),
        ],
        axis=1,
    )
    sea = (planes_ref[0] > 0.0).astype(jnp.float32)

    def around(v):
        return (
            pltpu.roll(v, 1, 0)
            + pltpu.roll(v, MID - 1, 0)
            + pltpu.roll(v, 1, 1)
            + pltpu.roll(v, 2 * COLS - 1, 1)
        )

    diagonal = planes_ref[1] + sea * around(sea)
    powers = [sea * (mean * (1.0 / LEV) + planes_ref[2])]
    for _ in range(ITERS):
        v = powers[-1]
        powers.append((diagonal * v - sea * around(v)) * 0.125)
    for index, v in enumerate(powers):
        powers_ref[index] = v
    row = lax.broadcasted_iota(jnp.int32, (MID, 2 * COLS), 0)
    column = lane_index((MID, 2 * COLS))
    own = (
        (row >= HALO) & (row < HALO + ROWS) & (column >= HALO) & (column < HALO + COLS)
    )
    owned = [jnp.where(own, v, 0.0) for v in powers]
    high_rows, low_rows = [], []
    for order in range(2 * ITERS):
        p, e = two_product(owned[order // 2], owned[order - order // 2])
        tiles = [
            (p[8 * i : 8 * i + 8, 128 * j : 128 * j + 128], e[8 * i : 8 * i + 8, 128 * j : 128 * j + 128])
            for i in range(MID // 8)
            for j in range(2)
        ]
        while len(tiles) > 1:
            tiles = [pair_add(a, b) for a, b in zip(tiles[::2], tiles[1::2])]
        total = tiles[0]
        for by in (4, 2, 1):
            total = pair_add(total, tuple(pltpu.roll(t, by, 0) for t in total))
        high_rows.append(total[0])
        low_rows.append(total[1])
    where = lax.broadcasted_iota(jnp.int32, (8, COLS), 0)
    high, low = high_rows[0], low_rows[0]
    for order in range(1, 2 * ITERS):
        high = jnp.where(where == order, high_rows[order], high)
        low = jnp.where(where == order, low_rows[order], low)
    total = (high, low)
    for by in (64, 32, 16, 8, 4, 2, 1):
        total = pair_add(total, tuple(pltpu.roll(t, by, 1) for t in total))
    spot = lax.broadcasted_iota(jnp.int32, (8, COLS), 0)
    message = jnp.where(lane == spot, total[0], 0.0) + jnp.where(lane == spot + 64, total[1], 0.0)
    message = jnp.sum(message, axis=0, keepdims=True)
    parts_ref[...] = jnp.broadcast_to(message, parts_ref.shape)


def sum_messages(parts_ref):
    count = parts_ref.shape[0] // 8
    if count == 1:
        total = (parts_ref[...], jnp.zeros((8, COLS), jnp.float32))
        for by in (4, 2, 1):
            total = pair_add(total, tuple(pltpu.roll(t, by, 0) for t in total))
        return pair_add(total, tuple(pltpu.roll(t, 64, 1) for t in total))
    tiles = [(parts_ref[8 * i : 8 * i + 8, :], None) for i in range(count)]
    merged = []
    for a, b in zip(tiles[::2], tiles[1::2]):
        merged.append(two_sum(a[0], b[0]))
    tiles = merged
    while len(tiles) > 1:
        tiles = [pair_add(a, b) for a, b in zip(tiles[::2], tiles[1::2])]
    total = tiles[0]
    for by in (4, 2, 1):
        total = pair_add(total, tuple(pltpu.roll(t, by, 0) for t in total))
    return pair_add(total, tuple(pltpu.roll(t, 64, 1) for t in total))


def merge_kernel(parts_ref, out_ref):
    total = sum_messages(parts_ref)
    lane = lane_index((8, COLS))
    out_ref[...] = jnp.where(lane < 64, total[0], total[1])


def combine_kernel(
    parts_ref, powers_ref, x_ref, temp_hbm, surface_ref, residual_ref, wide, temp, sem
):
    for level in range(LEV):
        temp[level] = x_ref[pl.ds(HALO * BLOCK + level, ROWS, stride=BLOCK), :]
    move = pltpu.make_async_copy(temp, temp_hbm, sem)
    move.start()
    total = sum_messages(parts_ref)
    moments = [
        tuple(jnp.broadcast_to(t[:, order : order + 1], (8, COLS)) for t in total)
        for order in range(2 * ITERS)
    ]
    rho = list(moments)
    delta = list(moments)
    one = jnp.ones((8, COLS), jnp.float32)
    zero = jnp.zeros((8, COLS), jnp.float32)
    res = [one] + [zero] * ITERS
    way = [one] + [zero] * ITERS
    sol = [zero] * ITERS
    for step in range(ITERS):
        alpha = pair_div(rho[step], delta[step + 1])
        sol = [s + alpha[0] * w for s, w in zip(sol, way)]
        res = [res[0]] + [r - alpha[0] * w for r, w in zip(res[1:], way)]
        if step == ITERS - 1:
            break
        before = rho[step]
        last = 2 * ITERS - 1 - step
        rho = [
            None if order <= step or order >= last
            else pair_add(rho[order], pair_neg(pair_mul(alpha, delta[order + 1])))
            for order in range(2 * ITERS)
        ]
        beta = pair_neg(pair_mul(alpha, pair_div(rho[step + 1], before)))
        delta = [
            None if order <= step or order >= last
            else pair_add(rho[order], pair_mul(beta, delta[order]))
            for order in range(2 * ITERS)
        ]
        way = [r + beta[0] * w for r, w in zip(res, way)]
    for weights, target, factor in ((sol, surface_ref, 0.125), (res, residual_ref, 1.0)):
        for i in range(MID // 8):
            for j in range(2):
                spot = (slice(8 * i, 8 * i + 8), slice(128 * j, 128 * j + 128))
                value = weights[0] * powers_ref[(0,) + spot]
                for index in range(1, len(weights)):
                    value = value + weights[index] * powers_ref[(index,) + spot]
                wide[spot] = value * factor
        target[...] = wide[HALO : HALO + ROWS, HALO : HALO + COLS]
    move.wait()


def forward(axis, periodic):
    count = lax.axis_size(axis)
    pairs = [(i, i + 1) for i in range(count - 1)]
    return pairs + [(count - 1, 0)] if periodic else pairs


def backward(axis, periodic):
    return [(target, source) for source, target in forward(axis, periodic)]


def swap_near():
    return [(i, i ^ 1) for i in range(lax.axis_size("lon"))]


def swap_far():
    count = lax.axis_size("lon")
    return [(i, (i + 1) % count if i % 2 else (i - 1) % count) for i in range(count)]


def body(temp, kmt, kappa, helm, forcing, cutoff, conv_in, conv_mid, conv_late, conv_out):
    f32 = jnp.float32
    shape = jax.ShapeDtypeStruct
    blocks = lax.axis_size("lon")
    bf16 = jnp.bfloat16
    vmem = pl.BlockSpec(memory_space=pltpu.VMEM)
    cutoff = cutoff.reshape(1, ROWS)
    fields = (temp, kmt, kappa, helm, forcing, cutoff)
    slab = shape((CUT + 1, DEEP, COLS), f32)
    top, bottom = pl.pallas_call(
        slab_kernel,
        out_shape=(slab, slab),
        in_specs=[pl.BlockSpec(memory_space=pltpu.HBM)] * 6,
        out_specs=(vmem, vmem),
        scratch_shapes=(
            pltpu.VMEM((ROWS, COLS), jnp.int32),
            pltpu.VMEM((1, ROWS), jnp.int32),
            pltpu.SemaphoreType.DMA((10,)),
        ),
        compiler_params=pltpu.CompilerParams(vmem_limit_bytes=VMEM_LIMIT),
    )(*(pltpu.with_memory_space_constraint(field, pltpu.HBM) for field in fields))
    north = lax.ppermute(bottom, "lat", forward("lat", False))
    south = lax.ppermute(top, "lat", backward("lat", False))
    own = fetching(rows_kernel, shape((ROWS, FIELDS, COLS), f32), fields, fields)
    ends = shape((TALL // SLOTS, FIELDS, COLS), f32)
    rows, to_far, to_near = call(
        pack_kernel, (shape((TALL, FIELDS, COLS), f32), ends, ends)
    )(own, north, south)
    far = lax.ppermute(to_far, "lon", swap_far())
    near = lax.ppermute(to_near, "lon", swap_near())

    tables = [jnp.asarray(table) for table in filter_tables(blocks, COLS)]
    sources = (jnp.transpose(conv_in, (0, 2, 1)), conv_mid, conv_late, conv_out, *tables)
    outs = (
        shape((4 * FIELDS, 640), bf16),
        shape((256, 384), bf16),
        shape((256, 384), bf16),
        shape((48, 256), bf16),
    )
    outs = outs + tuple(shape(table.shape, bf16) for table in tables[:3] for _ in range(2))
    outs = outs + tuple(shape(table.shape, f32) for table in tables[3:])
    def closure_scratch(chunks):
        cells = chunks * COLS
        return (
            pltpu.VMEM((cells, 128), f32),
            pltpu.VMEM((cells, 128), f32),
            pltpu.VMEM((cells, 128), bf16),
            pltpu.VMEM((cells, 128), bf16),
        )

    block = shape((MID, LEV, COLS), f32)
    inside, line, *prepared = fetching(
        interior_kernel,
        (block, shape((LEV, COLS), f32)) + outs,
        sources,
        sources[:7],
        (rows,),
        (pltpu.VMEM((TALL * FIELDS, COLS), bf16),) + closure_scratch(19),
        10**9,
    )
    weights, tables = prepared[:4], prepared[4:]
    lines, planes = call(
        edge_kernel,
        (block, shape((3, MID, 2 * COLS), f32)),
        (pltpu.VMEM((TALL, FIELDS, COLS), f32),) + closure_scratch(6),
    )(rows, far, near, inside, *weights)

    def filtered_block(lines, line, tables):
        whole = lax.all_to_all(lines, "lon", split_axis=0, concat_axis=0, tiled=True)
        result = call(filter_kernel, shape((BLOCK * blocks, COLS), f32))(whole, line, *tables)
        result = result.reshape(BLOCK * blocks, 1, COLS)
        result = lax.all_to_all(result, "lon", split_axis=0, concat_axis=0, tiled=True)
        return result.reshape(BLOCK * blocks, COLS)

    def plain_block(lines, line, tables):
        ends = shape((MID, COLS), f32)
        to_far, to_near = call(ends_kernel, (ends, ends))(lines)
        far = lax.ppermute(to_far, "lon", swap_far())
        near = lax.ppermute(to_near, "lon", swap_near())
        return call(plain_kernel, shape((BLOCK * MID, COLS), f32))(lines, far, near)

    top_row = lax.axis_index("lat") * ROWS - HALO
    polar = (top_row < BAND) | (top_row + MID > ROWS * lax.axis_size("lat") - BAND)
    back = lax.cond(polar, filtered_block, plain_block, lines, line, tables)
    everyone = blocks * lax.axis_size("lat")
    wide = everyone // 8
    both = ("lon", "lat")
    inner = [[wide * i + k for k in range(wide)] for i in range(8)]
    outer = [[wide * i + k for i in range(8)] for k in range(wide)]
    powers, parts = call(
        powers_kernel,
        (
            shape((ITERS + 1, MID, 2 * COLS), f32),
            shape((wide, COLS), f32),
        ),
    )(back, planes)
    parts = lax.all_to_all(
        parts, both, split_axis=0, concat_axis=0, tiled=True, axis_index_groups=inner
    )
    parts = call(merge_kernel, shape((8, COLS), f32))(parts)
    parts = lax.all_to_all(
        parts, both, split_axis=0, concat_axis=0, tiled=True, axis_index_groups=outer
    )
    temp_new, surface, residual = pl.pallas_call(
        combine_kernel,
        out_shape=(
            shape((LEV, ROWS, COLS), f32),
            shape((ROWS, COLS), f32),
            shape((ROWS, COLS), f32),
        ),
        in_specs=[vmem] * 3,
        out_specs=(pl.BlockSpec(memory_space=pltpu.HBM), vmem, vmem),
        scratch_shapes=(
            pltpu.VMEM((MID, 2 * COLS), f32),
            pltpu.VMEM((LEV, ROWS, COLS), f32),
            pltpu.SemaphoreType.DMA,
        ),
        compiler_params=pltpu.CompilerParams(vmem_limit_bytes=VMEM_LIMIT),
    )(parts, powers, back)
    return temp_new, surface, residual


def solution(mesh):
    return jax.shard_map(
        body,
        mesh=mesh,
        in_specs=(
            P(None, "lat", "lon"),
            P("lat", "lon"),
            P("lat", "lon"),
            P("lat", "lon"),
            P("lat", "lon"),
            P("lat"),
            P(),
            P(),
            P(),
            P(),
        ),
        out_specs=(P(None, "lat", "lon"), P("lat", "lon"), P("lat", "lon")),
        check_vma=False,
    )
```

```python
import math

import jax
import jax.numpy as jnp
import numpy as np
from jax import lax
from jax.experimental import pallas as pl
from jax.experimental.pallas import tpu as pltpu
from jax.sharding import PartitionSpec as P

ITERS = 4
STEP = 0.25
LEV = 8
FIELDS = 16
KMT, KAPPA, HELM, FORCING, CUT = 8, 9, 10, 11, 12
BAND = 48
HALO = 4
DEEP = 8
ROWS = 24
COLS = 128
TALL = ROWS + 2 * DEEP
MID = ROWS + 2 * HALO
BLOCK = LEV + 1
SLOTS = 20
VMEM_LIMIT = 48 * 1024 * 1024


def call(kernel, outs, scratch=(), flops=None):
    spec = pl.BlockSpec(memory_space=pltpu.VMEM)
    return pl.pallas_call(
        kernel,
        out_shape=outs,
        out_specs=jax.tree.map(lambda _: spec, outs),
        scratch_shapes=scratch,
        compiler_params=pltpu.CompilerParams(vmem_limit_bytes=VMEM_LIMIT),
    )


def lane_index(shape):
    return lax.broadcasted_iota(jnp.int32, shape, len(shape) - 1)


def fetching(kernel, outs, sources, held, rest=(), scratch=(), flops=10**6):
    spec = pl.BlockSpec(memory_space=pltpu.VMEM)
    return pl.pallas_call(
        kernel,
        out_shape=outs,
        in_specs=[pl.BlockSpec(memory_space=pltpu.HBM)] * len(sources),
        out_specs=jax.tree.map(lambda _: spec, outs),
        scratch_shapes=tuple(pltpu.VMEM(source.shape, source.dtype) for source in held)
        + (pltpu.SemaphoreType.DMA((len(sources),)),),
        compiler_params=pltpu.CompilerParams(vmem_limit_bytes=VMEM_LIMIT),
        cost_estimate=pl.CostEstimate(flops=10**6, bytes_accessed=2 * 10**6, transcendentals=0),
    )(*(pltpu.with_memory_space_constraint(source, pltpu.HBM) for source in sources))


def slab_kernel(
    temp_hbm, kmt_hbm, kappa_hbm, helm_hbm, forcing_hbm, cutoff_hbm,
    top_ref, bottom_ref, kmt, cutoff, sems,
):
    pairs = [(kmt_hbm, kmt), (cutoff_hbm, cutoff)]
    for target, start in ((top_ref, 0), (bottom_ref, ROWS - DEEP)):
        rows = pl.ds(start, DEEP)
        pairs.append((temp_hbm.at[:, rows], target.at[pl.ds(0, LEV)]))
        for source, field in ((kappa_hbm, KAPPA), (helm_hbm, HELM), (forcing_hbm, FORCING)):
            pairs.append((source.at[rows], target.at[field]))
    moves = [
        pltpu.make_async_copy(source, target, sems.at[index])
        for index, (source, target) in enumerate(pairs)
    ]
    for move in moves:
        move.start()
    for move in moves:
        move.wait()
    for target, start in ((top_ref, 0), (bottom_ref, ROWS - DEEP)):
        target[KMT] = kmt[start : start + DEEP].astype(jnp.float32)
        target[CUT] = cutoff_lanes(cutoff)


def cutoff_lanes(cutoff_ref):
    line = cutoff_ref[...].astype(jnp.float32)
    line = jnp.concatenate([line, jnp.zeros((1, COLS - ROWS), jnp.float32)], axis=1)
    return jnp.broadcast_to(line, (DEEP, COLS))


def fetch(sources, targets, sems):
    moves = [
        pltpu.make_async_copy(source, target, sems.at[index])
        for index, (source, target) in enumerate(zip(sources, targets))
    ]
    for move in moves:
        move.start()
    return moves


def rows_kernel(*refs):
    sources, own_ref, raw, held, sems = refs[:15], refs[15], refs[16:25], refs[25:31], refs[31]
    moves = fetch(sources, tuple(held) + tuple(raw), sems)
    for move in moves[: len(held)]:
        move.wait()
    fill_rows(*held, own_ref)
    for move in moves[len(held) :]:
        move.wait()


def fill_rows(temp_ref, kmt_ref, kappa_ref, helm_ref, forcing_ref, cutoff_ref, own_ref):
    own_ref[:, CUT + 1 :, :] = jnp.zeros((ROWS, FIELDS - CUT - 1, COLS), jnp.float32)
    for level in range(LEV):
        own_ref[:, level, :] = temp_ref[level]
    own_ref[:, KMT, :] = kmt_ref[...].astype(jnp.float32)
    own_ref[:, KAPPA, :] = kappa_ref[...]
    own_ref[:, HELM, :] = helm_ref[...]
    own_ref[:, FORCING, :] = forcing_ref[...]
    own_ref[:, CUT, :] = jnp.broadcast_to(cutoff_lanes(cutoff_ref)[:1], (ROWS, COLS))


def fill_weights(
    first_ref, mid_ref, late_ref, last_ref, w_in_ref, w_mid_ref, w_late_ref, w_out_ref
):
    w_in_ref[...] = jnp.zeros(w_in_ref.shape, w_in_ref.dtype)
    width = mid_ref.shape[1]
    none = jnp.zeros((LEV, width), jnp.float32)
    for row in range(4):
        parts = []
        for tap in range(3):
            for parity in range(2):
                a = row - parity
                parts.append(first_ref[3 * a + tap].astype(jnp.float32) if 0 <= a < 3 else none)
        top = jnp.concatenate(parts, axis=1)
        marks = [jnp.ones((1, width), jnp.float32) if row == at else none[:1] for at in (1, 2, 2, 3)]
        marks = jnp.concatenate(marks, axis=1)
        block = jnp.concatenate(
            [
                jnp.concatenate([top, jnp.zeros((LEV, 4 * width), jnp.float32)], axis=1),
                jnp.concatenate(
                    [
                        jnp.concatenate([jnp.zeros((1, 6 * width), jnp.float32), marks], axis=1),
                        jnp.zeros((LEV - 1, 10 * width), jnp.float32),
                    ],
                    axis=0,
                ),
            ],
            axis=0,
        )
        w_in_ref[FIELDS * row : FIELDS * (row + 1)] = block.astype(jnp.bfloat16)

    def rows_of(ref, tap, parity):
        outs = ref.shape[1]
        blank = jnp.zeros((outs, width), jnp.float32)
        parts = []
        for row in range(4):
            a = row - parity
            parts.append(ref[3 * a + tap].astype(jnp.float32) if 0 <= a < 3 else blank)
        return jnp.concatenate(parts, axis=1)

    for ref, out_ref in ((mid_ref, w_mid_ref), (late_ref, w_late_ref)):
        for tap in range(3):
            both = jnp.concatenate([rows_of(ref, tap, 0), rows_of(ref, tap, 1)], axis=0)
            out_ref[:, 2 * width * tap : 2 * width * (tap + 1)] = both.T.astype(jnp.bfloat16)
    w_out_ref[...] = jnp.concatenate(
        [rows_of(last_ref, tap, parity) for tap in range(3) for parity in range(2)], axis=0
    ).astype(jnp.bfloat16)


def pack_kernel(own_ref, north_ref, south_ref, rows_ref, far_ref, near_ref, cut_ref):
    even = lax.rem(lax.axis_index("lon"), 2) == 0
    rows_ref[DEEP : DEEP + ROWS] = own_ref[...]
    for slab_ref, start in ((north_ref, 0), (south_ref, DEEP + ROWS)):
        rows = slice(start, start + DEEP)
        rows_ref[rows, CUT + 1 :, :] = jnp.zeros((DEEP, FIELDS - CUT - 1, COLS), jnp.float32)
        for field in range(CUT + 1):
            rows_ref[rows, field, :] = slab_ref[field]
    lane = lane_index((DEEP, COLS))
    north = pltpu.roll(north_ref[CUT], COLS - (ROWS - DEEP), 1)
    south = pltpu.roll(south_ref[CUT], DEEP + ROWS, 1)
    own = pltpu.roll(jnp.broadcast_to(own_ref[0, CUT : CUT + 1, :], (DEEP, COLS)), DEEP, 1)
    cut_ref[...] = jnp.where(lane < DEEP, north, jnp.where(lane < DEEP + ROWS, own, south))
    lane = lane_index((FIELDS, COLS))
    for part in range(TALL // SLOTS):
        first = jnp.zeros((FIELDS, COLS), jnp.float32)
        last = jnp.zeros((FIELDS, COLS), jnp.float32)
        for slot in range(SLOTS):
            here = rows_ref[part * SLOTS + slot]
            inside = (lane >= HALO * slot) & (lane < HALO * (slot + 1))
            first = jnp.where(inside, pltpu.roll(here, HALO * slot, 1) if slot else here, first)
            last = jnp.where(inside, pltpu.roll(here, HALO * (slot + 1), 1), last)
        far_ref[part] = jnp.where(even, first, last)
        near_ref[part] = jnp.where(even, last, first)


def closure_layers(window, pairs, stride, weights, acts, masks):
    w_in_ref, w_mid_ref, w_late_ref, w_out_ref = weights
    act_a, act_b = acts
    mask_odd, mask_even = masks

    def chunks(count):
        return range(-(-count * stride // COLS))

    def at(chunk, shift=0):
        return slice(COLS * chunk + shift, COLS * (chunk + 1) + shift)

    def both(act, chunk):
        return jnp.concatenate([act[at(chunk)], act[at(chunk, stride)]], axis=1)

    def finish(total, mask):
        v = (
            pltpu.roll(total[:, 0:128], 1, 0)
            + total[:, 128:256]
            + pltpu.roll(total[:, 256:384], COLS - 1, 0)
        )
        return (mask * (v / (1.0 + jnp.exp(-v)))).astype(jnp.bfloat16)

    for chunk in chunks(pairs):
        total = lax.dot_general(
            window(chunk),
            w_in_ref[...],
            (((0,), (0,)), ((), ())),
            preferred_element_type=jnp.float32,
        )
        mask_odd[at(chunk)] = total[:, 384:512]
        mask_even[at(chunk)] = total[:, 512:640]
        act_a[at(chunk)] = finish(total, total[:, 384:512])
    for chunk in chunks(pairs - 1):
        total = jnp.dot(both(act_a, chunk), w_mid_ref[...], preferred_element_type=jnp.float32)
        act_b[at(chunk)] = finish(total, mask_even[at(chunk)])
    for chunk in chunks(pairs - 2):
        total = jnp.dot(both(act_b, chunk), w_late_ref[...], preferred_element_type=jnp.float32)
        act_a[at(chunk)] = finish(total, mask_odd[at(chunk, stride)])
    results = []
    for chunk in chunks(pairs - 3):
        total = lax.dot_general(
            w_out_ref[...],
            both(act_a, chunk),
            (((1,), (1,)), ((), ())),
            preferred_element_type=jnp.float32,
        )
        results.append(
            pltpu.roll(total[0:16], 1, 1) + total[16:32] + pltpu.roll(total[32:48], COLS - 1, 1)
        )
    return results


def level_index():
    return lax.broadcasted_iota(jnp.int32, (LEV, COLS), 0).astype(jnp.float32)


def wetness(block):
    return (level_index() < block[KMT : KMT + 1]).astype(jnp.float32)


def first_input(block):
    wet = wetness(block)
    sea = jnp.where(level_index() == 0.0, wet, 0.0)
    return jnp.concatenate([wet * block[0:LEV], sea], axis=0).astype(jnp.bfloat16)


def advance(here, north, south, closure):
    wet = wetness(here)
    temp = here[0:LEV]
    tracer = wet * temp
    kappa = jnp.broadcast_to(here[KAPPA : KAPPA + 1], (LEV, COLS))
    diff = jnp.zeros((LEV, COLS), jnp.float32)
    for near in (south, north):
        near_w = wetness(near)
        diff = diff + near_w * 0.5 * (kappa + near[KAPPA : KAPPA + 1]) * (
            near_w * near[0:LEV] - tracer
        )
    for by in (COLS - 1, 1):
        diff = diff + pltpu.roll(wet, by, 1) * 0.5 * (kappa + pltpu.roll(kappa, by, 1)) * (
            pltpu.roll(tracer, by, 1) - tracer
        )
    diff = wet * diff
    eddy = wet * closure
    return wet * (temp + STEP * (diff + eddy))


FIRST = DEEP - HALO


def interior_kernel(*refs):
    rows_ref, cut_ref, raw, refs = refs[0], refs[1], refs[2:9], refs[9:]
    out_ref, line_ref, weights, tables, refs = refs[0], refs[1], refs[2:6], refs[6:12], refs[12:]
    start, mask_odd, mask_even, act_a, act_b = refs
    fill_weights(*raw[:4], *weights)
    for index, table in enumerate(raw[4:]):
        tables[2 * index][...], tables[2 * index + 1][...] = halves(table[...])
    for row in range(TALL):
        start[row * FIELDS : (row + 1) * FIELDS] = first_input(rows_ref[row])
    results = closure_layers(
        lambda chunk: start[2 * FIELDS * chunk : 2 * FIELDS * (chunk + 2)],
        TALL // 2 - 1,
        COLS,
        weights,
        (act_a, act_b),
        (mask_odd, mask_even),
    )
    for pair, closure in enumerate(results):
        for parity in range(2):
            row = FIRST + 2 * pair + parity
            out_ref[2 * pair + parity] = advance(
                rows_ref[row],
                rows_ref[row - 1],
                rows_ref[row + 1],
                closure[LEV * parity : LEV * (parity + 1)],
            )
    own_line = lane_index((LEV, COLS)) == lax.axis_index("lon") + FIRST
    kept = jnp.sum(jnp.where(own_line, cut_ref[...], 0.0), axis=1, keepdims=True)
    line_ref[...] = jnp.broadcast_to(kept, (LEV, COLS))


STRIP = 32
PER = COLS // STRIP


def edge_kernel(
    rows_ref, far_ref, near_ref, inside_ref, w_in_ref, w_mid_ref, w_late_ref, w_out_ref,
    out_ref, planes_ref, strips, mask_odd, mask_even, act_a, act_b,
):
    lane = lane_index((FIELDS, COLS))
    even = lax.rem(lax.axis_index("lon"), 2) == 0
    parts = range(TALL // SLOTS)
    from_west = [jnp.where(even, far_ref[part], near_ref[part]) for part in parts]
    from_east = [jnp.where(even, near_ref[part], far_ref[part]) for part in parts]
    for row in range(TALL):
        part, slot = row // SLOTS, row % SLOTS
        here = rows_ref[row]
        strip = jnp.where(lane < 24, pltpu.roll(from_east[part], (20 - HALO * slot) % COLS, 1) if slot != 5 else from_east[part], 0.0)
        strip = jnp.where(lane < 20, pltpu.roll(here, 20, 1), strip)
        strip = jnp.where(lane < 12, pltpu.roll(here, 4, 1), strip)
        west = pltpu.roll(from_west[part], COLS - HALO * slot, 1) if slot else from_west[part]
        strips[row] = jnp.where(lane < 4, west, strip)

    def side_by_side(parity, start):
        total = None
        for slot in range(PER):
            row = 2 * (start + slot) + parity
            if row >= TALL:
                continue
            piece = strips[row]
            piece = pltpu.roll(piece, STRIP * slot, 1) if slot else piece
            total = piece if total is None else total + piece
        return total

    def window(chunk):
        at = PER * chunk
        return jnp.concatenate(
            [
                first_input(block)
                for block in (
                    side_by_side(0, at),
                    side_by_side(1, at),
                    side_by_side(0, at + 1),
                    side_by_side(1, at + 1),
                )
            ],
            axis=0,
        )

    act_a[5 * COLS :] = jnp.zeros((COLS, COLS), jnp.bfloat16)
    act_b[5 * COLS :] = jnp.zeros((COLS, COLS), jnp.bfloat16)
    mask_odd[5 * COLS :] = jnp.zeros((COLS, COLS), jnp.float32)
    results = closure_layers(
        window,
        TALL // 2 - 1,
        STRIP,
        (w_in_ref, w_mid_ref, w_late_ref, w_out_ref),
        (act_a, act_b),
        (mask_odd, mask_even),
    )
    at_lane = lane_index((LEV, COLS))
    for chunk in range(4):
        at = PER * chunk + FIRST // 2
        closure = results[chunk]
        north = side_by_side(1, at - 1)
        upper = side_by_side(0, at)
        lower = side_by_side(1, at)
        south = side_by_side(0, at + 1)
        for parity, value in (
            (0, advance(upper, north, lower, closure[0:LEV])),
            (1, advance(lower, upper, south, closure[LEV : 2 * LEV])),
        ):
            for slot in range(PER):
                row = 2 * (PER * chunk + slot) + parity
                left = pltpu.roll(value, COLS - STRIP * slot - 4, 1)
                shift = (108 - STRIP * slot) % COLS
                right = pltpu.roll(value, shift, 1)
                out_ref[row] = jnp.where(
                    at_lane < HALO,
                    left,
                    jnp.where(at_lane >= COLS - HALO, right, inside_ref[row]),
                )
    plane_lane = lane_index((MID, COLS))
    for index, field in enumerate((KMT, HELM, FORCING)):
        moved = pltpu.roll(rows_ref[FIRST : FIRST + MID, field, :], HALO, 1)
        edge = strips[FIRST : FIRST + MID, field, :]
        planes_ref[index, :, 0:COLS] = jnp.where(plane_lane < HALO, edge, moved)
        planes_ref[index, :, COLS:] = jnp.where(
            plane_lane < HALO,
            moved,
            jnp.where(plane_lane < 2 * HALO, pltpu.roll(edge, COLS - 16, 1), 0.0),
        )


def filter_tables(blocks, width):
    length = blocks * width
    half = LEV // 2
    k = np.arange(blocks)
    outer = np.exp(-2j * np.pi * ((k[:, None] * k[None, :]) % blocks) / blocks)
    spread = np.zeros((blocks, 2, half, blocks, 2, half))
    for line in range(half):
        spread[:, 0, line, :, 0, line] = outer.real
        spread[:, 0, line, :, 1, line] = -outer.imag
        spread[:, 1, line, :, 0, line] = outer.imag
        spread[:, 1, line, :, 1, line] = outer.real
    spread = spread.reshape(blocks * LEV, blocks * LEV)
    m = np.arange(width)
    twist = np.exp(-2j * np.pi * (k[:, None] * m[None, :]) / length)
    sign = np.where(np.arange(LEV) < half, -1.0, 1.0)[None, :, None]
    twist_re = np.broadcast_to(twist.real[:, None, :], (blocks, LEV, width))
    twist_im = twist.imag[:, None, :] * sign
    inner = np.exp(-2j * np.pi * ((m[:, None] * m[None, :]) % width) / width)
    inner = np.concatenate([inner.real, inner.imag], axis=1)
    return [
        np.asarray(t, np.float32)
        for t in (spread, spread.T / length, inner, twist_re, twist_im)
    ]


def halves(x):
    high = x.astype(jnp.bfloat16)
    return high, (x - high.astype(jnp.float32)).astype(jnp.bfloat16)


def split_dot(a, b):
    def dot(x, y):
        return jnp.dot(x, y, preferred_element_type=jnp.float32)

    return dot(a[0], b[0]) + (dot(a[0], b[1]) + dot(a[1], b[0]))


def filter_kernel(
    x_ref, line_ref, spread_ref, spread_low, back_ref, back_low, inner_ref, inner_low,
    twist_re_ref, twist_im_ref, out_ref,
):
    blocks, lev, width = x_ref.shape
    shape = (blocks, lev, width)
    flat = (blocks * lev, width)
    length = blocks * width
    inner = (inner_ref[...], inner_low[...])

    def partner(block):
        return pltpu.roll(block, lev // 2, 1)

    sign = jnp.where(lax.broadcasted_iota(jnp.int32, shape, 1) < lev // 2, -1.0, 1.0)
    y = split_dot((spread_ref[...], spread_low[...]), halves(x_ref[...].reshape(flat)))
    y = y.reshape(shape)
    y = y * twist_re_ref[...] + partner(y) * twist_im_ref[...]
    s = split_dot(halves(y.reshape(flat)), inner)
    s = s[:, 0:width].reshape(shape) + partner(s[:, width:].reshape(shape)) * sign
    wave = lax.broadcasted_iota(jnp.int32, shape, 0) + blocks * lane_index(shape)
    folded = jnp.minimum(wave, length - wave).astype(jnp.float32)
    s = jnp.where(folded < line_ref[0:1, :][None], s, 0.0)
    y = split_dot(halves(s.reshape(flat)), inner)
    y = y[:, 0:width].reshape(shape) - partner(y[:, width:].reshape(shape)) * sign
    y = y * twist_re_ref[...] - partner(y) * twist_im_ref[...]
    x = split_dot((back_ref[...], back_low[...]), halves(y.reshape(flat))).reshape(shape)
    lane = lane_index((lev, width))
    moved = [pltpu.roll(x[block], HALO, 1) for block in range(blocks)]
    for block in range(blocks):
        edge = jnp.where(lane < HALO, moved[block - 1], moved[(block + 1) % blocks])
        edge = jnp.where(lane < 2 * HALO, edge, 0.0)
        edge = pltpu.roll(edge, 0, 1, stride=2 * HALO, stride_axis=0)
        row = BLOCK * block
        out_ref[row : row + lev, :] = x[block]
        out_ref[row + lev : row + BLOCK, :] = jnp.sum(edge, axis=0, keepdims=True)


def ends_kernel(x_ref, far_ref, near_ref):
    even = lax.rem(lax.axis_index("lon"), 2) == 0
    lane = lane_index((LEV, COLS))
    packed = []
    for row in range(MID):
        edge = jnp.where(lane < 2 * HALO, pltpu.roll(x_ref[row], HALO, 1), 0.0)
        edge = pltpu.roll(edge, 0, 1, stride=2 * HALO, stride_axis=0)
        packed.append(jnp.sum(edge, axis=0, keepdims=True))
    packed = jnp.concatenate(packed, axis=0)
    to_east = lax.rem(lane_index((MID, COLS)), 2 * HALO) < HALO
    last = jnp.where(to_east, packed, 0.0)
    first = jnp.where(to_east, 0.0, packed)
    far_ref[...] = jnp.where(even, first, last)
    near_ref[...] = jnp.where(even, last, first)


def plain_kernel(x_ref, far_ref, near_ref, out_ref):
    edge = far_ref[...] + near_ref[...]
    for row in range(MID):
        out_ref[BLOCK * row : BLOCK * row + LEV, :] = x_ref[row]
        out_ref[BLOCK * row + LEV : BLOCK * (row + 1), :] = edge[row : row + 1]


def two_sum(a, b):
    s = a + b
    t = s - a
    return s, (a - (s - t)) + (b - t)


def quick_sum(a, b):
    s = a + b
    return s, b - (s - a)


def split(a):
    c = a * 4097.0
    high = c - (c - a)
    return high, a - high


def two_product(a, b):
    p = a * b
    ah, al = split(a)
    bh, bl = split(b)
    return p, ((ah * bh - p) + ah * bl + al * bh) + al * bl


def pair_add(a, b):
    s, e = two_sum(a[0], b[0])
    return quick_sum(s, e + (a[1] + b[1]))


def pair_neg(a):
    return -a[0], -a[1]


def pair_mul(a, b):
    p, e = two_product(a[0], b[0])
    return quick_sum(p, e + (a[0] * b[1] + a[1] * b[0]))


def pair_inverse(a):
    x = 1.0 / a[0]
    p, e = two_product(a[0], x)
    return quick_sum(x, x * (((1.0 - p) - e) - a[1] * x))


def powers_kernel(x_ref, planes_ref, temp_hbm, powers_ref, parts_ref, temp, sem):
    for level in range(LEV):
        temp[level] = x_ref[pl.ds(HALO * BLOCK + level, ROWS, stride=BLOCK), :]
    move = pltpu.make_async_copy(temp, temp_hbm, sem)
    move.start()
    lane = lane_index((LEV, COLS))
    wide_lane = lane_index((MID, COLS))
    kmt_left = planes_ref[0, :, 0:COLS]
    kmt_right = planes_ref[0, :, COLS:]
    kmt = pltpu.roll(jnp.where(wide_lane < HALO, kmt_right, kmt_left), COLS - HALO, 1)
    mean = jnp.zeros((MID, COLS), jnp.float32)
    for level in range(LEV):
        here = x_ref[pl.ds(level, MID, stride=BLOCK), :]
        mean = mean + jnp.where(kmt > level, here, 0.0)
    edge = x_ref[pl.ds(LEV, MID, stride=BLOCK), :]
    edge_kmt = jnp.where(wide_lane < HALO, kmt_left, kmt_right)
    edge_kmt = jnp.where(wide_lane < 2 * HALO, edge_kmt, 0.0)
    for by in (8, 16, 32, 64):
        edge_kmt = edge_kmt + pltpu.roll(edge_kmt, by, 1)
    edge = jnp.where(edge_kmt > (wide_lane // (2 * HALO)).astype(jnp.float32), edge, 0.0)
    for by in (64, 32, 16, 8):
        edge = edge + pltpu.roll(edge, by, 1)
    moved = pltpu.roll(mean, HALO, 1)
    mean = jnp.concatenate(
        [
            jnp.where(wide_lane < HALO, edge, moved),
            jnp.where(wide_lane < HALO, moved, jnp.where(wide_lane < 2 * HALO, edge, 0.0)),
        ],
        axis=1,
    )
    sea = (planes_ref[0] > 0.0).astype(jnp.float32)

    def around(v):
        return (
            pltpu.roll(v, 1, 0)
            + pltpu.roll(v, MID - 1, 0)
            + pltpu.roll(v, 1, 1)
            + pltpu.roll(v, 2 * COLS - 1, 1)
        )

    diagonal = planes_ref[1] + sea * around(sea)
    powers = [sea * (mean * (1.0 / LEV) + planes_ref[2])]
    for _ in range(ITERS):
        v = powers[-1]
        powers.append((diagonal * v - sea * around(v)) * 0.125)
    for index, v in enumerate(powers):
        powers_ref[index] = v
    row = lax.broadcasted_iota(jnp.int32, (MID, 2 * COLS), 0)
    column = lane_index((MID, 2 * COLS))
    own = (
        (row >= HALO) & (row < HALO + ROWS) & (column >= HALO) & (column < HALO + COLS)
    )
    owned = [jnp.where(own, v, 0.0) for v in powers]
    high_rows, low_rows = [], []
    for order in range(2 * ITERS):
        p, e = two_product(owned[order // 2], owned[order - order // 2])
        tiles = [
            (p[8 * i : 8 * i + 8, 128 * j : 128 * j + 128], e[8 * i : 8 * i + 8, 128 * j : 128 * j + 128])
            for i in range(MID // 8)
            for j in range(2)
        ]
        while len(tiles) > 1:
            tiles = [pair_add(a, b) for a, b in zip(tiles[::2], tiles[1::2])]
        total = tiles[0]
        for by in (4, 2, 1):
            total = pair_add(total, tuple(pltpu.roll(t, by, 0) for t in total))
        high_rows.append(total[0])
        low_rows.append(total[1])
    where = lax.broadcasted_iota(jnp.int32, (8, COLS), 0)
    high, low = high_rows[0], low_rows[0]
    for order in range(1, 2 * ITERS):
        high = jnp.where(where == order, high_rows[order], high)
        low = jnp.where(where == order, low_rows[order], low)
    total = (high, low)
    for by in (64, 32, 16, 8, 4, 2, 1):
        total = pair_add(total, tuple(pltpu.roll(t, by, 1) for t in total))
    spot = lax.broadcasted_iota(jnp.int32, (8, COLS), 0)
    message = jnp.where(lane == spot, total[0], 0.0) + jnp.where(lane == spot + 64, total[1], 0.0)
    message = jnp.sum(message, axis=0, keepdims=True)
    parts_ref[...] = jnp.broadcast_to(message, parts_ref.shape)
    move.wait()


def sum_messages(parts_ref):
    count = parts_ref.shape[0] // 8
    if count == 1:
        total = (parts_ref[...], jnp.zeros((8, COLS), jnp.float32))
        for by in (4, 2, 1):
            total = pair_add(total, tuple(pltpu.roll(t, by, 0) for t in total))
        return pair_add(total, tuple(pltpu.roll(t, 64, 1) for t in total))
    tiles = [(parts_ref[8 * i : 8 * i + 8, :], None) for i in range(count)]
    merged = []
    for a, b in zip(tiles[::2], tiles[1::2]):
        merged.append(two_sum(a[0], b[0]))
    tiles = merged
    while len(tiles) > 1:
        tiles = [pair_add(a, b) for a, b in zip(tiles[::2], tiles[1::2])]
    total = tiles[0]
    for by in (4, 2, 1):
        total = pair_add(total, tuple(pltpu.roll(t, by, 0) for t in total))
    return pair_add(total, tuple(pltpu.roll(t, 64, 1) for t in total))


def merge_kernel(parts_ref, out_ref):
    total = sum_messages(parts_ref)
    lane = lane_index((8, COLS))
    out_ref[...] = jnp.where(lane < 64, total[0], total[1])


def combine_kernel(parts_ref, powers_ref, surface_ref, residual_ref, wide):
    total = sum_messages(parts_ref)
    moments = [
        tuple(jnp.broadcast_to(t[:, order : order + 1], (8, COLS)) for t in total)
        for order in range(2 * ITERS)
    ]
    rho = list(moments)
    delta = list(moments)
    one = jnp.ones((8, COLS), jnp.float32)
    zero = jnp.zeros((8, COLS), jnp.float32)
    res = [one] + [zero] * ITERS
    way = [one] + [zero] * ITERS
    sol = [zero] * ITERS
    for step in range(ITERS):
        inverse = pair_inverse(delta[step + 1])
        alpha = pair_mul(rho[step], inverse)
        sol = [s + alpha[0] * w for s, w in zip(sol, way)]
        res = [res[0]] + [r - alpha[0] * w for r, w in zip(res[1:], way)]
        if step == ITERS - 1:
            break
        last = 2 * ITERS - 1 - step
        rho = [
            None if order <= step or order >= last
            else pair_add(rho[order], pair_neg(pair_mul(alpha, delta[order + 1])))
            for order in range(2 * ITERS)
        ]
        beta = pair_neg(pair_mul(rho[step + 1], inverse))
        delta = [
            None if order <= step or order >= last
            else pair_add(rho[order], pair_mul(beta, delta[order]))
            for order in range(2 * ITERS)
        ]
        way = [r + beta[0] * w for r, w in zip(res, way)]
    for weights, target, factor in ((sol, surface_ref, 0.125), (res, residual_ref, 1.0)):
        for i in range(MID // 8):
            for j in range(2):
                spot = (slice(8 * i, 8 * i + 8), slice(128 * j, 128 * j + 128))
                value = weights[0] * powers_ref[(0,) + spot]
                for index in range(1, len(weights)):
                    value = value + weights[index] * powers_ref[(index,) + spot]
                wide[spot] = value * factor
        target[...] = wide[HALO : HALO + ROWS, HALO : HALO + COLS]


def forward(axis, periodic):
    count = lax.axis_size(axis)
    pairs = [(i, i + 1) for i in range(count - 1)]
    return pairs + [(count - 1, 0)] if periodic else pairs


def backward(axis, periodic):
    return [(target, source) for source, target in forward(axis, periodic)]


def swap_near():
    return [(i, i ^ 1) for i in range(lax.axis_size("lon"))]


def swap_far():
    count = lax.axis_size("lon")
    return [(i, (i + 1) % count if i % 2 else (i - 1) % count) for i in range(count)]


def body(temp, kmt, kappa, helm, forcing, cutoff, conv_in, conv_mid, conv_late, conv_out):
    f32 = jnp.float32
    shape = jax.ShapeDtypeStruct
    blocks = lax.axis_size("lon")
    bf16 = jnp.bfloat16
    vmem = pl.BlockSpec(memory_space=pltpu.VMEM)
    cutoff = cutoff.reshape(1, ROWS)
    fields = (temp, kmt, kappa, helm, forcing, cutoff)
    slab = shape((CUT + 1, DEEP, COLS), f32)
    top, bottom = pl.pallas_call(
        slab_kernel,
        out_shape=(slab, slab),
        in_specs=[pl.BlockSpec(memory_space=pltpu.HBM)] * 6,
        out_specs=(vmem, vmem),
        scratch_shapes=(
            pltpu.VMEM((ROWS, COLS), jnp.int32),
            pltpu.VMEM((1, ROWS), jnp.int32),
            pltpu.SemaphoreType.DMA((10,)),
        ),
        compiler_params=pltpu.CompilerParams(vmem_limit_bytes=VMEM_LIMIT),
    )(*(pltpu.with_memory_space_constraint(field, pltpu.HBM) for field in fields))
    north = lax.ppermute(bottom, "lat", forward("lat", False))
    south = lax.ppermute(top, "lat", backward("lat", False))
    tables = tuple(jnp.asarray(table) for table in filter_tables(blocks, COLS))
    sources = (jnp.transpose(conv_in, (0, 2, 1)), conv_mid, conv_late, conv_out) + tables
    own, *raw = fetching(
        rows_kernel,
        (shape((ROWS, FIELDS, COLS), f32),)
        + tuple(shape(source.shape, source.dtype) for source in sources),
        fields + sources,
        fields,
    )
    ends = shape((TALL // SLOTS, FIELDS, COLS), f32)
    rows, to_far, to_near, cuts = call(
        pack_kernel, (shape((TALL, FIELDS, COLS), f32), ends, ends, shape((DEEP, COLS), f32))
    )(own, north, south)
    far = lax.ppermute(to_far, "lon", swap_far())
    near = lax.ppermute(to_near, "lon", swap_near())

    outs = (
        shape((4 * FIELDS, 640), bf16),
        shape((256, 384), bf16),
        shape((256, 384), bf16),
        shape((48, 256), bf16),
    )
    outs = outs + tuple(shape(table.shape, bf16) for table in tables[:3] for _ in range(2))
    def closure_scratch(chunks):
        cells = chunks * COLS
        return (
            pltpu.VMEM((cells, 128), f32),
            pltpu.VMEM((cells, 128), f32),
            pltpu.VMEM((cells, 128), bf16),
            pltpu.VMEM((cells, 128), bf16),
        )

    block = shape((MID, LEV, COLS), f32)
    inside, line, *prepared = call(
        interior_kernel,
        (block, shape((LEV, COLS), f32)) + outs,
        (pltpu.VMEM((TALL * FIELDS, COLS), bf16),) + closure_scratch(19),
        10**9,
    )(rows, cuts, *raw[:7])
    weights, tables = prepared[:4], prepared[4:] + raw[7:]
    lines, planes = call(
        edge_kernel,
        (block, shape((3, MID, 2 * COLS), f32)),
        (pltpu.VMEM((TALL, FIELDS, COLS), f32),) + closure_scratch(6),
    )(rows, far, near, inside, *weights)

    def filtered_block(lines, line, tables):
        whole = lax.all_to_all(lines, "lon", split_axis=0, concat_axis=0, tiled=True)
        result = call(filter_kernel, shape((BLOCK * blocks, COLS), f32))(whole, line, *tables)
        result = result.reshape(BLOCK * blocks, 1, COLS)
        result = lax.all_to_all(result, "lon", split_axis=0, concat_axis=0, tiled=True)
        return result.reshape(BLOCK * blocks, COLS)

    def plain_block(lines, line, tables):
        ends = shape((MID, COLS), f32)
        to_far, to_near = call(ends_kernel, (ends, ends))(lines)
        far = lax.ppermute(to_far, "lon", swap_far())
        near = lax.ppermute(to_near, "lon", swap_near())
        return call(plain_kernel, shape((BLOCK * MID, COLS), f32))(lines, far, near)

    top_row = lax.axis_index("lat") * ROWS - HALO
    polar = (top_row < BAND) | (top_row + MID > ROWS * lax.axis_size("lat") - BAND)
    back = lax.cond(polar, filtered_block, plain_block, lines, line, tables)
    everyone = blocks * lax.axis_size("lat")
    wide = everyone // 8
    both = ("lon", "lat")
    inner = [[wide * i + k for k in range(wide)] for i in range(8)]
    outer = [[wide * i + k for i in range(8)] for k in range(wide)]
    temp_new, powers, parts = pl.pallas_call(
        powers_kernel,
        out_shape=(
            shape((LEV, ROWS, COLS), f32),
            shape((ITERS + 1, MID, 2 * COLS), f32),
            shape((wide, COLS), f32),
        ),
        in_specs=[vmem] * 2,
        out_specs=(pl.BlockSpec(memory_space=pltpu.HBM), vmem, vmem),
        scratch_shapes=(pltpu.VMEM((LEV, ROWS, COLS), f32), pltpu.SemaphoreType.DMA),
        compiler_params=pltpu.CompilerParams(vmem_limit_bytes=VMEM_LIMIT),
    )(back, planes)
    parts = lax.all_to_all(
        parts, both, split_axis=0, concat_axis=0, tiled=True, axis_index_groups=inner
    )
    parts = call(merge_kernel, shape((8, COLS), f32))(parts)
    parts = lax.all_to_all(
        parts, both, split_axis=0, concat_axis=0, tiled=True, axis_index_groups=outer
    )
    surface, residual = call(
        combine_kernel,
        (shape((ROWS, COLS), f32), shape((ROWS, COLS), f32)),
        (pltpu.VMEM((MID, 2 * COLS), f32),),
    )(parts, powers)
    return temp_new, surface, residual


def solution(mesh):
    return jax.shard_map(
        body,
        mesh=mesh,
        in_specs=(
            P(None, "lat", "lon"),
            P("lat", "lon"),
            P("lat", "lon"),
            P("lat", "lon"),
            P("lat", "lon"),
            P("lat"),
            P(),
            P(),
            P(),
            P(),
        ),
        out_specs=(P(None, "lat", "lon"), P("lat", "lon"), P("lat", "lon")),
        check_vma=False,
    )
```

```python
import math

import jax
import jax.numpy as jnp
import numpy as np
from jax import lax
from jax.experimental import pallas as pl
from jax.experimental.pallas import tpu as pltpu
from jax.sharding import PartitionSpec as P

ITERS = 4
STEP = 0.25
LEV = 8
FIELDS = 16
KMT, KAPPA, HELM, FORCING, CUT = 8, 9, 10, 11, 12
BAND = 48
HALO = 4
DEEP = 8
ROWS = 24
COLS = 128
TALL = ROWS + 2 * DEEP
MID = ROWS + 2 * HALO
BLOCK = LEV + 1
SLOTS = 20
VMEM_LIMIT = 48 * 1024 * 1024


def call(kernel, outs, scratch=(), flops=None):
    spec = pl.BlockSpec(memory_space=pltpu.VMEM)
    return pl.pallas_call(
        kernel,
        out_shape=outs,
        out_specs=jax.tree.map(lambda _: spec, outs),
        scratch_shapes=scratch,
        compiler_params=pltpu.CompilerParams(vmem_limit_bytes=VMEM_LIMIT),
    )


def lane_index(shape):
    return lax.broadcasted_iota(jnp.int32, shape, len(shape) - 1)


def fetching(kernel, outs, sources, held, rest=(), scratch=(), flops=10**6):
    spec = pl.BlockSpec(memory_space=pltpu.VMEM)
    return pl.pallas_call(
        kernel,
        out_shape=outs,
        in_specs=[pl.BlockSpec(memory_space=pltpu.HBM)] * len(sources),
        out_specs=jax.tree.map(lambda _: spec, outs),
        scratch_shapes=tuple(pltpu.VMEM(source.shape, source.dtype) for source in held)
        + (pltpu.SemaphoreType.DMA((len(sources),)),),
        compiler_params=pltpu.CompilerParams(vmem_limit_bytes=VMEM_LIMIT),
        cost_estimate=pl.CostEstimate(flops=10**6, bytes_accessed=2 * 10**6, transcendentals=0),
    )(*(pltpu.with_memory_space_constraint(source, pltpu.HBM) for source in sources))


def slab_kernel(
    temp_hbm, kmt_hbm, kappa_hbm, helm_hbm, forcing_hbm, cutoff_hbm,
    top_ref, bottom_ref, kmt, cutoff, sems,
):
    pairs = [(kmt_hbm, kmt), (cutoff_hbm, cutoff)]
    for target, start in ((top_ref, 0), (bottom_ref, ROWS - DEEP)):
        rows = pl.ds(start, DEEP)
        pairs.append((temp_hbm.at[:, rows], target.at[pl.ds(0, LEV)]))
        for source, field in ((kappa_hbm, KAPPA), (helm_hbm, HELM), (forcing_hbm, FORCING)):
            pairs.append((source.at[rows], target.at[field]))
    moves = [
        pltpu.make_async_copy(source, target, sems.at[index])
        for index, (source, target) in enumerate(pairs)
    ]
    for move in moves:
        move.start()
    for move in moves:
        move.wait()
    for target, start in ((top_ref, 0), (bottom_ref, ROWS - DEEP)):
        target[KMT] = kmt[start : start + DEEP].astype(jnp.float32)
        target[CUT] = cutoff_lanes(cutoff)


def cutoff_lanes(cutoff_ref):
    line = cutoff_ref[...].astype(jnp.float32)
    line = jnp.concatenate([line, jnp.zeros((1, COLS - ROWS), jnp.float32)], axis=1)
    return jnp.broadcast_to(line, (DEEP, COLS))


def fetch(sources, targets, sems):
    moves = [
        pltpu.make_async_copy(source, target, sems.at[index])
        for index, (source, target) in enumerate(zip(sources, targets))
    ]
    for move in moves:
        move.start()
    return moves


def rows_kernel(*refs):
    sources, own_ref, raw, held, sems = refs[:15], refs[15], refs[16:25], refs[25:31], refs[31]
    moves = fetch(sources, tuple(held) + tuple(raw), sems)
    for move in moves[: len(held)]:
        move.wait()
    fill_rows(*held, own_ref)
    for move in moves[len(held) :]:
        move.wait()


def fill_rows(temp_ref, kmt_ref, kappa_ref, helm_ref, forcing_ref, cutoff_ref, own_ref):
    own_ref[:, CUT + 1 :, :] = jnp.zeros((ROWS, FIELDS - CUT - 1, COLS), jnp.float32)
    for level in range(LEV):
        own_ref[:, level, :] = temp_ref[level]
    own_ref[:, KMT, :] = kmt_ref[...].astype(jnp.float32)
    own_ref[:, KAPPA, :] = kappa_ref[...]
    own_ref[:, HELM, :] = helm_ref[...]
    own_ref[:, FORCING, :] = forcing_ref[...]
    own_ref[:, CUT, :] = jnp.broadcast_to(cutoff_lanes(cutoff_ref)[:1], (ROWS, COLS))


def fill_weights(
    first_ref, mid_ref, late_ref, last_ref, w_in_ref, w_mid_ref, w_late_ref, w_out_ref
):
    w_in_ref[...] = jnp.zeros(w_in_ref.shape, w_in_ref.dtype)
    width = mid_ref.shape[1]
    none = jnp.zeros((LEV, width), jnp.float32)
    for row in range(4):
        parts = []
        for tap in range(3):
            for parity in range(2):
                a = row - parity
                parts.append(first_ref[3 * a + tap].astype(jnp.float32) if 0 <= a < 3 else none)
        top = jnp.concatenate(parts, axis=1)
        marks = [jnp.ones((1, width), jnp.float32) if row == at else none[:1] for at in (1, 2, 2, 3)]
        marks = jnp.concatenate(marks, axis=1)
        block = jnp.concatenate(
            [
                jnp.concatenate([top, jnp.zeros((LEV, 4 * width), jnp.float32)], axis=1),
                jnp.concatenate(
                    [
                        jnp.concatenate([jnp.zeros((1, 6 * width), jnp.float32), marks], axis=1),
                        jnp.zeros((LEV - 1, 10 * width), jnp.float32),
                    ],
                    axis=0,
                ),
            ],
            axis=0,
        )
        w_in_ref[FIELDS * row : FIELDS * (row + 1)] = block.astype(jnp.bfloat16)

    def rows_of(ref, tap, parity):
        outs = ref.shape[1]
        blank = jnp.zeros((outs, width), jnp.float32)
        parts = []
        for row in range(4):
            a = row - parity
            parts.append(ref[3 * a + tap].astype(jnp.float32) if 0 <= a < 3 else blank)
        return jnp.concatenate(parts, axis=1)

    for ref, out_ref in ((mid_ref, w_mid_ref), (late_ref, w_late_ref)):
        for tap in range(3):
            both = jnp.concatenate([rows_of(ref, tap, 0), rows_of(ref, tap, 1)], axis=0)
            out_ref[:, 2 * width * tap : 2 * width * (tap + 1)] = both.T.astype(jnp.bfloat16)
    w_out_ref[...] = jnp.concatenate(
        [rows_of(last_ref, tap, parity) for tap in range(3) for parity in range(2)], axis=0
    ).astype(jnp.bfloat16)


def pack_kernel(own_ref, north_ref, south_ref, rows_ref, far_ref, near_ref, cut_ref):
    even = lax.rem(lax.axis_index("lon"), 2) == 0
    rows_ref[DEEP : DEEP + ROWS] = own_ref[...]
    for slab_ref, start in ((north_ref, 0), (south_ref, DEEP + ROWS)):
        rows = slice(start, start + DEEP)
        rows_ref[rows, CUT + 1 :, :] = jnp.zeros((DEEP, FIELDS - CUT - 1, COLS), jnp.float32)
        for field in range(CUT + 1):
            rows_ref[rows, field, :] = slab_ref[field]
    lane = lane_index((DEEP, COLS))
    north = pltpu.roll(north_ref[CUT], COLS - (ROWS - DEEP), 1)
    south = pltpu.roll(south_ref[CUT], DEEP + ROWS, 1)
    own = pltpu.roll(jnp.broadcast_to(own_ref[0, CUT : CUT + 1, :], (DEEP, COLS)), DEEP, 1)
    cut_ref[...] = jnp.where(lane < DEEP, north, jnp.where(lane < DEEP + ROWS, own, south))
    lane = lane_index((FIELDS, COLS))
    for part in range(TALL // SLOTS):
        first = jnp.zeros((FIELDS, COLS), jnp.float32)
        last = jnp.zeros((FIELDS, COLS), jnp.float32)
        for slot in range(SLOTS):
            here = rows_ref[part * SLOTS + slot]
            inside = (lane >= HALO * slot) & (lane < HALO * (slot + 1))
            first = jnp.where(inside, pltpu.roll(here, HALO * slot, 1) if slot else here, first)
            last = jnp.where(inside, pltpu.roll(here, HALO * (slot + 1), 1), last)
        far_ref[part] = jnp.where(even, first, last)
        near_ref[part] = jnp.where(even, last, first)


def closure_layers(window, pairs, stride, weights, acts, masks):
    w_in_ref, w_mid_ref, w_late_ref, w_out_ref = weights
    act_a, act_b = acts
    mask_odd, mask_even = masks

    def chunks(count):
        return range(-(-count * stride // COLS))

    def at(chunk, shift=0):
        return slice(COLS * chunk + shift, COLS * (chunk + 1) + shift)

    def both(act, chunk):
        return jnp.concatenate([act[at(chunk)], act[at(chunk, stride)]], axis=1)

    def finish(total, mask):
        v = (
            pltpu.roll(total[:, 0:128], 1, 0)
            + total[:, 128:256]
            + pltpu.roll(total[:, 256:384], COLS - 1, 0)
        )
        return (mask * (v / (1.0 + jnp.exp(-v)))).astype(jnp.bfloat16)

    for chunk in chunks(pairs):
        total = lax.dot_general(
            window(chunk),
            w_in_ref[...],
            (((0,), (0,)), ((), ())),
            preferred_element_type=jnp.float32,
        )
        mask_odd[at(chunk)] = total[:, 384:512]
        mask_even[at(chunk)] = total[:, 512:640]
        act_a[at(chunk)] = finish(total, total[:, 384:512])
    for chunk in chunks(pairs - 1):
        total = jnp.dot(both(act_a, chunk), w_mid_ref[...], preferred_element_type=jnp.float32)
        act_b[at(chunk)] = finish(total, mask_even[at(chunk)])
    for chunk in chunks(pairs - 2):
        total = jnp.dot(both(act_b, chunk), w_late_ref[...], preferred_element_type=jnp.float32)
        act_a[at(chunk)] = finish(total, mask_odd[at(chunk, stride)])
    results = []
    for chunk in chunks(pairs - 3):
        total = lax.dot_general(
            w_out_ref[...],
            both(act_a, chunk),
            (((1,), (1,)), ((), ())),
            preferred_element_type=jnp.float32,
        )
        results.append(
            pltpu.roll(total[0:16], 1, 1) + total[16:32] + pltpu.roll(total[32:48], COLS - 1, 1)
        )
    return results


def level_index():
    return lax.broadcasted_iota(jnp.int32, (LEV, COLS), 0).astype(jnp.float32)


def wetness(block):
    return (level_index() < block[KMT : KMT + 1]).astype(jnp.float32)


def first_input(block):
    wet = wetness(block)
    sea = jnp.where(level_index() == 0.0, wet, 0.0)
    return jnp.concatenate([wet * block[0:LEV], sea], axis=0).astype(jnp.bfloat16)


def advance(here, north, south, closure):
    wet = wetness(here)
    temp = here[0:LEV]
    tracer = wet * temp
    kappa = jnp.broadcast_to(here[KAPPA : KAPPA + 1], (LEV, COLS))
    diff = jnp.zeros((LEV, COLS), jnp.float32)
    for near in (south, north):
        near_w = wetness(near)
        diff = diff + near_w * 0.5 * (kappa + near[KAPPA : KAPPA + 1]) * (
            near_w * near[0:LEV] - tracer
        )
    for by in (COLS - 1, 1):
        diff = diff + pltpu.roll(wet, by, 1) * 0.5 * (kappa + pltpu.roll(kappa, by, 1)) * (
            pltpu.roll(tracer, by, 1) - tracer
        )
    diff = wet * diff
    eddy = wet * closure
    return wet * (temp + STEP * (diff + eddy))


FIRST = DEEP - HALO


def interior_kernel(*refs):
    rows_ref, cut_ref, raw, refs = refs[0], refs[1], refs[2:9], refs[9:]
    out_ref, line_ref, weights, tables, refs = refs[0], refs[1], refs[2:6], refs[6:12], refs[12:]
    start, mask_odd, mask_even, act_a, act_b = refs
    fill_weights(*raw[:4], *weights)
    for index, table in enumerate(raw[4:]):
        tables[2 * index][...], tables[2 * index + 1][...] = halves(table[...])
    for row in range(TALL):
        start[row * FIELDS : (row + 1) * FIELDS] = first_input(rows_ref[row])
    results = closure_layers(
        lambda chunk: start[2 * FIELDS * chunk : 2 * FIELDS * (chunk + 2)],
        TALL // 2 - 1,
        COLS,
        weights,
        (act_a, act_b),
        (mask_odd, mask_even),
    )
    for pair, closure in enumerate(results):
        for parity in range(2):
            row = FIRST + 2 * pair + parity
            out_ref[2 * pair + parity] = advance(
                rows_ref[row],
                rows_ref[row - 1],
                rows_ref[row + 1],
                closure[LEV * parity : LEV * (parity + 1)],
            )
    own_line = lane_index((LEV, COLS)) == lax.axis_index("lon") + FIRST
    kept = jnp.sum(jnp.where(own_line, cut_ref[...], 0.0), axis=1, keepdims=True)
    line_ref[...] = jnp.broadcast_to(kept, (LEV, COLS))


STRIP = 32
PER = COLS // STRIP


def edge_kernel(
    rows_ref, far_ref, near_ref, inside_ref, w_in_ref, w_mid_ref, w_late_ref, w_out_ref,
    out_ref, planes_ref, strips, mask_odd, mask_even, act_a, act_b,
):
    lane = lane_index((FIELDS, COLS))
    even = lax.rem(lax.axis_index("lon"), 2) == 0
    parts = range(TALL // SLOTS)
    from_west = [jnp.where(even, far_ref[part], near_ref[part]) for part in parts]
    from_east = [jnp.where(even, near_ref[part], far_ref[part]) for part in parts]
    for row in range(TALL):
        part, slot = row // SLOTS, row % SLOTS
        here = rows_ref[row]
        strip = jnp.where(lane < 24, pltpu.roll(from_east[part], (20 - HALO * slot) % COLS, 1) if slot != 5 else from_east[part], 0.0)
        strip = jnp.where(lane < 20, pltpu.roll(here, 20, 1), strip)
        strip = jnp.where(lane < 12, pltpu.roll(here, 4, 1), strip)
        west = pltpu.roll(from_west[part], COLS - HALO * slot, 1) if slot else from_west[part]
        strips[row] = jnp.where(lane < 4, west, strip)

    def side_by_side(parity, start):
        total = None
        for slot in range(PER):
            row = 2 * (start + slot) + parity
            if row >= TALL:
                continue
            piece = strips[row]
            piece = pltpu.roll(piece, STRIP * slot, 1) if slot else piece
            total = piece if total is None else total + piece
        return total

    def window(chunk):
        at = PER * chunk
        return jnp.concatenate(
            [
                first_input(block)
                for block in (
                    side_by_side(0, at),
                    side_by_side(1, at),
                    side_by_side(0, at + 1),
                    side_by_side(1, at + 1),
                )
            ],
            axis=0,
        )

    act_a[5 * COLS :] = jnp.zeros((COLS, COLS), jnp.bfloat16)
    act_b[5 * COLS :] = jnp.zeros((COLS, COLS), jnp.bfloat16)
    mask_odd[5 * COLS :] = jnp.zeros((COLS, COLS), jnp.float32)
    results = closure_layers(
        window,
        TALL // 2 - 1,
        STRIP,
        (w_in_ref, w_mid_ref, w_late_ref, w_out_ref),
        (act_a, act_b),
        (mask_odd, mask_even),
    )
    at_lane = lane_index((LEV, COLS))
    for chunk in range(4):
        at = PER * chunk + FIRST // 2
        closure = results[chunk]
        north = side_by_side(1, at - 1)
        upper = side_by_side(0, at)
        lower = side_by_side(1, at)
        south = side_by_side(0, at + 1)
        for parity, value in (
            (0, advance(upper, north, lower, closure[0:LEV])),
            (1, advance(lower, upper, south, closure[LEV : 2 * LEV])),
        ):
            for slot in range(PER):
                row = 2 * (PER * chunk + slot) + parity
                left = pltpu.roll(value, COLS - STRIP * slot - 4, 1)
                shift = (108 - STRIP * slot) % COLS
                right = pltpu.roll(value, shift, 1)
                out_ref[row] = jnp.where(
                    at_lane < HALO,
                    left,
                    jnp.where(at_lane >= COLS - HALO, right, inside_ref[row]),
                )
    plane_lane = lane_index((MID, COLS))
    for index, field in enumerate((KMT, HELM, FORCING)):
        moved = pltpu.roll(rows_ref[FIRST : FIRST + MID, field, :], HALO, 1)
        edge = strips[FIRST : FIRST + MID, field, :]
        planes_ref[index, :, 0:COLS] = jnp.where(plane_lane < HALO, edge, moved)
        planes_ref[index, :, COLS:] = jnp.where(
            plane_lane < HALO,
            moved,
            jnp.where(plane_lane < 2 * HALO, pltpu.roll(edge, COLS - 16, 1), 0.0),
        )


def filter_tables(blocks, width):
    length = blocks * width
    half = LEV // 2
    k = np.arange(blocks)
    outer = np.exp(-2j * np.pi * ((k[:, None] * k[None, :]) % blocks) / blocks)
    spread = np.zeros((blocks, 2, half, blocks, 2, half))
    for line in range(half):
        spread[:, 0, line, :, 0, line] = outer.real
        spread[:, 0, line, :, 1, line] = -outer.imag
        spread[:, 1, line, :, 0, line] = outer.imag
        spread[:, 1, line, :, 1, line] = outer.real
    spread = spread.reshape(blocks * LEV, blocks * LEV)
    m = np.arange(width)
    twist = np.exp(-2j * np.pi * (k[:, None] * m[None, :]) / length)
    sign = np.where(np.arange(LEV) < half, -1.0, 1.0)[None, :, None]
    twist_re = np.broadcast_to(twist.real[:, None, :], (blocks, LEV, width))
    twist_im = twist.imag[:, None, :] * sign
    inner = np.exp(-2j * np.pi * ((m[:, None] * m[None, :]) % width) / width)
    inner = np.concatenate([inner.real, inner.imag], axis=1)
    return [
        np.asarray(t, np.float32)
        for t in (spread, spread.T / length, inner, twist_re, twist_im)
    ]


def halves(x):
    high = x.astype(jnp.bfloat16)
    return high, (x - high.astype(jnp.float32)).astype(jnp.bfloat16)


def split_dot(a, b):
    def dot(x, y):
        return jnp.dot(x, y, preferred_element_type=jnp.float32)

    return dot(a[0], b[0]) + (dot(a[0], b[1]) + dot(a[1], b[0]))


def filter_kernel(
    x_ref, line_ref, spread_ref, spread_low, back_ref, back_low, inner_ref, inner_low,
    twist_re_ref, twist_im_ref, out_ref,
):
    blocks, lev, width = x_ref.shape
    shape = (blocks, lev, width)
    flat = (blocks * lev, width)
    length = blocks * width
    inner = (inner_ref[...], inner_low[...])

    def partner(block):
        return pltpu.roll(block, lev // 2, 1)

    sign = jnp.where(lax.broadcasted_iota(jnp.int32, shape, 1) < lev // 2, -1.0, 1.0)
    y = split_dot((spread_ref[...], spread_low[...]), halves(x_ref[...].reshape(flat)))
    y = y.reshape(shape)
    y = y * twist_re_ref[...] + partner(y) * twist_im_ref[...]
    s = split_dot(halves(y.reshape(flat)), inner)
    s = s[:, 0:width].reshape(shape) + partner(s[:, width:].reshape(shape)) * sign
    wave = lax.broadcasted_iota(jnp.int32, shape, 0) + blocks * lane_index(shape)
    folded = jnp.minimum(wave, length - wave).astype(jnp.float32)
    s = jnp.where(folded < line_ref[0:1, :][None], s, 0.0)
    y = split_dot(halves(s.reshape(flat)), inner)
    y = y[:, 0:width].reshape(shape) - partner(y[:, width:].reshape(shape)) * sign
    y = y * twist_re_ref[...] - partner(y) * twist_im_ref[...]
    x = split_dot((back_ref[...], back_low[...]), halves(y.reshape(flat))).reshape(shape)
    lane = lane_index((lev, width))
    moved = [pltpu.roll(x[block], HALO, 1) for block in range(blocks)]
    for block in range(blocks):
        edge = jnp.where(lane < HALO, moved[block - 1], moved[(block + 1) % blocks])
        edge = jnp.where(lane < 2 * HALO, edge, 0.0)
        edge = pltpu.roll(edge, 0, 1, stride=2 * HALO, stride_axis=0)
        row = BLOCK * block
        out_ref[row : row + lev, :] = x[block]
        out_ref[row + lev : row + BLOCK, :] = jnp.sum(edge, axis=0, keepdims=True)


def ends_kernel(x_ref, far_ref, near_ref):
    even = lax.rem(lax.axis_index("lon"), 2) == 0
    lane = lane_index((LEV, COLS))
    packed = []
    for row in range(MID):
        edge = jnp.where(lane < 2 * HALO, pltpu.roll(x_ref[row], HALO, 1), 0.0)
        edge = pltpu.roll(edge, 0, 1, stride=2 * HALO, stride_axis=0)
        packed.append(jnp.sum(edge, axis=0, keepdims=True))
    packed = jnp.concatenate(packed, axis=0)
    to_east = lax.rem(lane_index((MID, COLS)), 2 * HALO) < HALO
    last = jnp.where(to_east, packed, 0.0)
    first = jnp.where(to_east, 0.0, packed)
    far_ref[...] = jnp.where(even, first, last)
    near_ref[...] = jnp.where(even, last, first)


def plain_kernel(x_ref, far_ref, near_ref, out_ref):
    edge = far_ref[...] + near_ref[...]
    for row in range(MID):
        out_ref[BLOCK * row : BLOCK * row + LEV, :] = x_ref[row]
        out_ref[BLOCK * row + LEV : BLOCK * (row + 1), :] = edge[row : row + 1]


def two_sum(a, b):
    s = a + b
    t = s - a
    return s, (a - (s - t)) + (b - t)


def quick_sum(a, b):
    s = a + b
    return s, b - (s - a)


def split(a):
    c = a * 4097.0
    high = c - (c - a)
    return high, a - high


def two_product(a, b):
    p = a * b
    ah, al = split(a)
    bh, bl = split(b)
    return p, ((ah * bh - p) + ah * bl + al * bh) + al * bl


def pair_add(a, b):
    s, e = two_sum(a[0], b[0])
    return quick_sum(s, e + (a[1] + b[1]))


def pair_neg(a):
    return -a[0], -a[1]


def pair_mul(a, b):
    p, e = two_product(a[0], b[0])
    return quick_sum(p, e + (a[0] * b[1] + a[1] * b[0]))


def pair_inverse(a):
    x = 1.0 / a[0]
    p, e = two_product(a[0], x)
    return quick_sum(x, x * (((1.0 - p) - e) - a[1] * x))


def powers_kernel(x_ref, planes_ref, temp_hbm, powers_ref, parts_ref, temp, sems):
    moves = []
    for level in range(LEV):
        temp[level] = x_ref[pl.ds(HALO * BLOCK + level, ROWS, stride=BLOCK), :]
        moves.append(pltpu.make_async_copy(temp.at[level], temp_hbm.at[level], sems.at[level]))
        moves[-1].start()
    lane = lane_index((LEV, COLS))
    wide_lane = lane_index((MID, COLS))
    kmt_left = planes_ref[0, :, 0:COLS]
    kmt_right = planes_ref[0, :, COLS:]
    kmt = pltpu.roll(jnp.where(wide_lane < HALO, kmt_right, kmt_left), COLS - HALO, 1)
    mean = jnp.zeros((MID, COLS), jnp.float32)
    for level in range(LEV):
        here = x_ref[pl.ds(level, MID, stride=BLOCK), :]
        mean = mean + jnp.where(kmt > level, here, 0.0)
    edge = x_ref[pl.ds(LEV, MID, stride=BLOCK), :]
    edge_kmt = jnp.where(wide_lane < HALO, kmt_left, kmt_right)
    edge_kmt = jnp.where(wide_lane < 2 * HALO, edge_kmt, 0.0)
    for by in (8, 16, 32, 64):
        edge_kmt = edge_kmt + pltpu.roll(edge_kmt, by, 1)
    edge = jnp.where(edge_kmt > (wide_lane // (2 * HALO)).astype(jnp.float32), edge, 0.0)
    for by in (64, 32, 16, 8):
        edge = edge + pltpu.roll(edge, by, 1)
    moved = pltpu.roll(mean, HALO, 1)
    mean = jnp.concatenate(
        [
            jnp.where(wide_lane < HALO, edge, moved),
            jnp.where(wide_lane < HALO, moved, jnp.where(wide_lane < 2 * HALO, edge, 0.0)),
        ],
        axis=1,
    )
    sea = (planes_ref[0] > 0.0).astype(jnp.float32)

    def around(v):
        return (
            pltpu.roll(v, 1, 0)
            + pltpu.roll(v, MID - 1, 0)
            + pltpu.roll(v, 1, 1)
            + pltpu.roll(v, 2 * COLS - 1, 1)
        )

    diagonal = planes_ref[1] + sea * around(sea)
    powers = [sea * (mean * (1.0 / LEV) + planes_ref[2])]
    for _ in range(ITERS):
        v = powers[-1]
        powers.append((diagonal * v - sea * around(v)) * 0.125)
    for index, v in enumerate(powers):
        powers_ref[index] = v
    row = lax.broadcasted_iota(jnp.int32, (MID, 2 * COLS), 0)
    column = lane_index((MID, 2 * COLS))
    own = (
        (row >= HALO) & (row < HALO + ROWS) & (column >= HALO) & (column < HALO + COLS)
    )
    owned = [jnp.where(own, v, 0.0) for v in powers]
    high_rows, low_rows = [], []
    for order in range(2 * ITERS):
        p, e = two_product(owned[order // 2], owned[order - order // 2])
        tiles = [
            (p[8 * i : 8 * i + 8, 128 * j : 128 * j + 128], e[8 * i : 8 * i + 8, 128 * j : 128 * j + 128])
            for i in range(MID // 8)
            for j in range(2)
        ]
        while len(tiles) > 1:
            tiles = [pair_add(a, b) for a, b in zip(tiles[::2], tiles[1::2])]
        total = tiles[0]
        for by in (4, 2, 1):
            total = pair_add(total, tuple(pltpu.roll(t, by, 0) for t in total))
        high_rows.append(total[0])
        low_rows.append(total[1])
    where = lax.broadcasted_iota(jnp.int32, (8, COLS), 0)
    high, low = high_rows[0], low_rows[0]
    for order in range(1, 2 * ITERS):
        high = jnp.where(where == order, high_rows[order], high)
        low = jnp.where(where == order, low_rows[order], low)
    total = (high, low)
    for by in (64, 32, 16, 8, 4, 2, 1):
        total = pair_add(total, tuple(pltpu.roll(t, by, 1) for t in total))
    spot = lax.broadcasted_iota(jnp.int32, (8, COLS), 0)
    message = jnp.where(lane == spot, total[0], 0.0) + jnp.where(lane == spot + 64, total[1], 0.0)
    message = jnp.sum(message, axis=0, keepdims=True)
    parts_ref[...] = jnp.broadcast_to(message, parts_ref.shape)
    for move in moves:
        move.wait()


def sum_messages(parts_ref):
    count = parts_ref.shape[0] // 8
    tiles = [parts_ref[8 * i : 8 * i + 8, :] for i in range(count)]
    tiles = [two_sum(a, b) for a, b in zip(tiles[::2], tiles[1::2])]
    while len(tiles) > 1:
        tiles = [pair_add(a, b) for a, b in zip(tiles[::2], tiles[1::2])]
    total = tiles[0]
    for by in (4, 2, 1):
        total = pair_add(total, tuple(pltpu.roll(t, by, 0) for t in total))
    return pair_add(total, tuple(pltpu.roll(t, 64, 1) for t in total))


def merge_kernel(parts_ref, out_ref):
    total = sum_messages(parts_ref)
    lane = lane_index((8, COLS))
    merged = jnp.where(lane < 64, total[0], total[1])
    out_ref[...] = jnp.broadcast_to(merged[:1], out_ref.shape)


def combine_kernel(parts_ref, powers_ref, surface_ref, residual_ref, wide):
    total = sum_messages(parts_ref)
    moments = [
        tuple(jnp.broadcast_to(t[:, order : order + 1], (8, COLS)) for t in total)
        for order in range(2 * ITERS)
    ]
    rho = list(moments)
    delta = list(moments)
    one = jnp.ones((8, COLS), jnp.float32)
    zero = jnp.zeros((8, COLS), jnp.float32)
    res = [one] + [zero] * ITERS
    way = [one] + [zero] * ITERS
    sol = [zero] * ITERS
    for step in range(ITERS):
        inverse = pair_inverse(delta[step + 1])
        alpha = pair_mul(rho[step], inverse)
        sol = [s + alpha[0] * w for s, w in zip(sol, way)]
        res = [res[0]] + [r - alpha[0] * w for r, w in zip(res[1:], way)]
        if step == ITERS - 1:
            break
        last = 2 * ITERS - 1 - step
        rho = [
            None if order <= step or order >= last
            else pair_add(rho[order], pair_neg(pair_mul(alpha, delta[order + 1])))
            for order in range(2 * ITERS)
        ]
        beta = pair_neg(pair_mul(rho[step + 1], inverse))
        delta = [
            None if order <= step or order >= last
            else pair_add(rho[order], pair_mul(beta, delta[order]))
            for order in range(2 * ITERS)
        ]
        way = [r + beta[0] * w for r, w in zip(res, way)]
    for weights, target, factor in ((sol, surface_ref, 0.125), (res, residual_ref, 1.0)):
        for i in range(MID // 8):
            for j in range(2):
                spot = (slice(8 * i, 8 * i + 8), slice(128 * j, 128 * j + 128))
                value = weights[0] * powers_ref[(0,) + spot]
                for index in range(1, len(weights)):
                    value = value + weights[index] * powers_ref[(index,) + spot]
                wide[spot] = value * factor
        target[...] = wide[HALO : HALO + ROWS, HALO : HALO + COLS]


def forward(axis, periodic):
    count = lax.axis_size(axis)
    pairs = [(i, i + 1) for i in range(count - 1)]
    return pairs + [(count - 1, 0)] if periodic else pairs


def backward(axis, periodic):
    return [(target, source) for source, target in forward(axis, periodic)]


def reduction_groups(lon, lat):
    inner, outer = {}, {}
    for i in range(lon):
        for j in range(lat):
            inner.setdefault((i // 4, j // 4), []).append(i * lat + j)
            outer.setdefault((i % 4, j % 4), []).append(i * lat + j)
    return list(inner.values()), list(outer.values())


def swap_near():
    return [(i, i ^ 1) for i in range(lax.axis_size("lon"))]


def swap_far():
    count = lax.axis_size("lon")
    return [(i, (i + 1) % count if i % 2 else (i - 1) % count) for i in range(count)]


def body(temp, kmt, kappa, helm, forcing, cutoff, conv_in, conv_mid, conv_late, conv_out):
    f32 = jnp.float32
    shape = jax.ShapeDtypeStruct
    blocks = lax.axis_size("lon")
    bf16 = jnp.bfloat16
    vmem = pl.BlockSpec(memory_space=pltpu.VMEM)
    cutoff = cutoff.reshape(1, ROWS)
    fields = (temp, kmt, kappa, helm, forcing, cutoff)
    slab = shape((CUT + 1, DEEP, COLS), f32)
    top, bottom = pl.pallas_call(
        slab_kernel,
        out_shape=(slab, slab),
        in_specs=[pl.BlockSpec(memory_space=pltpu.HBM)] * 6,
        out_specs=(vmem, vmem),
        scratch_shapes=(
            pltpu.VMEM((ROWS, COLS), jnp.int32),
            pltpu.VMEM((1, ROWS), jnp.int32),
            pltpu.SemaphoreType.DMA((10,)),
        ),
        compiler_params=pltpu.CompilerParams(vmem_limit_bytes=VMEM_LIMIT),
    )(*(pltpu.with_memory_space_constraint(field, pltpu.HBM) for field in fields))
    north = lax.ppermute(bottom, "lat", forward("lat", False))
    south = lax.ppermute(top, "lat", backward("lat", False))
    tables = tuple(jnp.asarray(table) for table in filter_tables(blocks, COLS))
    sources = (jnp.transpose(conv_in, (0, 2, 1)), conv_mid, conv_late, conv_out) + tables
    own, *raw = fetching(
        rows_kernel,
        (shape((ROWS, FIELDS, COLS), f32),)
        + tuple(shape(source.shape, source.dtype) for source in sources),
        fields + sources,
        fields,
    )
    ends = shape((TALL // SLOTS, FIELDS, COLS), f32)
    rows, to_far, to_near, cuts = call(
        pack_kernel, (shape((TALL, FIELDS, COLS), f32), ends, ends, shape((DEEP, COLS), f32))
    )(own, north, south)
    far = lax.ppermute(to_far, "lon", swap_far())
    near = lax.ppermute(to_near, "lon", swap_near())

    outs = (
        shape((4 * FIELDS, 640), bf16),
        shape((256, 384), bf16),
        shape((256, 384), bf16),
        shape((48, 256), bf16),
    )
    outs = outs + tuple(shape(table.shape, bf16) for table in tables[:3] for _ in range(2))
    def closure_scratch(chunks):
        cells = chunks * COLS
        return (
            pltpu.VMEM((cells, 128), f32),
            pltpu.VMEM((cells, 128), f32),
            pltpu.VMEM((cells, 128), bf16),
            pltpu.VMEM((cells, 128), bf16),
        )

    block = shape((MID, LEV, COLS), f32)
    inside, line, *prepared = call(
        interior_kernel,
        (block, shape((LEV, COLS), f32)) + outs,
        (pltpu.VMEM((TALL * FIELDS, COLS), bf16),) + closure_scratch(19),
        10**9,
    )(rows, cuts, *raw[:7])
    weights, tables = prepared[:4], prepared[4:] + raw[7:]
    lines, planes = call(
        edge_kernel,
        (block, shape((3, MID, 2 * COLS), f32)),
        (pltpu.VMEM((TALL, FIELDS, COLS), f32),) + closure_scratch(6),
    )(rows, far, near, inside, *weights)

    def filtered_block(lines, line, tables):
        whole = lax.all_to_all(lines, "lon", split_axis=0, concat_axis=0, tiled=True)
        result = call(filter_kernel, shape((BLOCK * blocks, COLS), f32))(whole, line, *tables)
        result = result.reshape(BLOCK * blocks, 1, COLS)
        result = lax.all_to_all(result, "lon", split_axis=0, concat_axis=0, tiled=True)
        return result.reshape(BLOCK * blocks, COLS)

    def plain_block(lines, line, tables):
        ends = shape((MID, COLS), f32)
        to_far, to_near = call(ends_kernel, (ends, ends))(lines)
        far = lax.ppermute(to_far, "lon", swap_far())
        near = lax.ppermute(to_near, "lon", swap_near())
        return call(plain_kernel, shape((BLOCK * MID, COLS), f32))(lines, far, near)

    top_row = lax.axis_index("lat") * ROWS - HALO
    polar = (top_row < BAND) | (top_row + MID > ROWS * lax.axis_size("lat") - BAND)
    back = lax.cond(polar, filtered_block, plain_block, lines, line, tables)
    everyone = blocks * lax.axis_size("lat")
    both = ("lon", "lat")
    inner, outer = reduction_groups(blocks, lax.axis_size("lat"))
    wide = len(inner[0])
    temp_new, powers, parts = pl.pallas_call(
        powers_kernel,
        out_shape=(
            shape((LEV, ROWS, COLS), f32),
            shape((ITERS + 1, MID, 2 * COLS), f32),
            shape((wide, COLS), f32),
        ),
        in_specs=[vmem] * 2,
        out_specs=(pl.BlockSpec(memory_space=pltpu.HBM), vmem, vmem),
        scratch_shapes=(pltpu.VMEM((LEV, ROWS, COLS), f32), pltpu.SemaphoreType.DMA((LEV,))),
        compiler_params=pltpu.CompilerParams(vmem_limit_bytes=VMEM_LIMIT),
    )(back, planes)
    parts = lax.all_to_all(
        parts, both, split_axis=0, concat_axis=0, tiled=True, axis_index_groups=inner
    )
    parts = call(merge_kernel, shape((everyone // wide, COLS), f32))(parts)
    parts = lax.all_to_all(
        parts, both, split_axis=0, concat_axis=0, tiled=True, axis_index_groups=outer
    )
    surface, residual = call(
        combine_kernel,
        (shape((ROWS, COLS), f32), shape((ROWS, COLS), f32)),
        (pltpu.VMEM((MID, 2 * COLS), f32),),
    )(parts, powers)
    return temp_new, surface, residual


def solution(mesh):
    return jax.shard_map(
        body,
        mesh=mesh,
        in_specs=(
            P(None, "lat", "lon"),
            P("lat", "lon"),
            P("lat", "lon"),
            P("lat", "lon"),
            P("lat", "lon"),
            P("lat"),
            P(),
            P(),
            P(),
            P(),
        ),
        out_specs=(P(None, "lat", "lon"), P("lat", "lon"), P("lat", "lon")),
        check_vma=False,
    )
```

```python
import math

import jax
import jax.numpy as jnp
import numpy as np
from jax import lax
from jax.experimental import pallas as pl
from jax.experimental.pallas import tpu as pltpu
from jax.sharding import PartitionSpec as P

ITERS = 4
STEP = 0.25
LEV = 8
FIELDS = 16
KMT, HELM, FORCING, KAPPA, CUT = 8, 9, 10, 11, 12
BAND = 48
HALO = 4
DEEP = 8
ROWS = 24
COLS = 128
TALL = ROWS + 2 * DEEP
MID = ROWS + 2 * HALO
BLOCK = LEV + 3
FIRST = DEEP - HALO
SLOTS = 20
ENDS = TALL // SLOTS * FIELDS
VMEM_LIMIT = 48 * 1024 * 1024


def call(kernel, outs, scratch=(), flops=None):
    spec = pl.BlockSpec(memory_space=pltpu.VMEM)
    return pl.pallas_call(
        kernel,
        out_shape=outs,
        out_specs=jax.tree.map(lambda _: spec, outs),
        scratch_shapes=scratch,
        compiler_params=pltpu.CompilerParams(vmem_limit_bytes=VMEM_LIMIT),
    )


def lane_index(shape):
    return lax.broadcasted_iota(jnp.int32, shape, len(shape) - 1)


def fetching(kernel, outs, sources, held, rest=(), scratch=(), flops=10**6):
    spec = pl.BlockSpec(memory_space=pltpu.VMEM)
    return pl.pallas_call(
        kernel,
        out_shape=outs,
        in_specs=[pl.BlockSpec(memory_space=pltpu.HBM)] * len(sources),
        out_specs=jax.tree.map(lambda _: spec, outs),
        scratch_shapes=tuple(pltpu.VMEM(source.shape, source.dtype) for source in held)
        + (pltpu.SemaphoreType.DMA((len(sources),)),),
        compiler_params=pltpu.CompilerParams(vmem_limit_bytes=VMEM_LIMIT),
        cost_estimate=pl.CostEstimate(flops=10**6, bytes_accessed=2 * 10**6, transcendentals=0),
    )(*(pltpu.with_memory_space_constraint(source, pltpu.HBM) for source in sources))


def slab_kernel(
    temp_hbm, kmt_hbm, kappa_hbm, helm_hbm, forcing_hbm, cutoff_hbm,
    top_ref, bottom_ref, kmt, cutoff, sems,
):
    pairs = [(kmt_hbm, kmt), (cutoff_hbm, cutoff)]
    for target, start in ((top_ref, 0), (bottom_ref, ROWS - DEEP)):
        rows = pl.ds(start, DEEP)
        pairs.append((temp_hbm.at[:, rows], target.at[pl.ds(0, LEV)]))
        for source, field in ((kappa_hbm, KAPPA), (helm_hbm, HELM), (forcing_hbm, FORCING)):
            pairs.append((source.at[rows], target.at[field]))
    moves = [
        pltpu.make_async_copy(source, target, sems.at[index])
        for index, (source, target) in enumerate(pairs)
    ]
    for move in moves:
        move.start()
    for move in moves:
        move.wait()
    for target, start in ((top_ref, 0), (bottom_ref, ROWS - DEEP)):
        target[KMT] = kmt[start : start + DEEP].astype(jnp.float32)
        target[CUT] = cutoff_lanes(cutoff)


def cutoff_lanes(cutoff_ref):
    line = cutoff_ref[...].astype(jnp.float32)
    line = jnp.concatenate([line, jnp.zeros((1, COLS - ROWS), jnp.float32)], axis=1)
    return jnp.broadcast_to(line, (DEEP, COLS))


def fetch(sources, targets, sems):
    moves = [
        pltpu.make_async_copy(source, target, sems.at[index])
        for index, (source, target) in enumerate(zip(sources, targets))
    ]
    for move in moves:
        move.start()
    return moves


def rows_kernel(*refs):
    sources, own_ref, raw, held, sems = refs[:15], refs[15], refs[16:25], refs[25:31], refs[31]
    moves = fetch(sources, tuple(held) + tuple(raw), sems)
    for move in moves[: len(held)]:
        move.wait()
    fill_rows(*held, own_ref)
    for move in moves[len(held) :]:
        move.wait()


def fill_rows(temp_ref, kmt_ref, kappa_ref, helm_ref, forcing_ref, cutoff_ref, own_ref):
    own_ref[:, CUT + 1 :, :] = jnp.zeros((ROWS, FIELDS - CUT - 1, COLS), jnp.float32)
    for level in range(LEV):
        own_ref[:, level, :] = temp_ref[level]
    own_ref[:, KMT, :] = kmt_ref[...].astype(jnp.float32)
    own_ref[:, KAPPA, :] = kappa_ref[...]
    own_ref[:, HELM, :] = helm_ref[...]
    own_ref[:, FORCING, :] = forcing_ref[...]
    own_ref[:, CUT, :] = jnp.broadcast_to(cutoff_lanes(cutoff_ref)[:1], (ROWS, COLS))


def fill_weights(
    first_ref, mid_ref, late_ref, last_ref, w_in_ref, w_mid_ref, w_late_ref, w_out_ref
):
    w_in_ref[...] = jnp.zeros(w_in_ref.shape, w_in_ref.dtype)
    width = mid_ref.shape[1]
    none = jnp.zeros((LEV, width), jnp.float32)
    for row in range(4):
        parts = []
        for tap in range(3):
            for parity in range(2):
                a = row - parity
                parts.append(first_ref[3 * a + tap].astype(jnp.float32) if 0 <= a < 3 else none)
        top = jnp.concatenate(parts, axis=1)
        marks = [jnp.ones((1, width), jnp.float32) if row == at else none[:1] for at in (1, 2, 2, 3)]
        marks = jnp.concatenate(marks, axis=1)
        block = jnp.concatenate(
            [
                jnp.concatenate([top, jnp.zeros((LEV, 4 * width), jnp.float32)], axis=1),
                jnp.concatenate(
                    [
                        jnp.concatenate([jnp.zeros((1, 6 * width), jnp.float32), marks], axis=1),
                        jnp.zeros((LEV - 1, 10 * width), jnp.float32),
                    ],
                    axis=0,
                ),
            ],
            axis=0,
        )
        w_in_ref[FIELDS * row : FIELDS * (row + 1)] = block.astype(jnp.bfloat16)

    def rows_of(ref, tap, parity):
        outs = ref.shape[1]
        blank = jnp.zeros((outs, width), jnp.float32)
        parts = []
        for row in range(4):
            a = row - parity
            parts.append(ref[3 * a + tap].astype(jnp.float32) if 0 <= a < 3 else blank)
        return jnp.concatenate(parts, axis=1)

    for ref, out_ref in ((mid_ref, w_mid_ref), (late_ref, w_late_ref)):
        for tap in range(3):
            both = jnp.concatenate([rows_of(ref, tap, 0), rows_of(ref, tap, 1)], axis=0)
            out_ref[:, 2 * width * tap : 2 * width * (tap + 1)] = both.T.astype(jnp.bfloat16)
    w_out_ref[...] = jnp.concatenate(
        [rows_of(last_ref, tap, parity) for tap in range(3) for parity in range(2)], axis=0
    ).astype(jnp.bfloat16)


def pack_kernel(own_ref, north_ref, south_ref, rows_ref, far_ref, near_ref, cut_ref):
    even = lax.rem(lax.axis_index("lon"), 2) == 0
    rows_ref[DEEP : DEEP + ROWS] = own_ref[...]
    for slab_ref, start in ((north_ref, 0), (south_ref, DEEP + ROWS)):
        rows = slice(start, start + DEEP)
        rows_ref[rows, CUT + 1 :, :] = jnp.zeros((DEEP, FIELDS - CUT - 1, COLS), jnp.float32)
        for field in range(CUT + 1):
            rows_ref[rows, field, :] = slab_ref[field]
    lane = lane_index((DEEP, COLS))
    north = pltpu.roll(north_ref[CUT], COLS - (ROWS - DEEP), 1)
    south = pltpu.roll(south_ref[CUT], DEEP + ROWS, 1)
    own = pltpu.roll(jnp.broadcast_to(own_ref[0, CUT : CUT + 1, :], (DEEP, COLS)), DEEP, 1)
    cut_ref[...] = jnp.where(lane < DEEP, north, jnp.where(lane < DEEP + ROWS, own, south))
    lane = lane_index((FIELDS, COLS))
    for part in range(TALL // SLOTS):
        first = jnp.zeros((FIELDS, COLS), jnp.float32)
        last = jnp.zeros((FIELDS, COLS), jnp.float32)
        for slot in range(SLOTS):
            here = rows_ref[part * SLOTS + slot]
            inside = (lane >= HALO * slot) & (lane < HALO * (slot + 1))
            first = jnp.where(inside, pltpu.roll(here, HALO * slot, 1) if slot else here, first)
            last = jnp.where(inside, pltpu.roll(here, HALO * (slot + 1), 1), last)
        far_ref[part] = jnp.where(even, first, last)
        near_ref[FIELDS * part : FIELDS * (part + 1)] = jnp.where(even, last, first)
    for at, field in ((ENDS, KMT), (ENDS + MID, HELM)):
        near_ref[at : at + MID] = rows_ref[FIRST : FIRST + MID, field, :]


def closure_layers(window, pairs, stride, weights, acts, masks):
    w_in_ref, w_mid_ref, w_late_ref, w_out_ref = weights
    act_a, act_b = acts
    mask_odd, mask_even = masks

    def chunks(count):
        return range(-(-count * stride // COLS))

    def at(chunk, shift=0):
        return slice(COLS * chunk + shift, COLS * (chunk + 1) + shift)

    def both(act, chunk):
        return jnp.concatenate([act[at(chunk)], act[at(chunk, stride)]], axis=1)

    def finish(total, mask):
        v = (
            pltpu.roll(total[:, 0:128], 1, 0)
            + total[:, 128:256]
            + pltpu.roll(total[:, 256:384], COLS - 1, 0)
        )
        return (mask * (v / (1.0 + jnp.exp(-v)))).astype(jnp.bfloat16)

    for chunk in chunks(pairs):
        total = lax.dot_general(
            window(chunk),
            w_in_ref[...],
            (((0,), (0,)), ((), ())),
            preferred_element_type=jnp.float32,
        )
        mask_odd[at(chunk)] = total[:, 384:512]
        mask_even[at(chunk)] = total[:, 512:640]
        act_a[at(chunk)] = finish(total, total[:, 384:512])
    for chunk in chunks(pairs - 1):
        total = jnp.dot(both(act_a, chunk), w_mid_ref[...], preferred_element_type=jnp.float32)
        act_b[at(chunk)] = finish(total, mask_even[at(chunk)])
    for chunk in chunks(pairs - 2):
        total = jnp.dot(both(act_b, chunk), w_late_ref[...], preferred_element_type=jnp.float32)
        act_a[at(chunk)] = finish(total, mask_odd[at(chunk, stride)])
    results = []
    for chunk in chunks(pairs - 3):
        total = lax.dot_general(
            w_out_ref[...],
            both(act_a, chunk),
            (((1,), (1,)), ((), ())),
            preferred_element_type=jnp.float32,
        )
        results.append(
            pltpu.roll(total[0:16], 1, 1) + total[16:32] + pltpu.roll(total[32:48], COLS - 1, 1)
        )
    return results


def level_index():
    return lax.broadcasted_iota(jnp.int32, (LEV, COLS), 0).astype(jnp.float32)


def wetness(block):
    return (level_index() < block[KMT : KMT + 1]).astype(jnp.float32)


def first_input(block):
    wet = wetness(block)
    sea = jnp.where(level_index() == 0.0, wet, 0.0)
    return jnp.concatenate([wet * block[0:LEV], sea], axis=0).astype(jnp.bfloat16)


def advance(here, north, south, closure):
    wet = wetness(here)
    temp = here[0:LEV]
    tracer = wet * temp
    kappa = jnp.broadcast_to(here[KAPPA : KAPPA + 1], (LEV, COLS))
    diff = jnp.zeros((LEV, COLS), jnp.float32)
    for near in (south, north):
        near_w = wetness(near)
        diff = diff + near_w * 0.5 * (kappa + near[KAPPA : KAPPA + 1]) * (
            near_w * near[0:LEV] - tracer
        )
    for by in (COLS - 1, 1):
        diff = diff + pltpu.roll(wet, by, 1) * 0.5 * (kappa + pltpu.roll(kappa, by, 1)) * (
            pltpu.roll(tracer, by, 1) - tracer
        )
    diff = wet * diff
    eddy = wet * closure
    return wet * (temp + STEP * (diff + eddy))


def interior_kernel(*refs):
    rows_ref, cut_ref, slab_ref, raw, refs = refs[0], refs[1], refs[2], refs[3:10], refs[10:]
    out_ref, line_ref, near_ref, weights, tables = refs[0], refs[1], refs[2], refs[3:7], refs[7:13]
    refs = refs[13:]
    near_ref[...] = slab_ref[...]
    start, mask_odd, mask_even, act_a, act_b = refs
    fill_weights(*raw[:4], *weights)
    for index, table in enumerate(raw[4:]):
        tables[2 * index][...], tables[2 * index + 1][...] = halves(table[...])
    for row in range(TALL):
        start[row * FIELDS : (row + 1) * FIELDS] = first_input(rows_ref[row])
    results = closure_layers(
        lambda chunk: start[2 * FIELDS * chunk : 2 * FIELDS * (chunk + 2)],
        TALL // 2 - 1,
        COLS,
        weights,
        (act_a, act_b),
        (mask_odd, mask_even),
    )
    for pair, closure in enumerate(results):
        for parity in range(2):
            row = FIRST + 2 * pair + parity
            out_ref[2 * pair + parity] = advance(
                rows_ref[row],
                rows_ref[row - 1],
                rows_ref[row + 1],
                closure[LEV * parity : LEV * (parity + 1)],
            )
    own_line = lane_index((LEV, COLS)) == lax.axis_index("lon") + FIRST
    kept = jnp.sum(jnp.where(own_line, cut_ref[...], 0.0), axis=1, keepdims=True)
    line_ref[...] = jnp.broadcast_to(kept, (LEV, COLS))


STRIP = 32
PER = COLS // STRIP


def edge_kernel(
    rows_ref, far_ref, near_ref, inside_ref, w_in_ref, w_mid_ref, w_late_ref, w_out_ref,
    out_ref, strips, mask_odd, mask_even, act_a, act_b,
):
    lane = lane_index((FIELDS, COLS))
    even = lax.rem(lax.axis_index("lon"), 2) == 0
    parts = range(TALL // SLOTS)
    near = [near_ref[FIELDS * part : FIELDS * (part + 1)] for part in parts]
    from_west = [jnp.where(even, far_ref[part], near[part]) for part in parts]
    from_east = [jnp.where(even, near[part], far_ref[part]) for part in parts]
    for row in range(TALL):
        part, slot = row // SLOTS, row % SLOTS
        here = rows_ref[row]
        strip = jnp.where(lane < 24, pltpu.roll(from_east[part], (20 - HALO * slot) % COLS, 1) if slot != 5 else from_east[part], 0.0)
        strip = jnp.where(lane < 20, pltpu.roll(here, 20, 1), strip)
        strip = jnp.where(lane < 12, pltpu.roll(here, 4, 1), strip)
        west = pltpu.roll(from_west[part], COLS - HALO * slot, 1) if slot else from_west[part]
        strips[row] = jnp.where(lane < 4, west, strip)

    def side_by_side(parity, start):
        total = None
        for slot in range(PER):
            row = 2 * (start + slot) + parity
            if row >= TALL:
                continue
            piece = strips[row]
            piece = pltpu.roll(piece, STRIP * slot, 1) if slot else piece
            total = piece if total is None else total + piece
        return total

    def window(chunk):
        at = PER * chunk
        return jnp.concatenate(
            [
                first_input(block)
                for block in (
                    side_by_side(0, at),
                    side_by_side(1, at),
                    side_by_side(0, at + 1),
                    side_by_side(1, at + 1),
                )
            ],
            axis=0,
        )

    act_a[5 * COLS :] = jnp.zeros((COLS, COLS), jnp.bfloat16)
    act_b[5 * COLS :] = jnp.zeros((COLS, COLS), jnp.bfloat16)
    mask_odd[5 * COLS :] = jnp.zeros((COLS, COLS), jnp.float32)
    results = closure_layers(
        window,
        TALL // 2 - 1,
        STRIP,
        (w_in_ref, w_mid_ref, w_late_ref, w_out_ref),
        (act_a, act_b),
        (mask_odd, mask_even),
    )
    at_lane = lane_index((LEV, COLS))
    for chunk in range(4):
        at = PER * chunk + FIRST // 2
        closure = results[chunk]
        north = side_by_side(1, at - 1)
        upper = side_by_side(0, at)
        lower = side_by_side(1, at)
        south = side_by_side(0, at + 1)
        for parity, value in (
            (0, advance(upper, north, lower, closure[0:LEV])),
            (1, advance(lower, upper, south, closure[LEV : 2 * LEV])),
        ):
            for slot in range(PER):
                row = 2 * (PER * chunk + slot) + parity
                left = pltpu.roll(value, COLS - STRIP * slot - 4, 1)
                shift = (108 - STRIP * slot) % COLS
                right = pltpu.roll(value, shift, 1)
                out_ref[BLOCK * row : BLOCK * row + LEV] = jnp.where(
                    at_lane < HALO,
                    left,
                    jnp.where(at_lane >= COLS - HALO, right, inside_ref[row]),
                )
                out_ref[BLOCK * row + LEV : BLOCK * (row + 1)] = rows_ref[
                    FIRST + row, KMT : FORCING + 1, :
                ]


def filter_tables(blocks, width):
    length = blocks * width
    half = LEV // 2
    k = np.arange(blocks)
    outer = np.exp(-2j * np.pi * ((k[:, None] * k[None, :]) % blocks) / blocks)
    spread = np.zeros((2, half, blocks, 2, half, blocks))
    for line in range(half):
        spread[0, line, :, 0, line] = outer.real
        spread[0, line, :, 1, line] = -outer.imag
        spread[1, line, :, 0, line] = outer.imag
        spread[1, line, :, 1, line] = outer.real
    spread = spread.reshape(blocks * LEV, blocks * LEV)
    m = np.arange(width)
    twist = np.exp(-2j * np.pi * (k[:, None] * m[None, :]) / length)
    inner = np.exp(-2j * np.pi * ((m[:, None] * m[None, :]) % width) / width)
    inner = np.concatenate([inner.real, inner.imag], axis=1)
    return [
        np.asarray(t, np.float32)
        for t in (spread, spread.T / length, inner, twist.real, twist.imag)
    ]


def halves(x):
    high = x.astype(jnp.bfloat16)
    return high, (x - high.astype(jnp.float32)).astype(jnp.bfloat16)


def split_dot(a, b):
    def dot(x, y):
        return jnp.dot(x, y, preferred_element_type=jnp.float32)

    return dot(a[0], b[0]) + (dot(a[0], b[1]) + dot(a[1], b[0]))


def every(ref, row):
    return ref[pl.ds(row, ref.shape[0] // BLOCK, stride=BLOCK), :]


def solver_rows(levels, kmt, helm, forcing):
    mean = jnp.zeros(kmt.shape, jnp.float32)
    for level, plane in enumerate(levels):
        mean = mean + jnp.where(kmt > level, plane, 0.0)
    rhs = jnp.where(kmt > 0.0, mean * (1.0 / LEV) + forcing, 0.0)
    lane = lane_index(kmt.shape)
    ends = jnp.where(lane < 24, pltpu.roll(helm, 20, 1), 0.0)
    ends = jnp.where(lane < 16, pltpu.roll(kmt, 12, 1), ends)
    return rhs, jnp.where(lane < 8, pltpu.roll(rhs, 4, 1), ends)


def filter_kernel(
    x_ref, line_ref, spread_ref, spread_low, back_ref, back_low, inner_ref, inner_low,
    twist_re_ref, twist_im_ref, out_ref,
):
    blocks = x_ref.shape[0] // BLOCK
    length = blocks * COLS
    half = LEV // 2 * blocks
    shape = (half, COLS)
    inner = (inner_ref[...], inner_low[...])
    turn_re = jnp.concatenate([twist_re_ref[...]] * (LEV // 2), axis=0)
    turn_im = jnp.concatenate([twist_im_ref[...]] * (LEV // 2), axis=0)
    x = jnp.concatenate([every(x_ref, level) for level in range(LEV)], axis=0)
    y = split_dot((spread_ref[...], spread_low[...]), halves(x))
    re, im = y[:half], y[half:]
    re, im = re * turn_re - im * turn_im, im * turn_re + re * turn_im
    s = split_dot(halves(jnp.concatenate([re, im], axis=0)), inner)
    re, im = s[:half, :COLS] - s[half:, COLS:], s[half:, :COLS] + s[:half, COLS:]
    wave = lax.rem(lax.broadcasted_iota(jnp.int32, shape, 0), blocks) + blocks * lane_index(shape)
    folded = jnp.minimum(wave, length - wave).astype(jnp.float32)
    keep = folded < line_ref[0:1, :]
    re, im = jnp.where(keep, re, 0.0), jnp.where(keep, im, 0.0)
    s = split_dot(halves(jnp.concatenate([re, im], axis=0)), inner)
    re, im = s[:half, :COLS] + s[half:, COLS:], s[half:, :COLS] - s[:half, COLS:]
    re, im = re * turn_re + im * turn_im, im * turn_re - re * turn_im
    x = split_dot((back_ref[...], back_low[...]), halves(jnp.concatenate([re, im], axis=0)))
    levels = [x[blocks * level : blocks * (level + 1)] for level in range(LEV)]
    for level, plane in enumerate(levels):
        out_ref[pl.ds(level, blocks, stride=BLOCK), :] = plane
    rhs, ends = solver_rows(
        levels, every(x_ref, LEV), every(x_ref, LEV + 1), every(x_ref, LEV + 2)
    )
    shape = (blocks, COLS)
    even = lax.rem(lax.broadcasted_iota(jnp.int32, shape, 0), 2) == 0

    def ahead(plane, by):
        return pltpu.roll(plane, (blocks - by) % blocks, 0)

    border = jnp.where(
        lax.rem(lane_index(shape), 2 * HALO) < HALO,
        jnp.where(even, ahead(ends, -1), ahead(ends, -2)),
        jnp.where(even, ahead(ends, 2), ahead(ends, 1)),
    )
    out_ref[pl.ds(LEV, blocks, stride=BLOCK), :] = rhs
    out_ref[pl.ds(LEV + 1, blocks, stride=BLOCK), :] = jnp.where(
        even, ahead(rhs, 1), ahead(rhs, -1)
    )
    out_ref[pl.ds(LEV + 2, blocks, stride=BLOCK), :] = border


def ends_kernel(x_ref, rhs_ref, ends_ref):
    rhs_ref[...], ends_ref[...] = solver_rows(
        [every(x_ref, level) for level in range(LEV)],
        every(x_ref, LEV),
        every(x_ref, LEV + 1),
        every(x_ref, LEV + 2),
    )


def plain_kernel(x_ref, rhs_ref, far_ref, near_ref, out_ref):
    even = lax.rem(lax.axis_index("lon"), 2) == 0
    far = far_ref[...]
    peers = near_ref[MID:]
    west = lax.rem(lane_index((MID, COLS)), 2 * HALO) < HALO
    border = jnp.where(west, jnp.where(even, far, peers), jnp.where(even, peers, far))
    out_ref[...] = x_ref[...]
    out_ref[pl.ds(LEV, MID, stride=BLOCK), :] = rhs_ref[...]
    out_ref[pl.ds(LEV + 1, MID, stride=BLOCK), :] = near_ref[0:MID]
    out_ref[pl.ds(LEV + 2, MID, stride=BLOCK), :] = border


def two_sum(a, b):
    s = a + b
    t = s - a
    return s, (a - (s - t)) + (b - t)


def quick_sum(a, b):
    s = a + b
    return s, b - (s - a)


def split(a):
    c = a * 4097.0
    high = c - (c - a)
    return high, a - high


def two_product(a, b):
    p = a * b
    ah, al = split(a)
    bh, bl = split(b)
    return p, ((ah * bh - p) + ah * bl + al * bh) + al * bl


def pair_add(a, b):
    s, e = two_sum(a[0], b[0])
    return quick_sum(s, e + (a[1] + b[1]))


def pair_neg(a):
    return -a[0], -a[1]


def pair_mul(a, b):
    p, e = two_product(a[0], b[0])
    return quick_sum(p, e + (a[0] * b[1] + a[1] * b[0]))


def pair_inverse(a):
    x = 1.0 / a[0]
    p, e = two_product(a[0], x)
    return quick_sum(x, x * (((1.0 - p) - e) - a[1] * x))


def powers_kernel(x_ref, rows_ref, near_ref, temp_hbm, powers_ref, parts_ref, temp, sem):
    for level in range(LEV):
        temp[level] = x_ref[pl.ds(HALO * BLOCK + level, ROWS, stride=BLOCK), :]
    move = pltpu.make_async_copy(temp, temp_hbm, sem)
    move.start()
    even = lax.rem(lax.axis_index("lon"), 2) == 0
    lane = lane_index((LEV, COLS))
    plane_lane = lane_index((MID, COLS))
    border = every(x_ref, LEV + 2)

    def joined(own, peer, shift):
        first = pltpu.roll(jnp.where(even, own, peer), HALO, 1)
        second = pltpu.roll(jnp.where(even, peer, own), HALO, 1)
        ends = pltpu.roll(border, COLS - shift, 1) if shift else border
        tail = jnp.where(plane_lane < 2 * HALO, ends, 0.0)
        return jnp.concatenate(
            [
                jnp.where(plane_lane < HALO, ends, first),
                jnp.where(plane_lane < HALO, first, second),
                jnp.where(plane_lane < HALO, second, tail),
            ],
            axis=1,
        )

    rhs = joined(every(x_ref, LEV), every(x_ref, LEV + 1), 0)
    kmt = joined(rows_ref[FIRST : FIRST + MID, KMT, :], near_ref[ENDS : ENDS + MID], 8)
    helm = joined(rows_ref[FIRST : FIRST + MID, HELM, :], near_ref[ENDS + MID :], 16)
    sea = (kmt > 0.0).astype(jnp.float32)
    width = 3 * COLS

    def around(v):
        return (
            pltpu.roll(v, 1, 0)
            + pltpu.roll(v, MID - 1, 0)
            + pltpu.roll(v, 1, 1)
            + pltpu.roll(v, width - 1, 1)
        )

    diagonal = helm + sea * around(sea)
    powers = [rhs]
    for _ in range(ITERS):
        v = powers[-1]
        powers.append((diagonal * v - sea * around(v)) * 0.125)
    for index, v in enumerate(powers):
        tiles = [pltpu.roll(v[:, COLS * k : COLS * (k + 1)], COLS - HALO, 1) for k in range(3)]
        left = jnp.where(even, tiles[0], tiles[1])
        right = jnp.where(even, tiles[1], tiles[2])
        powers_ref[index] = jnp.where(plane_lane < COLS - HALO, left, right)
    row = lax.broadcasted_iota(jnp.int32, (MID, width), 0)
    column = lane_index((MID, width))
    own = (
        (row >= HALO) & (row < HALO + ROWS) & (column >= HALO) & (column < HALO + 2 * COLS)
    )
    owned = [jnp.where(own, v, 0.0) for v in powers]
    high_rows, low_rows = [], []
    for order in range(2 * ITERS):
        p, e = two_product(owned[order // 2], owned[order - order // 2])
        tiles = [
            (p[8 * i : 8 * i + 8, 128 * j : 128 * j + 128], e[8 * i : 8 * i + 8, 128 * j : 128 * j + 128])
            for i in range(MID // 8)
            for j in range(3)
        ]
        while len(tiles) > 1:
            tiles = [pair_add(a, b) for a, b in zip(tiles[::2], tiles[1::2])] + (
                tiles[-1:] if len(tiles) % 2 else []
            )
        total = tiles[0]
        for by in (4, 2, 1):
            total = pair_add(total, tuple(pltpu.roll(t, by, 0) for t in total))
        high_rows.append(total[0])
        low_rows.append(total[1])
    where = lax.broadcasted_iota(jnp.int32, (8, COLS), 0)
    high, low = high_rows[0], low_rows[0]
    for order in range(1, 2 * ITERS):
        high = jnp.where(where == order, high_rows[order], high)
        low = jnp.where(where == order, low_rows[order], low)
    total = (high, low)
    for by in (64, 32, 16, 8, 4, 2, 1):
        total = pair_add(total, tuple(pltpu.roll(t, by, 1) for t in total))
    spot = lax.broadcasted_iota(jnp.int32, (8, COLS), 0)
    message = jnp.where(lane == spot, total[0], 0.0) + jnp.where(lane == spot + 64, total[1], 0.0)
    message = jnp.sum(message, axis=0, keepdims=True)
    parts_ref[...] = jnp.broadcast_to(message, parts_ref.shape)
    move.wait()


def sum_messages(parts_ref):
    count = parts_ref.shape[0] // 8
    zero = jnp.zeros((8, COLS), jnp.float32)
    tiles = [(parts_ref[8 * i : 8 * i + 8, :], zero) for i in range(count)]
    while len(tiles) > 1:
        tiles = [pair_add(a, b) for a, b in zip(tiles[::2], tiles[1::2])]
    total = tiles[0]
    for by in (4, 2, 1):
        total = pair_add(total, tuple(pltpu.roll(t, by, 0) for t in total))
    return pair_add(total, tuple(pltpu.roll(t, 64, 1) for t in total))


def merge_kernel(parts_ref, out_ref):
    total = sum_messages(parts_ref)
    lane = lane_index((8, COLS))
    merged = jnp.where(lane < 64, total[0], total[1])
    out_ref[...] = jnp.broadcast_to(merged[:1], out_ref.shape)


def combine_kernel(parts_ref, powers_ref, surface_ref, residual_ref, wide):
    total = sum_messages(parts_ref)
    moments = [
        tuple(jnp.broadcast_to(t[:, order : order + 1], (8, COLS)) for t in total)
        for order in range(2 * ITERS)
    ]
    rho = list(moments)
    delta = list(moments)
    one = jnp.ones((8, COLS), jnp.float32)
    zero = jnp.zeros((8, COLS), jnp.float32)
    res = [one] + [zero] * ITERS
    way = [one] + [zero] * ITERS
    sol = [zero] * ITERS
    for step in range(ITERS):
        inverse = pair_inverse(delta[step + 1])
        alpha = pair_mul(rho[step], inverse)
        sol = [s + alpha[0] * w for s, w in zip(sol, way)]
        res = [res[0]] + [r - alpha[0] * w for r, w in zip(res[1:], way)]
        if step == ITERS - 1:
            break
        last = 2 * ITERS - 1 - step
        rho = [
            None if order <= step or order >= last
            else pair_add(rho[order], pair_neg(pair_mul(alpha, delta[order + 1])))
            for order in range(2 * ITERS)
        ]
        beta = pair_neg(pair_mul(rho[step + 1], inverse))
        delta = [
            None if order <= step or order >= last
            else pair_add(rho[order], pair_mul(beta, delta[order]))
            for order in range(2 * ITERS)
        ]
        way = [r + beta[0] * w for r, w in zip(res, way)]
    for weights, target, factor in ((sol, surface_ref, 0.125), (res, residual_ref, 1.0)):
        for i in range(MID // 8):
            spot = (slice(8 * i, 8 * i + 8), slice(None))
            value = weights[0] * powers_ref[(0,) + spot]
            for index in range(1, len(weights)):
                value = value + weights[index] * powers_ref[(index,) + spot]
            wide[spot] = value * factor
        target[...] = wide[HALO : HALO + ROWS]


def forward(axis, periodic):
    count = lax.axis_size(axis)
    pairs = [(i, i + 1) for i in range(count - 1)]
    return pairs + [(count - 1, 0)] if periodic else pairs


def backward(axis, periodic):
    return [(target, source) for source, target in forward(axis, periodic)]


def reduction_groups(lon, lat):
    inner, outer = {}, {}
    for i in range(lon):
        for j in range(lat):
            inner.setdefault((i // 4, i % 2), []).append(i * lat + j)
            outer.setdefault((i % 4, j), []).append(i * lat + j)
    return list(inner.values()), list(outer.values())


def swap_near():
    return [(i, i ^ 1) for i in range(lax.axis_size("lon"))]


def swap_far():
    count = lax.axis_size("lon")
    return [(i, (i + 1) % count if i % 2 else (i - 1) % count) for i in range(count)]


def body(temp, kmt, kappa, helm, forcing, cutoff, conv_in, conv_mid, conv_late, conv_out):
    f32 = jnp.float32
    shape = jax.ShapeDtypeStruct
    blocks = lax.axis_size("lon")
    bf16 = jnp.bfloat16
    vmem = pl.BlockSpec(memory_space=pltpu.VMEM)
    cutoff = cutoff.reshape(1, ROWS)
    fields = (temp, kmt, kappa, helm, forcing, cutoff)
    slab = shape((CUT + 1, DEEP, COLS), f32)
    top, bottom = pl.pallas_call(
        slab_kernel,
        out_shape=(slab, slab),
        in_specs=[pl.BlockSpec(memory_space=pltpu.HBM)] * 6,
        out_specs=(vmem, vmem),
        scratch_shapes=(
            pltpu.VMEM((ROWS, COLS), jnp.int32),
            pltpu.VMEM((1, ROWS), jnp.int32),
            pltpu.SemaphoreType.DMA((10,)),
        ),
        compiler_params=pltpu.CompilerParams(vmem_limit_bytes=VMEM_LIMIT),
    )(*(pltpu.with_memory_space_constraint(field, pltpu.HBM) for field in fields))
    north = lax.ppermute(bottom, "lat", forward("lat", False))
    south = lax.ppermute(top, "lat", backward("lat", False))
    tables = tuple(jnp.asarray(table) for table in filter_tables(blocks, COLS))
    sources = (jnp.transpose(conv_in, (0, 2, 1)), conv_mid, conv_late, conv_out) + tables
    own, *raw = fetching(
        rows_kernel,
        (shape((ROWS, FIELDS, COLS), f32),)
        + tuple(shape(source.shape, source.dtype) for source in sources),
        fields + sources,
        fields,
    )
    rows, to_far, to_near, cuts = call(
        pack_kernel,
        (
            shape((TALL, FIELDS, COLS), f32),
            shape((TALL // SLOTS, FIELDS, COLS), f32),
            shape((ENDS + 2 * MID, COLS), f32),
            shape((DEEP, COLS), f32),
        ),
    )(own, north, south)
    far = lax.ppermute(to_far, "lon", swap_far())

    outs = (
        shape((4 * FIELDS, 640), bf16),
        shape((256, 384), bf16),
        shape((256, 384), bf16),
        shape((48, 256), bf16),
    )
    outs = outs + tuple(shape(table.shape, bf16) for table in tables[:3] for _ in range(2))
    def closure_scratch(chunks):
        cells = chunks * COLS
        return (
            pltpu.VMEM((cells, 128), f32),
            pltpu.VMEM((cells, 128), f32),
            pltpu.VMEM((cells, 128), bf16),
            pltpu.VMEM((cells, 128), bf16),
        )

    block = shape((MID, LEV, COLS), f32)
    inside, line, to_near, *prepared = call(
        interior_kernel,
        (block, shape((LEV, COLS), f32), shape(to_near.shape, f32)) + outs,
        (pltpu.VMEM((TALL * FIELDS, COLS), bf16),) + closure_scratch(19),
        10**9,
    )(rows, cuts, to_near, *raw[:7])
    near = lax.ppermute(to_near, "lon", swap_near())
    weights, tables = prepared[:4], prepared[4:] + raw[7:]
    lines = call(
        edge_kernel,
        shape((BLOCK * MID, COLS), f32),
        (pltpu.VMEM((TALL, FIELDS, COLS), f32),) + closure_scratch(6),
    )(rows, far, near, inside, *weights)

    def regroup(block):
        block = block.reshape(BLOCK * blocks, 1, COLS)
        block = lax.all_to_all(block, "lon", split_axis=0, concat_axis=0, tiled=True)
        return block.reshape(BLOCK * blocks, COLS)

    def filtered_block(lines, line, tables):
        whole = regroup(lines)
        return regroup(
            call(filter_kernel, shape((BLOCK * blocks, COLS), f32))(whole, line, *tables)
        )

    def plain_block(lines, line, tables):
        plane = shape((MID, COLS), f32)
        rhs, ends = call(ends_kernel, (plane, plane))(lines)
        far = lax.ppermute(ends, "lon", swap_far())
        near = lax.ppermute(jnp.concatenate([rhs, far]), "lon", swap_near())
        return call(plain_kernel, shape((BLOCK * MID, COLS), f32))(lines, rhs, far, near)

    top_row = lax.axis_index("lat") * ROWS - HALO
    polar = (top_row < BAND) | (top_row + MID > ROWS * lax.axis_size("lat") - BAND)
    back = lax.cond(polar, filtered_block, plain_block, lines, line, tables)
    both = ("lon", "lat")
    inner, outer = reduction_groups(blocks, lax.axis_size("lat"))
    wide = len(inner[0])
    temp_new, powers, parts = pl.pallas_call(
        powers_kernel,
        out_shape=(
            shape((LEV, ROWS, COLS), f32),
            shape((ITERS + 1, MID, COLS), f32),
            shape((wide, COLS), f32),
        ),
        in_specs=[vmem] * 3,
        out_specs=(pl.BlockSpec(memory_space=pltpu.HBM), vmem, vmem),
        scratch_shapes=(pltpu.VMEM((LEV, ROWS, COLS), f32), pltpu.SemaphoreType.DMA),
        compiler_params=pltpu.CompilerParams(vmem_limit_bytes=VMEM_LIMIT),
    )(back, rows, near)
    parts = lax.all_to_all(
        parts, both, split_axis=0, concat_axis=0, tiled=True, axis_index_groups=inner
    )
    parts = call(merge_kernel, shape((len(outer[0]), COLS), f32))(parts)
    parts = lax.all_to_all(
        parts, both, split_axis=0, concat_axis=0, tiled=True, axis_index_groups=outer
    )
    surface, residual = call(
        combine_kernel,
        (shape((ROWS, COLS), f32), shape((ROWS, COLS), f32)),
        (pltpu.VMEM((MID, COLS), f32),),
    )(parts, powers)
    return temp_new, surface, residual


def solution(mesh):
    return jax.shard_map(
        body,
        mesh=mesh,
        in_specs=(
            P(None, "lat", "lon"),
            P("lat", "lon"),
            P("lat", "lon"),
            P("lat", "lon"),
            P("lat", "lon"),
            P("lat"),
            P(),
            P(),
            P(),
            P(),
        ),
        out_specs=(P(None, "lat", "lon"), P("lat", "lon"), P("lat", "lon")),
        check_vma=False,
    )
```

```python
import math

import jax
import jax.numpy as jnp
import numpy as np
from jax import lax
from jax.experimental import pallas as pl
from jax.experimental.pallas import tpu as pltpu
from jax.sharding import PartitionSpec as P

ITERS = 4
STEP = 0.25
LEV = 8
FIELDS = 16
KMT, HELM, FORCING, KAPPA, CUT = 8, 9, 10, 11, 12
BAND = 48
HALO = 4
DEEP = 8
ROWS = 24
COLS = 128
TALL = ROWS + 2 * DEEP
MID = ROWS + 2 * HALO
BLOCK = LEV + 3
RETURN = LEV + 4
FIRST = DEEP - HALO
SLOTS = 20
VMEM_LIMIT = 48 * 1024 * 1024


def call(kernel, outs, scratch=(), flops=None):
    spec = pl.BlockSpec(memory_space=pltpu.VMEM)
    return pl.pallas_call(
        kernel,
        out_shape=outs,
        out_specs=jax.tree.map(lambda _: spec, outs),
        scratch_shapes=scratch,
        compiler_params=pltpu.CompilerParams(vmem_limit_bytes=VMEM_LIMIT),
    )


def lane_index(shape):
    return lax.broadcasted_iota(jnp.int32, shape, len(shape) - 1)


def fetching(kernel, outs, sources, held, rest=(), scratch=(), flops=10**6):
    spec = pl.BlockSpec(memory_space=pltpu.VMEM)
    return pl.pallas_call(
        kernel,
        out_shape=outs,
        in_specs=[pl.BlockSpec(memory_space=pltpu.HBM)] * len(sources),
        out_specs=jax.tree.map(lambda _: spec, outs),
        scratch_shapes=tuple(pltpu.VMEM(source.shape, source.dtype) for source in held)
        + (pltpu.SemaphoreType.DMA((len(sources),)),),
        compiler_params=pltpu.CompilerParams(vmem_limit_bytes=VMEM_LIMIT),
        cost_estimate=pl.CostEstimate(flops=10**6, bytes_accessed=2 * 10**6, transcendentals=0),
    )(*(pltpu.with_memory_space_constraint(source, pltpu.HBM) for source in sources))


def slab_kernel(
    temp_hbm, kmt_hbm, kappa_hbm, helm_hbm, forcing_hbm, cutoff_hbm,
    top_ref, bottom_ref, kmt, cutoff, sems,
):
    pairs = [(kmt_hbm, kmt), (cutoff_hbm, cutoff)]
    for target, start in ((top_ref, 0), (bottom_ref, ROWS - DEEP)):
        rows = pl.ds(start, DEEP)
        pairs.append((temp_hbm.at[:, rows], target.at[pl.ds(0, LEV)]))
        for source, field in ((kappa_hbm, KAPPA), (helm_hbm, HELM), (forcing_hbm, FORCING)):
            pairs.append((source.at[rows], target.at[field]))
    moves = [
        pltpu.make_async_copy(source, target, sems.at[index])
        for index, (source, target) in enumerate(pairs)
    ]
    for move in moves:
        move.start()
    for move in moves:
        move.wait()
    for target, start in ((top_ref, 0), (bottom_ref, ROWS - DEEP)):
        target[KMT] = kmt[start : start + DEEP].astype(jnp.float32)
        target[CUT] = cutoff_lanes(cutoff)


def cutoff_lanes(cutoff_ref):
    line = cutoff_ref[...].astype(jnp.float32)
    line = jnp.concatenate([line, jnp.zeros((1, COLS - ROWS), jnp.float32)], axis=1)
    return jnp.broadcast_to(line, (DEEP, COLS))


def fetch(sources, targets, sems):
    moves = [
        pltpu.make_async_copy(source, target, sems.at[index])
        for index, (source, target) in enumerate(zip(sources, targets))
    ]
    for move in moves:
        move.start()
    return moves


def rows_kernel(*refs):
    sources, own_ref, raw, held, sems = refs[:15], refs[15], refs[16:25], refs[25:31], refs[31]
    moves = fetch(sources, tuple(held) + tuple(raw), sems)
    for move in moves[: len(held)]:
        move.wait()
    fill_rows(*held, own_ref)
    for move in moves[len(held) :]:
        move.wait()


def fill_rows(temp_ref, kmt_ref, kappa_ref, helm_ref, forcing_ref, cutoff_ref, own_ref):
    own_ref[:, CUT + 1 :, :] = jnp.zeros((ROWS, FIELDS - CUT - 1, COLS), jnp.float32)
    for level in range(LEV):
        own_ref[:, level, :] = temp_ref[level]
    own_ref[:, KMT, :] = kmt_ref[...].astype(jnp.float32)
    own_ref[:, KAPPA, :] = kappa_ref[...]
    own_ref[:, HELM, :] = helm_ref[...]
    own_ref[:, FORCING, :] = forcing_ref[...]
    own_ref[:, CUT, :] = jnp.broadcast_to(cutoff_lanes(cutoff_ref)[:1], (ROWS, COLS))


def fill_weights(
    first_ref, mid_ref, late_ref, last_ref, w_in_ref, w_mid_ref, w_late_ref, w_out_ref
):
    w_in_ref[...] = jnp.zeros(w_in_ref.shape, w_in_ref.dtype)
    width = mid_ref.shape[1]
    none = jnp.zeros((LEV, width), jnp.float32)
    for row in range(4):
        parts = []
        for tap in range(3):
            for parity in range(2):
                a = row - parity
                parts.append(first_ref[3 * a + tap].astype(jnp.float32) if 0 <= a < 3 else none)
        top = jnp.concatenate(parts, axis=1)
        marks = [jnp.ones((1, width), jnp.float32) if row == at else none[:1] for at in (1, 2, 2, 3)]
        marks = jnp.concatenate(marks, axis=1)
        block = jnp.concatenate(
            [
                jnp.concatenate([top, jnp.zeros((LEV, 4 * width), jnp.float32)], axis=1),
                jnp.concatenate(
                    [
                        jnp.concatenate([jnp.zeros((1, 6 * width), jnp.float32), marks], axis=1),
                        jnp.zeros((LEV - 1, 10 * width), jnp.float32),
                    ],
                    axis=0,
                ),
            ],
            axis=0,
        )
        w_in_ref[FIELDS * row : FIELDS * (row + 1)] = block.astype(jnp.bfloat16)

    def rows_of(ref, tap, parity):
        outs = ref.shape[1]
        blank = jnp.zeros((outs, width), jnp.float32)
        parts = []
        for row in range(4):
            a = row - parity
            parts.append(ref[3 * a + tap].astype(jnp.float32) if 0 <= a < 3 else blank)
        return jnp.concatenate(parts, axis=1)

    for ref, out_ref in ((mid_ref, w_mid_ref), (late_ref, w_late_ref)):
        for tap in range(3):
            both = jnp.concatenate([rows_of(ref, tap, 0), rows_of(ref, tap, 1)], axis=0)
            out_ref[:, 2 * width * tap : 2 * width * (tap + 1)] = both.T.astype(jnp.bfloat16)
    w_out_ref[...] = jnp.concatenate(
        [rows_of(last_ref, tap, parity) for tap in range(3) for parity in range(2)], axis=0
    ).astype(jnp.bfloat16)


def pack_kernel(own_ref, north_ref, south_ref, rows_ref, far_ref, near_ref, cut_ref):
    even = lax.rem(lax.axis_index("lon"), 2) == 0
    rows_ref[DEEP : DEEP + ROWS] = own_ref[...]
    for slab_ref, start in ((north_ref, 0), (south_ref, DEEP + ROWS)):
        rows = slice(start, start + DEEP)
        rows_ref[rows, CUT + 1 :, :] = jnp.zeros((DEEP, FIELDS - CUT - 1, COLS), jnp.float32)
        for field in range(CUT + 1):
            rows_ref[rows, field, :] = slab_ref[field]
    lane = lane_index((DEEP, COLS))
    north = pltpu.roll(north_ref[CUT], COLS - (ROWS - DEEP), 1)
    south = pltpu.roll(south_ref[CUT], DEEP + ROWS, 1)
    own = pltpu.roll(jnp.broadcast_to(own_ref[0, CUT : CUT + 1, :], (DEEP, COLS)), DEEP, 1)
    cut_ref[...] = jnp.where(lane < DEEP, north, jnp.where(lane < DEEP + ROWS, own, south))
    lane = lane_index((FIELDS, COLS))
    for part in range(TALL // SLOTS):
        first = jnp.zeros((FIELDS, COLS), jnp.float32)
        last = jnp.zeros((FIELDS, COLS), jnp.float32)
        for slot in range(SLOTS):
            here = rows_ref[part * SLOTS + slot]
            inside = (lane >= HALO * slot) & (lane < HALO * (slot + 1))
            first = jnp.where(inside, pltpu.roll(here, HALO * slot, 1) if slot else here, first)
            last = jnp.where(inside, pltpu.roll(here, HALO * (slot + 1), 1), last)
        far_ref[part] = jnp.where(even, first, last)
        near_ref[part] = jnp.where(even, last, first)


def closure_layers(window, pairs, stride, weights, acts, masks):
    w_in_ref, w_mid_ref, w_late_ref, w_out_ref = weights
    act_a, act_b = acts
    mask_odd, mask_even = masks

    def chunks(count):
        return range(-(-count * stride // COLS))

    def at(chunk, shift=0):
        return slice(COLS * chunk + shift, COLS * (chunk + 1) + shift)

    def both(act, chunk):
        return jnp.concatenate([act[at(chunk)], act[at(chunk, stride)]], axis=1)

    def finish(total, mask):
        v = (
            pltpu.roll(total[:, 0:128], 1, 0)
            + total[:, 128:256]
            + pltpu.roll(total[:, 256:384], COLS - 1, 0)
        )
        return (mask * (v / (1.0 + jnp.exp(-v)))).astype(jnp.bfloat16)

    for chunk in chunks(pairs):
        total = lax.dot_general(
            window(chunk),
            w_in_ref[...],
            (((0,), (0,)), ((), ())),
            preferred_element_type=jnp.float32,
        )
        mask_odd[at(chunk)] = total[:, 384:512]
        mask_even[at(chunk)] = total[:, 512:640]
        act_a[at(chunk)] = finish(total, total[:, 384:512])
    for chunk in chunks(pairs - 1):
        total = jnp.dot(both(act_a, chunk), w_mid_ref[...], preferred_element_type=jnp.float32)
        act_b[at(chunk)] = finish(total, mask_even[at(chunk)])
    for chunk in chunks(pairs - 2):
        total = jnp.dot(both(act_b, chunk), w_late_ref[...], preferred_element_type=jnp.float32)
        act_a[at(chunk)] = finish(total, mask_odd[at(chunk, stride)])
    results = []
    for chunk in chunks(pairs - 3):
        total = lax.dot_general(
            w_out_ref[...],
            both(act_a, chunk),
            (((1,), (1,)), ((), ())),
            preferred_element_type=jnp.float32,
        )
        results.append(
            pltpu.roll(total[0:16], 1, 1) + total[16:32] + pltpu.roll(total[32:48], COLS - 1, 1)
        )
    return results


def level_index():
    return lax.broadcasted_iota(jnp.int32, (LEV, COLS), 0).astype(jnp.float32)


def wetness(block):
    return (level_index() < block[KMT : KMT + 1]).astype(jnp.float32)


def first_input(block):
    wet = wetness(block)
    sea = jnp.where(level_index() == 0.0, wet, 0.0)
    return jnp.concatenate([wet * block[0:LEV], sea], axis=0).astype(jnp.bfloat16)


def advance(here, north, south, closure):
    wet = wetness(here)
    temp = here[0:LEV]
    tracer = wet * temp
    kappa = jnp.broadcast_to(here[KAPPA : KAPPA + 1], (LEV, COLS))
    diff = jnp.zeros((LEV, COLS), jnp.float32)
    for near in (south, north):
        near_w = wetness(near)
        diff = diff + near_w * 0.5 * (kappa + near[KAPPA : KAPPA + 1]) * (
            near_w * near[0:LEV] - tracer
        )
    for by in (COLS - 1, 1):
        diff = diff + pltpu.roll(wet, by, 1) * 0.5 * (kappa + pltpu.roll(kappa, by, 1)) * (
            pltpu.roll(tracer, by, 1) - tracer
        )
    diff = wet * diff
    eddy = wet * closure
    return wet * (temp + STEP * (diff + eddy))


def interior_kernel(*refs):
    rows_ref, cut_ref, raw, refs = refs[0], refs[1], refs[2:9], refs[9:]
    out_ref, line_ref, weights, tables, refs = refs[0], refs[1], refs[2:6], refs[6:12], refs[12:]
    start, mask_odd, mask_even, act_a, act_b = refs
    fill_weights(*raw[:4], *weights)
    for index, table in enumerate(raw[4:]):
        tables[2 * index][...], tables[2 * index + 1][...] = halves(table[...])
    for row in range(TALL):
        start[row * FIELDS : (row + 1) * FIELDS] = first_input(rows_ref[row])
    results = closure_layers(
        lambda chunk: start[2 * FIELDS * chunk : 2 * FIELDS * (chunk + 2)],
        TALL // 2 - 1,
        COLS,
        weights,
        (act_a, act_b),
        (mask_odd, mask_even),
    )
    for pair, closure in enumerate(results):
        for parity in range(2):
            row = FIRST + 2 * pair + parity
            out_ref[2 * pair + parity] = advance(
                rows_ref[row],
                rows_ref[row - 1],
                rows_ref[row + 1],
                closure[LEV * parity : LEV * (parity + 1)],
            )
    own_line = lane_index((LEV, COLS)) == lax.axis_index("lon") + FIRST
    kept = jnp.sum(jnp.where(own_line, cut_ref[...], 0.0), axis=1, keepdims=True)
    line_ref[...] = jnp.broadcast_to(kept, (LEV, COLS))


STRIP = 32
PER = COLS // STRIP


def edge_kernel(
    rows_ref, far_ref, near_ref, inside_ref, w_in_ref, w_mid_ref, w_late_ref, w_out_ref,
    out_ref, strips, mask_odd, mask_even, act_a, act_b,
):
    lane = lane_index((FIELDS, COLS))
    even = lax.rem(lax.axis_index("lon"), 2) == 0
    parts = range(TALL // SLOTS)
    from_west = [jnp.where(even, far_ref[part], near_ref[part]) for part in parts]
    from_east = [jnp.where(even, near_ref[part], far_ref[part]) for part in parts]
    for row in range(TALL):
        part, slot = row // SLOTS, row % SLOTS
        here = rows_ref[row]
        strip = jnp.where(lane < 24, pltpu.roll(from_east[part], (20 - HALO * slot) % COLS, 1) if slot != 5 else from_east[part], 0.0)
        strip = jnp.where(lane < 20, pltpu.roll(here, 20, 1), strip)
        strip = jnp.where(lane < 12, pltpu.roll(here, 4, 1), strip)
        west = pltpu.roll(from_west[part], COLS - HALO * slot, 1) if slot else from_west[part]
        strips[row] = jnp.where(lane < 4, west, strip)

    def side_by_side(parity, start):
        total = None
        for slot in range(PER):
            row = 2 * (start + slot) + parity
            if row >= TALL:
                continue
            piece = strips[row]
            piece = pltpu.roll(piece, STRIP * slot, 1) if slot else piece
            total = piece if total is None else total + piece
        return total

    def window(chunk):
        at = PER * chunk
        return jnp.concatenate(
            [
                first_input(block)
                for block in (
                    side_by_side(0, at),
                    side_by_side(1, at),
                    side_by_side(0, at + 1),
                    side_by_side(1, at + 1),
                )
            ],
            axis=0,
        )

    act_a[5 * COLS :] = jnp.zeros((COLS, COLS), jnp.bfloat16)
    act_b[5 * COLS :] = jnp.zeros((COLS, COLS), jnp.bfloat16)
    mask_odd[5 * COLS :] = jnp.zeros((COLS, COLS), jnp.float32)
    results = closure_layers(
        window,
        TALL // 2 - 1,
        STRIP,
        (w_in_ref, w_mid_ref, w_late_ref, w_out_ref),
        (act_a, act_b),
        (mask_odd, mask_even),
    )
    at_lane = lane_index((LEV, COLS))
    for chunk in range(4):
        at = PER * chunk + FIRST // 2
        closure = results[chunk]
        north = side_by_side(1, at - 1)
        upper = side_by_side(0, at)
        lower = side_by_side(1, at)
        south = side_by_side(0, at + 1)
        for parity, value in (
            (0, advance(upper, north, lower, closure[0:LEV])),
            (1, advance(lower, upper, south, closure[LEV : 2 * LEV])),
        ):
            for slot in range(PER):
                row = 2 * (PER * chunk + slot) + parity
                left = pltpu.roll(value, COLS - STRIP * slot - 4, 1)
                shift = (108 - STRIP * slot) % COLS
                right = pltpu.roll(value, shift, 1)
                out_ref[BLOCK * row : BLOCK * row + LEV] = jnp.where(
                    at_lane < HALO,
                    left,
                    jnp.where(at_lane >= COLS - HALO, right, inside_ref[row]),
                )
                out_ref[BLOCK * row + LEV : BLOCK * (row + 1)] = rows_ref[
                    FIRST + row, KMT : FORCING + 1, :
                ]


def filter_tables(blocks, width):
    length = blocks * width
    half = LEV // 2
    k = np.arange(blocks)
    outer = np.exp(-2j * np.pi * ((k[:, None] * k[None, :]) % blocks) / blocks)
    spread = np.zeros((2, half, blocks, 2, half, blocks))
    for line in range(half):
        spread[0, line, :, 0, line] = outer.real
        spread[0, line, :, 1, line] = -outer.imag
        spread[1, line, :, 0, line] = outer.imag
        spread[1, line, :, 1, line] = outer.real
    spread = spread.reshape(blocks * LEV, blocks * LEV)
    m = np.arange(width)
    twist = np.exp(-2j * np.pi * (k[:, None] * m[None, :]) / length)
    inner = np.exp(-2j * np.pi * ((m[:, None] * m[None, :]) % width) / width)
    inner = np.concatenate([inner.real, inner.imag], axis=1)
    return [
        np.asarray(t, np.float32)
        for t in (spread, spread.T / length, inner, twist.real, twist.imag)
    ]


def halves(x):
    high = x.astype(jnp.bfloat16)
    return high, (x - high.astype(jnp.float32)).astype(jnp.bfloat16)


def split_dot(a, b):
    def dot(x, y):
        return jnp.dot(x, y, preferred_element_type=jnp.float32)

    return dot(a[0], b[0]) + (dot(a[0], b[1]) + dot(a[1], b[0]))


def every(ref, row, size):
    return ref[pl.ds(row, ref.shape[0] // size, stride=size), :]


def put_every(ref, row, plane):
    ref[pl.ds(row, ref.shape[0] // RETURN, stride=RETURN), :] = plane


def solver_rows(x_ref, levels):
    kmt, helm, forcing = (every(x_ref, LEV + row, BLOCK) for row in range(3))
    mean = jnp.zeros(kmt.shape, jnp.float32)
    for level, plane in enumerate(levels):
        mean = mean + jnp.where(kmt > level, plane, 0.0)
    rhs = jnp.where(kmt > 0.0, mean * (1.0 / LEV) + forcing, 0.0)
    helm = jnp.where(kmt > 0.0, helm, 0.0)
    lane = lane_index(kmt.shape)
    ends = jnp.where(lane < 16, pltpu.roll(helm, 12, 1), 0.0)
    return rhs, helm, jnp.where(lane < 8, pltpu.roll(rhs, 4, 1), ends)


def filter_kernel(
    x_ref, line_ref, spread_ref, spread_low, back_ref, back_low, inner_ref, inner_low,
    twist_re_ref, twist_im_ref, out_ref,
):
    blocks = x_ref.shape[0] // BLOCK
    length = blocks * COLS
    half = LEV // 2 * blocks
    shape = (half, COLS)
    inner = (inner_ref[...], inner_low[...])
    turn_re = jnp.concatenate([twist_re_ref[...]] * (LEV // 2), axis=0)
    turn_im = jnp.concatenate([twist_im_ref[...]] * (LEV // 2), axis=0)
    x = jnp.concatenate([every(x_ref, level, BLOCK) for level in range(LEV)], axis=0)
    y = split_dot((spread_ref[...], spread_low[...]), halves(x))
    re, im = y[:half], y[half:]
    re, im = re * turn_re - im * turn_im, im * turn_re + re * turn_im
    s = split_dot(halves(jnp.concatenate([re, im], axis=0)), inner)
    re, im = s[:half, :COLS] - s[half:, COLS:], s[half:, :COLS] + s[:half, COLS:]
    wave = lax.rem(lax.broadcasted_iota(jnp.int32, shape, 0), blocks) + blocks * lane_index(shape)
    folded = jnp.minimum(wave, length - wave).astype(jnp.float32)
    keep = folded < line_ref[0:1, :]
    re, im = jnp.where(keep, re, 0.0), jnp.where(keep, im, 0.0)
    s = split_dot(halves(jnp.concatenate([re, im], axis=0)), inner)
    re, im = s[:half, :COLS] + s[half:, COLS:], s[half:, :COLS] - s[:half, COLS:]
    re, im = re * turn_re + im * turn_im, im * turn_re - re * turn_im
    x = split_dot((back_ref[...], back_low[...]), halves(jnp.concatenate([re, im], axis=0)))
    levels = [x[blocks * level : blocks * (level + 1)] for level in range(LEV)]
    for level, plane in enumerate(levels):
        put_every(out_ref, level, plane)
    rhs, helm, ends = solver_rows(x_ref, levels)
    shape = (blocks, COLS)
    even = lax.rem(lax.broadcasted_iota(jnp.int32, shape, 0), 2) == 0

    def ahead(plane, by):
        return pltpu.roll(plane, (blocks - by) % blocks, 0)

    border = jnp.where(
        lax.rem(lane_index(shape), 2 * HALO) < HALO,
        jnp.where(even, ahead(ends, -1), ahead(ends, -2)),
        jnp.where(even, ahead(ends, 2), ahead(ends, 1)),
    )
    put_every(out_ref, LEV, rhs)
    put_every(out_ref, LEV + 1, jnp.where(even, ahead(rhs, 1), ahead(rhs, -1)))
    put_every(out_ref, LEV + 2, jnp.where(even, ahead(helm, 1), ahead(helm, -1)))
    put_every(out_ref, LEV + 3, border)


def ends_kernel(x_ref, rhs_ref, helm_ref, ends_ref):
    levels = [every(x_ref, level, BLOCK) for level in range(LEV)]
    rhs_ref[...], helm_ref[...], ends_ref[...] = solver_rows(x_ref, levels)


def plain_kernel(x_ref, rhs_ref, far_ref, near_ref, out_ref):
    even = lax.rem(lax.axis_index("lon"), 2) == 0
    far = far_ref[...]
    peers = near_ref[2 * MID :]
    west = lax.rem(lane_index((MID, COLS)), 2 * HALO) < HALO
    border = jnp.where(west, jnp.where(even, far, peers), jnp.where(even, peers, far))
    for level in range(LEV):
        put_every(out_ref, level, every(x_ref, level, BLOCK))
    put_every(out_ref, LEV, rhs_ref[...])
    put_every(out_ref, LEV + 1, near_ref[0:MID])
    put_every(out_ref, LEV + 2, near_ref[MID : 2 * MID])
    put_every(out_ref, LEV + 3, border)


def two_sum(a, b):
    s = a + b
    t = s - a
    return s, (a - (s - t)) + (b - t)


def quick_sum(a, b):
    s = a + b
    return s, b - (s - a)


def split(a):
    c = a * 4097.0
    high = c - (c - a)
    return high, a - high


def two_product(a, b):
    p = a * b
    ah, al = split(a)
    bh, bl = split(b)
    return p, ((ah * bh - p) + ah * bl + al * bh) + al * bl


def pair_add(a, b):
    s, e = two_sum(a[0], b[0])
    return quick_sum(s, e + (a[1] + b[1]))


def pair_neg(a):
    return -a[0], -a[1]


def pair_mul(a, b):
    p, e = two_product(a[0], b[0])
    return quick_sum(p, e + (a[0] * b[1] + a[1] * b[0]))


def pair_inverse(a):
    x = 1.0 / a[0]
    p, e = two_product(a[0], x)
    return quick_sum(x, x * (((1.0 - p) - e) - a[1] * x))


def powers_kernel(x_ref, rows_ref, temp_hbm, powers_ref, parts_ref, temp, sem):
    for level in range(LEV):
        temp[level] = x_ref[pl.ds(HALO * RETURN + level, ROWS, stride=RETURN), :]
    move = pltpu.make_async_copy(temp, temp_hbm, sem)
    move.start()
    even = lax.rem(lax.axis_index("lon"), 2) == 0
    lane = lane_index((LEV, COLS))
    plane_lane = lane_index((MID, COLS))
    border = every(x_ref, LEV + 3, RETURN)

    def joined(own, peer, shift):
        first = pltpu.roll(jnp.where(even, own, peer), HALO, 1)
        second = pltpu.roll(jnp.where(even, peer, own), HALO, 1)
        ends = pltpu.roll(border, COLS - shift, 1) if shift else border
        tail = jnp.where(plane_lane < 2 * HALO, ends, 0.0)
        return jnp.concatenate(
            [
                jnp.where(plane_lane < HALO, ends, first),
                jnp.where(plane_lane < HALO, first, second),
                jnp.where(plane_lane < HALO, second, tail),
            ],
            axis=1,
        )

    rhs = joined(every(x_ref, LEV, RETURN), every(x_ref, LEV + 1, RETURN), 0)
    kmt, helm = (rows_ref[FIRST : FIRST + MID, field, :] for field in (KMT, HELM))
    helm = joined(jnp.where(kmt > 0.0, helm, 0.0), every(x_ref, LEV + 2, RETURN), 8)
    sea = (helm > 0.0).astype(jnp.float32)
    width = 3 * COLS

    def around(v):
        return (
            pltpu.roll(v, 1, 0)
            + pltpu.roll(v, MID - 1, 0)
            + pltpu.roll(v, 1, 1)
            + pltpu.roll(v, width - 1, 1)
        )

    diagonal = helm + sea * around(sea)
    powers = [rhs]
    for _ in range(ITERS):
        v = powers[-1]
        powers.append((diagonal * v - sea * around(v)) * 0.125)
    for index, v in enumerate(powers):
        tiles = [pltpu.roll(v[:, COLS * k : COLS * (k + 1)], COLS - HALO, 1) for k in range(3)]
        left = jnp.where(even, tiles[0], tiles[1])
        right = jnp.where(even, tiles[1], tiles[2])
        powers_ref[index] = jnp.where(plane_lane < COLS - HALO, left, right)
    row = lax.broadcasted_iota(jnp.int32, (MID, width), 0)
    column = lane_index((MID, width))
    own = (
        (row >= HALO) & (row < HALO + ROWS) & (column >= HALO) & (column < HALO + 2 * COLS)
    )
    owned = [jnp.where(own, v, 0.0) for v in powers]
    high_rows, low_rows = [], []
    for order in range(2 * ITERS):
        p, e = two_product(owned[order // 2], owned[order - order // 2])
        tiles = [
            (p[8 * i : 8 * i + 8, 128 * j : 128 * j + 128], e[8 * i : 8 * i + 8, 128 * j : 128 * j + 128])
            for i in range(MID // 8)
            for j in range(3)
        ]
        while len(tiles) > 1:
            tiles = [pair_add(a, b) for a, b in zip(tiles[::2], tiles[1::2])] + (
                tiles[-1:] if len(tiles) % 2 else []
            )
        total = tiles[0]
        for by in (4, 2, 1):
            total = pair_add(total, tuple(pltpu.roll(t, by, 0) for t in total))
        high_rows.append(total[0])
        low_rows.append(total[1])
    where = lax.broadcasted_iota(jnp.int32, (8, COLS), 0)
    high, low = high_rows[0], low_rows[0]
    for order in range(1, 2 * ITERS):
        high = jnp.where(where == order, high_rows[order], high)
        low = jnp.where(where == order, low_rows[order], low)
    total = (high, low)
    for by in (64, 32, 16, 8, 4, 2, 1):
        total = pair_add(total, tuple(pltpu.roll(t, by, 1) for t in total))
    spot = lax.broadcasted_iota(jnp.int32, (8, COLS), 0)
    message = jnp.where(lane == spot, total[0], 0.0) + jnp.where(lane == spot + 64, total[1], 0.0)
    message = jnp.sum(message, axis=0, keepdims=True)
    parts_ref[...] = jnp.broadcast_to(message, parts_ref.shape)
    move.wait()


def sum_messages(parts_ref):
    count = parts_ref.shape[0] // 8
    zero = jnp.zeros((8, COLS), jnp.float32)
    tiles = [(parts_ref[8 * i : 8 * i + 8, :], zero) for i in range(count)]
    while len(tiles) > 1:
        tiles = [pair_add(a, b) for a, b in zip(tiles[::2], tiles[1::2])]
    total = tiles[0]
    for by in (4, 2, 1):
        total = pair_add(total, tuple(pltpu.roll(t, by, 0) for t in total))
    return pair_add(total, tuple(pltpu.roll(t, 64, 1) for t in total))


def merge_kernel(parts_ref, out_ref):
    total = sum_messages(parts_ref)
    lane = lane_index((8, COLS))
    merged = jnp.where(lane < 64, total[0], total[1])
    out_ref[...] = jnp.broadcast_to(merged[:1], out_ref.shape)


def combine_kernel(parts_ref, powers_ref, surface_ref, residual_ref, wide):
    total = sum_messages(parts_ref)
    moments = [
        tuple(jnp.broadcast_to(t[:, order : order + 1], (8, COLS)) for t in total)
        for order in range(2 * ITERS)
    ]
    rho = list(moments)
    delta = list(moments)
    one = jnp.ones((8, COLS), jnp.float32)
    zero = jnp.zeros((8, COLS), jnp.float32)
    res = [one] + [zero] * ITERS
    way = [one] + [zero] * ITERS
    sol = [zero] * ITERS
    for step in range(ITERS):
        inverse = pair_inverse(delta[step + 1])
        alpha = pair_mul(rho[step], inverse)
        sol = [s + alpha[0] * w for s, w in zip(sol, way)]
        res = [res[0]] + [r - alpha[0] * w for r, w in zip(res[1:], way)]
        if step == ITERS - 1:
            break
        last = 2 * ITERS - 1 - step
        rho = [
            None if order <= step or order >= last
            else pair_add(rho[order], pair_neg(pair_mul(alpha, delta[order + 1])))
            for order in range(2 * ITERS)
        ]
        beta = pair_neg(pair_mul(rho[step + 1], inverse))
        delta = [
            None if order <= step or order >= last
            else pair_add(rho[order], pair_mul(beta, delta[order]))
            for order in range(2 * ITERS)
        ]
        way = [r + beta[0] * w for r, w in zip(res, way)]
    for weights, target, factor in ((sol, surface_ref, 0.125), (res, residual_ref, 1.0)):
        for i in range(MID // 8):
            spot = (slice(8 * i, 8 * i + 8), slice(None))
            value = weights[0] * powers_ref[(0,) + spot]
            for index in range(1, len(weights)):
                value = value + weights[index] * powers_ref[(index,) + spot]
            wide[spot] = value * factor
        target[...] = wide[HALO : HALO + ROWS]


def forward(axis, periodic):
    count = lax.axis_size(axis)
    pairs = [(i, i + 1) for i in range(count - 1)]
    return pairs + [(count - 1, 0)] if periodic else pairs


def backward(axis, periodic):
    return [(target, source) for source, target in forward(axis, periodic)]


def reduction_groups(lon, lat):
    inner, outer = {}, {}
    for i in range(lon):
        for j in range(lat):
            inner.setdefault((i // 4, i % 2), []).append(i * lat + j)
            outer.setdefault((i % 4, j), []).append(i * lat + j)
    return list(inner.values()), list(outer.values())


def swap_near():
    return [(i, i ^ 1) for i in range(lax.axis_size("lon"))]


def swap_far():
    count = lax.axis_size("lon")
    return [(i, (i + 1) % count if i % 2 else (i - 1) % count) for i in range(count)]


def body(temp, kmt, kappa, helm, forcing, cutoff, conv_in, conv_mid, conv_late, conv_out):
    f32 = jnp.float32
    shape = jax.ShapeDtypeStruct
    blocks = lax.axis_size("lon")
    bf16 = jnp.bfloat16
    vmem = pl.BlockSpec(memory_space=pltpu.VMEM)
    cutoff = cutoff.reshape(1, ROWS)
    fields = (temp, kmt, kappa, helm, forcing, cutoff)
    slab = shape((CUT + 1, DEEP, COLS), f32)
    top, bottom = pl.pallas_call(
        slab_kernel,
        out_shape=(slab, slab),
        in_specs=[pl.BlockSpec(memory_space=pltpu.HBM)] * 6,
        out_specs=(vmem, vmem),
        scratch_shapes=(
            pltpu.VMEM((ROWS, COLS), jnp.int32),
            pltpu.VMEM((1, ROWS), jnp.int32),
            pltpu.SemaphoreType.DMA((10,)),
        ),
        compiler_params=pltpu.CompilerParams(vmem_limit_bytes=VMEM_LIMIT),
    )(*(pltpu.with_memory_space_constraint(field, pltpu.HBM) for field in fields))
    north = lax.ppermute(bottom, "lat", forward("lat", False))
    south = lax.ppermute(top, "lat", backward("lat", False))
    tables = tuple(jnp.asarray(table) for table in filter_tables(blocks, COLS))
    sources = (jnp.transpose(conv_in, (0, 2, 1)), conv_mid, conv_late, conv_out) + tables
    own, *raw = fetching(
        rows_kernel,
        (shape((ROWS, FIELDS, COLS), f32),)
        + tuple(shape(source.shape, source.dtype) for source in sources),
        fields + sources,
        fields,
    )
    rows, to_far, to_near, cuts = call(
        pack_kernel,
        (
            shape((TALL, FIELDS, COLS), f32),
            shape((TALL // SLOTS, FIELDS, COLS), f32),
            shape((TALL // SLOTS, FIELDS, COLS), f32),
            shape((DEEP, COLS), f32),
        ),
    )(own, north, south)
    far = lax.ppermute(to_far, "lon", swap_far())
    near = lax.ppermute(to_near, "lon", swap_near())

    outs = (
        shape((4 * FIELDS, 640), bf16),
        shape((256, 384), bf16),
        shape((256, 384), bf16),
        shape((48, 256), bf16),
    )
    outs = outs + tuple(shape(table.shape, bf16) for table in tables[:3] for _ in range(2))
    def closure_scratch(chunks):
        cells = chunks * COLS
        return (
            pltpu.VMEM((cells, 128), f32),
            pltpu.VMEM((cells, 128), f32),
            pltpu.VMEM((cells, 128), bf16),
            pltpu.VMEM((cells, 128), bf16),
        )

    block = shape((MID, LEV, COLS), f32)
    inside, line, *prepared = call(
        interior_kernel,
        (block, shape((LEV, COLS), f32)) + outs,
        (pltpu.VMEM((TALL * FIELDS, COLS), bf16),) + closure_scratch(19),
        10**9,
    )(rows, cuts, *raw[:7])
    weights, tables = prepared[:4], prepared[4:] + raw[7:]
    lines = call(
        edge_kernel,
        shape((BLOCK * MID, COLS), f32),
        (pltpu.VMEM((TALL, FIELDS, COLS), f32),) + closure_scratch(6),
    )(rows, far, near, inside, *weights)

    def regroup(block):
        block = block.reshape(-1, 1, COLS)
        block = lax.all_to_all(block, "lon", split_axis=0, concat_axis=0, tiled=True)
        return block.reshape(-1, COLS)

    def filtered_block(lines, line, tables):
        whole = regroup(lines)
        return regroup(
            call(filter_kernel, shape((RETURN * blocks, COLS), f32))(whole, line, *tables)
        )

    def plain_block(lines, line, tables):
        plane = shape((MID, COLS), f32)
        rhs, helm, ends = call(ends_kernel, (plane, plane, plane))(lines)
        far = lax.ppermute(ends, "lon", swap_far())
        near = lax.ppermute(jnp.concatenate([rhs, helm, far]), "lon", swap_near())
        return call(plain_kernel, shape((RETURN * MID, COLS), f32))(lines, rhs, far, near)

    top_row = lax.axis_index("lat") * ROWS - HALO
    polar = (top_row < BAND) | (top_row + MID > ROWS * lax.axis_size("lat") - BAND)
    back = lax.cond(polar, filtered_block, plain_block, lines, line, tables)
    both = ("lon", "lat")
    inner, outer = reduction_groups(blocks, lax.axis_size("lat"))
    wide = len(inner[0])
    temp_new, powers, parts = pl.pallas_call(
        powers_kernel,
        out_shape=(
            shape((LEV, ROWS, COLS), f32),
            shape((ITERS + 1, MID, COLS), f32),
            shape((wide, COLS), f32),
        ),
        in_specs=[vmem] * 2,
        out_specs=(pl.BlockSpec(memory_space=pltpu.HBM), vmem, vmem),
        scratch_shapes=(pltpu.VMEM((LEV, ROWS, COLS), f32), pltpu.SemaphoreType.DMA),
        compiler_params=pltpu.CompilerParams(vmem_limit_bytes=VMEM_LIMIT),
    )(back, rows)
    parts = lax.all_to_all(
        parts, both, split_axis=0, concat_axis=0, tiled=True, axis_index_groups=inner
    )
    parts = call(merge_kernel, shape((len(outer[0]), COLS), f32))(parts)
    parts = lax.all_to_all(
        parts, both, split_axis=0, concat_axis=0, tiled=True, axis_index_groups=outer
    )
    surface, residual = call(
        combine_kernel,
        (shape((ROWS, COLS), f32), shape((ROWS, COLS), f32)),
        (pltpu.VMEM((MID, COLS), f32),),
    )(parts, powers)
    return temp_new, surface, residual


def solution(mesh):
    return jax.shard_map(
        body,
        mesh=mesh,
        in_specs=(
            P(None, "lat", "lon"),
            P("lat", "lon"),
            P("lat", "lon"),
            P("lat", "lon"),
            P("lat", "lon"),
            P("lat"),
            P(),
            P(),
            P(),
            P(),
        ),
        out_specs=(P(None, "lat", "lon"), P("lat", "lon"), P("lat", "lon")),
        check_vma=False,
    )
```

```python
import math

import jax
import jax.numpy as jnp
import numpy as np
from jax import lax
from jax.experimental import pallas as pl
from jax.experimental.pallas import tpu as pltpu
from jax.sharding import PartitionSpec as P

ITERS = 4
STEP = 0.25
LEV = 8
FIELDS = 16
KMT, KAPPA, HELM, FORCING, CUT = 8, 9, 10, 11, 12
BAND = 48
HALO = 4
DEEP = 8
ROWS = 24
COLS = 128
TALL = ROWS + 2 * DEEP
MID = ROWS + 2 * HALO
BLOCK = LEV + 1
SLOTS = 20
VMEM_LIMIT = 48 * 1024 * 1024


def call(kernel, outs, scratch=(), flops=None):
    spec = pl.BlockSpec(memory_space=pltpu.VMEM)
    return pl.pallas_call(
        kernel,
        out_shape=outs,
        out_specs=jax.tree.map(lambda _: spec, outs),
        scratch_shapes=scratch,
        compiler_params=pltpu.CompilerParams(vmem_limit_bytes=VMEM_LIMIT),
    )


def lane_index(shape):
    return lax.broadcasted_iota(jnp.int32, shape, len(shape) - 1)


def fetching(kernel, outs, sources, held, rest=(), scratch=(), flops=10**6):
    spec = pl.BlockSpec(memory_space=pltpu.VMEM)
    return pl.pallas_call(
        kernel,
        out_shape=outs,
        in_specs=[pl.BlockSpec(memory_space=pltpu.HBM)] * len(sources),
        out_specs=jax.tree.map(lambda _: spec, outs),
        scratch_shapes=tuple(pltpu.VMEM(source.shape, source.dtype) for source in held)
        + (pltpu.SemaphoreType.DMA((len(sources),)),),
        compiler_params=pltpu.CompilerParams(vmem_limit_bytes=VMEM_LIMIT),
        cost_estimate=pl.CostEstimate(flops=10**6, bytes_accessed=2 * 10**6, transcendentals=0),
    )(*(pltpu.with_memory_space_constraint(source, pltpu.HBM) for source in sources))


def even_row():
    return lax.rem(lax.axis_index("lat"), 2) == 0


def slab_kernel(
    temp_hbm, kmt_hbm, kappa_hbm, helm_hbm, forcing_hbm, cutoff_hbm,
    pair_ref, other_ref, kmt, cutoff, sems,
):
    last = jnp.where(even_row(), ROWS - DEEP, 0)
    slabs = [
        (target, pl.multiple_of(start, DEEP))
        for target, start in ((pair_ref, last), (other_ref, ROWS - DEEP - last))
    ]
    pairs = [(kmt_hbm, kmt), (cutoff_hbm, cutoff)]
    for target, start in slabs:
        rows = pl.ds(start, DEEP)
        pairs.append((temp_hbm.at[:, rows], target.at[pl.ds(0, LEV)]))
        for source, field in ((kappa_hbm, KAPPA), (helm_hbm, HELM), (forcing_hbm, FORCING)):
            pairs.append((source.at[rows], target.at[field]))
    moves = fetch(*zip(*pairs), sems)
    for move in moves:
        move.wait()
    for target, start in slabs:
        target[KMT] = kmt[pl.ds(start, DEEP), :].astype(jnp.float32)
        target[CUT] = cutoff_lanes(cutoff)


def cutoff_lanes(cutoff_ref):
    line = cutoff_ref[...].astype(jnp.float32)
    line = jnp.concatenate([line, jnp.zeros((1, COLS - ROWS), jnp.float32)], axis=1)
    return jnp.broadcast_to(line, (DEEP, COLS))


def fetch(sources, targets, sems):
    moves = [
        pltpu.make_async_copy(source, target, sems.at[index])
        for index, (source, target) in enumerate(zip(sources, targets))
    ]
    for move in moves:
        move.start()
    return moves


def rows_kernel(*refs):
    sources, own_ref, raw, held, sems = refs[:15], refs[15], refs[16:25], refs[25:31], refs[31]
    moves = fetch(sources, tuple(held) + tuple(raw), sems)
    for move in moves[: len(held)]:
        move.wait()
    fill_rows(*held, own_ref)
    for move in moves[len(held) :]:
        move.wait()


def fill_rows(temp_ref, kmt_ref, kappa_ref, helm_ref, forcing_ref, cutoff_ref, own_ref):
    own_ref[:, CUT + 1 :, :] = jnp.zeros((ROWS, FIELDS - CUT - 1, COLS), jnp.float32)
    for level in range(LEV):
        own_ref[:, level, :] = temp_ref[level]
    own_ref[:, KMT, :] = kmt_ref[...].astype(jnp.float32)
    own_ref[:, KAPPA, :] = kappa_ref[...]
    own_ref[:, HELM, :] = helm_ref[...]
    own_ref[:, FORCING, :] = forcing_ref[...]
    own_ref[:, CUT, :] = jnp.broadcast_to(cutoff_lanes(cutoff_ref)[:1], (ROWS, COLS))


def fill_weights(
    first_ref, mid_ref, late_ref, last_ref, w_in_ref, w_mid_ref, w_late_ref, w_out_ref
):
    w_in_ref[...] = jnp.zeros(w_in_ref.shape, w_in_ref.dtype)
    width = mid_ref.shape[1]
    none = jnp.zeros((LEV, width), jnp.float32)
    for row in range(4):
        parts = []
        for tap in range(3):
            for parity in range(2):
                a = row - parity
                parts.append(first_ref[3 * a + tap].astype(jnp.float32) if 0 <= a < 3 else none)
        top = jnp.concatenate(parts, axis=1)
        marks = [jnp.ones((1, width), jnp.float32) if row == at else none[:1] for at in (1, 2, 2, 3)]
        marks = jnp.concatenate(marks, axis=1)
        block = jnp.concatenate(
            [
                jnp.concatenate([top, jnp.zeros((LEV, 4 * width), jnp.float32)], axis=1),
                jnp.concatenate(
                    [
                        jnp.concatenate([jnp.zeros((1, 6 * width), jnp.float32), marks], axis=1),
                        jnp.zeros((LEV - 1, 10 * width), jnp.float32),
                    ],
                    axis=0,
                ),
            ],
            axis=0,
        )
        w_in_ref[FIELDS * row : FIELDS * (row + 1)] = block.astype(jnp.bfloat16)

    def rows_of(ref, tap, parity):
        outs = ref.shape[1]
        blank = jnp.zeros((outs, width), jnp.float32)
        parts = []
        for row in range(4):
            a = row - parity
            parts.append(ref[3 * a + tap].astype(jnp.float32) if 0 <= a < 3 else blank)
        return jnp.concatenate(parts, axis=1)

    for ref, out_ref in ((mid_ref, w_mid_ref), (late_ref, w_late_ref)):
        for tap in range(3):
            both = jnp.concatenate([rows_of(ref, tap, 0), rows_of(ref, tap, 1)], axis=0)
            out_ref[:, 2 * width * tap : 2 * width * (tap + 1)] = both.T.astype(jnp.bfloat16)
    w_out_ref[...] = jnp.concatenate(
        [rows_of(last_ref, tap, parity) for tap in range(3) for parity in range(2)], axis=0
    ).astype(jnp.bfloat16)


def pack_kernel(own_ref, pair_ref, other_ref, rows_ref, far_ref, near_ref, cut_ref):
    north = [jnp.where(even_row(), other_ref[k], pair_ref[k]) for k in range(CUT + 1)]
    south = [jnp.where(even_row(), pair_ref[k], other_ref[k]) for k in range(CUT + 1)]
    even = lax.rem(lax.axis_index("lon"), 2) == 0
    rows_ref[DEEP : DEEP + ROWS] = own_ref[...]
    for slab, start in ((north, 0), (south, DEEP + ROWS)):
        rows = slice(start, start + DEEP)
        rows_ref[rows, CUT + 1 :, :] = jnp.zeros((DEEP, FIELDS - CUT - 1, COLS), jnp.float32)
        for field in range(CUT + 1):
            rows_ref[rows, field, :] = slab[field]
    lane = lane_index((DEEP, COLS))
    north = pltpu.roll(north[CUT], COLS - (ROWS - DEEP), 1)
    south = pltpu.roll(south[CUT], DEEP + ROWS, 1)
    own = pltpu.roll(jnp.broadcast_to(own_ref[0, CUT : CUT + 1, :], (DEEP, COLS)), DEEP, 1)
    cut_ref[...] = jnp.where(lane < DEEP, north, jnp.where(lane < DEEP + ROWS, own, south))
    lane = lane_index((FIELDS, COLS))
    for part in range(TALL // SLOTS):
        first = jnp.zeros((FIELDS, COLS), jnp.float32)
        last = jnp.zeros((FIELDS, COLS), jnp.float32)
        for slot in range(SLOTS):
            here = rows_ref[part * SLOTS + slot]
            inside = (lane >= HALO * slot) & (lane < HALO * (slot + 1))
            first = jnp.where(inside, pltpu.roll(here, HALO * slot, 1) if slot else here, first)
            last = jnp.where(inside, pltpu.roll(here, HALO * (slot + 1), 1), last)
        far_ref[part] = jnp.where(even, first, last)
        near_ref[part] = jnp.where(even, last, first)


def closure_layers(window, pairs, stride, weights, acts, masks):
    w_in_ref, w_mid_ref, w_late_ref, w_out_ref = weights
    act_a, act_b = acts
    mask_odd, mask_even = masks

    def chunks(count):
        return range(-(-count * stride // COLS))

    def at(chunk, shift=0):
        return slice(COLS * chunk + shift, COLS * (chunk + 1) + shift)

    def both(act, chunk):
        return jnp.concatenate([act[at(chunk)], act[at(chunk, stride)]], axis=1)

    def finish(total, mask):
        v = (
            pltpu.roll(total[:, 0:128], 1, 0)
            + total[:, 128:256]
            + pltpu.roll(total[:, 256:384], COLS - 1, 0)
        )
        return (mask * (v / (1.0 + jnp.exp(-v)))).astype(jnp.bfloat16)

    for chunk in chunks(pairs):
        total = lax.dot_general(
            window(chunk),
            w_in_ref[...],
            (((0,), (0,)), ((), ())),
            preferred_element_type=jnp.float32,
        )
        mask_odd[at(chunk)] = total[:, 384:512]
        mask_even[at(chunk)] = total[:, 512:640]
        act_a[at(chunk)] = finish(total, total[:, 384:512])
    for chunk in chunks(pairs - 1):
        total = jnp.dot(both(act_a, chunk), w_mid_ref[...], preferred_element_type=jnp.float32)
        act_b[at(chunk)] = finish(total, mask_even[at(chunk)])
    for chunk in chunks(pairs - 2):
        total = jnp.dot(both(act_b, chunk), w_late_ref[...], preferred_element_type=jnp.float32)
        act_a[at(chunk)] = finish(total, mask_odd[at(chunk, stride)])
    results = []
    for chunk in chunks(pairs - 3):
        total = lax.dot_general(
            w_out_ref[...],
            both(act_a, chunk),
            (((1,), (1,)), ((), ())),
            preferred_element_type=jnp.float32,
        )
        results.append(
            pltpu.roll(total[0:16], 1, 1) + total[16:32] + pltpu.roll(total[32:48], COLS - 1, 1)
        )
    return results


def level_index():
    return lax.broadcasted_iota(jnp.int32, (LEV, COLS), 0).astype(jnp.float32)


def wetness(block):
    return (level_index() < block[KMT : KMT + 1]).astype(jnp.float32)


def first_input(block):
    wet = wetness(block)
    sea = jnp.where(level_index() == 0.0, wet, 0.0)
    return jnp.concatenate([wet * block[0:LEV], sea], axis=0).astype(jnp.bfloat16)


def advance(here, north, south, closure):
    wet = wetness(here)
    temp = here[0:LEV]
    tracer = wet * temp
    kappa = jnp.broadcast_to(here[KAPPA : KAPPA + 1], (LEV, COLS))
    diff = jnp.zeros((LEV, COLS), jnp.float32)
    for near in (south, north):
        near_w = wetness(near)
        diff = diff + near_w * 0.5 * (kappa + near[KAPPA : KAPPA + 1]) * (
            near_w * near[0:LEV] - tracer
        )
    for by in (COLS - 1, 1):
        diff = diff + pltpu.roll(wet, by, 1) * 0.5 * (kappa + pltpu.roll(kappa, by, 1)) * (
            pltpu.roll(tracer, by, 1) - tracer
        )
    diff = wet * diff
    eddy = wet * closure
    return wet * (temp + STEP * (diff + eddy))


FIRST = DEEP - HALO


def interior_kernel(*refs):
    rows_ref, cut_ref, raw, refs = refs[0], refs[1], refs[2:9], refs[9:]
    out_ref, line_ref, strips_ref, refs = refs[0], refs[1], refs[2], refs[3:]
    weights, tables, refs = refs[:4], refs[4:10], refs[10:]
    start, mask_odd, mask_even, act_a, act_b = refs
    fill_weights(*raw[:4], *weights)
    for index, table in enumerate(raw[4:]):
        tables[2 * index][...], tables[2 * index + 1][...] = halves(table[...])
    lane = lane_index((FIELDS, COLS))
    for row in range(TALL):
        here = rows_ref[row]
        start[row * FIELDS : (row + 1) * FIELDS] = first_input(here)
        strip = jnp.where(lane < 12, pltpu.roll(here, 4, 1), pltpu.roll(here, 20, 1))
        strips_ref[row] = jnp.where((lane >= 4) & (lane < 20), strip, 0.0)
    results = closure_layers(
        lambda chunk: start[2 * FIELDS * chunk : 2 * FIELDS * (chunk + 2)],
        TALL // 2 - 1,
        COLS,
        weights,
        (act_a, act_b),
        (mask_odd, mask_even),
    )
    for pair, closure in enumerate(results):
        for parity in range(2):
            row = FIRST + 2 * pair + parity
            out_ref[2 * pair + parity] = advance(
                rows_ref[row],
                rows_ref[row - 1],
                rows_ref[row + 1],
                closure[LEV * parity : LEV * (parity + 1)],
            )
    own_line = lane_index((LEV, COLS)) == lax.axis_index("lon") + FIRST
    kept = jnp.sum(jnp.where(own_line, cut_ref[...], 0.0), axis=1, keepdims=True)
    line_ref[...] = jnp.broadcast_to(kept, (LEV, COLS))


STRIP = 32
PER = COLS // STRIP


def edge_kernel(
    rows_ref, far_ref, near_ref, inside_ref, own_ref, w_in_ref, w_mid_ref, w_late_ref, w_out_ref,
    out_ref, planes_ref, strips, mask_odd, mask_even, act_a, act_b,
):
    lane = lane_index((FIELDS, COLS))
    even = lax.rem(lax.axis_index("lon"), 2) == 0
    parts = range(TALL // SLOTS)
    from_west = [jnp.where(even, far_ref[part], near_ref[part]) for part in parts]
    from_east = [jnp.where(even, near_ref[part], far_ref[part]) for part in parts]
    for row in range(TALL):
        part, slot = row // SLOTS, row % SLOTS
        west, east = from_west[part], from_east[part]
        west = pltpu.roll(west, COLS - HALO * slot, 1) if slot else west
        east = pltpu.roll(east, (20 - HALO * slot) % COLS, 1) if slot != 5 else east
        strip = jnp.where((lane >= 20) & (lane < 24), east, own_ref[row])
        strips[row] = jnp.where(lane < 4, west, strip)

    def side_by_side(parity, start):
        total = None
        for slot in range(PER):
            row = 2 * (start + slot) + parity
            if row >= TALL:
                continue
            piece = strips[row]
            piece = pltpu.roll(piece, STRIP * slot, 1) if slot else piece
            total = piece if total is None else total + piece
        return total

    def window(chunk):
        at = PER * chunk
        return jnp.concatenate(
            [
                first_input(block)
                for block in (
                    side_by_side(0, at),
                    side_by_side(1, at),
                    side_by_side(0, at + 1),
                    side_by_side(1, at + 1),
                )
            ],
            axis=0,
        )

    act_a[5 * COLS :] = jnp.zeros((COLS, COLS), jnp.bfloat16)
    act_b[5 * COLS :] = jnp.zeros((COLS, COLS), jnp.bfloat16)
    mask_odd[5 * COLS :] = jnp.zeros((COLS, COLS), jnp.float32)
    results = closure_layers(
        window,
        TALL // 2 - 1,
        STRIP,
        (w_in_ref, w_mid_ref, w_late_ref, w_out_ref),
        (act_a, act_b),
        (mask_odd, mask_even),
    )
    at_lane = lane_index((LEV, COLS))
    for chunk in range(4):
        at = PER * chunk + FIRST // 2
        closure = results[chunk]
        north = side_by_side(1, at - 1)
        upper = side_by_side(0, at)
        lower = side_by_side(1, at)
        south = side_by_side(0, at + 1)
        for parity, value in (
            (0, advance(upper, north, lower, closure[0:LEV])),
            (1, advance(lower, upper, south, closure[LEV : 2 * LEV])),
        ):
            for slot in range(PER):
                row = 2 * (PER * chunk + slot) + parity
                left = pltpu.roll(value, COLS - STRIP * slot - 4, 1)
                shift = (108 - STRIP * slot) % COLS
                right = pltpu.roll(value, shift, 1)
                out_ref[row] = jnp.where(
                    at_lane < HALO,
                    left,
                    jnp.where(at_lane >= COLS - HALO, right, inside_ref[row]),
                )
    plane_lane = lane_index((MID, COLS))
    for index, field in enumerate((KMT, HELM, FORCING)):
        moved = pltpu.roll(rows_ref[FIRST : FIRST + MID, field, :], HALO, 1)
        edge = strips[FIRST : FIRST + MID, field, :]
        planes_ref[index, :, 0:COLS] = jnp.where(plane_lane < HALO, edge, moved)
        planes_ref[index, :, COLS:] = jnp.where(
            plane_lane < HALO,
            moved,
            jnp.where(plane_lane < 2 * HALO, pltpu.roll(edge, COLS - 16, 1), 0.0),
        )


def filter_tables(blocks, width):
    length = blocks * width
    half = LEV // 2
    k = np.arange(blocks)
    outer = np.exp(-2j * np.pi * ((k[:, None] * k[None, :]) % blocks) / blocks)
    spread = np.zeros((blocks, 2, half, blocks, 2, half))
    for line in range(half):
        spread[:, 0, line, :, 0, line] = outer.real
        spread[:, 0, line, :, 1, line] = -outer.imag
        spread[:, 1, line, :, 0, line] = outer.imag
        spread[:, 1, line, :, 1, line] = outer.real
    spread = spread.reshape(blocks * LEV, blocks * LEV)
    m = np.arange(width)
    twist = np.exp(-2j * np.pi * (k[:, None] * m[None, :]) / length)
    sign = np.where(np.arange(LEV) < half, -1.0, 1.0)[None, :, None]
    twist_re = np.broadcast_to(twist.real[:, None, :], (blocks, LEV, width))
    twist_im = twist.imag[:, None, :] * sign
    inner = np.exp(-2j * np.pi * ((m[:, None] * m[None, :]) % width) / width)
    inner = np.concatenate([inner.real, inner.imag], axis=1)
    return [
        np.asarray(t, np.float32)
        for t in (spread, spread.T / length, inner, twist_re, twist_im)
    ]


def halves(x):
    high = x.astype(jnp.bfloat16)
    return high, (x - high.astype(jnp.float32)).astype(jnp.bfloat16)


def split_dot(a, b):
    def dot(x, y):
        return jnp.dot(x, y, preferred_element_type=jnp.float32)

    return dot(a[0], b[0]) + (dot(a[0], b[1]) + dot(a[1], b[0]))


def filter_kernel(
    x_ref, line_ref, spread_ref, spread_low, back_ref, back_low, inner_ref, inner_low,
    twist_re_ref, twist_im_ref, out_ref,
):
    blocks, lev, width = x_ref.shape
    shape = (blocks, lev, width)
    flat = (blocks * lev, width)
    length = blocks * width
    inner = (inner_ref[...], inner_low[...])

    def partner(block):
        return pltpu.roll(block, lev // 2, 1)

    sign = jnp.where(lax.broadcasted_iota(jnp.int32, shape, 1) < lev // 2, -1.0, 1.0)
    y = split_dot((spread_ref[...], spread_low[...]), halves(x_ref[...].reshape(flat)))
    y = y.reshape(shape)
    y = y * twist_re_ref[...] + partner(y) * twist_im_ref[...]
    s = split_dot(halves(y.reshape(flat)), inner)
    s = s[:, 0:width].reshape(shape) + partner(s[:, width:].reshape(shape)) * sign
    wave = lax.broadcasted_iota(jnp.int32, shape, 0) + blocks * lane_index(shape)
    folded = jnp.minimum(wave, length - wave).astype(jnp.float32)
    s = jnp.where(folded < line_ref[0:1, :][None], s, 0.0)
    y = split_dot(halves(s.reshape(flat)), inner)
    y = y[:, 0:width].reshape(shape) - partner(y[:, width:].reshape(shape)) * sign
    y = y * twist_re_ref[...] - partner(y) * twist_im_ref[...]
    x = split_dot((back_ref[...], back_low[...]), halves(y.reshape(flat))).reshape(shape)
    lane = lane_index((lev, width))
    moved = [pltpu.roll(x[block], HALO, 1) for block in range(blocks)]
    for block in range(blocks):
        edge = jnp.where(lane < HALO, moved[block - 1], moved[(block + 1) % blocks])
        edge = jnp.where(lane < 2 * HALO, edge, 0.0)
        edge = pltpu.roll(edge, 0, 1, stride=2 * HALO, stride_axis=0)
        row = BLOCK * block
        out_ref[row : row + lev, :] = x[block]
        out_ref[row + lev : row + BLOCK, :] = jnp.sum(edge, axis=0, keepdims=True)


def ends_kernel(x_ref, far_ref, near_ref):
    even = lax.rem(lax.axis_index("lon"), 2) == 0
    lane = lane_index((LEV, COLS))
    packed = []
    for row in range(MID):
        edge = jnp.where(lane < 2 * HALO, pltpu.roll(x_ref[row], HALO, 1), 0.0)
        edge = pltpu.roll(edge, 0, 1, stride=2 * HALO, stride_axis=0)
        packed.append(jnp.sum(edge, axis=0, keepdims=True))
    packed = jnp.concatenate(packed, axis=0)
    to_east = lax.rem(lane_index((MID, COLS)), 2 * HALO) < HALO
    last = jnp.where(to_east, packed, 0.0)
    first = jnp.where(to_east, 0.0, packed)
    far_ref[...] = jnp.where(even, first, last)
    near_ref[...] = jnp.where(even, last, first)


def plain_kernel(x_ref, far_ref, near_ref, out_ref):
    edge = far_ref[...] + near_ref[...]
    for row in range(MID):
        out_ref[BLOCK * row : BLOCK * row + LEV, :] = x_ref[row]
        out_ref[BLOCK * row + LEV : BLOCK * (row + 1), :] = edge[row : row + 1]


def two_sum(a, b):
    s = a + b
    t = s - a
    return s, (a - (s - t)) + (b - t)


def quick_sum(a, b):
    s = a + b
    return s, b - (s - a)


def split(a):
    c = a * 4097.0
    high = c - (c - a)
    return high, a - high


def two_product(a, b):
    p = a * b
    ah, al = split(a)
    bh, bl = split(b)
    return p, ((ah * bh - p) + ah * bl + al * bh) + al * bl


def pair_add(a, b):
    s, e = two_sum(a[0], b[0])
    return quick_sum(s, e + (a[1] + b[1]))


def pair_neg(a):
    return -a[0], -a[1]


def pair_mul(a, b):
    p, e = two_product(a[0], b[0])
    return quick_sum(p, e + (a[0] * b[1] + a[1] * b[0]))


def pair_inverse(a):
    x = 1.0 / a[0]
    p, e = two_product(a[0], x)
    return quick_sum(x, x * (((1.0 - p) - e) - a[1] * x))


def powers_kernel(x_ref, planes_ref, temp_hbm, powers_ref, parts_ref, temp, sem):
    for level in range(LEV):
        temp[level] = x_ref[pl.ds(HALO * BLOCK + level, ROWS, stride=BLOCK), :]
    move = pltpu.make_async_copy(temp, temp_hbm, sem)
    move.start()
    lane = lane_index((LEV, COLS))
    wide_lane = lane_index((MID, COLS))
    kmt_left = planes_ref[0, :, 0:COLS]
    kmt_right = planes_ref[0, :, COLS:]
    kmt = pltpu.roll(jnp.where(wide_lane < HALO, kmt_right, kmt_left), COLS - HALO, 1)
    mean = jnp.zeros((MID, COLS), jnp.float32)
    for level in range(LEV):
        here = x_ref[pl.ds(level, MID, stride=BLOCK), :]
        mean = mean + jnp.where(kmt > level, here, 0.0)
    edge = x_ref[pl.ds(LEV, MID, stride=BLOCK), :]
    edge_kmt = jnp.where(wide_lane < HALO, kmt_left, kmt_right)
    edge_kmt = jnp.where(wide_lane < 2 * HALO, edge_kmt, 0.0)
    for by in (8, 16, 32, 64):
        edge_kmt = edge_kmt + pltpu.roll(edge_kmt, by, 1)
    edge = jnp.where(edge_kmt > (wide_lane // (2 * HALO)).astype(jnp.float32), edge, 0.0)
    for by in (64, 32, 16, 8):
        edge = edge + pltpu.roll(edge, by, 1)
    moved = pltpu.roll(mean, HALO, 1)
    mean = jnp.concatenate(
        [
            jnp.where(wide_lane < HALO, edge, moved),
            jnp.where(wide_lane < HALO, moved, jnp.where(wide_lane < 2 * HALO, edge, 0.0)),
        ],
        axis=1,
    )
    sea = (planes_ref[0] > 0.0).astype(jnp.float32)

    def around(v):
        return (
            pltpu.roll(v, 1, 0)
            + pltpu.roll(v, MID - 1, 0)
            + pltpu.roll(v, 1, 1)
            + pltpu.roll(v, 2 * COLS - 1, 1)
        )

    diagonal = planes_ref[1] + sea * around(sea)
    powers = [sea * (mean * (1.0 / LEV) + planes_ref[2])]
    for _ in range(ITERS):
        v = powers[-1]
        powers.append((diagonal * v - sea * around(v)) * 0.125)
    for index, v in enumerate(powers):
        powers_ref[index] = v
    row = lax.broadcasted_iota(jnp.int32, (MID, 2 * COLS), 0)
    column = lane_index((MID, 2 * COLS))
    own = (
        (row >= HALO) & (row < HALO + ROWS) & (column >= HALO) & (column < HALO + COLS)
    )
    owned = [jnp.where(own, v, 0.0) for v in powers]
    high_rows, low_rows = [], []
    for order in range(2 * ITERS):
        p, e = two_product(owned[order // 2], owned[order - order // 2])
        tiles = [
            (p[8 * i : 8 * i + 8, 128 * j : 128 * j + 128], e[8 * i : 8 * i + 8, 128 * j : 128 * j + 128])
            for i in range(MID // 8)
            for j in range(2)
        ]
        while len(tiles) > 1:
            tiles = [pair_add(a, b) for a, b in zip(tiles[::2], tiles[1::2])]
        total = tiles[0]
        for by in (4, 2, 1):
            total = pair_add(total, tuple(pltpu.roll(t, by, 0) for t in total))
        high_rows.append(total[0])
        low_rows.append(total[1])
    where = lax.broadcasted_iota(jnp.int32, (8, COLS), 0)
    high, low = high_rows[0], low_rows[0]
    for order in range(1, 2 * ITERS):
        high = jnp.where(where == order, high_rows[order], high)
        low = jnp.where(where == order, low_rows[order], low)
    total = (high, low)
    for by in (64, 32, 16, 8, 4, 2, 1):
        total = pair_add(total, tuple(pltpu.roll(t, by, 1) for t in total))
    spot = lax.broadcasted_iota(jnp.int32, (8, COLS), 0)
    message = jnp.where(lane == spot, total[0], 0.0) + jnp.where(lane == spot + 64, total[1], 0.0)
    message = jnp.sum(message, axis=0, keepdims=True)
    parts_ref[...] = jnp.broadcast_to(message, parts_ref.shape)
    move.wait()


def sum_messages(parts_ref):
    count = parts_ref.shape[0] // 8
    tiles = [parts_ref[8 * i : 8 * i + 8, :] for i in range(count)]
    tiles = [two_sum(a, b) for a, b in zip(tiles[::2], tiles[1::2])]
    while len(tiles) > 1:
        tiles = [pair_add(a, b) for a, b in zip(tiles[::2], tiles[1::2])]
    total = tiles[0]
    for by in (4, 2, 1):
        total = pair_add(total, tuple(pltpu.roll(t, by, 0) for t in total))
    return pair_add(total, tuple(pltpu.roll(t, 64, 1) for t in total))


def merge_kernel(parts_ref, out_ref):
    total = sum_messages(parts_ref)
    lane = lane_index((8, COLS))
    merged = jnp.where(lane < 64, total[0], total[1])
    out_ref[...] = jnp.broadcast_to(merged[:1], out_ref.shape)


def combine_kernel(parts_ref, powers_ref, surface_ref, residual_ref, wide):
    total = sum_messages(parts_ref)
    moments = [
        tuple(jnp.broadcast_to(t[:, order : order + 1], (8, COLS)) for t in total)
        for order in range(2 * ITERS)
    ]
    rho = list(moments)
    delta = list(moments)
    one = jnp.ones((8, COLS), jnp.float32)
    zero = jnp.zeros((8, COLS), jnp.float32)
    res = [one] + [zero] * ITERS
    way = [one] + [zero] * ITERS
    sol = [zero] * ITERS
    for step in range(ITERS):
        inverse = pair_inverse(delta[step + 1])
        alpha = pair_mul(rho[step], inverse)
        sol = [s + alpha[0] * w for s, w in zip(sol, way)]
        res = [res[0]] + [r - alpha[0] * w for r, w in zip(res[1:], way)]
        if step == ITERS - 1:
            break
        last = 2 * ITERS - 1 - step
        rho = [
            None if order <= step or order >= last
            else pair_add(rho[order], pair_neg(pair_mul(alpha, delta[order + 1])))
            for order in range(2 * ITERS)
        ]
        beta = pair_neg(pair_mul(rho[step + 1], inverse))
        delta = [
            None if order <= step or order >= last
            else pair_add(rho[order], pair_mul(beta, delta[order]))
            for order in range(2 * ITERS)
        ]
        way = [r + beta[0] * w for r, w in zip(res, way)]
    for weights, target, factor in ((sol, surface_ref, 0.125), (res, residual_ref, 1.0)):
        for i in range(MID // 8):
            for j in range(2):
                spot = (slice(8 * i, 8 * i + 8), slice(128 * j, 128 * j + 128))
                value = weights[0] * powers_ref[(0,) + spot]
                for index in range(1, len(weights)):
                    value = value + weights[index] * powers_ref[(index,) + spot]
                wide[spot] = value * factor
        target[...] = wide[HALO : HALO + ROWS, HALO : HALO + COLS]


def swap_pair():
    return [(i, i ^ 1) for i in range(lax.axis_size("lat"))]


def swap_other():
    count = lax.axis_size("lat")
    pairs = [(i, i + 1) for i in range(1, count - 1, 2)]
    return pairs + [(j, i) for i, j in pairs]


def reduction_groups(lon, lat):
    inner, outer = {}, {}
    for i in range(lon):
        for j in range(lat):
            inner.setdefault((i // 4, j // 4), []).append(i * lat + j)
            outer.setdefault((i % 4, j % 4), []).append(i * lat + j)
    return list(inner.values()), list(outer.values())


def swap_near():
    return [(i, i ^ 1) for i in range(lax.axis_size("lon"))]


def swap_far():
    count = lax.axis_size("lon")
    return [(i, (i + 1) % count if i % 2 else (i - 1) % count) for i in range(count)]


def body(temp, kmt, kappa, helm, forcing, cutoff, conv_in, conv_mid, conv_late, conv_out):
    f32 = jnp.float32
    shape = jax.ShapeDtypeStruct
    blocks = lax.axis_size("lon")
    bf16 = jnp.bfloat16
    vmem = pl.BlockSpec(memory_space=pltpu.VMEM)
    cutoff = cutoff.reshape(1, ROWS)
    fields = (temp, kmt, kappa, helm, forcing, cutoff)
    slab = shape((CUT + 1, DEEP, COLS), f32)
    to_pair, to_other = pl.pallas_call(
        slab_kernel,
        out_shape=(slab, slab),
        in_specs=[pl.BlockSpec(memory_space=pltpu.HBM)] * 6,
        out_specs=(vmem, vmem),
        scratch_shapes=(
            pltpu.VMEM((ROWS, COLS), jnp.int32),
            pltpu.VMEM((1, ROWS), jnp.int32),
            pltpu.SemaphoreType.DMA((10,)),
        ),
        compiler_params=pltpu.CompilerParams(vmem_limit_bytes=VMEM_LIMIT),
    )(*(pltpu.with_memory_space_constraint(field, pltpu.HBM) for field in fields))
    other = lax.ppermute(to_other, "lat", swap_other())
    pair = lax.ppermute(to_pair, "lat", swap_pair())
    tables = tuple(jnp.asarray(table) for table in filter_tables(blocks, COLS))
    sources = (jnp.transpose(conv_in, (0, 2, 1)), conv_mid, conv_late, conv_out) + tables
    own, *raw = fetching(
        rows_kernel,
        (shape((ROWS, FIELDS, COLS), f32),)
        + tuple(shape(source.shape, source.dtype) for source in sources),
        fields + sources,
        fields,
    )
    ends = shape((TALL // SLOTS, FIELDS, COLS), f32)
    rows, to_far, to_near, cuts = call(
        pack_kernel, (shape((TALL, FIELDS, COLS), f32), ends, ends, shape((DEEP, COLS), f32))
    )(own, pair, other)
    far = lax.ppermute(to_far, "lon", swap_far())
    near = lax.ppermute(to_near, "lon", swap_near())

    outs = (
        shape((4 * FIELDS, 640), bf16),
        shape((256, 384), bf16),
        shape((256, 384), bf16),
        shape((48, 256), bf16),
    )
    outs = outs + tuple(shape(table.shape, bf16) for table in tables[:3] for _ in range(2))
    def closure_scratch(chunks):
        cells = chunks * COLS
        return (
            pltpu.VMEM((cells, 128), f32),
            pltpu.VMEM((cells, 128), f32),
            pltpu.VMEM((cells, 128), bf16),
            pltpu.VMEM((cells, 128), bf16),
        )

    block = shape((MID, LEV, COLS), f32)
    inside, line, strips, *prepared = call(
        interior_kernel,
        (block, shape((LEV, COLS), f32), shape((TALL, FIELDS, COLS), f32)) + outs,
        (pltpu.VMEM((TALL * FIELDS, COLS), bf16),) + closure_scratch(19),
        10**9,
    )(rows, cuts, *raw[:7])
    weights, tables = prepared[:4], prepared[4:] + raw[7:]
    lines, planes = call(
        edge_kernel,
        (block, shape((3, MID, 2 * COLS), f32)),
        (pltpu.VMEM((TALL, FIELDS, COLS), f32),) + closure_scratch(6),
    )(rows, far, near, inside, strips, *weights)

    def filtered_block(lines, line, tables):
        whole = lax.all_to_all(lines, "lon", split_axis=0, concat_axis=0, tiled=True)
        result = call(filter_kernel, shape((BLOCK * blocks, COLS), f32))(whole, line, *tables)
        result = result.reshape(BLOCK * blocks, 1, COLS)
        result = lax.all_to_all(result, "lon", split_axis=0, concat_axis=0, tiled=True)
        return result.reshape(BLOCK * blocks, COLS)

    def plain_block(lines, line, tables):
        ends = shape((MID, COLS), f32)
        to_far, to_near = call(ends_kernel, (ends, ends))(lines)
        far = lax.ppermute(to_far, "lon", swap_far())
        near = lax.ppermute(to_near, "lon", swap_near())
        return call(plain_kernel, shape((BLOCK * MID, COLS), f32))(lines, far, near)

    top_row = lax.axis_index("lat") * ROWS - HALO
    polar = (top_row < BAND) | (top_row + MID > ROWS * lax.axis_size("lat") - BAND)
    back = lax.cond(polar, filtered_block, plain_block, lines, line, tables)
    everyone = blocks * lax.axis_size("lat")
    both = ("lon", "lat")
    inner, outer = reduction_groups(blocks, lax.axis_size("lat"))
    wide = len(inner[0])
    temp_new, powers, parts = pl.pallas_call(
        powers_kernel,
        out_shape=(
            shape((LEV, ROWS, COLS), f32),
            shape((ITERS + 1, MID, 2 * COLS), f32),
            shape((wide, COLS), f32),
        ),
        in_specs=[vmem] * 2,
        out_specs=(pl.BlockSpec(memory_space=pltpu.HBM), vmem, vmem),
        scratch_shapes=(pltpu.VMEM((LEV, ROWS, COLS), f32), pltpu.SemaphoreType.DMA),
        compiler_params=pltpu.CompilerParams(vmem_limit_bytes=VMEM_LIMIT),
    )(back, planes)
    parts = lax.all_to_all(
        parts, both, split_axis=0, concat_axis=0, tiled=True, axis_index_groups=inner
    )
    parts = call(merge_kernel, shape((everyone // wide, COLS), f32))(parts)
    parts = lax.all_to_all(
        parts, both, split_axis=0, concat_axis=0, tiled=True, axis_index_groups=outer
    )
    surface, residual = call(
        combine_kernel,
        (shape((ROWS, COLS), f32), shape((ROWS, COLS), f32)),
        (pltpu.VMEM((MID, 2 * COLS), f32),),
    )(parts, powers)
    return temp_new, surface, residual


def solution(mesh):
    return jax.shard_map(
        body,
        mesh=mesh,
        in_specs=(
            P(None, "lat", "lon"),
            P("lat", "lon"),
            P("lat", "lon"),
            P("lat", "lon"),
            P("lat", "lon"),
            P("lat"),
            P(),
            P(),
            P(),
            P(),
        ),
        out_specs=(P(None, "lat", "lon"), P("lat", "lon"), P("lat", "lon")),
        check_vma=False,
    )
```

```python
import math

import jax
import jax.numpy as jnp
import numpy as np
from jax import lax
from jax.experimental import pallas as pl
from jax.experimental.pallas import tpu as pltpu
from jax.sharding import PartitionSpec as P

ITERS = 4
STEP = 0.25
LEV = 8
FIELDS = 16
KMT, KAPPA, HELM, FORCING, CUT = 8, 9, 10, 11, 12
BAND = 48
HALO = 4
DEEP = 8
ROWS = 24
COLS = 128
TALL = ROWS + 2 * DEEP
MID = ROWS + 2 * HALO
BLOCK = LEV + 1
SLOTS = 20
VMEM_LIMIT = 48 * 1024 * 1024


def call(kernel, outs, scratch=(), flops=None):
    spec = pl.BlockSpec(memory_space=pltpu.VMEM)
    return pl.pallas_call(
        kernel,
        out_shape=outs,
        out_specs=jax.tree.map(lambda _: spec, outs),
        scratch_shapes=scratch,
        compiler_params=pltpu.CompilerParams(vmem_limit_bytes=VMEM_LIMIT),
    )


def lane_index(shape):
    return lax.broadcasted_iota(jnp.int32, shape, len(shape) - 1)


def fetching(kernel, outs, sources, held, rest=(), scratch=(), flops=10**6):
    spec = pl.BlockSpec(memory_space=pltpu.VMEM)
    return pl.pallas_call(
        kernel,
        out_shape=outs,
        in_specs=[pl.BlockSpec(memory_space=pltpu.HBM)] * len(sources),
        out_specs=jax.tree.map(lambda _: spec, outs),
        scratch_shapes=tuple(pltpu.VMEM(source.shape, source.dtype) for source in held)
        + (pltpu.SemaphoreType.DMA((len(sources),)),),
        compiler_params=pltpu.CompilerParams(vmem_limit_bytes=VMEM_LIMIT),
        cost_estimate=pl.CostEstimate(flops=10**6, bytes_accessed=2 * 10**6, transcendentals=0),
    )(*(pltpu.with_memory_space_constraint(source, pltpu.HBM) for source in sources))


def even_row():
    return lax.rem(lax.axis_index("lat"), 2) == 0


def slab_kernel(
    temp_hbm, kmt_hbm, kappa_hbm, helm_hbm, forcing_hbm, cutoff_hbm,
    pair_ref, other_ref, cross_ref, kmt, cutoff, sems,
):
    last = jnp.where(even_row(), ROWS - DEEP, 0)
    slabs = [
        (target, pl.multiple_of(start, DEEP))
        for target, start in ((pair_ref, last), (other_ref, ROWS - DEEP - last))
    ]
    pairs = [(kmt_hbm, kmt), (cutoff_hbm, cutoff)]
    for target, start in slabs:
        rows = pl.ds(start, DEEP)
        pairs.append((temp_hbm.at[:, rows], target.at[pl.ds(0, LEV)]))
        for source, field in ((kappa_hbm, KAPPA), (helm_hbm, HELM), (forcing_hbm, FORCING)):
            pairs.append((source.at[rows], target.at[field]))
    moves = fetch(*zip(*pairs), sems)
    for move in moves:
        move.wait()
    for target, start in slabs:
        target[KMT] = kmt[pl.ds(start, DEEP), :].astype(jnp.float32)
        target[CUT] = cutoff_lanes(cutoff)
    cross_ref[...] = other_ref[...]


def cutoff_lanes(cutoff_ref):
    line = cutoff_ref[...].astype(jnp.float32)
    line = jnp.concatenate([line, jnp.zeros((1, COLS - ROWS), jnp.float32)], axis=1)
    return jnp.broadcast_to(line, (DEEP, COLS))


def fetch(sources, targets, sems):
    moves = [
        pltpu.make_async_copy(source, target, sems.at[index])
        for index, (source, target) in enumerate(zip(sources, targets))
    ]
    for move in moves:
        move.start()
    return moves


def rows_kernel(*refs):
    sources, own_ref, raw, held, sems = refs[:15], refs[15], refs[16:25], refs[25:31], refs[31]
    moves = fetch(sources, tuple(held) + tuple(raw), sems)
    for move in moves[: len(held)]:
        move.wait()
    fill_rows(*held, own_ref)
    for move in moves[len(held) :]:
        move.wait()


def fill_rows(temp_ref, kmt_ref, kappa_ref, helm_ref, forcing_ref, cutoff_ref, own_ref):
    own_ref[:, CUT + 1 :, :] = jnp.zeros((ROWS, FIELDS - CUT - 1, COLS), jnp.float32)
    for level in range(LEV):
        own_ref[:, level, :] = temp_ref[level]
    own_ref[:, KMT, :] = kmt_ref[...].astype(jnp.float32)
    own_ref[:, KAPPA, :] = kappa_ref[...]
    own_ref[:, HELM, :] = helm_ref[...]
    own_ref[:, FORCING, :] = forcing_ref[...]
    own_ref[:, CUT, :] = jnp.broadcast_to(cutoff_lanes(cutoff_ref)[:1], (ROWS, COLS))


def fill_weights(
    first_ref, mid_ref, late_ref, last_ref, w_in_ref, w_mid_ref, w_late_ref, w_out_ref
):
    w_in_ref[...] = jnp.zeros(w_in_ref.shape, w_in_ref.dtype)
    width = mid_ref.shape[1]
    none = jnp.zeros((LEV, width), jnp.float32)
    for row in range(4):
        parts = []
        for tap in range(3):
            for parity in range(2):
                a = row - parity
                parts.append(first_ref[3 * a + tap].astype(jnp.float32) if 0 <= a < 3 else none)
        top = jnp.concatenate(parts, axis=1)
        marks = [jnp.ones((1, width), jnp.float32) if row == at else none[:1] for at in (1, 2, 2, 3)]
        marks = jnp.concatenate(marks, axis=1)
        block = jnp.concatenate(
            [
                jnp.concatenate([top, jnp.zeros((LEV, 4 * width), jnp.float32)], axis=1),
                jnp.concatenate(
                    [
                        jnp.concatenate([jnp.zeros((1, 6 * width), jnp.float32), marks], axis=1),
                        jnp.zeros((LEV - 1, 10 * width), jnp.float32),
                    ],
                    axis=0,
                ),
            ],
            axis=0,
        )
        w_in_ref[FIELDS * row : FIELDS * (row + 1)] = block.astype(jnp.bfloat16)

    def rows_of(ref, tap, parity):
        outs = ref.shape[1]
        blank = jnp.zeros((outs, width), jnp.float32)
        parts = []
        for row in range(4):
            a = row - parity
            parts.append(ref[3 * a + tap].astype(jnp.float32) if 0 <= a < 3 else blank)
        return jnp.concatenate(parts, axis=1)

    for ref, out_ref in ((mid_ref, w_mid_ref), (late_ref, w_late_ref)):
        for tap in range(3):
            both = jnp.concatenate([rows_of(ref, tap, 0), rows_of(ref, tap, 1)], axis=0)
            out_ref[:, 2 * width * tap : 2 * width * (tap + 1)] = both.T.astype(jnp.bfloat16)
    w_out_ref[...] = jnp.concatenate(
        [rows_of(last_ref, tap, parity) for tap in range(3) for parity in range(2)], axis=0
    ).astype(jnp.bfloat16)


def pack_kernel(
    own_ref, other_ref, pair_ref, cross_ref, rows_ref, far_ref, near_ref, cut_ref
):
    others = [other_ref[k] + cross_ref[k] for k in range(CUT + 1)]
    north = [jnp.where(even_row(), others[k], pair_ref[k]) for k in range(CUT + 1)]
    south = [jnp.where(even_row(), pair_ref[k], others[k]) for k in range(CUT + 1)]
    even = lax.rem(lax.axis_index("lon"), 2) == 0
    rows_ref[DEEP : DEEP + ROWS] = own_ref[...]
    for slab, start in ((north, 0), (south, DEEP + ROWS)):
        rows = slice(start, start + DEEP)
        rows_ref[rows, CUT + 1 :, :] = jnp.zeros((DEEP, FIELDS - CUT - 1, COLS), jnp.float32)
        for field in range(CUT + 1):
            rows_ref[rows, field, :] = slab[field]
    lane = lane_index((DEEP, COLS))
    north = pltpu.roll(north[CUT], COLS - (ROWS - DEEP), 1)
    south = pltpu.roll(south[CUT], DEEP + ROWS, 1)
    own = pltpu.roll(jnp.broadcast_to(own_ref[0, CUT : CUT + 1, :], (DEEP, COLS)), DEEP, 1)
    cut_ref[...] = jnp.where(lane < DEEP, north, jnp.where(lane < DEEP + ROWS, own, south))
    lane = lane_index((FIELDS, COLS))
    for part in range(TALL // SLOTS):
        first = jnp.zeros((FIELDS, COLS), jnp.float32)
        last = jnp.zeros((FIELDS, COLS), jnp.float32)
        for slot in range(SLOTS):
            here = rows_ref[part * SLOTS + slot]
            inside = (lane >= HALO * slot) & (lane < HALO * (slot + 1))
            first = jnp.where(inside, pltpu.roll(here, HALO * slot, 1) if slot else here, first)
            last = jnp.where(inside, pltpu.roll(here, HALO * (slot + 1), 1), last)
        far_ref[part] = jnp.where(even, first, last)
        near_ref[part] = jnp.where(even, last, first)


def closure_layers(window, pairs, stride, weights, acts, masks):
    w_in_ref, w_mid_ref, w_late_ref, w_out_ref = weights
    act_a, act_b = acts
    mask_odd, mask_even = masks

    def chunks(count):
        return range(-(-count * stride // COLS))

    def at(chunk, shift=0):
        return slice(COLS * chunk + shift, COLS * (chunk + 1) + shift)

    def both(act, chunk):
        return jnp.concatenate([act[at(chunk)], act[at(chunk, stride)]], axis=1)

    def finish(total, mask):
        v = (
            pltpu.roll(total[:, 0:128], 1, 0)
            + total[:, 128:256]
            + pltpu.roll(total[:, 256:384], COLS - 1, 0)
        )
        return (mask * (v / (1.0 + jnp.exp(-v)))).astype(jnp.bfloat16)

    for chunk in chunks(pairs):
        total = lax.dot_general(
            window(chunk),
            w_in_ref[...],
            (((0,), (0,)), ((), ())),
            preferred_element_type=jnp.float32,
        )
        mask_odd[at(chunk)] = total[:, 384:512]
        mask_even[at(chunk)] = total[:, 512:640]
        act_a[at(chunk)] = finish(total, total[:, 384:512])
    for chunk in chunks(pairs - 1):
        total = jnp.dot(both(act_a, chunk), w_mid_ref[...], preferred_element_type=jnp.float32)
        act_b[at(chunk)] = finish(total, mask_even[at(chunk)])
    for chunk in chunks(pairs - 2):
        total = jnp.dot(both(act_b, chunk), w_late_ref[...], preferred_element_type=jnp.float32)
        act_a[at(chunk)] = finish(total, mask_odd[at(chunk, stride)])
    results = []
    for chunk in chunks(pairs - 3):
        total = lax.dot_general(
            w_out_ref[...],
            both(act_a, chunk),
            (((1,), (1,)), ((), ())),
            preferred_element_type=jnp.float32,
        )
        results.append(
            pltpu.roll(total[0:16], 1, 1) + total[16:32] + pltpu.roll(total[32:48], COLS - 1, 1)
        )
    return results


def level_index():
    return lax.broadcasted_iota(jnp.int32, (LEV, COLS), 0).astype(jnp.float32)


def wetness(block):
    return (level_index() < block[KMT : KMT + 1]).astype(jnp.float32)


def first_input(block):
    wet = wetness(block)
    sea = jnp.where(level_index() == 0.0, wet, 0.0)
    return jnp.concatenate([wet * block[0:LEV], sea], axis=0).astype(jnp.bfloat16)


def advance(here, north, south, closure):
    wet = wetness(here)
    temp = here[0:LEV]
    tracer = wet * temp
    kappa = jnp.broadcast_to(here[KAPPA : KAPPA + 1], (LEV, COLS))
    diff = jnp.zeros((LEV, COLS), jnp.float32)
    for near in (south, north):
        near_w = wetness(near)
        diff = diff + near_w * 0.5 * (kappa + near[KAPPA : KAPPA + 1]) * (
            near_w * near[0:LEV] - tracer
        )
    for by in (COLS - 1, 1):
        diff = diff + pltpu.roll(wet, by, 1) * 0.5 * (kappa + pltpu.roll(kappa, by, 1)) * (
            pltpu.roll(tracer, by, 1) - tracer
        )
    diff = wet * diff
    eddy = wet * closure
    return wet * (temp + STEP * (diff + eddy))


FIRST = DEEP - HALO


def interior_kernel(*refs):
    rows_ref, cut_ref, raw, refs = refs[0], refs[1], refs[2:9], refs[9:]
    out_ref, line_ref, strips_ref, refs = refs[0], refs[1], refs[2], refs[3:]
    weights, tables, refs = refs[:4], refs[4:10], refs[10:]
    start, mask_odd, mask_even, act_a, act_b = refs
    fill_weights(*raw[:4], *weights)
    for index, table in enumerate(raw[4:]):
        tables[2 * index][...], tables[2 * index + 1][...] = halves(table[...])
    lane = lane_index((FIELDS, COLS))
    for row in range(TALL):
        here = rows_ref[row]
        start[row * FIELDS : (row + 1) * FIELDS] = first_input(here)
        strip = jnp.where(lane < 12, pltpu.roll(here, 4, 1), pltpu.roll(here, 20, 1))
        strips_ref[row] = jnp.where((lane >= 4) & (lane < 20), strip, 0.0)
    results = closure_layers(
        lambda chunk: start[2 * FIELDS * chunk : 2 * FIELDS * (chunk + 2)],
        TALL // 2 - 1,
        COLS,
        weights,
        (act_a, act_b),
        (mask_odd, mask_even),
    )
    for pair, closure in enumerate(results):
        for parity in range(2):
            row = FIRST + 2 * pair + parity
            out_ref[2 * pair + parity] = advance(
                rows_ref[row],
                rows_ref[row - 1],
                rows_ref[row + 1],
                closure[LEV * parity : LEV * (parity + 1)],
            )
    own_line = lane_index((LEV, COLS)) == lax.axis_index("lon") + FIRST
    kept = jnp.sum(jnp.where(own_line, cut_ref[...], 0.0), axis=1, keepdims=True)
    line_ref[...] = jnp.broadcast_to(kept, (LEV, COLS))


STRIP = 32
PER = COLS // STRIP


def edge_kernel(
    rows_ref, far_ref, near_ref, inside_ref, own_ref, w_in_ref, w_mid_ref, w_late_ref, w_out_ref,
    out_ref, planes_ref, strips, mask_odd, mask_even, act_a, act_b,
):
    lane = lane_index((FIELDS, COLS))
    even = lax.rem(lax.axis_index("lon"), 2) == 0
    parts = range(TALL // SLOTS)
    from_west = [jnp.where(even, far_ref[part], near_ref[part]) for part in parts]
    from_east = [jnp.where(even, near_ref[part], far_ref[part]) for part in parts]
    for row in range(TALL):
        part, slot = row // SLOTS, row % SLOTS
        west, east = from_west[part], from_east[part]
        west = pltpu.roll(west, COLS - HALO * slot, 1) if slot else west
        east = pltpu.roll(east, (20 - HALO * slot) % COLS, 1) if slot != 5 else east
        strip = jnp.where((lane >= 20) & (lane < 24), east, own_ref[row])
        strips[row] = jnp.where(lane < 4, west, strip)

    def side_by_side(parity, start):
        total = None
        for slot in range(PER):
            row = 2 * (start + slot) + parity
            if row >= TALL:
                continue
            piece = strips[row]
            piece = pltpu.roll(piece, STRIP * slot, 1) if slot else piece
            total = piece if total is None else total + piece
        return total

    def window(chunk):
        at = PER * chunk
        return jnp.concatenate(
            [
                first_input(block)
                for block in (
                    side_by_side(0, at),
                    side_by_side(1, at),
                    side_by_side(0, at + 1),
                    side_by_side(1, at + 1),
                )
            ],
            axis=0,
        )

    act_a[5 * COLS :] = jnp.zeros((COLS, COLS), jnp.bfloat16)
    act_b[5 * COLS :] = jnp.zeros((COLS, COLS), jnp.bfloat16)
    mask_odd[5 * COLS :] = jnp.zeros((COLS, COLS), jnp.float32)
    results = closure_layers(
        window,
        TALL // 2 - 1,
        STRIP,
        (w_in_ref, w_mid_ref, w_late_ref, w_out_ref),
        (act_a, act_b),
        (mask_odd, mask_even),
    )
    at_lane = lane_index((LEV, COLS))
    for chunk in range(4):
        at = PER * chunk + FIRST // 2
        closure = results[chunk]
        north = side_by_side(1, at - 1)
        upper = side_by_side(0, at)
        lower = side_by_side(1, at)
        south = side_by_side(0, at + 1)
        for parity, value in (
            (0, advance(upper, north, lower, closure[0:LEV])),
            (1, advance(lower, upper, south, closure[LEV : 2 * LEV])),
        ):
            for slot in range(PER):
                row = 2 * (PER * chunk + slot) + parity
                left = pltpu.roll(value, COLS - STRIP * slot - 4, 1)
                shift = (108 - STRIP * slot) % COLS
                right = pltpu.roll(value, shift, 1)
                out_ref[row] = jnp.where(
                    at_lane < HALO,
                    left,
                    jnp.where(at_lane >= COLS - HALO, right, inside_ref[row]),
                )
    plane_lane = lane_index((MID, COLS))
    for index, field in enumerate((KMT, HELM, FORCING)):
        moved = pltpu.roll(rows_ref[FIRST : FIRST + MID, field, :], HALO, 1)
        edge = strips[FIRST : FIRST + MID, field, :]
        planes_ref[index, :, 0:COLS] = jnp.where(plane_lane < HALO, edge, moved)
        planes_ref[index, :, COLS:] = jnp.where(
            plane_lane < HALO,
            moved,
            jnp.where(plane_lane < 2 * HALO, pltpu.roll(edge, COLS - 16, 1), 0.0),
        )


def filter_tables(blocks, width):
    length = blocks * width
    half = LEV // 2
    k = np.arange(blocks)
    outer = np.exp(-2j * np.pi * ((k[:, None] * k[None, :]) % blocks) / blocks)
    spread = np.zeros((blocks, 2, half, blocks, 2, half))
    for line in range(half):
        spread[:, 0, line, :, 0, line] = outer.real
        spread[:, 0, line, :, 1, line] = -outer.imag
        spread[:, 1, line, :, 0, line] = outer.imag
        spread[:, 1, line, :, 1, line] = outer.real
    spread = spread.reshape(blocks * LEV, blocks * LEV)
    m = np.arange(width)
    twist = np.exp(-2j * np.pi * (k[:, None] * m[None, :]) / length)
    sign = np.where(np.arange(LEV) < half, -1.0, 1.0)[None, :, None]
    twist_re = np.broadcast_to(twist.real[:, None, :], (blocks, LEV, width))
    twist_im = twist.imag[:, None, :] * sign
    inner = np.exp(-2j * np.pi * ((m[:, None] * m[None, :]) % width) / width)
    inner = np.concatenate([inner.real, inner.imag], axis=1)
    return [
        np.asarray(t, np.float32)
        for t in (spread, spread.T / length, inner, twist_re, twist_im)
    ]


def halves(x):
    high = x.astype(jnp.bfloat16)
    return high, (x - high.astype(jnp.float32)).astype(jnp.bfloat16)


def split_dot(a, b):
    def dot(x, y):
        return jnp.dot(x, y, preferred_element_type=jnp.float32)

    return dot(a[0], b[0]) + (dot(a[0], b[1]) + dot(a[1], b[0]))


def filter_kernel(
    x_ref, line_ref, spread_ref, spread_low, back_ref, back_low, inner_ref, inner_low,
    twist_re_ref, twist_im_ref, out_ref,
):
    blocks, lev, width = x_ref.shape
    shape = (blocks, lev, width)
    flat = (blocks * lev, width)
    length = blocks * width
    inner = (inner_ref[...], inner_low[...])

    def partner(block):
        return pltpu.roll(block, lev // 2, 1)

    sign = jnp.where(lax.broadcasted_iota(jnp.int32, shape, 1) < lev // 2, -1.0, 1.0)
    y = split_dot((spread_ref[...], spread_low[...]), halves(x_ref[...].reshape(flat)))
    y = y.reshape(shape)
    y = y * twist_re_ref[...] + partner(y) * twist_im_ref[...]
    s = split_dot(halves(y.reshape(flat)), inner)
    s = s[:, 0:width].reshape(shape) + partner(s[:, width:].reshape(shape)) * sign
    wave = lax.broadcasted_iota(jnp.int32, shape, 0) + blocks * lane_index(shape)
    folded = jnp.minimum(wave, length - wave).astype(jnp.float32)
    s = jnp.where(folded < line_ref[0:1, :][None], s, 0.0)
    y = split_dot(halves(s.reshape(flat)), inner)
    y = y[:, 0:width].reshape(shape) - partner(y[:, width:].reshape(shape)) * sign
    y = y * twist_re_ref[...] - partner(y) * twist_im_ref[...]
    x = split_dot((back_ref[...], back_low[...]), halves(y.reshape(flat))).reshape(shape)
    lane = lane_index((lev, width))
    moved = [pltpu.roll(x[block], HALO, 1) for block in range(blocks)]
    for block in range(blocks):
        edge = jnp.where(lane < HALO, moved[block - 1], moved[(block + 1) % blocks])
        edge = jnp.where(lane < 2 * HALO, edge, 0.0)
        edge = pltpu.roll(edge, 0, 1, stride=2 * HALO, stride_axis=0)
        row = BLOCK * block
        out_ref[row : row + lev, :] = x[block]
        out_ref[row + lev : row + BLOCK, :] = jnp.sum(edge, axis=0, keepdims=True)


def ends_kernel(x_ref, far_ref, near_ref):
    even = lax.rem(lax.axis_index("lon"), 2) == 0
    lane = lane_index((LEV, COLS))
    packed = []
    for row in range(MID):
        edge = jnp.where(lane < 2 * HALO, pltpu.roll(x_ref[row], HALO, 1), 0.0)
        edge = pltpu.roll(edge, 0, 1, stride=2 * HALO, stride_axis=0)
        packed.append(jnp.sum(edge, axis=0, keepdims=True))
    packed = jnp.concatenate(packed, axis=0)
    to_east = lax.rem(lane_index((MID, COLS)), 2 * HALO) < HALO
    last = jnp.where(to_east, packed, 0.0)
    first = jnp.where(to_east, 0.0, packed)
    far_ref[...] = jnp.where(even, first, last)
    near_ref[...] = jnp.where(even, last, first)


def plain_kernel(x_ref, far_ref, near_ref, out_ref):
    edge = far_ref[...] + near_ref[...]
    for row in range(MID):
        out_ref[BLOCK * row : BLOCK * row + LEV, :] = x_ref[row]
        out_ref[BLOCK * row + LEV : BLOCK * (row + 1), :] = edge[row : row + 1]


def two_sum(a, b):
    s = a + b
    t = s - a
    return s, (a - (s - t)) + (b - t)


def quick_sum(a, b):
    s = a + b
    return s, b - (s - a)


def split(a):
    c = a * 4097.0
    high = c - (c - a)
    return high, a - high


def two_product(a, b):
    p = a * b
    ah, al = split(a)
    bh, bl = split(b)
    return p, ((ah * bh - p) + ah * bl + al * bh) + al * bl


def pair_add(a, b):
    s, e = two_sum(a[0], b[0])
    return quick_sum(s, e + (a[1] + b[1]))


def pair_neg(a):
    return -a[0], -a[1]


def pair_mul(a, b):
    p, e = two_product(a[0], b[0])
    return quick_sum(p, e + (a[0] * b[1] + a[1] * b[0]))


def pair_inverse(a):
    x = 1.0 / a[0]
    p, e = two_product(a[0], x)
    return quick_sum(x, x * (((1.0 - p) - e) - a[1] * x))


def powers_kernel(x_ref, planes_ref, temp_hbm, powers_ref, parts_ref, temp, sem):
    for level in range(LEV):
        temp[level] = x_ref[pl.ds(HALO * BLOCK + level, ROWS, stride=BLOCK), :]
    move = pltpu.make_async_copy(temp, temp_hbm, sem)
    move.start()
    lane = lane_index((LEV, COLS))
    wide_lane = lane_index((MID, COLS))
    kmt_left = planes_ref[0, :, 0:COLS]
    kmt_right = planes_ref[0, :, COLS:]
    kmt = pltpu.roll(jnp.where(wide_lane < HALO, kmt_right, kmt_left), COLS - HALO, 1)
    mean = jnp.zeros((MID, COLS), jnp.float32)
    for level in range(LEV):
        here = x_ref[pl.ds(level, MID, stride=BLOCK), :]
        mean = mean + jnp.where(kmt > level, here, 0.0)
    edge = x_ref[pl.ds(LEV, MID, stride=BLOCK), :]
    edge_kmt = jnp.where(wide_lane < HALO, kmt_left, kmt_right)
    edge_kmt = jnp.where(wide_lane < 2 * HALO, edge_kmt, 0.0)
    for by in (8, 16, 32, 64):
        edge_kmt = edge_kmt + pltpu.roll(edge_kmt, by, 1)
    edge = jnp.where(edge_kmt > (wide_lane // (2 * HALO)).astype(jnp.float32), edge, 0.0)
    for by in (64, 32, 16, 8):
        edge = edge + pltpu.roll(edge, by, 1)
    moved = pltpu.roll(mean, HALO, 1)
    mean = jnp.concatenate(
        [
            jnp.where(wide_lane < HALO, edge, moved),
            jnp.where(wide_lane < HALO, moved, jnp.where(wide_lane < 2 * HALO, edge, 0.0)),
        ],
        axis=1,
    )
    sea = (planes_ref[0] > 0.0).astype(jnp.float32)

    def around(v):
        return (
            pltpu.roll(v, 1, 0)
            + pltpu.roll(v, MID - 1, 0)
            + pltpu.roll(v, 1, 1)
            + pltpu.roll(v, 2 * COLS - 1, 1)
        )

    diagonal = planes_ref[1] + sea * around(sea)
    powers = [sea * (mean * (1.0 / LEV) + planes_ref[2])]
    for _ in range(ITERS):
        v = powers[-1]
        powers.append((diagonal * v - sea * around(v)) * 0.125)
    for index, v in enumerate(powers):
        powers_ref[index] = v
    row = lax.broadcasted_iota(jnp.int32, (MID, 2 * COLS), 0)
    column = lane_index((MID, 2 * COLS))
    own = (
        (row >= HALO) & (row < HALO + ROWS) & (column >= HALO) & (column < HALO + COLS)
    )
    owned = [jnp.where(own, v, 0.0) for v in powers]
    high_rows, low_rows = [], []
    for order in range(2 * ITERS):
        p, e = two_product(owned[order // 2], owned[order - order // 2])
        tiles = [
            (p[8 * i : 8 * i + 8, 128 * j : 128 * j + 128], e[8 * i : 8 * i + 8, 128 * j : 128 * j + 128])
            for i in range(MID // 8)
            for j in range(2)
        ]
        while len(tiles) > 1:
            tiles = [pair_add(a, b) for a, b in zip(tiles[::2], tiles[1::2])]
        total = tiles[0]
        for by in (4, 2, 1):
            total = pair_add(total, tuple(pltpu.roll(t, by, 0) for t in total))
        high_rows.append(total[0])
        low_rows.append(total[1])
    where = lax.broadcasted_iota(jnp.int32, (8, COLS), 0)
    high, low = high_rows[0], low_rows[0]
    for order in range(1, 2 * ITERS):
        high = jnp.where(where == order, high_rows[order], high)
        low = jnp.where(where == order, low_rows[order], low)
    total = (high, low)
    for by in (64, 32, 16, 8, 4, 2, 1):
        total = pair_add(total, tuple(pltpu.roll(t, by, 1) for t in total))
    spot = lax.broadcasted_iota(jnp.int32, (8, COLS), 0)
    message = jnp.where(lane == spot, total[0], 0.0) + jnp.where(lane == spot + 64, total[1], 0.0)
    message = jnp.sum(message, axis=0, keepdims=True)
    parts_ref[...] = jnp.broadcast_to(message, parts_ref.shape)
    move.wait()


def sum_messages(parts_ref):
    count = parts_ref.shape[0] // 8
    tiles = [parts_ref[8 * i : 8 * i + 8, :] for i in range(count)]
    tiles = [two_sum(a, b) for a, b in zip(tiles[::2], tiles[1::2])]
    while len(tiles) > 1:
        tiles = [pair_add(a, b) for a, b in zip(tiles[::2], tiles[1::2])]
    total = tiles[0]
    for by in (4, 2, 1):
        total = pair_add(total, tuple(pltpu.roll(t, by, 0) for t in total))
    return pair_add(total, tuple(pltpu.roll(t, 64, 1) for t in total))


def merge_kernel(parts_ref, out_ref):
    total = sum_messages(parts_ref)
    lane = lane_index((8, COLS))
    merged = jnp.where(lane < 64, total[0], total[1])
    out_ref[...] = jnp.broadcast_to(merged[:1], out_ref.shape)


def combine_kernel(parts_ref, powers_ref, surface_ref, residual_ref, wide):
    total = sum_messages(parts_ref)
    moments = [
        tuple(jnp.broadcast_to(t[:, order : order + 1], (8, COLS)) for t in total)
        for order in range(2 * ITERS)
    ]
    rho = list(moments)
    delta = list(moments)
    one = jnp.ones((8, COLS), jnp.float32)
    zero = jnp.zeros((8, COLS), jnp.float32)
    res = [one] + [zero] * ITERS
    way = [one] + [zero] * ITERS
    sol = [zero] * ITERS
    for step in range(ITERS):
        inverse = pair_inverse(delta[step + 1])
        alpha = pair_mul(rho[step], inverse)
        sol = [s + alpha[0] * w for s, w in zip(sol, way)]
        res = [res[0]] + [r - alpha[0] * w for r, w in zip(res[1:], way)]
        if step == ITERS - 1:
            break
        last = 2 * ITERS - 1 - step
        rho = [
            None if order <= step or order >= last
            else pair_add(rho[order], pair_neg(pair_mul(alpha, delta[order + 1])))
            for order in range(2 * ITERS)
        ]
        beta = pair_neg(pair_mul(rho[step + 1], inverse))
        delta = [
            None if order <= step or order >= last
            else pair_add(rho[order], pair_mul(beta, delta[order]))
            for order in range(2 * ITERS)
        ]
        way = [r + beta[0] * w for r, w in zip(res, way)]
    for weights, target, factor in ((sol, surface_ref, 0.125), (res, residual_ref, 1.0)):
        for i in range(MID // 8):
            for j in range(2):
                spot = (slice(8 * i, 8 * i + 8), slice(128 * j, 128 * j + 128))
                value = weights[0] * powers_ref[(0,) + spot]
                for index in range(1, len(weights)):
                    value = value + weights[index] * powers_ref[(index,) + spot]
                wide[spot] = value * factor
        target[...] = wide[HALO : HALO + ROWS, HALO : HALO + COLS]


def swap_pair():
    return [(i, i ^ 1) for i in range(lax.axis_size("lat"))]


def swap_other(cross):
    pairs = [(i, i + 1) for i in range(3 if cross else 1, lax.axis_size("lat") - 1, 4)]
    return pairs + [(j, i) for i, j in pairs]


def reduction_groups(lon, lat):
    inner, outer = {}, {}
    for i in range(lon):
        for j in range(lat):
            inner.setdefault((i // 4, j // 4), []).append(i * lat + j)
            outer.setdefault((i % 4, j % 4), []).append(i * lat + j)
    return list(inner.values()), list(outer.values())


def swap_near():
    return [(i, i ^ 1) for i in range(lax.axis_size("lon"))]


def swap_far():
    count = lax.axis_size("lon")
    return [(i, (i + 1) % count if i % 2 else (i - 1) % count) for i in range(count)]


def body(temp, kmt, kappa, helm, forcing, cutoff, conv_in, conv_mid, conv_late, conv_out):
    f32 = jnp.float32
    shape = jax.ShapeDtypeStruct
    blocks = lax.axis_size("lon")
    bf16 = jnp.bfloat16
    vmem = pl.BlockSpec(memory_space=pltpu.VMEM)
    cutoff = cutoff.reshape(1, ROWS)
    fields = (temp, kmt, kappa, helm, forcing, cutoff)
    slab = shape((CUT + 1, DEEP, COLS), f32)
    to_pair, to_other, to_cross = pl.pallas_call(
        slab_kernel,
        out_shape=(slab, slab, slab),
        in_specs=[pl.BlockSpec(memory_space=pltpu.HBM)] * 6,
        out_specs=(vmem, vmem, vmem),
        scratch_shapes=(
            pltpu.VMEM((ROWS, COLS), jnp.int32),
            pltpu.VMEM((1, ROWS), jnp.int32),
            pltpu.SemaphoreType.DMA((10,)),
        ),
        compiler_params=pltpu.CompilerParams(vmem_limit_bytes=VMEM_LIMIT),
    )(*(pltpu.with_memory_space_constraint(field, pltpu.HBM) for field in fields))
    other = lax.ppermute(to_other, "lat", swap_other(False))
    pair = lax.ppermute(to_pair, "lat", swap_pair())
    cross = lax.ppermute(to_cross, "lat", swap_other(True))
    tables = tuple(jnp.asarray(table) for table in filter_tables(blocks, COLS))
    sources = (jnp.transpose(conv_in, (0, 2, 1)), conv_mid, conv_late, conv_out) + tables
    own, *raw = fetching(
        rows_kernel,
        (shape((ROWS, FIELDS, COLS), f32),)
        + tuple(shape(source.shape, source.dtype) for source in sources),
        fields + sources,
        fields,
    )
    ends = shape((TALL // SLOTS, FIELDS, COLS), f32)
    rows, to_far, to_near, cuts = call(
        pack_kernel, (shape((TALL, FIELDS, COLS), f32), ends, ends, shape((DEEP, COLS), f32))
    )(own, other, pair, cross)
    far = lax.ppermute(to_far, "lon", swap_far())
    near = lax.ppermute(to_near, "lon", swap_near())

    outs = (
        shape((4 * FIELDS, 640), bf16),
        shape((256, 384), bf16),
        shape((256, 384), bf16),
        shape((48, 256), bf16),
    )
    outs = outs + tuple(shape(table.shape, bf16) for table in tables[:3] for _ in range(2))
    def closure_scratch(chunks):
        cells = chunks * COLS
        return (
            pltpu.VMEM((cells, 128), f32),
            pltpu.VMEM((cells, 128), f32),
            pltpu.VMEM((cells, 128), bf16),
            pltpu.VMEM((cells, 128), bf16),
        )

    block = shape((MID, LEV, COLS), f32)
    inside, line, strips, *prepared = call(
        interior_kernel,
        (block, shape((LEV, COLS), f32), shape((TALL, FIELDS, COLS), f32)) + outs,
        (pltpu.VMEM((TALL * FIELDS, COLS), bf16),) + closure_scratch(19),
        10**9,
    )(rows, cuts, *raw[:7])
    weights, tables = prepared[:4], prepared[4:] + raw[7:]
    lines, planes = call(
        edge_kernel,
        (block, shape((3, MID, 2 * COLS), f32)),
        (pltpu.VMEM((TALL, FIELDS, COLS), f32),) + closure_scratch(6),
    )(rows, far, near, inside, strips, *weights)

    def filtered_block(lines, line, tables):
        whole = lax.all_to_all(lines, "lon", split_axis=0, concat_axis=0, tiled=True)
        result = call(filter_kernel, shape((BLOCK * blocks, COLS), f32))(whole, line, *tables)
        result = result.reshape(BLOCK * blocks, 1, COLS)
        result = lax.all_to_all(result, "lon", split_axis=0, concat_axis=0, tiled=True)
        return result.reshape(BLOCK * blocks, COLS)

    def plain_block(lines, line, tables):
        ends = shape((MID, COLS), f32)
        to_far, to_near = call(ends_kernel, (ends, ends))(lines)
        far = lax.ppermute(to_far, "lon", swap_far())
        near = lax.ppermute(to_near, "lon", swap_near())
        return call(plain_kernel, shape((BLOCK * MID, COLS), f32))(lines, far, near)

    top_row = lax.axis_index("lat") * ROWS - HALO
    polar = (top_row < BAND) | (top_row + MID > ROWS * lax.axis_size("lat") - BAND)
    back = lax.cond(polar, filtered_block, plain_block, lines, line, tables)
    everyone = blocks * lax.axis_size("lat")
    both = ("lon", "lat")
    inner, outer = reduction_groups(blocks, lax.axis_size("lat"))
    wide = len(inner[0])
    temp_new, powers, parts = pl.pallas_call(
        powers_kernel,
        out_shape=(
            shape((LEV, ROWS, COLS), f32),
            shape((ITERS + 1, MID, 2 * COLS), f32),
            shape((wide, COLS), f32),
        ),
        in_specs=[vmem] * 2,
        out_specs=(pl.BlockSpec(memory_space=pltpu.HBM), vmem, vmem),
        scratch_shapes=(pltpu.VMEM((LEV, ROWS, COLS), f32), pltpu.SemaphoreType.DMA),
        compiler_params=pltpu.CompilerParams(vmem_limit_bytes=VMEM_LIMIT),
    )(back, planes)
    parts = lax.all_to_all(
        parts, both, split_axis=0, concat_axis=0, tiled=True, axis_index_groups=inner
    )
    parts = call(merge_kernel, shape((everyone // wide, COLS), f32))(parts)
    parts = lax.all_to_all(
        parts, both, split_axis=0, concat_axis=0, tiled=True, axis_index_groups=outer
    )
    surface, residual = call(
        combine_kernel,
        (shape((ROWS, COLS), f32), shape((ROWS, COLS), f32)),
        (pltpu.VMEM((MID, 2 * COLS), f32),),
    )(parts, powers)
    return temp_new, surface, residual


def solution(mesh):
    return jax.shard_map(
        body,
        mesh=mesh,
        in_specs=(
            P(None, "lat", "lon"),
            P("lat", "lon"),
            P("lat", "lon"),
            P("lat", "lon"),
            P("lat", "lon"),
            P("lat"),
            P(),
            P(),
            P(),
            P(),
        ),
        out_specs=(P(None, "lat", "lon"), P("lat", "lon"), P("lat", "lon")),
        check_vma=False,
    )
```

```python
import math

import jax
import jax.numpy as jnp
import numpy as np
from jax import lax
from jax.experimental import pallas as pl
from jax.experimental.pallas import tpu as pltpu
from jax.sharding import PartitionSpec as P

ITERS = 4
STEP = 0.25
LEV = 8
FIELDS = 16
KMT, KAPPA, HELM, FORCING, CUT = 8, 9, 10, 11, 12
BAND = 48
HALO = 4
DEEP = 8
ROWS = 24
COLS = 128
TALL = ROWS + 2 * DEEP
MID = ROWS + 2 * HALO
BLOCK = LEV + 1
SLOTS = 20
VMEM_LIMIT = 48 * 1024 * 1024


def call(kernel, outs, scratch=(), flops=None):
    spec = pl.BlockSpec(memory_space=pltpu.VMEM)
    return pl.pallas_call(
        kernel,
        out_shape=outs,
        out_specs=jax.tree.map(lambda _: spec, outs),
        scratch_shapes=scratch,
        compiler_params=pltpu.CompilerParams(vmem_limit_bytes=VMEM_LIMIT),
    )


def lane_index(shape):
    return lax.broadcasted_iota(jnp.int32, shape, len(shape) - 1)


def fetching(kernel, outs, sources, held, rest=(), scratch=(), flops=10**6):
    spec = pl.BlockSpec(memory_space=pltpu.VMEM)
    return pl.pallas_call(
        kernel,
        out_shape=outs,
        in_specs=[pl.BlockSpec(memory_space=pltpu.HBM)] * len(sources),
        out_specs=jax.tree.map(lambda _: spec, outs),
        scratch_shapes=tuple(pltpu.VMEM(source.shape, source.dtype) for source in held)
        + (pltpu.SemaphoreType.DMA((len(sources),)),),
        compiler_params=pltpu.CompilerParams(vmem_limit_bytes=VMEM_LIMIT),
        cost_estimate=pl.CostEstimate(flops=10**6, bytes_accessed=2 * 10**6, transcendentals=0),
    )(*(pltpu.with_memory_space_constraint(source, pltpu.HBM) for source in sources))


def even_row():
    return lax.rem(lax.axis_index("lat"), 2) == 0


def slab_kernel(
    temp_hbm, kmt_hbm, kappa_hbm, helm_hbm, forcing_hbm, cutoff_hbm,
    pair_ref, other_ref, cross_ref, kmt, cutoff, sems,
):
    last = jnp.where(even_row(), ROWS - DEEP, 0)
    slabs = [
        (target, pl.multiple_of(start, DEEP))
        for target, start in ((pair_ref, last), (other_ref, ROWS - DEEP - last))
    ]
    pairs = [(kmt_hbm, kmt), (cutoff_hbm, cutoff)]
    for target, start in slabs:
        rows = pl.ds(start, DEEP)
        pairs.append((temp_hbm.at[:, rows], target.at[pl.ds(0, LEV)]))
        for source, field in ((kappa_hbm, KAPPA), (helm_hbm, HELM), (forcing_hbm, FORCING)):
            pairs.append((source.at[rows], target.at[field]))
    moves = fetch(*zip(*pairs), sems)
    for move in moves:
        move.wait()
    for target, start in slabs:
        target[KMT] = kmt[pl.ds(start, DEEP), :].astype(jnp.float32)
        target[CUT] = cutoff_lanes(cutoff)
    cross_ref[...] = other_ref[...]


def cutoff_lanes(cutoff_ref):
    line = cutoff_ref[...].astype(jnp.float32)
    line = jnp.concatenate([line, jnp.zeros((1, COLS - ROWS), jnp.float32)], axis=1)
    return jnp.broadcast_to(line, (DEEP, COLS))


def fetch(sources, targets, sems):
    moves = [
        pltpu.make_async_copy(source, target, sems.at[index])
        for index, (source, target) in enumerate(zip(sources, targets))
    ]
    for move in moves:
        move.start()
    return moves


def rows_kernel(*refs):
    sources, own_ref, raw, held, sems = refs[:15], refs[15], refs[16:25], refs[25:31], refs[31]
    moves = fetch(sources, tuple(held) + tuple(raw), sems)
    for move in moves[: len(held)]:
        move.wait()
    fill_rows(*held, own_ref)
    for move in moves[len(held) :]:
        move.wait()


def fill_rows(temp_ref, kmt_ref, kappa_ref, helm_ref, forcing_ref, cutoff_ref, own_ref):
    own_ref[:, CUT + 1 :, :] = jnp.zeros((ROWS, FIELDS - CUT - 1, COLS), jnp.float32)
    for level in range(LEV):
        own_ref[:, level, :] = temp_ref[level]
    own_ref[:, KMT, :] = kmt_ref[...].astype(jnp.float32)
    own_ref[:, KAPPA, :] = kappa_ref[...]
    own_ref[:, HELM, :] = helm_ref[...]
    own_ref[:, FORCING, :] = forcing_ref[...]
    own_ref[:, CUT, :] = jnp.broadcast_to(cutoff_lanes(cutoff_ref)[:1], (ROWS, COLS))


def fill_weights(
    first_ref, mid_ref, late_ref, last_ref, w_in_ref, w_mid_ref, w_late_ref, w_out_ref
):
    w_in_ref[...] = jnp.zeros(w_in_ref.shape, w_in_ref.dtype)
    width = mid_ref.shape[1]
    none = jnp.zeros((LEV, width), jnp.float32)
    for row in range(4):
        parts = []
        for tap in range(3):
            for parity in range(2):
                a = row - parity
                parts.append(first_ref[3 * a + tap].astype(jnp.float32) if 0 <= a < 3 else none)
        top = jnp.concatenate(parts, axis=1)
        marks = [jnp.ones((1, width), jnp.float32) if row == at else none[:1] for at in (1, 2, 2, 3)]
        marks = jnp.concatenate(marks, axis=1)
        block = jnp.concatenate(
            [
                jnp.concatenate([top, jnp.zeros((LEV, 4 * width), jnp.float32)], axis=1),
                jnp.concatenate(
                    [
                        jnp.concatenate([jnp.zeros((1, 6 * width), jnp.float32), marks], axis=1),
                        jnp.zeros((LEV - 1, 10 * width), jnp.float32),
                    ],
                    axis=0,
                ),
            ],
            axis=0,
        )
        w_in_ref[FIELDS * row : FIELDS * (row + 1)] = block.astype(jnp.bfloat16)

    def rows_of(ref, tap, parity):
        outs = ref.shape[1]
        blank = jnp.zeros((outs, width), jnp.float32)
        parts = []
        for row in range(4):
            a = row - parity
            parts.append(ref[3 * a + tap].astype(jnp.float32) if 0 <= a < 3 else blank)
        return jnp.concatenate(parts, axis=1)

    for ref, out_ref in ((mid_ref, w_mid_ref), (late_ref, w_late_ref)):
        for tap in range(3):
            both = jnp.concatenate([rows_of(ref, tap, 0), rows_of(ref, tap, 1)], axis=0)
            out_ref[:, 2 * width * tap : 2 * width * (tap + 1)] = both.T.astype(jnp.bfloat16)
    w_out_ref[...] = jnp.concatenate(
        [rows_of(last_ref, tap, parity) for tap in range(3) for parity in range(2)], axis=0
    ).astype(jnp.bfloat16)


def pack_kernel(
    own_ref, other_ref, pair_ref, cross_ref, rows_ref, far_ref, near_ref, cut_ref
):
    others = [other_ref[k] + cross_ref[k] for k in range(CUT + 1)]
    north = [jnp.where(even_row(), others[k], pair_ref[k]) for k in range(CUT + 1)]
    south = [jnp.where(even_row(), pair_ref[k], others[k]) for k in range(CUT + 1)]
    even = lax.rem(lax.axis_index("lon"), 2) == 0
    rows_ref[DEEP : DEEP + ROWS] = own_ref[...]
    for slab, start in ((north, 0), (south, DEEP + ROWS)):
        rows = slice(start, start + DEEP)
        rows_ref[rows, CUT + 1 :, :] = jnp.zeros((DEEP, FIELDS - CUT - 1, COLS), jnp.float32)
        for field in range(CUT + 1):
            rows_ref[rows, field, :] = slab[field]
    lane = lane_index((DEEP, COLS))
    north = pltpu.roll(north[CUT], COLS - (ROWS - DEEP), 1)
    south = pltpu.roll(south[CUT], DEEP + ROWS, 1)
    own = pltpu.roll(jnp.broadcast_to(own_ref[0, CUT : CUT + 1, :], (DEEP, COLS)), DEEP, 1)
    cut_ref[...] = jnp.where(lane < DEEP, north, jnp.where(lane < DEEP + ROWS, own, south))
    lane = lane_index((FIELDS, COLS))
    for part in range(TALL // SLOTS):
        first = jnp.zeros((FIELDS, COLS), jnp.float32)
        last = jnp.zeros((FIELDS, COLS), jnp.float32)
        for slot in range(SLOTS):
            here = rows_ref[part * SLOTS + slot]
            inside = (lane >= HALO * slot) & (lane < HALO * (slot + 1))
            first = jnp.where(inside, pltpu.roll(here, HALO * slot, 1) if slot else here, first)
            last = jnp.where(inside, pltpu.roll(here, HALO * (slot + 1), 1), last)
        far_ref[part] = jnp.where(even, first, last)
        near_ref[part] = jnp.where(even, last, first)


def closure_layers(window, pairs, stride, weights, acts, masks):
    w_in_ref, w_mid_ref, w_late_ref, w_out_ref = weights
    act_a, act_b = acts
    mask_odd, mask_even = masks

    def chunks(count):
        return range(-(-count * stride // COLS))

    def at(chunk, shift=0):
        return slice(COLS * chunk + shift, COLS * (chunk + 1) + shift)

    def both(act, chunk):
        return jnp.concatenate([act[at(chunk)], act[at(chunk, stride)]], axis=1)

    def finish(total, mask):
        v = (
            pltpu.roll(total[:, 0:128], 1, 0)
            + total[:, 128:256]
            + pltpu.roll(total[:, 256:384], COLS - 1, 0)
        )
        return (mask * (v / (1.0 + jnp.exp(-v)))).astype(jnp.bfloat16)

    for chunk in chunks(pairs):
        total = lax.dot_general(
            window(chunk),
            w_in_ref[...],
            (((0,), (0,)), ((), ())),
            preferred_element_type=jnp.float32,
        )
        mask_odd[at(chunk)] = total[:, 384:512]
        mask_even[at(chunk)] = total[:, 512:640]
        act_a[at(chunk)] = finish(total, total[:, 384:512])
    for chunk in chunks(pairs - 1):
        total = jnp.dot(both(act_a, chunk), w_mid_ref[...], preferred_element_type=jnp.float32)
        act_b[at(chunk)] = finish(total, mask_even[at(chunk)])
    for chunk in chunks(pairs - 2):
        total = jnp.dot(both(act_b, chunk), w_late_ref[...], preferred_element_type=jnp.float32)
        act_a[at(chunk)] = finish(total, mask_odd[at(chunk, stride)])
    results = []
    for chunk in chunks(pairs - 3):
        total = lax.dot_general(
            w_out_ref[...],
            both(act_a, chunk),
            (((1,), (1,)), ((), ())),
            preferred_element_type=jnp.float32,
        )
        results.append(
            pltpu.roll(total[0:16], 1, 1) + total[16:32] + pltpu.roll(total[32:48], COLS - 1, 1)
        )
    return results


def level_index():
    return lax.broadcasted_iota(jnp.int32, (LEV, COLS), 0).astype(jnp.float32)


def wetness(block):
    return (level_index() < block[KMT : KMT + 1]).astype(jnp.float32)


def first_input(block):
    wet = wetness(block)
    sea = jnp.where(level_index() == 0.0, wet, 0.0)
    return jnp.concatenate([wet * block[0:LEV], sea], axis=0).astype(jnp.bfloat16)


def advance(here, north, south, closure):
    wet = wetness(here)
    temp = here[0:LEV]
    tracer = wet * temp
    kappa = jnp.broadcast_to(here[KAPPA : KAPPA + 1], (LEV, COLS))
    diff = jnp.zeros((LEV, COLS), jnp.float32)
    for near in (south, north):
        near_w = wetness(near)
        diff = diff + near_w * 0.5 * (kappa + near[KAPPA : KAPPA + 1]) * (
            near_w * near[0:LEV] - tracer
        )
    for by in (COLS - 1, 1):
        diff = diff + pltpu.roll(wet, by, 1) * 0.5 * (kappa + pltpu.roll(kappa, by, 1)) * (
            pltpu.roll(tracer, by, 1) - tracer
        )
    diff = wet * diff
    eddy = wet * closure
    return wet * (temp + STEP * (diff + eddy))


FIRST = DEEP - HALO


def interior_kernel(*refs):
    rows_ref, cut_ref, raw, refs = refs[0], refs[1], refs[2:9], refs[9:]
    out_ref, line_ref, strips_ref, refs = refs[0], refs[1], refs[2], refs[3:]
    weights, tables, refs = refs[:4], refs[4:10], refs[10:]
    start, mask_odd, mask_even, act_a, act_b = refs
    fill_weights(*raw[:4], *weights)
    for index, table in enumerate(raw[4:]):
        tables[2 * index][...], tables[2 * index + 1][...] = halves(table[...])
    lane = lane_index((FIELDS, COLS))
    for row in range(TALL):
        here = rows_ref[row]
        start[row * FIELDS : (row + 1) * FIELDS] = first_input(here)
        strip = jnp.where(lane < 12, pltpu.roll(here, 4, 1), pltpu.roll(here, 20, 1))
        strips_ref[row] = jnp.where((lane >= 4) & (lane < 20), strip, 0.0)
    results = closure_layers(
        lambda chunk: start[2 * FIELDS * chunk : 2 * FIELDS * (chunk + 2)],
        TALL // 2 - 1,
        COLS,
        weights,
        (act_a, act_b),
        (mask_odd, mask_even),
    )
    for pair, closure in enumerate(results):
        for parity in range(2):
            row = FIRST + 2 * pair + parity
            out_ref[2 * pair + parity] = advance(
                rows_ref[row],
                rows_ref[row - 1],
                rows_ref[row + 1],
                closure[LEV * parity : LEV * (parity + 1)],
            )
    own_line = lane_index((LEV, COLS)) == lax.axis_index("lon") + FIRST
    kept = jnp.sum(jnp.where(own_line, cut_ref[...], 0.0), axis=1, keepdims=True)
    line_ref[...] = jnp.broadcast_to(kept, (LEV, COLS))


STRIP = 32
PER = COLS // STRIP


def edge_kernel(
    rows_ref, far_ref, near_ref, inside_ref, own_ref, w_in_ref, w_mid_ref, w_late_ref, w_out_ref,
    out_ref, planes_ref, strips, mask_odd, mask_even, act_a, act_b,
):
    lane = lane_index((FIELDS, COLS))
    even = lax.rem(lax.axis_index("lon"), 2) == 0
    parts = range(TALL // SLOTS)
    from_west = [jnp.where(even, far_ref[part], near_ref[part]) for part in parts]
    from_east = [jnp.where(even, near_ref[part], far_ref[part]) for part in parts]
    for row in range(TALL):
        part, slot = row // SLOTS, row % SLOTS
        west, east = from_west[part], from_east[part]
        west = pltpu.roll(west, COLS - HALO * slot, 1) if slot else west
        east = pltpu.roll(east, (20 - HALO * slot) % COLS, 1) if slot != 5 else east
        strip = jnp.where((lane >= 20) & (lane < 24), east, own_ref[row])
        strips[row] = jnp.where(lane < 4, west, strip)

    def side_by_side(parity, start):
        total = None
        for slot in range(PER):
            row = 2 * (start + slot) + parity
            if row >= TALL:
                continue
            piece = strips[row]
            piece = pltpu.roll(piece, STRIP * slot, 1) if slot else piece
            total = piece if total is None else total + piece
        return total

    def window(chunk):
        at = PER * chunk
        return jnp.concatenate(
            [
                first_input(block)
                for block in (
                    side_by_side(0, at),
                    side_by_side(1, at),
                    side_by_side(0, at + 1),
                    side_by_side(1, at + 1),
                )
            ],
            axis=0,
        )

    act_a[5 * COLS :] = jnp.zeros((COLS, COLS), jnp.bfloat16)
    act_b[5 * COLS :] = jnp.zeros((COLS, COLS), jnp.bfloat16)
    mask_odd[5 * COLS :] = jnp.zeros((COLS, COLS), jnp.float32)
    results = closure_layers(
        window,
        TALL // 2 - 1,
        STRIP,
        (w_in_ref, w_mid_ref, w_late_ref, w_out_ref),
        (act_a, act_b),
        (mask_odd, mask_even),
    )
    at_lane = lane_index((LEV, COLS))
    for chunk in range(4):
        at = PER * chunk + FIRST // 2
        closure = results[chunk]
        north = side_by_side(1, at - 1)
        upper = side_by_side(0, at)
        lower = side_by_side(1, at)
        south = side_by_side(0, at + 1)
        for parity, value in (
            (0, advance(upper, north, lower, closure[0:LEV])),
            (1, advance(lower, upper, south, closure[LEV : 2 * LEV])),
        ):
            for slot in range(PER):
                row = 2 * (PER * chunk + slot) + parity
                left = pltpu.roll(value, COLS - STRIP * slot - 4, 1)
                shift = (108 - STRIP * slot) % COLS
                right = pltpu.roll(value, shift, 1)
                out_ref[row] = jnp.where(
                    at_lane < HALO,
                    left,
                    jnp.where(at_lane >= COLS - HALO, right, inside_ref[row]),
                )
    plane_lane = lane_index((MID, COLS))
    for index, field in enumerate((KMT, HELM, FORCING)):
        moved = pltpu.roll(rows_ref[FIRST : FIRST + MID, field, :], HALO, 1)
        edge = strips[FIRST : FIRST + MID, field, :]
        planes_ref[index, :, 0:COLS] = jnp.where(plane_lane < HALO, edge, moved)
        planes_ref[index, :, COLS:] = jnp.where(
            plane_lane < HALO,
            moved,
            jnp.where(plane_lane < 2 * HALO, pltpu.roll(edge, COLS - 16, 1), 0.0),
        )


def filter_tables(blocks, width):
    length = blocks * width
    half = LEV // 2
    k = np.arange(blocks)
    outer = np.exp(-2j * np.pi * ((k[:, None] * k[None, :]) % blocks) / blocks)
    spread = np.zeros((blocks, 2, half, blocks, 2, half))
    for line in range(half):
        spread[:, 0, line, :, 0, line] = outer.real
        spread[:, 0, line, :, 1, line] = -outer.imag
        spread[:, 1, line, :, 0, line] = outer.imag
        spread[:, 1, line, :, 1, line] = outer.real
    spread = spread.reshape(blocks * LEV, blocks * LEV)
    m = np.arange(width)
    twist = np.exp(-2j * np.pi * (k[:, None] * m[None, :]) / length)
    sign = np.where(np.arange(LEV) < half, -1.0, 1.0)[None, :, None]
    twist_re = np.broadcast_to(twist.real[:, None, :], (blocks, LEV, width))
    twist_im = twist.imag[:, None, :] * sign
    inner = np.exp(-2j * np.pi * ((m[:, None] * m[None, :]) % width) / width)
    inner = np.concatenate([inner.real, inner.imag], axis=1)
    return [
        np.asarray(t, np.float32)
        for t in (spread, spread.T / length, inner, twist_re, twist_im)
    ]


def halves(x):
    high = x.astype(jnp.bfloat16)
    return high, (x - high.astype(jnp.float32)).astype(jnp.bfloat16)


def split_dot(a, b):
    def dot(x, y):
        return jnp.dot(x, y, preferred_element_type=jnp.float32)

    return dot(a[0], b[0]) + (dot(a[0], b[1]) + dot(a[1], b[0]))


def filter_kernel(
    x_ref, line_ref, spread_ref, spread_low, back_ref, back_low, inner_ref, inner_low,
    twist_re_ref, twist_im_ref, out_ref,
):
    blocks, lev, width = x_ref.shape
    shape = (blocks, lev, width)
    flat = (blocks * lev, width)
    length = blocks * width
    inner = (inner_ref[...], inner_low[...])

    def partner(block):
        return pltpu.roll(block, lev // 2, 1)

    sign = jnp.where(lax.broadcasted_iota(jnp.int32, shape, 1) < lev // 2, -1.0, 1.0)
    y = split_dot((spread_ref[...], spread_low[...]), halves(x_ref[...].reshape(flat)))
    y = y.reshape(shape)
    y = y * twist_re_ref[...] + partner(y) * twist_im_ref[...]
    s = split_dot(halves(y.reshape(flat)), inner)
    s = s[:, 0:width].reshape(shape) + partner(s[:, width:].reshape(shape)) * sign
    wave = lax.broadcasted_iota(jnp.int32, shape, 0) + blocks * lane_index(shape)
    folded = jnp.minimum(wave, length - wave).astype(jnp.float32)
    s = jnp.where(folded < line_ref[0:1, :][None], s, 0.0)
    y = split_dot(halves(s.reshape(flat)), inner)
    y = y[:, 0:width].reshape(shape) - partner(y[:, width:].reshape(shape)) * sign
    y = y * twist_re_ref[...] - partner(y) * twist_im_ref[...]
    x = split_dot((back_ref[...], back_low[...]), halves(y.reshape(flat))).reshape(shape)
    lane = lane_index((lev, width))
    moved = [pltpu.roll(x[block], HALO, 1) for block in range(blocks)]
    for block in range(blocks):
        edge = jnp.where(lane < HALO, moved[block - 1], moved[(block + 1) % blocks])
        edge = jnp.where(lane < 2 * HALO, edge, 0.0)
        edge = pltpu.roll(edge, 0, 1, stride=2 * HALO, stride_axis=0)
        row = BLOCK * block
        out_ref[row : row + lev, :] = x[block]
        out_ref[row + lev : row + BLOCK, :] = jnp.sum(edge, axis=0, keepdims=True)


def ends_kernel(x_ref, far_ref, near_ref):
    even = lax.rem(lax.axis_index("lon"), 2) == 0
    lane = lane_index((LEV, COLS))
    packed = []
    for row in range(MID):
        edge = jnp.where(lane < 2 * HALO, pltpu.roll(x_ref[row], HALO, 1), 0.0)
        edge = pltpu.roll(edge, 0, 1, stride=2 * HALO, stride_axis=0)
        packed.append(jnp.sum(edge, axis=0, keepdims=True))
    packed = jnp.concatenate(packed, axis=0)
    to_east = lax.rem(lane_index((MID, COLS)), 2 * HALO) < HALO
    last = jnp.where(to_east, packed, 0.0)
    first = jnp.where(to_east, 0.0, packed)
    far_ref[...] = jnp.where(even, first, last)
    near_ref[...] = jnp.where(even, last, first)


def plain_kernel(x_ref, far_ref, near_ref, out_ref):
    edge = far_ref[...] + near_ref[...]
    for row in range(MID):
        out_ref[BLOCK * row : BLOCK * row + LEV, :] = x_ref[row]
        out_ref[BLOCK * row + LEV : BLOCK * (row + 1), :] = edge[row : row + 1]


def two_sum(a, b):
    s = a + b
    t = s - a
    return s, (a - (s - t)) + (b - t)


def quick_sum(a, b):
    s = a + b
    return s, b - (s - a)


def split(a):
    c = a * 4097.0
    high = c - (c - a)
    return high, a - high


def two_product(a, b):
    p = a * b
    ah, al = split(a)
    bh, bl = split(b)
    return p, ((ah * bh - p) + ah * bl + al * bh) + al * bl


def pair_add(a, b):
    s, e = two_sum(a[0], b[0])
    return quick_sum(s, e + (a[1] + b[1]))


def pair_neg(a):
    return -a[0], -a[1]


def pair_mul(a, b):
    p, e = two_product(a[0], b[0])
    return quick_sum(p, e + (a[0] * b[1] + a[1] * b[0]))


def pair_inverse(a):
    x = 1.0 / a[0]
    p, e = two_product(a[0], x)
    return quick_sum(x, x * (((1.0 - p) - e) - a[1] * x))


def powers_kernel(x_ref, planes_ref, temp_hbm, powers_ref, parts_ref, temp, sem):
    for level in range(LEV):
        temp[level] = x_ref[pl.ds(HALO * BLOCK + level, ROWS, stride=BLOCK), :]
    move = pltpu.make_async_copy(temp, temp_hbm, sem)
    move.start()
    lane = lane_index((LEV, COLS))
    wide_lane = lane_index((MID, COLS))
    kmt_left = planes_ref[0, :, 0:COLS]
    kmt_right = planes_ref[0, :, COLS:]
    kmt = pltpu.roll(jnp.where(wide_lane < HALO, kmt_right, kmt_left), COLS - HALO, 1)
    mean = jnp.zeros((MID, COLS), jnp.float32)
    for level in range(LEV):
        here = x_ref[pl.ds(level, MID, stride=BLOCK), :]
        mean = mean + jnp.where(kmt > level, here, 0.0)
    edge = x_ref[pl.ds(LEV, MID, stride=BLOCK), :]
    edge_kmt = jnp.where(wide_lane < HALO, kmt_left, kmt_right)
    edge_kmt = jnp.where(wide_lane < 2 * HALO, edge_kmt, 0.0)
    for by in (8, 16, 32, 64):
        edge_kmt = edge_kmt + pltpu.roll(edge_kmt, by, 1)
    edge = jnp.where(edge_kmt > (wide_lane // (2 * HALO)).astype(jnp.float32), edge, 0.0)
    for by in (64, 32, 16, 8):
        edge = edge + pltpu.roll(edge, by, 1)
    moved = pltpu.roll(mean, HALO, 1)
    mean = jnp.concatenate(
        [
            jnp.where(wide_lane < HALO, edge, moved),
            jnp.where(wide_lane < HALO, moved, jnp.where(wide_lane < 2 * HALO, edge, 0.0)),
        ],
        axis=1,
    )
    sea = (planes_ref[0] > 0.0).astype(jnp.float32)

    def around(v):
        return (
            pltpu.roll(v, 1, 0)
            + pltpu.roll(v, MID - 1, 0)
            + pltpu.roll(v, 1, 1)
            + pltpu.roll(v, 2 * COLS - 1, 1)
        )

    diagonal = planes_ref[1] + sea * around(sea)
    powers = [sea * (mean * (1.0 / LEV) + planes_ref[2])]
    for _ in range(ITERS):
        v = powers[-1]
        powers.append((diagonal * v - sea * around(v)) * 0.125)
    row = lax.broadcasted_iota(jnp.int32, (MID, COLS), 0)
    inside = (row >= HALO) & (row < HALO + ROWS)
    owned = []
    for index, v in enumerate(powers):
        left, right = (pltpu.roll(v[:, k : k + COLS], COLS - HALO, 1) for k in (0, COLS))
        cut = jnp.where(wide_lane < COLS - HALO, left, right)
        powers_ref[index] = cut
        owned.append(jnp.where(inside, cut, 0.0))
    high_rows, low_rows = [], []
    for order in range(2 * ITERS):
        p, e = two_product(owned[order // 2], owned[order - order // 2])
        tiles = [(p[8 * i : 8 * i + 8], e[8 * i : 8 * i + 8]) for i in range(MID // 8)]
        while len(tiles) > 1:
            tiles = [pair_add(a, b) for a, b in zip(tiles[::2], tiles[1::2])]
        total = tiles[0]
        for by in (4, 2, 1):
            total = pair_add(total, tuple(pltpu.roll(t, by, 0) for t in total))
        high_rows.append(total[0])
        low_rows.append(total[1])
    where = lax.broadcasted_iota(jnp.int32, (8, COLS), 0)
    high, low = high_rows[0], low_rows[0]
    for order in range(1, 2 * ITERS):
        high = jnp.where(where == order, high_rows[order], high)
        low = jnp.where(where == order, low_rows[order], low)
    total = (high, low)
    for by in (64, 32, 16, 8, 4, 2, 1):
        total = pair_add(total, tuple(pltpu.roll(t, by, 1) for t in total))
    spot = lax.broadcasted_iota(jnp.int32, (8, COLS), 0)
    message = jnp.where(lane == spot, total[0], 0.0) + jnp.where(lane == spot + 64, total[1], 0.0)
    message = jnp.sum(message, axis=0, keepdims=True)
    parts_ref[...] = jnp.broadcast_to(message, parts_ref.shape)
    move.wait()


def sum_messages(parts_ref):
    count = parts_ref.shape[0] // 8
    tiles = [parts_ref[8 * i : 8 * i + 8, :] for i in range(count)]
    tiles = [two_sum(a, b) for a, b in zip(tiles[::2], tiles[1::2])]
    while len(tiles) > 1:
        tiles = [pair_add(a, b) for a, b in zip(tiles[::2], tiles[1::2])]
    total = tiles[0]
    for by in (4, 2, 1):
        total = pair_add(total, tuple(pltpu.roll(t, by, 0) for t in total))
    return pair_add(total, tuple(pltpu.roll(t, 64, 1) for t in total))


def merge_kernel(parts_ref, out_ref):
    total = sum_messages(parts_ref)
    lane = lane_index((8, COLS))
    merged = jnp.where(lane < 64, total[0], total[1])
    out_ref[...] = jnp.broadcast_to(merged[:1], out_ref.shape)


def combine_kernel(parts_ref, powers_ref, surface_ref, residual_ref, wide):
    total = sum_messages(parts_ref)
    moments = [
        tuple(jnp.broadcast_to(t[:, order : order + 1], (8, COLS)) for t in total)
        for order in range(2 * ITERS)
    ]
    rho = list(moments)
    delta = list(moments)
    one = jnp.ones((8, COLS), jnp.float32)
    zero = jnp.zeros((8, COLS), jnp.float32)
    res = [one] + [zero] * ITERS
    way = [one] + [zero] * ITERS
    sol = [zero] * ITERS
    for step in range(ITERS):
        inverse = pair_inverse(delta[step + 1])
        alpha = pair_mul(rho[step], inverse)
        sol = [s + alpha[0] * w for s, w in zip(sol, way)]
        res = [res[0]] + [r - alpha[0] * w for r, w in zip(res[1:], way)]
        if step == ITERS - 1:
            break
        last = 2 * ITERS - 1 - step
        rho = [
            None if order <= step or order >= last
            else pair_add(rho[order], pair_neg(pair_mul(alpha, delta[order + 1])))
            for order in range(2 * ITERS)
        ]
        beta = pair_neg(pair_mul(rho[step + 1], inverse))
        delta = [
            None if order <= step or order >= last
            else pair_add(rho[order], pair_mul(beta, delta[order]))
            for order in range(2 * ITERS)
        ]
        way = [r + beta[0] * w for r, w in zip(res, way)]
    for weights, target, factor in ((sol, surface_ref, 0.125), (res, residual_ref, 1.0)):
        for i in range(MID // 8):
            spot = slice(8 * i, 8 * i + 8)
            value = weights[0] * powers_ref[0, spot]
            for index in range(1, len(weights)):
                value = value + weights[index] * powers_ref[index, spot]
            wide[spot] = value * factor
        target[...] = wide[HALO : HALO + ROWS]


def swap_pair():
    return [(i, i ^ 1) for i in range(lax.axis_size("lat"))]


def swap_other(cross):
    pairs = [(i, i + 1) for i in range(3 if cross else 1, lax.axis_size("lat") - 1, 4)]
    return pairs + [(j, i) for i, j in pairs]


def reduction_groups(lon, lat):
    inner, outer = {}, {}
    for i in range(lon):
        for j in range(lat):
            inner.setdefault((i // 4, j // 4), []).append(i * lat + j)
            outer.setdefault((i % 4, j % 4), []).append(i * lat + j)
    return list(inner.values()), list(outer.values())


def swap_near():
    return [(i, i ^ 1) for i in range(lax.axis_size("lon"))]


def swap_far():
    count = lax.axis_size("lon")
    return [(i, (i + 1) % count if i % 2 else (i - 1) % count) for i in range(count)]


def body(temp, kmt, kappa, helm, forcing, cutoff, conv_in, conv_mid, conv_late, conv_out):
    f32 = jnp.float32
    shape = jax.ShapeDtypeStruct
    blocks = lax.axis_size("lon")
    bf16 = jnp.bfloat16
    vmem = pl.BlockSpec(memory_space=pltpu.VMEM)
    cutoff = cutoff.reshape(1, ROWS)
    fields = (temp, kmt, kappa, helm, forcing, cutoff)
    slab = shape((CUT + 1, DEEP, COLS), f32)
    to_pair, to_other, to_cross = pl.pallas_call(
        slab_kernel,
        out_shape=(slab, slab, slab),
        in_specs=[pl.BlockSpec(memory_space=pltpu.HBM)] * 6,
        out_specs=(vmem, vmem, vmem),
        scratch_shapes=(
            pltpu.VMEM((ROWS, COLS), jnp.int32),
            pltpu.VMEM((1, ROWS), jnp.int32),
            pltpu.SemaphoreType.DMA((10,)),
        ),
        compiler_params=pltpu.CompilerParams(vmem_limit_bytes=VMEM_LIMIT),
    )(*(pltpu.with_memory_space_constraint(field, pltpu.HBM) for field in fields))
    other = lax.ppermute(to_other, "lat", swap_other(False))
    pair = lax.ppermute(to_pair, "lat", swap_pair())
    cross = lax.ppermute(to_cross, "lat", swap_other(True))
    tables = tuple(jnp.asarray(table) for table in filter_tables(blocks, COLS))
    sources = (jnp.transpose(conv_in, (0, 2, 1)), conv_mid, conv_late, conv_out) + tables
    own, *raw = fetching(
        rows_kernel,
        (shape((ROWS, FIELDS, COLS), f32),)
        + tuple(shape(source.shape, source.dtype) for source in sources),
        fields + sources,
        fields,
    )
    ends = shape((TALL // SLOTS, FIELDS, COLS), f32)
    rows, to_far, to_near, cuts = call(
        pack_kernel, (shape((TALL, FIELDS, COLS), f32), ends, ends, shape((DEEP, COLS), f32))
    )(own, other, pair, cross)
    far = lax.ppermute(to_far, "lon", swap_far())
    near = lax.ppermute(to_near, "lon", swap_near())

    outs = (
        shape((4 * FIELDS, 640), bf16),
        shape((256, 384), bf16),
        shape((256, 384), bf16),
        shape((48, 256), bf16),
    )
    outs = outs + tuple(shape(table.shape, bf16) for table in tables[:3] for _ in range(2))
    def closure_scratch(chunks):
        cells = chunks * COLS
        return (
            pltpu.VMEM((cells, 128), f32),
            pltpu.VMEM((cells, 128), f32),
            pltpu.VMEM((cells, 128), bf16),
            pltpu.VMEM((cells, 128), bf16),
        )

    block = shape((MID, LEV, COLS), f32)
    inside, line, strips, *prepared = call(
        interior_kernel,
        (block, shape((LEV, COLS), f32), shape((TALL, FIELDS, COLS), f32)) + outs,
        (pltpu.VMEM((TALL * FIELDS, COLS), bf16),) + closure_scratch(19),
        10**9,
    )(rows, cuts, *raw[:7])
    weights, tables = prepared[:4], prepared[4:] + raw[7:]
    lines, planes = call(
        edge_kernel,
        (block, shape((3, MID, 2 * COLS), f32)),
        (pltpu.VMEM((TALL, FIELDS, COLS), f32),) + closure_scratch(6),
    )(rows, far, near, inside, strips, *weights)

    def filtered_block(lines, line, tables):
        whole = lax.all_to_all(lines, "lon", split_axis=0, concat_axis=0, tiled=True)
        result = call(filter_kernel, shape((BLOCK * blocks, COLS), f32))(whole, line, *tables)
        result = result.reshape(BLOCK * blocks, 1, COLS)
        result = lax.all_to_all(result, "lon", split_axis=0, concat_axis=0, tiled=True)
        return result.reshape(BLOCK * blocks, COLS)

    def plain_block(lines, line, tables):
        ends = shape((MID, COLS), f32)
        to_far, to_near = call(ends_kernel, (ends, ends))(lines)
        far = lax.ppermute(to_far, "lon", swap_far())
        near = lax.ppermute(to_near, "lon", swap_near())
        return call(plain_kernel, shape((BLOCK * MID, COLS), f32))(lines, far, near)

    top_row = lax.axis_index("lat") * ROWS - HALO
    polar = (top_row < BAND) | (top_row + MID > ROWS * lax.axis_size("lat") - BAND)
    back = lax.cond(polar, filtered_block, plain_block, lines, line, tables)
    everyone = blocks * lax.axis_size("lat")
    both = ("lon", "lat")
    inner, outer = reduction_groups(blocks, lax.axis_size("lat"))
    wide = len(inner[0])
    temp_new, powers, parts = pl.pallas_call(
        powers_kernel,
        out_shape=(
            shape((LEV, ROWS, COLS), f32),
            shape((ITERS + 1, MID, COLS), f32),
            shape((wide, COLS), f32),
        ),
        in_specs=[vmem] * 2,
        out_specs=(pl.BlockSpec(memory_space=pltpu.HBM), vmem, vmem),
        scratch_shapes=(pltpu.VMEM((LEV, ROWS, COLS), f32), pltpu.SemaphoreType.DMA),
        compiler_params=pltpu.CompilerParams(vmem_limit_bytes=VMEM_LIMIT),
    )(back, planes)
    parts = lax.all_to_all(
        parts, both, split_axis=0, concat_axis=0, tiled=True, axis_index_groups=inner
    )
    parts = call(merge_kernel, shape((everyone // wide, COLS), f32))(parts)
    parts = lax.all_to_all(
        parts, both, split_axis=0, concat_axis=0, tiled=True, axis_index_groups=outer
    )
    surface, residual = call(
        combine_kernel,
        (shape((ROWS, COLS), f32), shape((ROWS, COLS), f32)),
        (pltpu.VMEM((MID, COLS), f32),),
    )(parts, powers)
    return temp_new, surface, residual


def solution(mesh):
    return jax.shard_map(
        body,
        mesh=mesh,
        in_specs=(
            P(None, "lat", "lon"),
            P("lat", "lon"),
            P("lat", "lon"),
            P("lat", "lon"),
            P("lat", "lon"),
            P("lat"),
            P(),
            P(),
            P(),
            P(),
        ),
        out_specs=(P(None, "lat", "lon"), P("lat", "lon"), P("lat", "lon")),
        check_vma=False,
    )
```

```python
import math

import jax
import jax.numpy as jnp
import numpy as np
from jax import lax
from jax.experimental import pallas as pl
from jax.experimental.pallas import tpu as pltpu
from jax.sharding import PartitionSpec as P

ITERS = 4
STEP = 0.25
LEV = 8
FIELDS = 16
KMT, KAPPA, HELM, FORCING, CUT = 8, 9, 10, 11, 12
BAND = 48
HALO = 4
DEEP = 8
ROWS = 24
COLS = 128
TALL = ROWS + 2 * DEEP
MID = ROWS + 2 * HALO
BLOCK = LEV + 1
SLOTS = 20
VMEM_LIMIT = 48 * 1024 * 1024


def call(kernel, outs, scratch=(), flops=None):
    spec = pl.BlockSpec(memory_space=pltpu.VMEM)
    return pl.pallas_call(
        kernel,
        out_shape=outs,
        out_specs=jax.tree.map(lambda _: spec, outs),
        scratch_shapes=scratch,
        compiler_params=pltpu.CompilerParams(vmem_limit_bytes=VMEM_LIMIT),
    )


def lane_index(shape):
    return lax.broadcasted_iota(jnp.int32, shape, len(shape) - 1)


def fetching(kernel, outs, sources, held, rest=(), scratch=(), flops=10**6):
    spec = pl.BlockSpec(memory_space=pltpu.VMEM)
    return pl.pallas_call(
        kernel,
        out_shape=outs,
        in_specs=[pl.BlockSpec(memory_space=pltpu.HBM)] * len(sources),
        out_specs=jax.tree.map(lambda _: spec, outs),
        scratch_shapes=tuple(pltpu.VMEM(source.shape, source.dtype) for source in held)
        + (pltpu.SemaphoreType.DMA((len(sources),)),),
        compiler_params=pltpu.CompilerParams(vmem_limit_bytes=VMEM_LIMIT),
        cost_estimate=pl.CostEstimate(flops=10**6, bytes_accessed=2 * 10**6, transcendentals=0),
    )(*(pltpu.with_memory_space_constraint(source, pltpu.HBM) for source in sources))


def even_row():
    return lax.rem(lax.axis_index("lat"), 2) == 0


def slab_kernel(
    temp_hbm, kmt_hbm, kappa_hbm, helm_hbm, forcing_hbm, cutoff_hbm,
    pair_ref, other_ref, cross_ref, kmt, cutoff, sems,
):
    last = jnp.where(even_row(), ROWS - DEEP, 0)
    slabs = [
        (target, pl.multiple_of(start, DEEP))
        for target, start in ((pair_ref, last), (other_ref, ROWS - DEEP - last))
    ]
    pairs = [(kmt_hbm, kmt), (cutoff_hbm, cutoff)]
    for target, start in slabs:
        rows = pl.ds(start, DEEP)
        pairs.append((temp_hbm.at[:, rows], target.at[pl.ds(0, LEV)]))
        for source, field in ((kappa_hbm, KAPPA), (helm_hbm, HELM), (forcing_hbm, FORCING)):
            pairs.append((source.at[rows], target.at[field]))
    moves = fetch(*zip(*pairs), sems)
    for move in moves:
        move.wait()
    for target, start in slabs:
        target[KMT] = kmt[pl.ds(start, DEEP), :].astype(jnp.float32)
        target[CUT] = cutoff_lanes(cutoff)
    cross_ref[...] = other_ref[...]


def cutoff_lanes(cutoff_ref):
    line = cutoff_ref[...].astype(jnp.float32)
    line = jnp.concatenate([line, jnp.zeros((1, COLS - ROWS), jnp.float32)], axis=1)
    return jnp.broadcast_to(line, (DEEP, COLS))


def fetch(sources, targets, sems):
    moves = [
        pltpu.make_async_copy(source, target, sems.at[index])
        for index, (source, target) in enumerate(zip(sources, targets))
    ]
    for move in moves:
        move.start()
    return moves


def rows_kernel(*refs):
    sources, own_ref, raw, held, sems = refs[:15], refs[15], refs[16:25], refs[25:31], refs[31]
    moves = fetch(sources, tuple(held) + tuple(raw), sems)
    for move in moves[: len(held)]:
        move.wait()
    fill_rows(*held, own_ref)
    for move in moves[len(held) :]:
        move.wait()


def fill_rows(temp_ref, kmt_ref, kappa_ref, helm_ref, forcing_ref, cutoff_ref, own_ref):
    own_ref[:, CUT + 1 :, :] = jnp.zeros((ROWS, FIELDS - CUT - 1, COLS), jnp.float32)
    for level in range(LEV):
        own_ref[:, level, :] = temp_ref[level]
    own_ref[:, KMT, :] = kmt_ref[...].astype(jnp.float32)
    own_ref[:, KAPPA, :] = kappa_ref[...]
    own_ref[:, HELM, :] = helm_ref[...]
    own_ref[:, FORCING, :] = forcing_ref[...]
    own_ref[:, CUT, :] = jnp.broadcast_to(cutoff_lanes(cutoff_ref)[:1], (ROWS, COLS))


def fill_weights(
    first_ref, mid_ref, late_ref, last_ref, w_in_ref, w_mid_ref, w_late_ref, w_out_ref
):
    w_in_ref[...] = jnp.zeros(w_in_ref.shape, w_in_ref.dtype)
    width = mid_ref.shape[1]
    none = jnp.zeros((LEV, width), jnp.float32)
    for row in range(4):
        parts = []
        for tap in range(3):
            for parity in range(2):
                a = row - parity
                parts.append(first_ref[3 * a + tap].astype(jnp.float32) if 0 <= a < 3 else none)
        top = jnp.concatenate(parts, axis=1)
        marks = [jnp.ones((1, width), jnp.float32) if row == at else none[:1] for at in (1, 2, 2, 3)]
        marks = jnp.concatenate(marks, axis=1)
        block = jnp.concatenate(
            [
                jnp.concatenate([top, jnp.zeros((LEV, 4 * width), jnp.float32)], axis=1),
                jnp.concatenate(
                    [
                        jnp.concatenate([jnp.zeros((1, 6 * width), jnp.float32), marks], axis=1),
                        jnp.zeros((LEV - 1, 10 * width), jnp.float32),
                    ],
                    axis=0,
                ),
            ],
            axis=0,
        )
        w_in_ref[FIELDS * row : FIELDS * (row + 1)] = block.astype(jnp.bfloat16)

    def rows_of(ref, tap, parity):
        outs = ref.shape[1]
        blank = jnp.zeros((outs, width), jnp.float32)
        parts = []
        for row in range(4):
            a = row - parity
            parts.append(ref[3 * a + tap].astype(jnp.float32) if 0 <= a < 3 else blank)
        return jnp.concatenate(parts, axis=1)

    for ref, out_ref in ((mid_ref, w_mid_ref), (late_ref, w_late_ref)):
        for tap in range(3):
            both = jnp.concatenate([rows_of(ref, tap, 0), rows_of(ref, tap, 1)], axis=0)
            out_ref[:, 2 * width * tap : 2 * width * (tap + 1)] = both.T.astype(jnp.bfloat16)
    w_out_ref[...] = jnp.concatenate(
        [rows_of(last_ref, tap, parity) for tap in range(3) for parity in range(2)], axis=0
    ).astype(jnp.bfloat16)


def pack_kernel(
    own_ref, other_ref, pair_ref, cross_ref, rows_ref, far_ref, near_ref, cut_ref
):
    others = [other_ref[k] + cross_ref[k] for k in range(CUT + 1)]
    north = [jnp.where(even_row(), others[k], pair_ref[k]) for k in range(CUT + 1)]
    south = [jnp.where(even_row(), pair_ref[k], others[k]) for k in range(CUT + 1)]
    even = lax.rem(lax.axis_index("lon"), 2) == 0
    rows_ref[DEEP : DEEP + ROWS] = own_ref[...]
    for slab, start in ((north, 0), (south, DEEP + ROWS)):
        rows = slice(start, start + DEEP)
        rows_ref[rows, CUT + 1 :, :] = jnp.zeros((DEEP, FIELDS - CUT - 1, COLS), jnp.float32)
        for field in range(CUT + 1):
            rows_ref[rows, field, :] = slab[field]
    lane = lane_index((DEEP, COLS))
    north = pltpu.roll(north[CUT], COLS - (ROWS - DEEP), 1)
    south = pltpu.roll(south[CUT], DEEP + ROWS, 1)
    own = pltpu.roll(jnp.broadcast_to(own_ref[0, CUT : CUT + 1, :], (DEEP, COLS)), DEEP, 1)
    cut_ref[...] = jnp.where(lane < DEEP, north, jnp.where(lane < DEEP + ROWS, own, south))
    lane = lane_index((FIELDS, COLS))
    for part in range(TALL // SLOTS):
        first = jnp.zeros((FIELDS, COLS), jnp.float32)
        last = jnp.zeros((FIELDS, COLS), jnp.float32)
        for slot in range(SLOTS):
            here = rows_ref[part * SLOTS + slot]
            inside = (lane >= HALO * slot) & (lane < HALO * (slot + 1))
            first = jnp.where(inside, pltpu.roll(here, HALO * slot, 1) if slot else here, first)
            last = jnp.where(inside, pltpu.roll(here, HALO * (slot + 1), 1), last)
        far_ref[part] = jnp.where(even, first, last)
        near_ref[part] = jnp.where(even, last, first)


def closure_layers(window, pairs, stride, weights, acts, masks):
    w_in_ref, w_mid_ref, w_late_ref, w_out_ref = weights
    act_a, act_b = acts
    mask_odd, mask_even = masks

    def chunks(count):
        return range(-(-count * stride // COLS))

    def at(chunk, shift=0):
        return slice(COLS * chunk + shift, COLS * (chunk + 1) + shift)

    def both(act, chunk):
        return jnp.concatenate([act[at(chunk)], act[at(chunk, stride)]], axis=1)

    def finish(total, mask):
        v = (
            pltpu.roll(total[:, 0:128], 1, 0)
            + total[:, 128:256]
            + pltpu.roll(total[:, 256:384], COLS - 1, 0)
        )
        return (mask * (v / (1.0 + jnp.exp(-v)))).astype(jnp.bfloat16)

    for chunk in chunks(pairs):
        total = lax.dot_general(
            window(chunk),
            w_in_ref[...],
            (((0,), (0,)), ((), ())),
            preferred_element_type=jnp.float32,
        )
        mask_odd[at(chunk)] = total[:, 384:512]
        mask_even[at(chunk)] = total[:, 512:640]
        act_a[at(chunk)] = finish(total, total[:, 384:512])
    for chunk in chunks(pairs - 1):
        total = jnp.dot(both(act_a, chunk), w_mid_ref[...], preferred_element_type=jnp.float32)
        act_b[at(chunk)] = finish(total, mask_even[at(chunk)])
    for chunk in chunks(pairs - 2):
        total = jnp.dot(both(act_b, chunk), w_late_ref[...], preferred_element_type=jnp.float32)
        act_a[at(chunk)] = finish(total, mask_odd[at(chunk, stride)])
    results = []
    for chunk in chunks(pairs - 3):
        total = lax.dot_general(
            w_out_ref[...],
            both(act_a, chunk),
            (((1,), (1,)), ((), ())),
            preferred_element_type=jnp.float32,
        )
        results.append(
            pltpu.roll(total[0:16], 1, 1) + total[16:32] + pltpu.roll(total[32:48], COLS - 1, 1)
        )
    return results


def level_index():
    return lax.broadcasted_iota(jnp.int32, (LEV, COLS), 0).astype(jnp.float32)


def wetness(block):
    return (level_index() < block[KMT : KMT + 1]).astype(jnp.float32)


def first_input(block):
    wet = wetness(block)
    sea = jnp.where(level_index() == 0.0, wet, 0.0)
    return jnp.concatenate([wet * block[0:LEV], sea], axis=0).astype(jnp.bfloat16)


def advance(here, north, south, closure):
    wet = wetness(here)
    temp = here[0:LEV]
    tracer = wet * temp
    kappa = jnp.broadcast_to(here[KAPPA : KAPPA + 1], (LEV, COLS))
    diff = jnp.zeros((LEV, COLS), jnp.float32)
    for near in (south, north):
        near_w = wetness(near)
        diff = diff + near_w * 0.5 * (kappa + near[KAPPA : KAPPA + 1]) * (
            near_w * near[0:LEV] - tracer
        )
    for by in (COLS - 1, 1):
        diff = diff + pltpu.roll(wet, by, 1) * 0.5 * (kappa + pltpu.roll(kappa, by, 1)) * (
            pltpu.roll(tracer, by, 1) - tracer
        )
    diff = wet * diff
    eddy = wet * closure
    return wet * (temp + STEP * (diff + eddy))


FIRST = DEEP - HALO


def interior_kernel(*refs):
    rows_ref, cut_ref, raw, refs = refs[0], refs[1], refs[2:9], refs[9:]
    out_ref, line_ref, strips_ref, refs = refs[0], refs[1], refs[2], refs[3:]
    weights, tables, refs = refs[:4], refs[4:10], refs[10:]
    start, mask_odd, mask_even, act_a, act_b = refs
    fill_weights(*raw[:4], *weights)
    for index, table in enumerate(raw[4:]):
        tables[2 * index][...], tables[2 * index + 1][...] = halves(table[...])
    lane = lane_index((FIELDS, COLS))
    for row in range(TALL):
        here = rows_ref[row]
        start[row * FIELDS : (row + 1) * FIELDS] = first_input(here)
        strip = jnp.where(lane < 12, pltpu.roll(here, 4, 1), pltpu.roll(here, 20, 1))
        strips_ref[row] = jnp.where((lane >= 4) & (lane < 20), strip, 0.0)
    results = closure_layers(
        lambda chunk: start[2 * FIELDS * chunk : 2 * FIELDS * (chunk + 2)],
        TALL // 2 - 1,
        COLS,
        weights,
        (act_a, act_b),
        (mask_odd, mask_even),
    )
    for pair, closure in enumerate(results):
        for parity in range(2):
            row = FIRST + 2 * pair + parity
            out_ref[2 * pair + parity] = advance(
                rows_ref[row],
                rows_ref[row - 1],
                rows_ref[row + 1],
                closure[LEV * parity : LEV * (parity + 1)],
            )
    own_line = lane_index((LEV, COLS)) == lax.axis_index("lon") + FIRST
    kept = jnp.sum(jnp.where(own_line, cut_ref[...], 0.0), axis=1, keepdims=True)
    line_ref[...] = jnp.broadcast_to(kept, (LEV, COLS))


STRIP = 32
PER = COLS // STRIP


def edge_kernel(
    rows_ref, far_ref, near_ref, inside_ref, own_ref, w_in_ref, w_mid_ref, w_late_ref, w_out_ref,
    out_ref, planes_ref, strips, mask_odd, mask_even, act_a, act_b,
):
    lane = lane_index((FIELDS, COLS))
    even = lax.rem(lax.axis_index("lon"), 2) == 0
    parts = range(TALL // SLOTS)
    from_west = [jnp.where(even, far_ref[part], near_ref[part]) for part in parts]
    from_east = [jnp.where(even, near_ref[part], far_ref[part]) for part in parts]
    for row in range(TALL):
        part, slot = row // SLOTS, row % SLOTS
        west, east = from_west[part], from_east[part]
        west = pltpu.roll(west, COLS - HALO * slot, 1) if slot else west
        east = pltpu.roll(east, (20 - HALO * slot) % COLS, 1) if slot != 5 else east
        strip = jnp.where((lane >= 20) & (lane < 24), east, own_ref[row])
        strips[row] = jnp.where(lane < 4, west, strip)

    def side_by_side(parity, start):
        total = None
        for slot in range(PER):
            row = 2 * (start + slot) + parity
            if row >= TALL:
                continue
            piece = strips[row]
            piece = pltpu.roll(piece, STRIP * slot, 1) if slot else piece
            total = piece if total is None else total + piece
        return total

    def window(chunk):
        at = PER * chunk
        return jnp.concatenate(
            [
                first_input(block)
                for block in (
                    side_by_side(0, at),
                    side_by_side(1, at),
                    side_by_side(0, at + 1),
                    side_by_side(1, at + 1),
                )
            ],
            axis=0,
        )

    act_a[5 * COLS :] = jnp.zeros((COLS, COLS), jnp.bfloat16)
    act_b[5 * COLS :] = jnp.zeros((COLS, COLS), jnp.bfloat16)
    mask_odd[5 * COLS :] = jnp.zeros((COLS, COLS), jnp.float32)
    results = closure_layers(
        window,
        TALL // 2 - 1,
        STRIP,
        (w_in_ref, w_mid_ref, w_late_ref, w_out_ref),
        (act_a, act_b),
        (mask_odd, mask_even),
    )
    at_lane = lane_index((LEV, COLS))
    for chunk in range(4):
        at = PER * chunk + FIRST // 2
        closure = results[chunk]
        north = side_by_side(1, at - 1)
        upper = side_by_side(0, at)
        lower = side_by_side(1, at)
        south = side_by_side(0, at + 1)
        for parity, value in (
            (0, advance(upper, north, lower, closure[0:LEV])),
            (1, advance(lower, upper, south, closure[LEV : 2 * LEV])),
        ):
            for slot in range(PER):
                row = 2 * (PER * chunk + slot) + parity
                left = pltpu.roll(value, COLS - STRIP * slot - 4, 1)
                shift = (108 - STRIP * slot) % COLS
                right = pltpu.roll(value, shift, 1)
                out_ref[row] = jnp.where(
                    at_lane < HALO,
                    left,
                    jnp.where(at_lane >= COLS - HALO, right, inside_ref[row]),
                )
    plane_lane = lane_index((MID, COLS))
    for index, field in enumerate((KMT, HELM, FORCING)):
        moved = pltpu.roll(rows_ref[FIRST : FIRST + MID, field, :], HALO, 1)
        edge = strips[FIRST : FIRST + MID, field, :]
        planes_ref[index, :, 0:COLS] = jnp.where(plane_lane < HALO, edge, moved)
        planes_ref[index, :, COLS:] = jnp.where(
            plane_lane < HALO,
            moved,
            jnp.where(plane_lane < 2 * HALO, pltpu.roll(edge, COLS - 16, 1), 0.0),
        )


def filter_tables(blocks, width):
    length = blocks * width
    half = LEV // 2
    k = np.arange(blocks)
    outer = np.exp(-2j * np.pi * ((k[:, None] * k[None, :]) % blocks) / blocks)
    spread = np.zeros((blocks, 2, half, blocks, 2, half))
    for line in range(half):
        spread[:, 0, line, :, 0, line] = outer.real
        spread[:, 0, line, :, 1, line] = -outer.imag
        spread[:, 1, line, :, 0, line] = outer.imag
        spread[:, 1, line, :, 1, line] = outer.real
    spread = spread.reshape(blocks * LEV, blocks * LEV)
    m = np.arange(width)
    twist = np.exp(-2j * np.pi * (k[:, None] * m[None, :]) / length)
    sign = np.where(np.arange(LEV) < half, -1.0, 1.0)[None, :, None]
    twist_re = np.broadcast_to(twist.real[:, None, :], (blocks, LEV, width))
    twist_im = twist.imag[:, None, :] * sign
    inner = np.exp(-2j * np.pi * ((m[:, None] * m[None, :]) % width) / width)
    inner = np.concatenate([inner.real, inner.imag], axis=1)
    return [
        np.asarray(t, np.float32)
        for t in (spread, spread.T / length, inner, twist_re, twist_im)
    ]


def halves(x):
    high = x.astype(jnp.bfloat16)
    return high, (x - high.astype(jnp.float32)).astype(jnp.bfloat16)


def split_dot(a, b):
    def dot(x, y):
        return jnp.dot(x, y, preferred_element_type=jnp.float32)

    return dot(a[0], b[0]) + (dot(a[0], b[1]) + dot(a[1], b[0]))


def filter_kernel(
    x_ref, line_ref, spread_ref, spread_low, back_ref, back_low, inner_ref, inner_low,
    twist_re_ref, twist_im_ref, out_ref,
):
    blocks, lev, width = x_ref.shape
    shape = (blocks, lev, width)
    flat = (blocks * lev, width)
    length = blocks * width
    inner = (inner_ref[...], inner_low[...])

    def partner(block):
        return pltpu.roll(block, lev // 2, 1)

    sign = jnp.where(lax.broadcasted_iota(jnp.int32, shape, 1) < lev // 2, -1.0, 1.0)
    y = split_dot((spread_ref[...], spread_low[...]), halves(x_ref[...].reshape(flat)))
    y = y.reshape(shape)
    y = y * twist_re_ref[...] + partner(y) * twist_im_ref[...]
    s = split_dot(halves(y.reshape(flat)), inner)
    s = s[:, 0:width].reshape(shape) + partner(s[:, width:].reshape(shape)) * sign
    wave = lax.broadcasted_iota(jnp.int32, shape, 0) + blocks * lane_index(shape)
    folded = jnp.minimum(wave, length - wave).astype(jnp.float32)
    s = jnp.where(folded < line_ref[0:1, :][None], s, 0.0)
    y = split_dot(halves(s.reshape(flat)), inner)
    y = y[:, 0:width].reshape(shape) - partner(y[:, width:].reshape(shape)) * sign
    y = y * twist_re_ref[...] - partner(y) * twist_im_ref[...]
    x = split_dot((back_ref[...], back_low[...]), halves(y.reshape(flat))).reshape(shape)
    lane = lane_index((lev, width))
    moved = [pltpu.roll(x[block], HALO, 1) for block in range(blocks)]
    for block in range(blocks):
        edge = jnp.where(lane < HALO, moved[block - 1], moved[(block + 1) % blocks])
        edge = jnp.where(lane < 2 * HALO, edge, 0.0)
        edge = pltpu.roll(edge, 0, 1, stride=2 * HALO, stride_axis=0)
        row = BLOCK * block
        out_ref[row : row + lev, :] = x[block]
        out_ref[row + lev : row + BLOCK, :] = jnp.sum(edge, axis=0, keepdims=True)


def ends_kernel(x_ref, far_ref, near_ref):
    even = lax.rem(lax.axis_index("lon"), 2) == 0
    lane = lane_index((LEV, COLS))
    packed = []
    for row in range(MID):
        edge = jnp.where(lane < 2 * HALO, pltpu.roll(x_ref[row], HALO, 1), 0.0)
        edge = pltpu.roll(edge, 0, 1, stride=2 * HALO, stride_axis=0)
        packed.append(jnp.sum(edge, axis=0, keepdims=True))
    packed = jnp.concatenate(packed, axis=0)
    to_east = lax.rem(lane_index((MID, COLS)), 2 * HALO) < HALO
    last = jnp.where(to_east, packed, 0.0)
    first = jnp.where(to_east, 0.0, packed)
    far_ref[...] = jnp.where(even, first, last)
    near_ref[...] = jnp.where(even, last, first)


def plain_kernel(x_ref, far_ref, near_ref, out_ref):
    edge = far_ref[...] + near_ref[...]
    for row in range(MID):
        out_ref[BLOCK * row : BLOCK * row + LEV, :] = x_ref[row]
        out_ref[BLOCK * row + LEV : BLOCK * (row + 1), :] = edge[row : row + 1]


def two_sum(a, b):
    s = a + b
    t = s - a
    return s, (a - (s - t)) + (b - t)


def quick_sum(a, b):
    s = a + b
    return s, b - (s - a)


def split(a):
    c = a * 4097.0
    high = c - (c - a)
    return high, a - high


def two_product(a, b):
    p = a * b
    ah, al = split(a)
    bh, bl = split(b)
    return p, ((ah * bh - p) + ah * bl + al * bh) + al * bl


def pair_add(a, b):
    s, e = two_sum(a[0], b[0])
    return quick_sum(s, e + (a[1] + b[1]))


def pair_neg(a):
    return -a[0], -a[1]


def pair_mul(a, b):
    p, e = two_product(a[0], b[0])
    return quick_sum(p, e + (a[0] * b[1] + a[1] * b[0]))


def pair_inverse(a):
    x = 1.0 / a[0]
    p, e = two_product(a[0], x)
    return quick_sum(x, x * (((1.0 - p) - e) - a[1] * x))


def powers_kernel(x_ref, planes_ref, temp_hbm, powers_ref, parts_ref, temp, sem):
    for level in range(LEV):
        temp[level] = x_ref[pl.ds(HALO * BLOCK + level, ROWS, stride=BLOCK), :]
    move = pltpu.make_async_copy(temp, temp_hbm, sem)
    move.start()
    lane = lane_index((LEV, COLS))
    wide_lane = lane_index((MID, COLS))
    kmt_left = planes_ref[0, :, 0:COLS]
    kmt_right = planes_ref[0, :, COLS:]
    kmt = pltpu.roll(jnp.where(wide_lane < HALO, kmt_right, kmt_left), COLS - HALO, 1)
    mean = jnp.zeros((MID, COLS), jnp.float32)
    for level in range(LEV):
        here = x_ref[pl.ds(level, MID, stride=BLOCK), :]
        mean = mean + jnp.where(kmt > level, here, 0.0)
    edge = x_ref[pl.ds(LEV, MID, stride=BLOCK), :]
    edge_kmt = jnp.where(wide_lane < HALO, kmt_left, kmt_right)
    edge_kmt = jnp.where(wide_lane < 2 * HALO, edge_kmt, 0.0)
    for by in (8, 16, 32, 64):
        edge_kmt = edge_kmt + pltpu.roll(edge_kmt, by, 1)
    edge = jnp.where(edge_kmt > (wide_lane // (2 * HALO)).astype(jnp.float32), edge, 0.0)
    for by in (64, 32, 16, 8):
        edge = edge + pltpu.roll(edge, by, 1)
    moved = pltpu.roll(mean, HALO, 1)
    mean = jnp.concatenate(
        [
            jnp.where(wide_lane < HALO, edge, moved),
            jnp.where(wide_lane < HALO, moved, jnp.where(wide_lane < 2 * HALO, edge, 0.0)),
        ],
        axis=1,
    )
    sea = (planes_ref[0] > 0.0).astype(jnp.float32)

    def around(v):
        return (
            pltpu.roll(v, 1, 0)
            + pltpu.roll(v, MID - 1, 0)
            + pltpu.roll(v, 1, 1)
            + pltpu.roll(v, 2 * COLS - 1, 1)
        )

    diagonal = planes_ref[1] + sea * around(sea)
    powers = [sea * (mean * (1.0 / LEV) + planes_ref[2])]
    for _ in range(ITERS):
        v = powers[-1]
        powers.append((diagonal * v - sea * around(v)) * 0.125)
    row = lax.broadcasted_iota(jnp.int32, (MID, COLS), 0)
    inside = (row >= HALO) & (row < HALO + ROWS)
    owned = []
    for index, v in enumerate(powers):
        left, right = (pltpu.roll(v[:, k : k + COLS], COLS - HALO, 1) for k in (0, COLS))
        cut = jnp.where(wide_lane < COLS - HALO, left, right)
        powers_ref[index] = cut
        owned.append(jnp.where(inside, cut, 0.0))
    high_rows, low_rows = [], []
    for order in range(2 * ITERS):
        p, e = two_product(owned[order // 2], owned[order - order // 2])
        tiles = [(p[8 * i : 8 * i + 8], e[8 * i : 8 * i + 8]) for i in range(MID // 8)]
        while len(tiles) > 1:
            tiles = [pair_add(a, b) for a, b in zip(tiles[::2], tiles[1::2])]
        total = tiles[0]
        for by in (4, 2, 1):
            total = pair_add(total, tuple(pltpu.roll(t, by, 0) for t in total))
        high_rows.append(total[0])
        low_rows.append(total[1])
    where = lax.broadcasted_iota(jnp.int32, (8, COLS), 0)
    high, low = high_rows[0], low_rows[0]
    for order in range(1, 2 * ITERS):
        high = jnp.where(where == order, high_rows[order], high)
        low = jnp.where(where == order, low_rows[order], low)
    high, low = high.T, low.T
    tiles = [(high[8 * i : 8 * i + 8], low[8 * i : 8 * i + 8]) for i in range(COLS // 8)]
    while len(tiles) > 1:
        tiles = [pair_add(a, b) for a, b in zip(tiles[::2], tiles[1::2])]
    total = tiles[0]
    for by in (4, 2, 1):
        total = pair_add(total, tuple(pltpu.roll(t, by, 0) for t in total))
    gap = jnp.zeros((1, COLS // 2 - 2 * ITERS), jnp.float32)
    message = jnp.concatenate([total[0][:1], gap, total[1][:1], gap], axis=1)
    parts_ref[...] = jnp.broadcast_to(message, parts_ref.shape)
    move.wait()


def sum_messages(parts_ref):
    count = parts_ref.shape[0] // 8
    tiles = [parts_ref[8 * i : 8 * i + 8, :] for i in range(count)]
    tiles = [two_sum(a, b) for a, b in zip(tiles[::2], tiles[1::2])]
    while len(tiles) > 1:
        tiles = [pair_add(a, b) for a, b in zip(tiles[::2], tiles[1::2])]
    total = tiles[0]
    for by in (4, 2, 1):
        total = pair_add(total, tuple(pltpu.roll(t, by, 0) for t in total))
    return pair_add(total, tuple(pltpu.roll(t, 64, 1) for t in total))


def merge_kernel(parts_ref, out_ref):
    total = sum_messages(parts_ref)
    lane = lane_index((8, COLS))
    merged = jnp.where(lane < 64, total[0], total[1])
    out_ref[...] = jnp.broadcast_to(merged[:1], out_ref.shape)


def combine_kernel(parts_ref, powers_ref, surface_ref, residual_ref, wide):
    total = sum_messages(parts_ref)
    moments = [
        tuple(jnp.broadcast_to(t[:, order : order + 1], (8, COLS)) for t in total)
        for order in range(2 * ITERS)
    ]
    rho = list(moments)
    delta = list(moments)
    one = jnp.ones((8, COLS), jnp.float32)
    zero = jnp.zeros((8, COLS), jnp.float32)
    res = [one] + [zero] * ITERS
    way = [one] + [zero] * ITERS
    sol = [zero] * ITERS
    for step in range(ITERS):
        inverse = pair_inverse(delta[step + 1])
        alpha = pair_mul(rho[step], inverse)
        sol = [s + alpha[0] * w for s, w in zip(sol, way)]
        res = [res[0]] + [r - alpha[0] * w for r, w in zip(res[1:], way)]
        if step == ITERS - 1:
            break
        last = 2 * ITERS - 1 - step
        rho = [
            None if order <= step or order >= last
            else pair_add(rho[order], pair_neg(pair_mul(alpha, delta[order + 1])))
            for order in range(2 * ITERS)
        ]
        beta = pair_neg(pair_mul(rho[step + 1], inverse))
        delta = [
            None if order <= step or order >= last
            else pair_add(rho[order], pair_mul(beta, delta[order]))
            for order in range(2 * ITERS)
        ]
        way = [r + beta[0] * w for r, w in zip(res, way)]
    for weights, target, factor in ((sol, surface_ref, 0.125), (res, residual_ref, 1.0)):
        for i in range(MID // 8):
            spot = slice(8 * i, 8 * i + 8)
            value = weights[0] * powers_ref[0, spot]
            for index in range(1, len(weights)):
                value = value + weights[index] * powers_ref[index, spot]
            wide[spot] = value * factor
        target[...] = wide[HALO : HALO + ROWS]


def swap_pair():
    return [(i, i ^ 1) for i in range(lax.axis_size("lat"))]


def swap_other(cross):
    pairs = [(i, i + 1) for i in range(3 if cross else 1, lax.axis_size("lat") - 1, 4)]
    return pairs + [(j, i) for i, j in pairs]


def reduction_groups(lon, lat):
    inner, outer = {}, {}
    for i in range(lon):
        for j in range(lat):
            inner.setdefault((i // 4, j // 4), []).append(i * lat + j)
            outer.setdefault((i % 4, j % 4), []).append(i * lat + j)
    return list(inner.values()), list(outer.values())


def swap_near():
    return [(i, i ^ 1) for i in range(lax.axis_size("lon"))]


def swap_far():
    count = lax.axis_size("lon")
    return [(i, (i + 1) % count if i % 2 else (i - 1) % count) for i in range(count)]


def body(temp, kmt, kappa, helm, forcing, cutoff, conv_in, conv_mid, conv_late, conv_out):
    f32 = jnp.float32
    shape = jax.ShapeDtypeStruct
    blocks = lax.axis_size("lon")
    bf16 = jnp.bfloat16
    vmem = pl.BlockSpec(memory_space=pltpu.VMEM)
    cutoff = cutoff.reshape(1, ROWS)
    fields = (temp, kmt, kappa, helm, forcing, cutoff)
    slab = shape((CUT + 1, DEEP, COLS), f32)
    to_pair, to_other, to_cross = pl.pallas_call(
        slab_kernel,
        out_shape=(slab, slab, slab),
        in_specs=[pl.BlockSpec(memory_space=pltpu.HBM)] * 6,
        out_specs=(vmem, vmem, vmem),
        scratch_shapes=(
            pltpu.VMEM((ROWS, COLS), jnp.int32),
            pltpu.VMEM((1, ROWS), jnp.int32),
            pltpu.SemaphoreType.DMA((10,)),
        ),
        compiler_params=pltpu.CompilerParams(vmem_limit_bytes=VMEM_LIMIT),
    )(*(pltpu.with_memory_space_constraint(field, pltpu.HBM) for field in fields))
    other = lax.ppermute(to_other, "lat", swap_other(False))
    pair = lax.ppermute(to_pair, "lat", swap_pair())
    cross = lax.ppermute(to_cross, "lat", swap_other(True))
    tables = tuple(jnp.asarray(table) for table in filter_tables(blocks, COLS))
    sources = (jnp.transpose(conv_in, (0, 2, 1)), conv_mid, conv_late, conv_out) + tables
    own, *raw = fetching(
        rows_kernel,
        (shape((ROWS, FIELDS, COLS), f32),)
        + tuple(shape(source.shape, source.dtype) for source in sources),
        fields + sources,
        fields,
    )
    ends = shape((TALL // SLOTS, FIELDS, COLS), f32)
    rows, to_far, to_near, cuts = call(
        pack_kernel, (shape((TALL, FIELDS, COLS), f32), ends, ends, shape((DEEP, COLS), f32))
    )(own, other, pair, cross)
    far = lax.ppermute(to_far, "lon", swap_far())
    near = lax.ppermute(to_near, "lon", swap_near())

    outs = (
        shape((4 * FIELDS, 640), bf16),
        shape((256, 384), bf16),
        shape((256, 384), bf16),
        shape((48, 256), bf16),
    )
    outs = outs + tuple(shape(table.shape, bf16) for table in tables[:3] for _ in range(2))
    def closure_scratch(chunks):
        cells = chunks * COLS
        return (
            pltpu.VMEM((cells, 128), f32),
            pltpu.VMEM((cells, 128), f32),
            pltpu.VMEM((cells, 128), bf16),
            pltpu.VMEM((cells, 128), bf16),
        )

    block = shape((MID, LEV, COLS), f32)
    inside, line, strips, *prepared = call(
        interior_kernel,
        (block, shape((LEV, COLS), f32), shape((TALL, FIELDS, COLS), f32)) + outs,
        (pltpu.VMEM((TALL * FIELDS, COLS), bf16),) + closure_scratch(19),
        10**9,
    )(rows, cuts, *raw[:7])
    weights, tables = prepared[:4], prepared[4:] + raw[7:]
    lines, planes = call(
        edge_kernel,
        (block, shape((3, MID, 2 * COLS), f32)),
        (pltpu.VMEM((TALL, FIELDS, COLS), f32),) + closure_scratch(6),
    )(rows, far, near, inside, strips, *weights)

    def filtered_block(lines, line, tables):
        whole = lax.all_to_all(lines, "lon", split_axis=0, concat_axis=0, tiled=True)
        result = call(filter_kernel, shape((BLOCK * blocks, COLS), f32))(whole, line, *tables)
        result = result.reshape(BLOCK * blocks, 1, COLS)
        result = lax.all_to_all(result, "lon", split_axis=0, concat_axis=0, tiled=True)
        return result.reshape(BLOCK * blocks, COLS)

    def plain_block(lines, line, tables):
        ends = shape((MID, COLS), f32)
        to_far, to_near = call(ends_kernel, (ends, ends))(lines)
        far = lax.ppermute(to_far, "lon", swap_far())
        near = lax.ppermute(to_near, "lon", swap_near())
        return call(plain_kernel, shape((BLOCK * MID, COLS), f32))(lines, far, near)

    top_row = lax.axis_index("lat") * ROWS - HALO
    polar = (top_row < BAND) | (top_row + MID > ROWS * lax.axis_size("lat") - BAND)
    back = lax.cond(polar, filtered_block, plain_block, lines, line, tables)
    everyone = blocks * lax.axis_size("lat")
    both = ("lon", "lat")
    inner, outer = reduction_groups(blocks, lax.axis_size("lat"))
    wide = len(inner[0])
    temp_new, powers, parts = pl.pallas_call(
        powers_kernel,
        out_shape=(
            shape((LEV, ROWS, COLS), f32),
            shape((ITERS + 1, MID, COLS), f32),
            shape((wide, COLS), f32),
        ),
        in_specs=[vmem] * 2,
        out_specs=(pl.BlockSpec(memory_space=pltpu.HBM), vmem, vmem),
        scratch_shapes=(pltpu.VMEM((LEV, ROWS, COLS), f32), pltpu.SemaphoreType.DMA),
        compiler_params=pltpu.CompilerParams(vmem_limit_bytes=VMEM_LIMIT),
    )(back, planes)
    parts = lax.all_to_all(
        parts, both, split_axis=0, concat_axis=0, tiled=True, axis_index_groups=inner
    )
    parts = call(merge_kernel, shape((everyone // wide, COLS), f32))(parts)
    parts = lax.all_to_all(
        parts, both, split_axis=0, concat_axis=0, tiled=True, axis_index_groups=outer
    )
    surface, residual = call(
        combine_kernel,
        (shape((ROWS, COLS), f32), shape((ROWS, COLS), f32)),
        (pltpu.VMEM((MID, COLS), f32),),
    )(parts, powers)
    return temp_new, surface, residual


def solution(mesh):
    return jax.shard_map(
        body,
        mesh=mesh,
        in_specs=(
            P(None, "lat", "lon"),
            P("lat", "lon"),
            P("lat", "lon"),
            P("lat", "lon"),
            P("lat", "lon"),
            P("lat"),
            P(),
            P(),
            P(),
            P(),
        ),
        out_specs=(P(None, "lat", "lon"), P("lat", "lon"), P("lat", "lon")),
        check_vma=False,
    )
```

```python
import math

import jax
import jax.numpy as jnp
import numpy as np
from jax import lax
from jax.experimental import pallas as pl
from jax.experimental.pallas import tpu as pltpu
from jax.sharding import PartitionSpec as P

ITERS = 4
STEP = 0.25
LEV = 8
FIELDS = 16
KMT, KAPPA, HELM, FORCING, CUT = 8, 9, 10, 11, 12
BAND = 48
HALO = 4
DEEP = 8
ROWS = 24
COLS = 128
TALL = ROWS + 2 * DEEP
MID = ROWS + 2 * HALO
BLOCK = LEV + 1
SLOTS = 20
VMEM_LIMIT = 48 * 1024 * 1024


def call(kernel, outs, scratch=(), flops=None):
    spec = pl.BlockSpec(memory_space=pltpu.VMEM)
    return pl.pallas_call(
        kernel,
        out_shape=outs,
        out_specs=jax.tree.map(lambda _: spec, outs),
        scratch_shapes=scratch,
        compiler_params=pltpu.CompilerParams(vmem_limit_bytes=VMEM_LIMIT),
    )


def lane_index(shape):
    return lax.broadcasted_iota(jnp.int32, shape, len(shape) - 1)


def fetching(kernel, outs, sources, held, rest=(), scratch=(), flops=10**6):
    spec = pl.BlockSpec(memory_space=pltpu.VMEM)
    return pl.pallas_call(
        kernel,
        out_shape=outs,
        in_specs=[pl.BlockSpec(memory_space=pltpu.HBM)] * len(sources),
        out_specs=jax.tree.map(lambda _: spec, outs),
        scratch_shapes=tuple(pltpu.VMEM(source.shape, source.dtype) for source in held)
        + (pltpu.SemaphoreType.DMA((len(sources),)),),
        compiler_params=pltpu.CompilerParams(vmem_limit_bytes=VMEM_LIMIT),
        cost_estimate=pl.CostEstimate(flops=10**6, bytes_accessed=2 * 10**6, transcendentals=0),
    )(*(pltpu.with_memory_space_constraint(source, pltpu.HBM) for source in sources))


def even_row():
    return lax.rem(lax.axis_index("lat"), 2) == 0


def slab_kernel(
    temp_hbm, kmt_hbm, kappa_hbm, helm_hbm, forcing_hbm, cutoff_hbm,
    pair_ref, other_ref, cross_ref, kmt, cutoff, sems,
):
    last = jnp.where(even_row(), ROWS - DEEP, 0)
    slabs = [
        (target, pl.multiple_of(start, DEEP))
        for target, start in ((pair_ref, last), (other_ref, ROWS - DEEP - last))
    ]
    pairs = [(kmt_hbm, kmt), (cutoff_hbm, cutoff)]
    for target, start in slabs:
        rows = pl.ds(start, DEEP)
        pairs.append((temp_hbm.at[:, rows], target.at[pl.ds(0, LEV)]))
        for source, field in ((kappa_hbm, KAPPA), (helm_hbm, HELM), (forcing_hbm, FORCING)):
            pairs.append((source.at[rows], target.at[field]))
    moves = fetch(*zip(*pairs), sems)
    for move in moves:
        move.wait()
    for target, start in slabs:
        target[KMT] = kmt[pl.ds(start, DEEP), :].astype(jnp.float32)
        target[CUT] = cutoff_lanes(cutoff)
    cross_ref[...] = other_ref[...]


def cutoff_lanes(cutoff_ref):
    line = cutoff_ref[...].astype(jnp.float32)
    line = jnp.concatenate([line, jnp.zeros((1, COLS - ROWS), jnp.float32)], axis=1)
    return jnp.broadcast_to(line, (DEEP, COLS))


def fetch(sources, targets, sems):
    moves = [
        pltpu.make_async_copy(source, target, sems.at[index])
        for index, (source, target) in enumerate(zip(sources, targets))
    ]
    for move in moves:
        move.start()
    return moves


def rows_kernel(*refs):
    sources, own_ref, raw, held, sems = refs[:15], refs[15], refs[16:25], refs[25:31], refs[31]
    moves = fetch(sources, tuple(held) + tuple(raw), sems)
    for move in moves[: len(held)]:
        move.wait()
    fill_rows(*held, own_ref)
    for move in moves[len(held) :]:
        move.wait()


def fill_rows(temp_ref, kmt_ref, kappa_ref, helm_ref, forcing_ref, cutoff_ref, own_ref):
    own_ref[:, CUT + 1 :, :] = jnp.zeros((ROWS, FIELDS - CUT - 1, COLS), jnp.float32)
    for level in range(LEV):
        own_ref[:, level, :] = temp_ref[level]
    own_ref[:, KMT, :] = kmt_ref[...].astype(jnp.float32)
    own_ref[:, KAPPA, :] = kappa_ref[...]
    own_ref[:, HELM, :] = helm_ref[...]
    own_ref[:, FORCING, :] = forcing_ref[...]
    own_ref[:, CUT, :] = jnp.broadcast_to(cutoff_lanes(cutoff_ref)[:1], (ROWS, COLS))


def fill_weights(
    first_ref, mid_ref, late_ref, last_ref, w_in_ref, w_mid_ref, w_late_ref, w_out_ref
):
    w_in_ref[...] = jnp.zeros(w_in_ref.shape, w_in_ref.dtype)
    width = mid_ref.shape[1]
    none = jnp.zeros((LEV, width), jnp.float32)
    for row in range(4):
        parts = []
        for tap in range(3):
            for parity in range(2):
                a = row - parity
                parts.append(first_ref[3 * a + tap].astype(jnp.float32) if 0 <= a < 3 else none)
        top = jnp.concatenate(parts, axis=1)
        marks = [jnp.ones((1, width), jnp.float32) if row == at else none[:1] for at in (1, 2, 2, 3)]
        marks = jnp.concatenate(marks, axis=1)
        block = jnp.concatenate(
            [
                jnp.concatenate([top, jnp.zeros((LEV, 4 * width), jnp.float32)], axis=1),
                jnp.concatenate(
                    [
                        jnp.concatenate([jnp.zeros((1, 6 * width), jnp.float32), marks], axis=1),
                        jnp.zeros((LEV - 1, 10 * width), jnp.float32),
                    ],
                    axis=0,
                ),
            ],
            axis=0,
        )
        w_in_ref[FIELDS * row : FIELDS * (row + 1)] = block.astype(jnp.bfloat16)

    def rows_of(ref, tap, parity):
        outs = ref.shape[1]
        blank = jnp.zeros((outs, width), jnp.float32)
        parts = []
        for row in range(4):
            a = row - parity
            parts.append(ref[3 * a + tap].astype(jnp.float32) if 0 <= a < 3 else blank)
        return jnp.concatenate(parts, axis=1)

    for ref, out_ref in ((mid_ref, w_mid_ref), (late_ref, w_late_ref)):
        for tap in range(3):
            both = jnp.concatenate([rows_of(ref, tap, 0), rows_of(ref, tap, 1)], axis=0)
            out_ref[:, 2 * width * tap : 2 * width * (tap + 1)] = both.T.astype(jnp.bfloat16)
    w_out_ref[...] = jnp.concatenate(
        [rows_of(last_ref, tap, parity) for tap in range(3) for parity in range(2)], axis=0
    ).astype(jnp.bfloat16)


def pack_kernel(
    own_ref, other_ref, pair_ref, cross_ref, rows_ref, far_ref, near_ref, cut_ref
):
    others = [other_ref[k] + cross_ref[k] for k in range(CUT + 1)]
    north = [jnp.where(even_row(), others[k], pair_ref[k]) for k in range(CUT + 1)]
    south = [jnp.where(even_row(), pair_ref[k], others[k]) for k in range(CUT + 1)]
    even = lax.rem(lax.axis_index("lon"), 2) == 0
    rows_ref[DEEP : DEEP + ROWS] = own_ref[...]
    for slab, start in ((north, 0), (south, DEEP + ROWS)):
        rows = slice(start, start + DEEP)
        rows_ref[rows, CUT + 1 :, :] = jnp.zeros((DEEP, FIELDS - CUT - 1, COLS), jnp.float32)
        for field in range(CUT + 1):
            rows_ref[rows, field, :] = slab[field]
    lane = lane_index((DEEP, COLS))
    north = pltpu.roll(north[CUT], COLS - (ROWS - DEEP), 1)
    south = pltpu.roll(south[CUT], DEEP + ROWS, 1)
    own = pltpu.roll(jnp.broadcast_to(own_ref[0, CUT : CUT + 1, :], (DEEP, COLS)), DEEP, 1)
    cut_ref[...] = jnp.where(lane < DEEP, north, jnp.where(lane < DEEP + ROWS, own, south))
    lane = lane_index((FIELDS, COLS))
    for part in range(TALL // SLOTS):
        first = jnp.zeros((FIELDS, COLS), jnp.float32)
        last = jnp.zeros((FIELDS, COLS), jnp.float32)
        for slot in range(SLOTS):
            here = rows_ref[part * SLOTS + slot]
            inside = (lane >= HALO * slot) & (lane < HALO * (slot + 1))
            first = jnp.where(inside, pltpu.roll(here, HALO * slot, 1) if slot else here, first)
            last = jnp.where(inside, pltpu.roll(here, HALO * (slot + 1), 1), last)
        far_ref[part] = jnp.where(even, first, last)
        near_ref[part] = jnp.where(even, last, first)


def closure_layers(window, pairs, stride, weights, acts, masks):
    w_in_ref, w_mid_ref, w_late_ref, w_out_ref = weights
    act_a, act_b = acts
    mask_odd, mask_even = masks

    def chunks(count):
        return range(-(-count * stride // COLS))

    def at(chunk, shift=0):
        return slice(COLS * chunk + shift, COLS * (chunk + 1) + shift)

    def both(act, chunk):
        return jnp.concatenate([act[at(chunk)], act[at(chunk, stride)]], axis=1)

    def finish(total, mask):
        v = (
            pltpu.roll(total[:, 0:128], 1, 0)
            + total[:, 128:256]
            + pltpu.roll(total[:, 256:384], COLS - 1, 0)
        )
        return (mask * (v / (1.0 + jnp.exp(-v)))).astype(jnp.bfloat16)

    for chunk in chunks(pairs):
        total = lax.dot_general(
            window(chunk),
            w_in_ref[...],
            (((0,), (0,)), ((), ())),
            preferred_element_type=jnp.float32,
        )
        mask_odd[at(chunk)] = total[:, 384:512]
        mask_even[at(chunk)] = total[:, 512:640]
        act_a[at(chunk)] = finish(total, total[:, 384:512])
    for chunk in chunks(pairs - 1):
        total = jnp.dot(both(act_a, chunk), w_mid_ref[...], preferred_element_type=jnp.float32)
        act_b[at(chunk)] = finish(total, mask_even[at(chunk)])
    for chunk in chunks(pairs - 2):
        total = jnp.dot(both(act_b, chunk), w_late_ref[...], preferred_element_type=jnp.float32)
        act_a[at(chunk)] = finish(total, mask_odd[at(chunk, stride)])
    results = []
    for chunk in chunks(pairs - 3):
        total = lax.dot_general(
            w_out_ref[...],
            both(act_a, chunk),
            (((1,), (1,)), ((), ())),
            preferred_element_type=jnp.float32,
        )
        results.append(
            pltpu.roll(total[0:16], 1, 1) + total[16:32] + pltpu.roll(total[32:48], COLS - 1, 1)
        )
    return results


def level_index():
    return lax.broadcasted_iota(jnp.int32, (LEV, COLS), 0).astype(jnp.float32)


def wetness(block):
    return (level_index() < block[KMT : KMT + 1]).astype(jnp.float32)


def first_input(block):
    wet = wetness(block)
    sea = jnp.where(level_index() == 0.0, wet, 0.0)
    return jnp.concatenate([wet * block[0:LEV], sea], axis=0).astype(jnp.bfloat16)


def advance(here, north, south, closure):
    wet = wetness(here)
    temp = here[0:LEV]
    tracer = wet * temp
    kappa = jnp.broadcast_to(here[KAPPA : KAPPA + 1], (LEV, COLS))
    diff = jnp.zeros((LEV, COLS), jnp.float32)
    for near in (south, north):
        near_w = wetness(near)
        diff = diff + near_w * 0.5 * (kappa + near[KAPPA : KAPPA + 1]) * (
            near_w * near[0:LEV] - tracer
        )
    for by in (COLS - 1, 1):
        diff = diff + pltpu.roll(wet, by, 1) * 0.5 * (kappa + pltpu.roll(kappa, by, 1)) * (
            pltpu.roll(tracer, by, 1) - tracer
        )
    diff = wet * diff
    eddy = wet * closure
    return wet * (temp + STEP * (diff + eddy))


FIRST = DEEP - HALO


def interior_kernel(*refs):
    rows_ref, cut_ref, raw, refs = refs[0], refs[1], refs[2:9], refs[9:]
    out_ref, line_ref, strips_ref, refs = refs[0], refs[1], refs[2], refs[3:]
    weights, tables, refs = refs[:4], refs[4:10], refs[10:]
    start, mask_odd, mask_even, act_a, act_b = refs
    fill_weights(*raw[:4], *weights)
    for index, table in enumerate(raw[4:]):
        tables[2 * index][...], tables[2 * index + 1][...] = halves(table[...])
    lane = lane_index((FIELDS, COLS))
    for row in range(TALL):
        here = rows_ref[row]
        start[row * FIELDS : (row + 1) * FIELDS] = first_input(here)
        strip = jnp.where(lane < 12, pltpu.roll(here, 4, 1), pltpu.roll(here, 20, 1))
        strips_ref[row] = jnp.where((lane >= 4) & (lane < 20), strip, 0.0)
    results = closure_layers(
        lambda chunk: start[2 * FIELDS * chunk : 2 * FIELDS * (chunk + 2)],
        TALL // 2 - 1,
        COLS,
        weights,
        (act_a, act_b),
        (mask_odd, mask_even),
    )
    for pair, closure in enumerate(results):
        for parity in range(2):
            row = FIRST + 2 * pair + parity
            out_ref[2 * pair + parity] = advance(
                rows_ref[row],
                rows_ref[row - 1],
                rows_ref[row + 1],
                closure[LEV * parity : LEV * (parity + 1)],
            )
    own_line = lane_index((LEV, COLS)) == lax.axis_index("lon") + FIRST
    kept = jnp.sum(jnp.where(own_line, cut_ref[...], 0.0), axis=1, keepdims=True)
    line_ref[...] = jnp.broadcast_to(kept, (LEV, COLS))


STRIP = 32
PER = COLS // STRIP


def edge_kernel(
    rows_ref, far_ref, near_ref, inside_ref, own_ref, w_in_ref, w_mid_ref, w_late_ref, w_out_ref,
    out_ref, planes_ref, strips, mask_odd, mask_even, act_a, act_b,
):
    lane = lane_index((FIELDS, COLS))
    even = lax.rem(lax.axis_index("lon"), 2) == 0
    parts = range(TALL // SLOTS)
    from_west = [jnp.where(even, far_ref[part], near_ref[part]) for part in parts]
    from_east = [jnp.where(even, near_ref[part], far_ref[part]) for part in parts]
    for row in range(TALL):
        part, slot = row // SLOTS, row % SLOTS
        west, east = from_west[part], from_east[part]
        west = pltpu.roll(west, COLS - HALO * slot, 1) if slot else west
        east = pltpu.roll(east, (20 - HALO * slot) % COLS, 1) if slot != 5 else east
        strip = jnp.where((lane >= 20) & (lane < 24), east, own_ref[row])
        strips[row] = jnp.where(lane < 4, west, strip)

    def side_by_side(parity, start):
        total = None
        for slot in range(PER):
            row = 2 * (start + slot) + parity
            if row >= TALL:
                continue
            piece = strips[row]
            piece = pltpu.roll(piece, STRIP * slot, 1) if slot else piece
            total = piece if total is None else total + piece
        return total

    def window(chunk):
        at = PER * chunk
        return jnp.concatenate(
            [
                first_input(block)
                for block in (
                    side_by_side(0, at),
                    side_by_side(1, at),
                    side_by_side(0, at + 1),
                    side_by_side(1, at + 1),
                )
            ],
            axis=0,
        )

    act_a[5 * COLS :] = jnp.zeros((COLS, COLS), jnp.bfloat16)
    act_b[5 * COLS :] = jnp.zeros((COLS, COLS), jnp.bfloat16)
    mask_odd[5 * COLS :] = jnp.zeros((COLS, COLS), jnp.float32)
    results = closure_layers(
        window,
        TALL // 2 - 1,
        STRIP,
        (w_in_ref, w_mid_ref, w_late_ref, w_out_ref),
        (act_a, act_b),
        (mask_odd, mask_even),
    )
    at_lane = lane_index((LEV, COLS))
    for chunk in range(4):
        at = PER * chunk + FIRST // 2
        closure = results[chunk]
        north = side_by_side(1, at - 1)
        upper = side_by_side(0, at)
        lower = side_by_side(1, at)
        south = side_by_side(0, at + 1)
        for parity, value in (
            (0, advance(upper, north, lower, closure[0:LEV])),
            (1, advance(lower, upper, south, closure[LEV : 2 * LEV])),
        ):
            for slot in range(PER):
                row = 2 * (PER * chunk + slot) + parity
                left = pltpu.roll(value, COLS - STRIP * slot - 4, 1)
                shift = (108 - STRIP * slot) % COLS
                right = pltpu.roll(value, shift, 1)
                out_ref[row] = jnp.where(
                    at_lane < HALO,
                    left,
                    jnp.where(at_lane >= COLS - HALO, right, inside_ref[row]),
                )
    plane_lane = lane_index((MID, COLS))
    for index, field in enumerate((KMT, HELM, FORCING)):
        moved = pltpu.roll(rows_ref[FIRST : FIRST + MID, field, :], HALO, 1)
        edge = strips[FIRST : FIRST + MID, field, :]
        planes_ref[index, :, 0:COLS] = jnp.where(plane_lane < HALO, edge, moved)
        planes_ref[index, :, COLS:] = jnp.where(
            plane_lane < HALO,
            moved,
            jnp.where(plane_lane < 2 * HALO, pltpu.roll(edge, COLS - 16, 1), 0.0),
        )


def filter_tables(blocks, width):
    length = blocks * width
    half = LEV // 2
    k = np.arange(blocks)
    outer = np.exp(-2j * np.pi * ((k[:, None] * k[None, :]) % blocks) / blocks)
    spread = np.zeros((blocks, 2, half, blocks, 2, half))
    for line in range(half):
        spread[:, 0, line, :, 0, line] = outer.real
        spread[:, 0, line, :, 1, line] = -outer.imag
        spread[:, 1, line, :, 0, line] = outer.imag
        spread[:, 1, line, :, 1, line] = outer.real
    spread = spread.reshape(blocks * LEV, blocks * LEV)
    m = np.arange(width)
    twist = np.exp(-2j * np.pi * (k[:, None] * m[None, :]) / length)
    sign = np.where(np.arange(LEV) < half, -1.0, 1.0)[None, :, None]
    twist_re = np.broadcast_to(twist.real[:, None, :], (blocks, LEV, width))
    twist_im = twist.imag[:, None, :] * sign
    inner = np.exp(-2j * np.pi * ((m[:, None] * m[None, :]) % width) / width)
    inner = np.concatenate([inner.real, inner.imag], axis=1)
    return [
        np.asarray(t, np.float32)
        for t in (spread, spread.T / length, inner, twist_re, twist_im)
    ]


def halves(x):
    high = x.astype(jnp.bfloat16)
    return high, (x - high.astype(jnp.float32)).astype(jnp.bfloat16)


def split_dot(a, b):
    def dot(x, y):
        return jnp.dot(x, y, preferred_element_type=jnp.float32)

    return dot(a[0], b[0]) + (dot(a[0], b[1]) + dot(a[1], b[0]))


def filter_kernel(
    x_ref, line_ref, spread_ref, spread_low, back_ref, back_low, inner_ref, inner_low,
    twist_re_ref, twist_im_ref, out_ref,
):
    blocks, lev, width = x_ref.shape
    shape = (blocks, lev, width)
    flat = (blocks * lev, width)
    length = blocks * width
    inner = (inner_ref[...], inner_low[...])

    def partner(block):
        return pltpu.roll(block, lev // 2, 1)

    sign = jnp.where(lax.broadcasted_iota(jnp.int32, shape, 1) < lev // 2, -1.0, 1.0)
    y = split_dot((spread_ref[...], spread_low[...]), halves(x_ref[...].reshape(flat)))
    y = y.reshape(shape)
    y = y * twist_re_ref[...] + partner(y) * twist_im_ref[...]
    s = split_dot(halves(y.reshape(flat)), inner)
    s = s[:, 0:width].reshape(shape) + partner(s[:, width:].reshape(shape)) * sign
    wave = lax.broadcasted_iota(jnp.int32, shape, 0) + blocks * lane_index(shape)
    folded = jnp.minimum(wave, length - wave).astype(jnp.float32)
    s = jnp.where(folded < line_ref[0:1, :][None], s, 0.0)
    y = split_dot(halves(s.reshape(flat)), inner)
    y = y[:, 0:width].reshape(shape) - partner(y[:, width:].reshape(shape)) * sign
    y = y * twist_re_ref[...] - partner(y) * twist_im_ref[...]
    x = split_dot((back_ref[...], back_low[...]), halves(y.reshape(flat))).reshape(shape)
    lane = lane_index((lev, width))
    moved = [pltpu.roll(x[block], HALO, 1) for block in range(blocks)]
    for block in range(blocks):
        edge = jnp.where(lane < HALO, moved[block - 1], moved[(block + 1) % blocks])
        edge = jnp.where(lane < 2 * HALO, edge, 0.0)
        edge = pltpu.roll(edge, 0, 1, stride=2 * HALO, stride_axis=0)
        row = BLOCK * block
        out_ref[row : row + lev, :] = x[block]
        out_ref[row + lev : row + BLOCK, :] = jnp.sum(edge, axis=0, keepdims=True)


def ends_kernel(x_ref, far_ref, near_ref):
    even = lax.rem(lax.axis_index("lon"), 2) == 0
    lane = lane_index((LEV, COLS))
    packed = []
    for row in range(MID):
        edge = jnp.where(lane < 2 * HALO, pltpu.roll(x_ref[row], HALO, 1), 0.0)
        edge = pltpu.roll(edge, 0, 1, stride=2 * HALO, stride_axis=0)
        packed.append(jnp.sum(edge, axis=0, keepdims=True))
    packed = jnp.concatenate(packed, axis=0)
    to_east = lax.rem(lane_index((MID, COLS)), 2 * HALO) < HALO
    last = jnp.where(to_east, packed, 0.0)
    first = jnp.where(to_east, 0.0, packed)
    far_ref[...] = jnp.where(even, first, last)
    near_ref[...] = jnp.where(even, last, first)


def plain_kernel(x_ref, far_ref, near_ref, out_ref):
    edge = far_ref[...] + near_ref[...]
    for row in range(MID):
        out_ref[BLOCK * row : BLOCK * row + LEV, :] = x_ref[row]
        out_ref[BLOCK * row + LEV : BLOCK * (row + 1), :] = edge[row : row + 1]


def two_sum(a, b):
    s = a + b
    t = s - a
    return s, (a - (s - t)) + (b - t)


def quick_sum(a, b):
    s = a + b
    return s, b - (s - a)


def split(a):
    c = a * 4097.0
    high = c - (c - a)
    return high, a - high


def two_product(a, b):
    p = a * b
    ah, al = split(a)
    bh, bl = split(b)
    return p, ((ah * bh - p) + ah * bl + al * bh) + al * bl


def pair_add(a, b):
    s, e = two_sum(a[0], b[0])
    return quick_sum(s, e + (a[1] + b[1]))


def pair_neg(a):
    return -a[0], -a[1]


def pair_mul(a, b):
    p, e = two_product(a[0], b[0])
    return quick_sum(p, e + (a[0] * b[1] + a[1] * b[0]))


def pair_inverse(a):
    x = 1.0 / a[0]
    p, e = two_product(a[0], x)
    return quick_sum(x, x * (((1.0 - p) - e) - a[1] * x))


def powers_kernel(x_ref, planes_ref, temp_hbm, powers_ref, parts_ref, temp, sem):
    for level in range(LEV):
        temp[level] = x_ref[pl.ds(HALO * BLOCK + level, ROWS, stride=BLOCK), :]
    move = pltpu.make_async_copy(temp, temp_hbm, sem)
    move.start()
    lane = lane_index((LEV, COLS))
    wide_lane = lane_index((MID, COLS))
    kmt_left = planes_ref[0, :, 0:COLS]
    kmt_right = planes_ref[0, :, COLS:]
    kmt = pltpu.roll(jnp.where(wide_lane < HALO, kmt_right, kmt_left), COLS - HALO, 1)
    mean = jnp.zeros((MID, COLS), jnp.float32)
    for level in range(LEV):
        here = x_ref[pl.ds(level, MID, stride=BLOCK), :]
        mean = mean + jnp.where(kmt > level, here, 0.0)
    edge = x_ref[pl.ds(LEV, MID, stride=BLOCK), :]
    edge_kmt = jnp.where(wide_lane < HALO, kmt_left, kmt_right)
    edge_kmt = jnp.where(wide_lane < 2 * HALO, edge_kmt, 0.0)
    for by in (8, 16, 32, 64):
        edge_kmt = edge_kmt + pltpu.roll(edge_kmt, by, 1)
    edge = jnp.where(edge_kmt > (wide_lane // (2 * HALO)).astype(jnp.float32), edge, 0.0)
    for by in (64, 32, 16, 8):
        edge = edge + pltpu.roll(edge, by, 1)
    moved = pltpu.roll(mean, HALO, 1)
    mean = jnp.concatenate(
        [
            jnp.where(wide_lane < HALO, edge, moved),
            jnp.where(wide_lane < HALO, moved, jnp.where(wide_lane < 2 * HALO, edge, 0.0)),
        ],
        axis=1,
    )
    sea = (planes_ref[0] > 0.0).astype(jnp.float32)

    def around(v):
        return (
            pltpu.roll(v, 1, 0)
            + pltpu.roll(v, MID - 1, 0)
            + pltpu.roll(v, 1, 1)
            + pltpu.roll(v, 2 * COLS - 1, 1)
        )

    diagonal = planes_ref[1] + sea * around(sea)
    powers = [sea * (mean * (1.0 / LEV) + planes_ref[2])]
    for _ in range(ITERS):
        v = powers[-1]
        powers.append((diagonal * v - sea * around(v)) * 0.125)
    for index, v in enumerate(powers):
        powers_ref[index] = v
    row = lax.broadcasted_iota(jnp.int32, (MID, 2 * COLS), 0)
    column = lane_index((MID, 2 * COLS))
    own = (
        (row >= HALO) & (row < HALO + ROWS) & (column >= HALO) & (column < HALO + COLS)
    )
    owned = [jnp.where(own, v, 0.0) for v in powers]
    high_rows, low_rows = [], []
    for order in range(2 * ITERS):
        p, e = two_product(owned[order // 2], owned[order - order // 2])
        tiles = [
            (p[8 * i : 8 * i + 8, 128 * j : 128 * j + 128], e[8 * i : 8 * i + 8, 128 * j : 128 * j + 128])
            for i in range(MID // 8)
            for j in range(2)
        ]
        while len(tiles) > 1:
            tiles = [pair_add(a, b) for a, b in zip(tiles[::2], tiles[1::2])]
        total = tiles[0]
        for by in (4, 2, 1):
            total = pair_add(total, tuple(pltpu.roll(t, by, 0) for t in total))
        high_rows.append(total[0])
        low_rows.append(total[1])
    where = lax.broadcasted_iota(jnp.int32, (8, COLS), 0)
    high, low = high_rows[0], low_rows[0]
    for order in range(1, 2 * ITERS):
        high = jnp.where(where == order, high_rows[order], high)
        low = jnp.where(where == order, low_rows[order], low)
    high, low = high.T, low.T
    tiles = [(high[8 * i : 8 * i + 8], low[8 * i : 8 * i + 8]) for i in range(COLS // 8)]
    while len(tiles) > 1:
        tiles = [pair_add(a, b) for a, b in zip(tiles[::2], tiles[1::2])]
    total = tiles[0]
    for by in (4, 2, 1):
        total = pair_add(total, tuple(pltpu.roll(t, by, 0) for t in total))
    gap = jnp.zeros((1, COLS // 2 - 2 * ITERS), jnp.float32)
    message = jnp.concatenate([total[0][:1], gap, total[1][:1], gap], axis=1)
    parts_ref[...] = jnp.broadcast_to(message, parts_ref.shape)
    move.wait()


def sum_messages(parts_ref):
    count = parts_ref.shape[0] // 8
    tiles = [parts_ref[8 * i : 8 * i + 8, :] for i in range(count)]
    tiles = [two_sum(a, b) for a, b in zip(tiles[::2], tiles[1::2])]
    while len(tiles) > 1:
        tiles = [pair_add(a, b) for a, b in zip(tiles[::2], tiles[1::2])]
    total = tiles[0]
    for by in (4, 2, 1):
        total = pair_add(total, tuple(pltpu.roll(t, by, 0) for t in total))
    return pair_add(total, tuple(pltpu.roll(t, 64, 1) for t in total))


def merge_kernel(parts_ref, out_ref):
    total = sum_messages(parts_ref)
    lane = lane_index((8, COLS))
    merged = jnp.where(lane < 64, total[0], total[1])
    out_ref[...] = jnp.broadcast_to(merged[:1], out_ref.shape)


def combine_kernel(parts_ref, powers_ref, surface_ref, residual_ref, wide):
    total = sum_messages(parts_ref)
    moments = [
        tuple(jnp.broadcast_to(t[:, order : order + 1], (8, COLS)) for t in total)
        for order in range(2 * ITERS)
    ]
    rho = list(moments)
    delta = list(moments)
    one = jnp.ones((8, COLS), jnp.float32)
    zero = jnp.zeros((8, COLS), jnp.float32)
    res = [one] + [zero] * ITERS
    way = [one] + [zero] * ITERS
    sol = [zero] * ITERS
    for step in range(ITERS):
        inverse = pair_inverse(delta[step + 1])
        alpha = pair_mul(rho[step], inverse)
        sol = [s + alpha[0] * w for s, w in zip(sol, way)]
        res = [res[0]] + [r - alpha[0] * w for r, w in zip(res[1:], way)]
        if step == ITERS - 1:
            break
        last = 2 * ITERS - 1 - step
        rho = [
            None if order <= step or order >= last
            else pair_add(rho[order], pair_neg(pair_mul(alpha, delta[order + 1])))
            for order in range(2 * ITERS)
        ]
        beta = pair_neg(pair_mul(rho[step + 1], inverse))
        delta = [
            None if order <= step or order >= last
            else pair_add(rho[order], pair_mul(beta, delta[order]))
            for order in range(2 * ITERS)
        ]
        way = [r + beta[0] * w for r, w in zip(res, way)]
    for weights, target, factor in ((sol, surface_ref, 0.125), (res, residual_ref, 1.0)):
        for i in range(MID // 8):
            for j in range(2):
                spot = (slice(8 * i, 8 * i + 8), slice(128 * j, 128 * j + 128))
                value = weights[0] * powers_ref[(0,) + spot]
                for index in range(1, len(weights)):
                    value = value + weights[index] * powers_ref[(index,) + spot]
                wide[spot] = value * factor
        target[...] = wide[HALO : HALO + ROWS, HALO : HALO + COLS]


def swap_pair():
    return [(i, i ^ 1) for i in range(lax.axis_size("lat"))]


def swap_other(cross):
    pairs = [(i, i + 1) for i in range(3 if cross else 1, lax.axis_size("lat") - 1, 4)]
    return pairs + [(j, i) for i, j in pairs]


def reduction_groups(lon, lat):
    inner, outer = {}, {}
    for i in range(lon):
        for j in range(lat):
            inner.setdefault((i // 4, j // 4), []).append(i * lat + j)
            outer.setdefault((i % 4, j % 4), []).append(i * lat + j)
    return list(inner.values()), list(outer.values())


def swap_near():
    return [(i, i ^ 1) for i in range(lax.axis_size("lon"))]


def swap_far():
    count = lax.axis_size("lon")
    return [(i, (i + 1) % count if i % 2 else (i - 1) % count) for i in range(count)]


def body(temp, kmt, kappa, helm, forcing, cutoff, conv_in, conv_mid, conv_late, conv_out):
    f32 = jnp.float32
    shape = jax.ShapeDtypeStruct
    blocks = lax.axis_size("lon")
    bf16 = jnp.bfloat16
    vmem = pl.BlockSpec(memory_space=pltpu.VMEM)
    cutoff = cutoff.reshape(1, ROWS)
    fields = (temp, kmt, kappa, helm, forcing, cutoff)
    slab = shape((CUT + 1, DEEP, COLS), f32)
    to_pair, to_other, to_cross = pl.pallas_call(
        slab_kernel,
        out_shape=(slab, slab, slab),
        in_specs=[pl.BlockSpec(memory_space=pltpu.HBM)] * 6,
        out_specs=(vmem, vmem, vmem),
        scratch_shapes=(
            pltpu.VMEM((ROWS, COLS), jnp.int32),
            pltpu.VMEM((1, ROWS), jnp.int32),
            pltpu.SemaphoreType.DMA((10,)),
        ),
        compiler_params=pltpu.CompilerParams(vmem_limit_bytes=VMEM_LIMIT),
    )(*(pltpu.with_memory_space_constraint(field, pltpu.HBM) for field in fields))
    other = lax.ppermute(to_other, "lat", swap_other(False))
    pair = lax.ppermute(to_pair, "lat", swap_pair())
    cross = lax.ppermute(to_cross, "lat", swap_other(True))
    tables = tuple(jnp.asarray(table) for table in filter_tables(blocks, COLS))
    sources = (jnp.transpose(conv_in, (0, 2, 1)), conv_mid, conv_late, conv_out) + tables
    own, *raw = fetching(
        rows_kernel,
        (shape((ROWS, FIELDS, COLS), f32),)
        + tuple(shape(source.shape, source.dtype) for source in sources),
        fields + sources,
        fields,
    )
    ends = shape((TALL // SLOTS, FIELDS, COLS), f32)
    rows, to_far, to_near, cuts = call(
        pack_kernel, (shape((TALL, FIELDS, COLS), f32), ends, ends, shape((DEEP, COLS), f32))
    )(own, other, pair, cross)
    far = lax.ppermute(to_far, "lon", swap_far())
    near = lax.ppermute(to_near, "lon", swap_near())

    outs = (
        shape((4 * FIELDS, 640), bf16),
        shape((256, 384), bf16),
        shape((256, 384), bf16),
        shape((48, 256), bf16),
    )
    outs = outs + tuple(shape(table.shape, bf16) for table in tables[:3] for _ in range(2))
    def closure_scratch(chunks):
        cells = chunks * COLS
        return (
            pltpu.VMEM((cells, 128), f32),
            pltpu.VMEM((cells, 128), f32),
            pltpu.VMEM((cells, 128), bf16),
            pltpu.VMEM((cells, 128), bf16),
        )

    block = shape((MID, LEV, COLS), f32)
    inside, line, strips, *prepared = call(
        interior_kernel,
        (block, shape((LEV, COLS), f32), shape((TALL, FIELDS, COLS), f32)) + outs,
        (pltpu.VMEM((TALL * FIELDS, COLS), bf16),) + closure_scratch(19),
        10**9,
    )(rows, cuts, *raw[:7])
    weights, tables = prepared[:4], prepared[4:] + raw[7:]
    lines, planes = call(
        edge_kernel,
        (block, shape((3, MID, 2 * COLS), f32)),
        (pltpu.VMEM((TALL, FIELDS, COLS), f32),) + closure_scratch(6),
    )(rows, far, near, inside, strips, *weights)

    def filtered_block(lines, line, tables):
        whole = lax.all_to_all(lines, "lon", split_axis=0, concat_axis=0, tiled=True)
        result = call(filter_kernel, shape((BLOCK * blocks, COLS), f32))(whole, line, *tables)
        result = result.reshape(BLOCK * blocks, 1, COLS)
        result = lax.all_to_all(result, "lon", split_axis=0, concat_axis=0, tiled=True)
        return result.reshape(BLOCK * blocks, COLS)

    def plain_block(lines, line, tables):
        ends = shape((MID, COLS), f32)
        to_far, to_near = call(ends_kernel, (ends, ends))(lines)
        far = lax.ppermute(to_far, "lon", swap_far())
        near = lax.ppermute(to_near, "lon", swap_near())
        return call(plain_kernel, shape((BLOCK * MID, COLS), f32))(lines, far, near)

    top_row = lax.axis_index("lat") * ROWS - HALO
    polar = (top_row < BAND) | (top_row + MID > ROWS * lax.axis_size("lat") - BAND)
    back = lax.cond(polar, filtered_block, plain_block, lines, line, tables)
    everyone = blocks * lax.axis_size("lat")
    both = ("lon", "lat")
    inner, outer = reduction_groups(blocks, lax.axis_size("lat"))
    wide = len(inner[0])
    temp_new, powers, parts = pl.pallas_call(
        powers_kernel,
        out_shape=(
            shape((LEV, ROWS, COLS), f32),
            shape((ITERS + 1, MID, 2 * COLS), f32),
            shape((wide, COLS), f32),
        ),
        in_specs=[vmem] * 2,
        out_specs=(pl.BlockSpec(memory_space=pltpu.HBM), vmem, vmem),
        scratch_shapes=(pltpu.VMEM((LEV, ROWS, COLS), f32), pltpu.SemaphoreType.DMA),
        compiler_params=pltpu.CompilerParams(vmem_limit_bytes=VMEM_LIMIT),
    )(back, planes)
    parts = lax.all_to_all(
        parts, both, split_axis=0, concat_axis=0, tiled=True, axis_index_groups=inner
    )
    parts = call(merge_kernel, shape((everyone // wide, COLS), f32))(parts)
    parts = lax.all_to_all(
        parts, both, split_axis=0, concat_axis=0, tiled=True, axis_index_groups=outer
    )
    surface, residual = call(
        combine_kernel,
        (shape((ROWS, COLS), f32), shape((ROWS, COLS), f32)),
        (pltpu.VMEM((MID, 2 * COLS), f32),),
    )(parts, powers)
    return temp_new, surface, residual


def solution(mesh):
    return jax.shard_map(
        body,
        mesh=mesh,
        in_specs=(
            P(None, "lat", "lon"),
            P("lat", "lon"),
            P("lat", "lon"),
            P("lat", "lon"),
            P("lat", "lon"),
            P("lat"),
            P(),
            P(),
            P(),
            P(),
        ),
        out_specs=(P(None, "lat", "lon"), P("lat", "lon"), P("lat", "lon")),
        check_vma=False,
    )
```
